32 devices in a mesh: rows: 8 (over z, y), width: 4 (over x, core).
Axes of the slice: x: 2, y: 2, z: 4, core: 2. Of those that a mesh axis runs over, the one named last changes fastest.
Arguments:
- inputs: bfloat16 [16384, 512], P('rows'), may hold values from -6 to 6
- w_first: bfloat16 [8, 512, 256], P('width'), may hold values from -0.25 to 0.25
- w_second: bfloat16 [8, 256, 256], P('width'), may hold values from -0.375 to 0.375
- w_gate: bfloat16 [3, 512, 8], replicated, may hold values from -0.1875 to 0.1875
- w_tower: bfloat16 [3, 256, 128], replicated, may hold values from -0.375 to 0.375
- norm_scale: float32 [3, 128], replicated, may hold values from 0.5 to 1.5
- norm_shift: float32 [3, 128], replicated, may hold values from -1 to 1
- w_head: float32 [3, 128], replicated, may hold values from -1 to 1
- domains: int32 [16384], P(('rows', 'width')), may hold values from 0 to 2
- labels: int32 [16384], P(('rows', 'width')), may hold values 0 or 1
Outputs:
- mean_loss: float32 [], replicated
- grad_inputs: float32 [16384, 512], P(('rows', 'width'))
- grad_first: float32 [8, 512, 256], P('width')
- grad_second: float32 [8, 256, 256], P('width')
- grad_gate: float32 [3, 512, 8], replicated
- grad_tower: float32 [3, 256, 128], replicated
- grad_scale: float32 [3, 128], replicated
- grad_shift: float32 [3, 128], replicated
- grad_head: float32 [3, 128], replicated
The draws below stay inside these ranges and needn't reach their ends.
Inputs may be any that keep to these rules, and one draw needn't show every extreme that they name: `domains`: a domain number.
All inputs are finite; a program needn't handle non-finite values. No bound on the sum of `labels` on one device may be relied on, other than what follows from the above.
Results may differ from the reference program's by a relative error of at most 0.0074.
Values may be sent and summed in bfloat16 or wider, within the bound.
No kernel may reach another device: no remote copies, remote signals or barrier semaphores. Data moves between devices by JAX's collectives and lax.ppermute only.
A program may use at most 64 MiB of HBM per device.

```python
import math
import jax
import jax.numpy as jnp
import numpy as np
from jax import lax

D = 512
H = 256
O = 256
TH = 128
E = 8
K = 3
TOKENS = 16384


def set_ends(drawn, rng, least, top_value):
    longest = drawn.shape.index(max(drawn.shape))
    spots = []
    for shift in (0, 1):
        where = [jax.random.randint(jax.random.fold_in(rng, axis), (), 0, length) for axis, length in enumerate(drawn.shape)]
        where[longest] = (where[longest] + shift) % drawn.shape[longest]
        spots.append(tuple(where))
    return drawn.at[spots[0]].set(least).at[spots[1]].set(top_value)


def block_levels(rng, dims, split, low, top_value):
    def one(position, shards_of):
        heights = jax.random.uniform(jax.random.fold_in(jax.random.fold_in(rng, 6), position), (shards_of,), jnp.float32, low / len(split), top_value / len(split))
        return jnp.repeat(jnp.exp(heights), dims[position] // shards_of).reshape((-1,) + (1,) * (len(dims) - position - 1))

    gain = one(*split[0])
    for cut in split[1:]:
        gain = gain * one(*cut)
    return gain


def rank_bounds(count, slope):
    weights = [(1 << 20) // math.isqrt(grade ** slope) + 1 for grade in range(1, count + 1)]
    spread = 1 + sum(weights) // (1 << 30)
    return np.cumsum(np.array([max(1, weight // spread) for weight in weights]))


def ranked(own_key, extent, number_of, slope):
    grid = rank_bounds(number_of, slope)
    lot = jax.random.randint(jax.random.fold_in(own_key, 1), extent, 0, int(grid[number_of - 1]))
    grade = jnp.searchsorted(jnp.asarray(grid, jnp.int32), lot, side="right")
    return jax.random.permutation(jax.random.fold_in(own_key, 2), number_of)[grade].astype(jnp.int32)


def noise(stream_key, dims, width, bound, split=(), kind=jnp.bfloat16):
    drawn = jax.random.normal(stream_key, dims, jnp.float32) * width
    if len(split) > 0:
        drawn = block_levels(stream_key, dims, split, -0.22, 0.18) * drawn
    return jnp.clip(drawn, min=-bound, max=bound).astype(kind)


def setup_inputs(seed: int = 0) -> dict:
    keys = jax.random.split(jax.random.key(seed), 11)
    inputs = noise(keys[0], (TOKENS, D), 1.0, 6.0, ((0, 8),))
    w_first = noise(keys[1], (E, D, H), D ** -0.5, 0.25, ((0, 4),))
    w_second = noise(keys[2], (E, H, O), H ** -0.5, 0.375, ((0, 4),))
    w_gate = noise(keys[3], (K, D, E), (2 * D) ** -0.5, 0.1875)
    w_tower = noise(keys[4], (K, O, TH), O ** -0.5, 0.375)
    norm_scale = jnp.clip(1.0 + 0.1 * jax.random.normal(keys[5], (K, TH), jnp.float32), 0.5, 1.5)
    norm_shift = noise(keys[6], (K, TH), 0.3, 1.0, (), jnp.float32)
    w_head = noise(keys[7], (K, TH), (TH // 4) ** -0.5, 1.0, (), jnp.float32)
    domains = set_ends(ranked(keys[8], (TOKENS,), K, 2), jax.random.fold_in(keys[8], 3), 0, K - 1).astype(jnp.int32)
    labels = set_ends((jax.random.randint(keys[9], (TOKENS,), 0, 2) < 1).astype(jnp.int32), jax.random.fold_in(keys[9], 1), 0, 1)
    return dict(inputs=inputs, w_first=w_first, w_second=w_second, w_gate=w_gate, w_tower=w_tower, norm_scale=norm_scale, norm_shift=norm_shift, w_head=w_head, domains=domains, labels=labels)


@jax.custom_vjp
def low(v):
    return lax.optimization_barrier(v.astype(jnp.bfloat16)).astype(jnp.float32)

@jax.custom_vjp
def low_back(v):
    return v

def low_keep(v):
    return (low(v), None)

def low_pass(kept, grad):
    return (grad,)

def back_keep(v):
    return (v, None)

def back_low(kept, grad):
    return (low(grad),)
low.defvjp(low_keep, low_pass)
low_back.defvjp(back_keep, back_low)
HIGH = lax.Precision.HIGHEST

def reference(inputs, w_first, w_second, w_gate, w_tower, norm_scale, norm_shift, w_head, domains, labels):
    one_hot = (domains[None, :] == jnp.arange(K, dtype=jnp.int32)[:, None]).astype(jnp.float32)
    target = labels.astype(jnp.float32)

    def forward(features, first, second, gating, tower, scales, shifts, head):
        preact = low_back(jnp.einsum('bd,edh->beh', features, first, precision=HIGH))
        hidden = low(jax.nn.silu(preact))
        expert_vals = low_back(low(jnp.einsum('beh,eho->beo', hidden, second, precision=HIGH)))
        logits = low_back(jnp.einsum('bd,kde->kbe', features, gating, precision=HIGH))
        gate = jax.nn.softmax(logits, axis=-1)
        mixed = low(jnp.einsum('kbe,beo->kbo', gate, expert_vals, precision=HIGH))
        tower_pre = low_back(jnp.einsum('kbo,kot->kbt', mixed, tower, precision=HIGH))
        column_mean = lax.optimization_barrier(jnp.mean(tower_pre, axis=1, keepdims=True))
        variance = lax.optimization_barrier(jnp.mean(jnp.square(tower_pre - column_mean), axis=1, keepdims=True))
        normalized = (tower_pre - column_mean) * lax.rsqrt(variance + 1e-05)
        activated = jax.nn.silu(normalized * scales[:, None, :] + shifts[:, None, :])
        score = lax.optimization_barrier(jnp.sum(activated * head[:, None, :], axis=-1))
        chosen = lax.optimization_barrier(jnp.sum(one_hot * score, axis=0))
        return jnp.mean(jax.nn.softplus(chosen) - target * chosen)
    floats = (inputs.astype(jnp.float32), w_first.astype(jnp.float32), w_second.astype(jnp.float32), w_gate.astype(jnp.float32), w_tower.astype(jnp.float32), norm_scale.astype(jnp.float32), norm_shift.astype(jnp.float32), w_head.astype(jnp.float32))
    mean_loss, pullback = jax.vjp(forward, *floats)
    grads = pullback(jnp.ones_like(mean_loss))
    return (mean_loss, grads[0], grads[1], grads[2], grads[3], grads[4], grads[5], grads[6], grads[7])
```

```python
import jax
import jax.numpy as jnp
from jax import lax
from jax.experimental import pallas as pl
from jax.experimental.pallas import tpu as pltpu
from jax.sharding import PartitionSpec as P

F32 = jnp.float32
BF16 = jnp.bfloat16
EPS = 1e-05
LANE = 128
MIB = 1 << 20
ROWS = "rows"
WIDTH = "width"
BOTH = (ROWS, WIDTH)


def mm(a, b):
    return jnp.dot(a, b, preferred_element_type=F32)


def mm_t(a, b):
    return lax.dot_general(a, b, (((1,), (1,)), ((), ())), preferred_element_type=F32)


def sigmoid(v):
    return 1.0 / (1.0 + jnp.exp(-v))


def call(body, outs, n_in, scratch, name, any_args=(), limit=16):
    vm = pl.BlockSpec(memory_space=pltpu.VMEM)
    anywhere = pl.BlockSpec(memory_space=pl.ANY)
    return pl.pallas_call(
        body,
        out_shape=outs,
        in_specs=[anywhere if i in any_args else vm for i in range(n_in)],
        out_specs=[vm for _ in outs],
        scratch_shapes=scratch,
        compiler_params=pltpu.CompilerParams(vmem_limit_bytes=limit * MIB),
        name=name,
    )


def held(shape, dtype):
    return pltpu.VMEM(shape, dtype)


def plain(shape, dtype):
    return jax.ShapeDtypeStruct(shape, dtype)


def forward(slots, inputs, w1, w2, wgate_t, wtower_t, own):
    ns = len(slots)
    dim = inputs.shape[1]
    epd, _, hid_n = w1[0].shape
    out_n = w2[0].shape[2]
    ce = 2 * epd
    ke = wgate_t.shape[0]
    doms, th, _ = wtower_t.shape
    exps = ke // doms
    tb = min(256, own)

    def body(x_hbm, w1o, w1s, w2o, w2s, wg, wt, hid, slope, vals, gate, mixed, tower, xbuf, w1t, pre, sem):
        w = lax.axis_index(WIDTH)
        copies = []
        for n, s in enumerate(slots):
            block = lax.bitwise_xor(w, 2 * s)
            start = pl.multiple_of(block * own, own)
            cp = pltpu.make_async_copy(x_hbm.at[pl.ds(start, own), :], xbuf.at[n], sem.at[n])
            cp.start()
            copies.append(cp)
        for g, ref in enumerate((w1o, w1s)):
            for i in range(epd):
                e = g * epd + i
                w1t[e * hid_n : (e + 1) * hid_n, :] = ref[i].T
        w1t[ce * hid_n : ce * hid_n + ke, :] = mm(reorder(ke, epd), wg[...]).astype(BF16)
        for n in range(ns):
            copies[n].wait()
            for t in range(own // tb):
                lanes = slice(t * tb, (t + 1) * tb)
                pre[...] = mm_t(w1t[...], xbuf[n, lanes, :])
                logits = pre[ce * hid_n : ce * hid_n + ke, :].reshape(doms, exps, tb)
                top = jnp.exp(logits - jnp.max(logits, axis=1, keepdims=True))
                soft = top / jnp.sum(top, axis=1, keepdims=True)
                gate[n, :, lanes] = soft.reshape(ke, tb)

                def act(i, carry):
                    at = pl.ds(pl.multiple_of(i * 32, 32), 32)
                    v = pre[at, :]
                    s = sigmoid(v)
                    h = v * s
                    hid[n, at, lanes] = h.astype(BF16)
                    slope[n, at, lanes] = (s + h * (1.0 - s)).astype(BF16)
                    return carry

                lax.fori_loop(0, ce * hid_n // 32, act, 0, unroll=4)
                for g, ref in enumerate((w2o, w2s)):
                    for i in range(epd):
                        e = g * epd + i
                        vals[n, e * out_n : (e + 1) * out_n, lanes] = mm(
                            ref[i].T, hid[n, e * hid_n : (e + 1) * hid_n, lanes]
                        ).astype(BF16)
                for u in range(tb // LANE):
                    part = slice(t * tb + u * LANE, t * tb + (u + 1) * LANE)
                    rows = gate_rows(gate, n, part, doms, exps, ce)

                    def mix(i, carry):
                        acc = [None] * doms
                        for e in range(ce):
                            at = pl.ds(pl.multiple_of(e * out_n + i * 32, 32), 32)
                            v = vals[n, at, part].astype(F32)
                            for k in range(doms):
                                term = rows[k][e] * v
                                acc[k] = term if e == 0 else acc[k] + term
                        for k in range(doms):
                            at = pl.ds(pl.multiple_of(k * out_n + i * 32, 32), 32)
                            mixed[n, at, part] = acc[k].astype(BF16)
                        return carry

                    lax.fori_loop(0, out_n // 32, mix, 0, unroll=2)
                for k in range(doms):
                    tower[n, k * th : (k + 1) * th, lanes] = mm(
                        wt[k], mixed[n, k * out_n : (k + 1) * out_n, lanes]
                    ).astype(tower.dtype)

    foreign = slots[0] != 0
    outs = [
        held((ns, ce * hid_n, own), BF16),
        held((ns, ce * hid_n, own), BF16),
        held((ns, ce * out_n, own), BF16),
        held((ns, ke, own), F32),
        held((ns, doms * out_n, own), BF16),
        held((ns, doms * th, own), BF16 if foreign else F32),
    ]
    scratch = [
        pltpu.VMEM((ns, own, dim), BF16),
        pltpu.VMEM((ce * hid_n + ke, dim), BF16),
        pltpu.VMEM((ce * hid_n + ke, tb), F32),
        pltpu.SemaphoreType.DMA((ns,)),
    ]
    name = "forward_foreign" if foreign else "forward_own"
    return call(body, outs, 7, scratch, name, any_args=(0,), limit=24)(
        inputs, w1[0], w1[1], w2[0], w2[1], wgate_t, wtower_t
    )


def gate_rows(gate, n, part, doms, exps, ce):
    return [[gate[n, k * exps + e : k * exps + e + 1, part] for e in range(ce)] for k in range(doms)]


def reorder(ke, epd):
    first = lax.axis_index(WIDTH) * epd
    down = lax.broadcasted_iota(jnp.int32, (ke, ke), 0)
    across = lax.broadcasted_iota(jnp.int32, (ke, ke), 1)
    return jnp.where(lax.bitwise_xor(down, first) == across, 1.0, 0.0).astype(BF16)


def combine(own_part, received, devices):
    _, rows, own = own_part.shape
    doms = rows // LANE

    def body(*refs):
        part, got = refs[0], refs[1 : 1 + len(received)]
        tower, message, cols = refs[1 + len(received) :]
        cols[...] = jnp.zeros_like(cols)
        for k in range(doms):
            at = slice(k * LANE, (k + 1) * LANE)
            total = part[0, at, :]
            for ref in got:
                total = total + ref[0, at, :].astype(F32)
            tower[at, :] = total
            mean = jnp.sum(total, axis=1, keepdims=True) * (1.0 / own)
            dev = total - mean
            cols[:, k : k + 1] = mean
            cols[:, doms + k : doms + k + 1] = jnp.sum(dev * dev, axis=1, keepdims=True)
        tile = cols[...].T[:8, :]
        for d in range(devices):
            message[d * 8 : (d + 1) * 8, :] = tile

    return call(
        body,
        [held((rows, own), F32), plain((devices * 8, LANE), F32)],
        1 + len(received),
        [pltpu.VMEM((LANE, LANE), F32)],
        "combine",
    )(own_part, *received)


def chosen_tower(tower, dom, cols, lanes, doms):
    norm = []
    for k in range(doms):
        at = slice(k * LANE, (k + 1) * LANE)
        norm.append((tower[at, lanes] - cols[:, k : k + 1]) * cols[:, doms + k : doms + k + 1])

    def pick(values):
        got = values[doms - 1]
        for k in range(doms - 2, -1, -1):
            got = jnp.where(dom == k, values[k], got)
        return got

    shape = norm[0].shape
    scale, shift, head = (
        pick([jnp.broadcast_to(cols[:, j * doms + k : j * doms + k + 1], shape) for k in range(doms)])
        for j in (2, 3, 4)
    )
    own = pick(norm)
    return norm, own, own * scale + shift, head


def normalise(stats, tower, marks, scale, shift, head, devices, count):
    rows, own = tower.shape
    doms = rows // LANE

    def body(st, tw, mk, sc, sh, hd, cols, message, prm, q):
        got = st[...].reshape(devices, 8, LANE)
        total = jnp.sum(got, axis=0)
        mean = total * (1.0 / devices)
        dev = got - mean[None]
        spread = jnp.sum(dev * dev, axis=0) * float(own)
        var = (total[doms : 2 * doms] + spread[:doms]) * (1.0 / count)
        prm[...] = jnp.zeros_like(prm)
        prm[0:doms, :] = mean[:doms]
        prm[doms : 2 * doms, :] = lax.rsqrt(var + EPS)
        prm[2 * doms : 3 * doms, :] = sc[...]
        prm[3 * doms : 4 * doms, :] = sh[...]
        prm[4 * doms : 5 * doms, :] = hd[...]
        cols[...] = prm[...].T
        loss = jnp.zeros((1, LANE), F32)
        for u in range(own // LANE):
            part = slice(u * LANE, (u + 1) * LANE)
            dom = mk[0:1, part]
            target = mk[1:2, part].astype(F32)
            _, own_norm, affine, head_w = chosen_tower(tw, dom, cols, part, doms)
            s = sigmoid(affine)
            act = affine * s
            chosen = jnp.sum(act * head_w, axis=0, keepdims=True)
            soft = jnp.maximum(chosen, 0.0) + jnp.log(1.0 + jnp.exp(-jnp.abs(chosen)))
            loss = loss + (soft - target * chosen)
            score_grad = (sigmoid(chosen) - target) * (1.0 / count)
            grad = score_grad * head_w * (s + act * (1.0 - s))
            q[0, :, part] = grad
            q[1, :, part] = grad * own_norm
            q[2, :, part] = score_grad * act
        kinds = lax.broadcasted_iota(jnp.int32, (8, own), 0)
        one_hot = (kinds == mk[0:1, :]).astype(F32)
        tile = [
            lax.dot_general(
                one_hot,
                q[j],
                (((1,), (1,)), ((), ())),
                preferred_element_type=F32,
                precision=lax.Precision.HIGHEST,
            )[:doms]
            for j in range(3)
        ]
        rest = jnp.zeros((16 - 3 * doms - 1, LANE), F32)
        whole = jnp.concatenate(tile + [loss, rest], axis=0)
        for d in range(devices):
            message[d * 16 : (d + 1) * 16, :] = whole

    return call(
        body,
        [held((LANE, LANE), F32), plain((devices * 16, LANE), F32)],
        6,
        [pltpu.VMEM((LANE, LANE), F32), pltpu.VMEM((3, LANE, own), F32)],
        "normalise",
    )(stats, tower, marks, scale, shift, head)


def backward(sums, cols, towers, marks, acts, inputs, w1, w2, wgate, wtower, own, devices, rows_n, count):
    ns = len(towers)
    dim = inputs.shape[1]
    epd, _, hid_n = w1[0].shape
    out_n = w2[0].shape[2]
    ce = 2 * epd
    ke = wgate.shape[1]
    doms, _, th = wtower.shape
    exps = ke // doms
    groups, index = [], []
    for arrays, n in acts:
        if not any(arrays is g for g in groups):
            groups.append(arrays)
        index.append(([arrays is g for g in groups].index(True), n))
    n_groups = len(groups)
    sec_rows = epd * (out_n // LANE) * hid_n
    first_rows = (dim // LANE) * hid_n
    tg_rows = doms * out_n + (dim // LANE) * 32
    per = -(-tg_rows // (16 * devices)) * 16
    n_width = devices // rows_n

    def body(*refs):
        refs = list(refs)
        take = lambda n: [refs.pop(0) for _ in range(n)]
        (sm, cl) = take(2)
        tw = take(ns)
        mk = take(ns)
        act = [take(5) for _ in range(n_groups)]
        x_hbm, w1o, w1s, w2o, w2s, wg, wt = take(7)
        gi_own, gi_out, small, loss_out, tgp, sec_own, sec_sib = take(7)
        first_own, first_sib = take(epd), take(epd)
        xbuf, w1c, tg, mg, eg, pg, lg, gg, sacc, facc, tacc, gacc, tgf, srow, prm, col2, sem = refs
        w = lax.axis_index(WIDTH)
        r = lax.axis_index(ROWS)
        copies = []
        for n in range(ns):
            block = lax.bitwise_xor(w, 2 * n)
            start = pl.multiple_of(block * own, own)
            cp = pltpu.make_async_copy(x_hbm.at[pl.ds(start, own), :], xbuf.at[n], sem.at[n])
            cp.start()
            copies.append(cp)
        total = jnp.sum(sm[...].reshape(devices, 16, LANE), axis=0)
        small[...] = total
        loss_out[...] = jnp.sum(total[3 * doms : 3 * doms + 1, :], axis=1, keepdims=True) * (1.0 / count)
        prm[...] = jnp.zeros_like(prm)
        prm[0:16, :] = total * (1.0 / count)
        col2[...] = prm[...].T
        for g, ref in enumerate((w1o, w1s)):
            for i in range(epd):
                e = g * epd + i
                w1c[:, e * hid_n : (e + 1) * hid_n] = ref[i]
        w1c[:, ce * hid_n :] = jnp.zeros((dim, LANE), BF16)
        w1c[:, ce * hid_n : ce * hid_n + ke] = wg[...]
        pg[ce * hid_n :, :] = jnp.zeros((LANE, own), BF16)
        for n in range(ns):
            hid, slope, vals, gate, mixed = act[index[n][0]]
            m = index[n][1]
            for u in range(own // LANE):
                part = slice(u * LANE, (u + 1) * LANE)
                dom = mk[n][0:1, part]
                target = mk[n][1:2, part].astype(F32)
                norm, own_norm, affine, head_w = chosen_tower(tw[n], dom, cl, part, doms)
                s = sigmoid(affine)
                a = affine * s
                chosen = jnp.sum(a * head_w, axis=0, keepdims=True)
                score_grad = (sigmoid(chosen) - target) * (1.0 / count)
                grad = score_grad * head_w * (s + a * (1.0 - s))
                for k in range(doms):
                    lead = cl[:, 2 * doms + k : 2 * doms + k + 1] * cl[:, doms + k : doms + k + 1]
                    g_k = jnp.where(dom == k, grad, 0.0)
                    v = lead * (g_k - col2[:, k : k + 1] - norm[k] * col2[:, doms + k : doms + k + 1])
                    low = v.astype(BF16)
                    at = slice(k * th, (k + 1) * th)
                    tg[at, part] = low
                    srow[k : k + 1, part] = jnp.sum(low.astype(F32) * tw[n][at, part], axis=0, keepdims=True)
            for k in range(doms):
                mg[k * out_n : (k + 1) * out_n, :] = mm(wt[k], tg[k * th : (k + 1) * th, :])
                part_t = mm_t(mixed[m, k * out_n : (k + 1) * out_n, :], tg[k * th : (k + 1) * th, :])
                if n == 0:
                    tacc[k] = part_t
                else:
                    tacc[k] += part_t
            gg[...] = jnp.zeros_like(gg)
            for u in range(own // LANE):
                part = slice(u * LANE, (u + 1) * LANE)
                rows = gate_rows(gate, m, part, doms, exps, ce)

                def spread(i, acc):
                    up = [mg[pl.ds(pl.multiple_of(k * out_n + i * 16, 16), 16), part] for k in range(doms)]
                    acc = list(acc)
                    for e in range(ce):
                        at = pl.ds(pl.multiple_of(e * out_n + i * 16, 16), 16)
                        v = vals[m, at, part].astype(F32)
                        back = None
                        for k in range(doms):
                            term = rows[k][e] * up[k]
                            back = term if k == 0 else back + term
                            prod = up[k] * v
                            acc[k * ce + e] = acc[k * ce + e] + (prod[:8] + prod[8:])
                        eg[at, part] = back.astype(BF16)
                    return tuple(acc)

                acc = lax.fori_loop(
                    0, out_n // 16, spread, tuple(jnp.zeros((8, LANE), F32) for _ in range(doms * ce)), unroll=2
                )
                for k in range(doms):
                    for e in range(ce):
                        dot = jnp.sum(acc[k * ce + e], axis=0, keepdims=True)
                        gg[k * exps + e : k * exps + e + 1, part] = rows[k][e] * (dot - srow[k : k + 1, part])
            lg[...] = mm(reorder(ke, epd), gg[...].astype(BF16)).astype(BF16)
            pg[ce * hid_n : ce * hid_n + ke, :] = lg[...]
            for g, ref in enumerate((w2o, w2s)):
                for i in range(epd):
                    e = g * epd + i
                    at = slice(e * hid_n, (e + 1) * hid_n)
                    at_o = slice(e * out_n, (e + 1) * out_n)
                    for u in range(own // min(256, own)):
                        part = slice(u * 256, (u + 1) * 256)
                        pg[at, part] = (mm(ref[i], eg[at_o, part]) * slope[m, at, part].astype(F32)).astype(BF16)
                    part_s = mm_t(hid[m, at, :], eg[at_o, :])
                    if n == 0:
                        sacc[e] = part_s
                    else:
                        sacc[e] += part_s
            copies[n].wait()
            part_f = mm(pg[: ce * hid_n, :], xbuf[n])
            part_g = mm(lg[...], xbuf[n])
            if n == 0:
                facc[...] = part_f
                gacc[...] = part_g
            else:
                facc[...] += part_f
                gacc[...] += part_g
            gi = mm(w1c[...], pg[...])
            if n == 0:
                gi_own[...] = gi
            else:
                gi_out[n - 1] = gi.astype(BF16)

        def place(ref, size, flat, piece):
            count_r = piece.shape[0]
            step = min(size, count_r)
            for off in range(0, count_r, step):
                j, o = divmod(flat + off, size)
                ref[lax.bitwise_xor(r, j), o : o + step, :] = piece[off : off + step, :].astype(ref.dtype)

        for g, ref in enumerate((sec_own, sec_sib)):
            size = sec_rows // rows_n
            for i in range(epd):
                for q in range(out_n // LANE):
                    flat = (i * (out_n // LANE) + q) * hid_n
                    place(ref, size, flat, sacc[g * epd + i, :, q * LANE : (q + 1) * LANE])
        for g, group in enumerate((first_own, first_sib)):
            size = first_rows // rows_n
            for i in range(epd):
                base = (g * epd + i) * hid_n
                for q in range(dim // LANE):
                    place(group[i], size, q * hid_n, facc[base : base + hid_n, q * LANE : (q + 1) * LANE])
        tgf[...] = jnp.zeros_like(tgf)
        for k in range(doms):
            tgf[k * out_n : (k + 1) * out_n, :] = tacc[k]
        for q in range(dim // LANE):
            tgf[doms * out_n + q * 32 : doms * out_n + q * 32 + ke, :] = gacc[:, q * LANE : (q + 1) * LANE]
        for a in range(n_width):
            for b in range(rows_n):
                base = (a * rows_n + b) * per
                tgp[lax.bitwise_xor(w, a), lax.bitwise_xor(r, b), :, :] = tgf[base : base + per, :].astype(BF16)

    outs = [
        held((dim, own), F32),
        plain((ns - 1, dim, own), BF16),
        plain((16, LANE), F32),
        plain((1, 1), F32),
        plain((n_width, rows_n, per, LANE), BF16),
        plain((rows_n, sec_rows // rows_n, LANE), F32),
        plain((rows_n, sec_rows // rows_n, LANE), BF16),
    ]
    outs += [plain((rows_n, first_rows // rows_n, LANE), F32) for _ in range(epd)]
    outs += [plain((rows_n, first_rows // rows_n, LANE), BF16) for _ in range(epd)]
    scratch = [
        pltpu.VMEM((ns, own, dim), BF16),
        pltpu.VMEM((dim, ce * hid_n + LANE), BF16),
        pltpu.VMEM((doms * th, own), BF16),
        pltpu.VMEM((doms * out_n, own), F32),
        pltpu.VMEM((ce * out_n, own), BF16),
        pltpu.VMEM((ce * hid_n + LANE, own), BF16),
        pltpu.VMEM((ke, own), BF16),
        pltpu.VMEM((ke, own), F32),
        pltpu.VMEM((ce, hid_n, out_n), F32),
        pltpu.VMEM((ce * hid_n, dim), F32),
        pltpu.VMEM((doms, out_n, th), F32),
        pltpu.VMEM((ke, dim), F32),
        pltpu.VMEM((devices * per, LANE), F32),
        pltpu.VMEM((8, own), F32),
        pltpu.VMEM((LANE, LANE), F32),
        pltpu.VMEM((LANE, LANE), F32),
        pltpu.SemaphoreType.DMA((ns,)),
    ]
    args = [sums, cols] + list(towers) + list(marks)
    for g in groups:
        args += list(g)
    spot = len(args)
    args += [inputs, w1[0], w1[1], w2[0], w2[1], wgate, wtower]
    return call(body, outs, len(args), scratch, "backward", any_args=(spot,), limit=36)(*args)


def finish_inputs(own_part, received):
    dim, own = own_part.shape

    def body(*refs):
        part, got, out = refs[0], refs[1:-1], refs[-1]
        for u in range(own // LANE):
            lanes = slice(u * LANE, (u + 1) * LANE)
            total = part[:, lanes]
            for ref in got:
                total = total + ref[:, lanes].astype(F32)
            out[lanes, :] = total.T

    return call(body, [plain((own, dim), F32)], 1 + len(received), [], "finish_inputs")(own_part, *received)[0]


def finish_weights(second, first, epd, hid_n, out_n, dim, rows_n):
    def body(*refs):
        sec, fir = refs[0], refs[1 : 1 + epd]
        out_f, out_s = refs[1 + epd : 3 + epd]
        buf = refs[3 + epd]
        r = lax.axis_index(ROWS)

        def fetch(ref, flat, count_r):
            size = ref.shape[1]
            step = min(size, count_r)
            got = []
            for off in range(0, count_r, step):
                j, o = divmod(flat + off, size)
                got.append(ref[lax.bitwise_xor(r, j), o : o + step, :].astype(F32))
            return got, step

        for i in range(epd):
            for q in range(out_n // LANE):
                got, step = fetch(sec, (i * (out_n // LANE) + q) * hid_n, hid_n)
                for n, piece in enumerate(got):
                    out_s[i, n * step : (n + 1) * step, q * LANE : (q + 1) * LANE] = piece
            for q in range(dim // LANE):
                got, step = fetch(fir[i], q * hid_n, hid_n)
                for n, piece in enumerate(got):
                    buf[n * step : (n + 1) * step, :] = piece
                out_f[i, q * LANE : (q + 1) * LANE, :] = buf[...].T

    return call(
        body,
        [plain((epd, dim, hid_n), F32), plain((epd, hid_n, out_n), F32)],
        1 + epd,
        [pltpu.VMEM((hid_n, LANE), F32)],
        "finish_weights",
    )(second, *first)


def swap(value, axis, mask):
    size = lax.axis_size(axis)
    return lax.ppermute(value, axis, [(i, i ^ mask) for i in range(size)])


def fold(value, axis):
    size = lax.axis_size(axis)
    mask = 1
    while mask < size:
        halves = value.reshape((value.shape[0] // 2, 2) + value.shape[1:])
        got = swap(halves[:, 1].astype(BF16), axis, mask)
        value = halves[:, 0].astype(F32) + got.astype(F32)
        mask *= 2
    return value[0]


def unfold(value, axis):
    size = lax.axis_size(axis)
    value = value[None]
    mask = size // 2
    while mask:
        got = swap(value, axis, mask)
        value = jnp.stack([value, got], axis=1).reshape((-1,) + value.shape[1:])
        mask //= 2
    return value


def local(inputs, w_first, w_second, w_gate, w_tower, norm_scale, norm_shift, w_head, domains, labels):
    n_width, n_rows = lax.axis_size(WIDTH), lax.axis_size(ROWS)
    devices = n_width * n_rows
    own = inputs.shape[0] // n_width
    count = float(own * devices)
    dim = inputs.shape[1]
    epd, _, hid_n = w_first.shape
    out_n = w_second.shape[2]
    doms, _, exps = w_gate.shape
    ke = doms * exps
    n_x = n_width // 2
    w1 = (w_first, swap(w_first, WIDTH, 1))
    w2 = (w_second, swap(w_second, WIDTH, 1))
    wgate_t = jnp.transpose(w_gate, (0, 2, 1)).reshape(ke, dim)
    wgate = jnp.transpose(w_gate, (1, 0, 2)).reshape(dim, ke)
    wtower_t = jnp.transpose(w_tower, (0, 2, 1))
    marks = [jnp.stack([domains, labels])]
    marks += [swap(marks[0], WIDTH, 2 * s) for s in range(1, n_x)]

    foreign = forward(list(range(1, n_x)), inputs, w1, w2, wgate_t, wtower_t, own)
    sent = [swap(foreign[5][s - 1 : s], WIDTH, 2 * s) for s in range(1, n_x)]
    mine = forward([0], inputs, w1, w2, wgate_t, wtower_t, own)
    tower, message = combine(mine[5], sent, devices)
    stats = lax.all_to_all(message, BOTH, 0, 0, tiled=True)
    towers = [tower] + [swap(tower, WIDTH, 2 * s) for s in range(1, n_x)]
    cols, message = normalise(stats, tower, marks[0], norm_scale, norm_shift, w_head, devices, count)
    sums = lax.all_to_all(message, BOTH, 0, 0, tiled=True)

    acts = [(mine[:5], 0)] + [(foreign[:5], s - 1) for s in range(1, n_x)]
    got = backward(
        sums, cols, towers, marks, acts, inputs, w1, w2, wgate, w_tower, own, devices, n_rows, count
    )
    gi_own, gi_out, small, loss, tgp, sec_own, sec_sib = got[:7]
    first_own, first_sib = got[7 : 7 + epd], got[7 + epd :]

    second = sec_own + swap(sec_sib, WIDTH, 1).astype(F32)
    first = [a + swap(b, WIDTH, 1).astype(F32) for a, b in zip(first_own, first_sib)]
    tg = fold(tgp, WIDTH)
    tg, second = fold(tg, ROWS), fold(second, ROWS)
    first = [fold(v, ROWS) for v in first]
    received = [swap(gi_out[s - 1], WIDTH, 2 * s) for s in range(1, n_x)]
    grad_inputs = finish_inputs(gi_own, received)
    tg = unfold(tg.astype(BF16), ROWS)
    second = unfold(second.astype(BF16), ROWS)
    first = [unfold(v.astype(BF16), ROWS) for v in first]
    grad_first, grad_second = finish_weights(second, first, epd, hid_n, out_n, dim, n_rows)
    tg = unfold(tg, WIDTH)
    order_w = lax.axis_index(WIDTH) ^ jnp.arange(n_width)
    order_r = lax.axis_index(ROWS) ^ jnp.arange(n_rows)
    tg = tg[order_w][:, order_r].reshape(-1, LANE).astype(F32)
    grad_tower = tg[: doms * out_n].reshape(doms, out_n, LANE)
    gates = tg[doms * out_n : doms * out_n + (dim // LANE) * 32].reshape(dim // LANE, 32, LANE)[:, :ke]
    grad_gate = gates.reshape(dim // LANE, doms, exps, LANE).transpose(1, 0, 3, 2).reshape(doms, dim, exps)
    return (
        loss[0, 0],
        grad_inputs,
        grad_first,
        grad_second,
        grad_gate,
        grad_tower,
        small[doms : 2 * doms],
        small[:doms],
        small[2 * doms : 3 * doms],
    )


def solution(mesh):
    placed = (
        P(ROWS, None),
        P(WIDTH, None, None),
        P(WIDTH, None, None),
        P(),
        P(),
        P(),
        P(),
        P(),
        P(BOTH),
        P(BOTH),
    )
    return jax.shard_map(
        local,
        mesh=mesh,
        in_specs=placed,
        out_specs=(
            P(),
            P(BOTH, None),
            P(WIDTH, None, None),
            P(WIDTH, None, None),
            P(),
            P(),
            P(),
            P(),
            P(),
        ),
        check_vma=False,
    )
```

```python
import math

import jax
import jax.numpy as jnp
from jax import lax
from jax.experimental import pallas as pl
from jax.experimental.pallas import tpu as pltpu
from jax.sharding import PartitionSpec as P

F32 = jnp.float32
BF16 = jnp.bfloat16
EPS = 1e-05
LANE = 128
MIB = 1 << 20
ROWS = "rows"
WIDTH = "width"
BOTH = (ROWS, WIDTH)


def mm(a, b):
    return jnp.dot(a, b, preferred_element_type=F32)


def mm_t(a, b, precision=None):
    return lax.dot_general(a, b, (((1,), (1,)), ((), ())), preferred_element_type=F32, precision=precision)


def sigmoid(v):
    return 0.5 * jnp.tanh(0.5 * v) + 0.5


class Source:
    def __init__(self, buf, copies):
        self.buf = buf
        self.waiting = copies
        for copy in copies:
            copy.start()

    def get(self):
        for copy in self.waiting:
            copy.wait()
        self.waiting = []
        return self.buf


class Target:
    def __init__(self, ref, buf, sems):
        self.ref, self.buf, self.sems = ref, buf, sems
        self.waiting = []

    def flush(self, *at):
        if self.ref is None:
            return
        src = self.buf.at[at] if at else self.buf
        dst = self.ref.at[at] if at else self.ref
        copy = pltpu.make_async_copy(src, dst, next(self.sems))
        copy.start()
        self.waiting.append(copy)


class Near:
    def __init__(self, what):
        self.what = what


class Far:
    def __init__(self, arrays, shape=None, pairs=None):
        self.arrays = arrays if isinstance(arrays, (list, tuple)) else [arrays]
        self.shape = shape or self.arrays[0].shape
        self.dtype = self.arrays[0].dtype
        self.pairs = pairs or (lambda refs, buf: [(refs[0], buf)])


def staged(body, ins, outs, scratch, name, limit, n_sems=64):
    far_in = [i for i, s in enumerate(ins) if isinstance(s, Far)]
    far_out = [i for i, s in enumerate(outs) if not isinstance(s, Near)]
    args, specs, spans = [], [], []
    hbm = pl.BlockSpec(memory_space=pltpu.HBM)
    vmem = pl.BlockSpec(memory_space=pltpu.VMEM)
    for s in ins:
        if isinstance(s, Far):
            spans.append((len(args), len(args) + len(s.arrays)))
            args += [pltpu.with_memory_space_constraint(a, pltpu.HBM) for a in s.arrays]
            specs += [hbm] * len(s.arrays)
        else:
            spans.append((len(args), len(args) + 1))
            args.append(s.what)
            specs.append(vmem)
    n_in, n_out = len(args), len(outs)

    def kernel(*refs):
        refs_in, refs_out = refs[:n_in], refs[n_in : n_in + n_out]
        bufs = refs[n_in + n_out :]
        in_bufs = dict(zip(far_in, bufs))
        out_bufs = dict(zip(far_out, bufs[len(far_in) :]))
        rest = bufs[len(far_in) + len(far_out) : -1]
        sems = iter([bufs[-1].at[i] for i in range(n_sems)])
        sources = []
        for i, (start, stop) in enumerate(spans):
            if i in in_bufs:
                pairs = ins[i].pairs(refs_in[start:stop], in_bufs[i])
                sources.append(Source(in_bufs[i], [pltpu.make_async_copy(a, b, next(sems)) for a, b in pairs]))
            else:
                sources.append(Source(refs_in[start], []))
        targets = []
        for i, ref in enumerate(refs_out):
            targets.append(Target(ref, out_bufs[i], sems) if i in out_bufs else Target(None, ref, sems))
        body(sources, targets, *rest)
        for s in sources:
            s.get()
        for t in targets:
            for copy in t.waiting:
                copy.wait()

    return pl.pallas_call(
        kernel,
        out_shape=[o.what if isinstance(o, Near) else pltpu.HBM(o.shape, o.dtype) for o in outs],
        in_specs=specs,
        out_specs=[hbm if i in far_out else vmem for i in range(n_out)],
        scratch_shapes=[pltpu.VMEM(ins[i].shape, ins[i].dtype) for i in far_in]
        + [pltpu.VMEM(outs[i].shape, outs[i].dtype) for i in far_out]
        + list(scratch)
        + [pltpu.SemaphoreType.DMA((n_sems,))],
        compiler_params=pltpu.CompilerParams(vmem_limit_bytes=limit * MIB),
        name=name,
    )(*args)


def plain(shape, dtype):
    return jax.ShapeDtypeStruct(shape, dtype)


def row_blocks(slots, own):
    def pairs(refs, buf):
        w = lax.axis_index(WIDTH)
        got = []
        for n, s in enumerate(slots):
            start = pl.multiple_of(lax.bitwise_xor(w, 2 * s) * own, own)
            got.append((refs[0].at[pl.ds(start, own), :], buf.at[n * own : (n + 1) * own, :]))
        return got

    return pairs


def reorder(ke, epd):
    first = lax.axis_index(WIDTH) * epd
    down = lax.broadcasted_iota(jnp.int32, (ke, ke), 0)
    across = lax.broadcasted_iota(jnp.int32, (ke, ke), 1)
    return jnp.where(lax.bitwise_xor(down, first) == across, 1.0, 0.0).astype(BF16)


def forward(slots, inputs, w1, w2, wgate_t, wtower, own, keep, send, name):
    ns = len(slots)
    dim = inputs.shape[1]
    epd, _, hid_n = w1[0].shape
    out_n = w2[0].shape[2]
    ce = 2 * epd
    ke = wgate_t.shape[0]
    doms, _, th = wtower.shape
    exps = ke // doms

    def body(ins, outs, w1t, w2t, wt, pre, *bufs):
        xs, w1o, w1s, w2o, w2s, wgs, wts = ins
        if keep:
            hid, slope, vals, gate, mixed = (o.buf for o in outs[:5])
        else:
            hid, vals, gate, mixed = bufs
        x = xs.get()
        for g, src in enumerate((w1o, w1s)):
            ref = src.get()
            for i in range(epd):
                e = g * epd + i
                w1t[e * hid_n : (e + 1) * hid_n, :] = ref[i].T
        w1t[ce * hid_n : ce * hid_n + ke, :] = mm(reorder(ke, epd), wgs.get()[...]).astype(BF16)
        for n in range(ns):
            pre[...] = mm_t(w1t[...], x[n * own : (n + 1) * own, :])
            if n == 0:
                for g, src in enumerate((w2o, w2s)):
                    ref = src.get()
                    for i in range(epd):
                        w2t[g * epd + i] = ref[i].T
                ref = wts.get()
                for k in range(doms):
                    wt[k] = ref[k].T
            logits = pre[ce * hid_n : ce * hid_n + ke, :].reshape(doms, exps, own)
            top = jnp.exp(logits - jnp.max(logits, axis=1, keepdims=True))
            soft = top / jnp.sum(top, axis=1, keepdims=True)
            gate[n] = soft.reshape(ke, own)

            def act(i, carry):
                at = pl.ds(pl.multiple_of(i * 16, 16), 16)
                v = pre[at, :]
                s = sigmoid(v)
                h = v * s
                hid[n, at, :] = h.astype(BF16)
                if keep:
                    slope[n, at, :] = (s + h * (1.0 - s)).astype(BF16)
                return carry

            lax.fori_loop(0, ce * hid_n // 16, act, 0, unroll=4)
            for e in range(ce):
                vals[n, e * out_n : (e + 1) * out_n, :] = mm(
                    w2t[e], hid[n, e * hid_n : (e + 1) * hid_n, :]
                ).astype(BF16)
            if keep:
                for o in outs[:4]:
                    o.flush(n)
            for u in range(own // LANE):
                part = slice(u * LANE, (u + 1) * LANE)
                rows = [[gate[n, k * exps + e : k * exps + e + 1, part] for e in range(ce)] for k in range(doms)]

                def mix(i, carry):
                    acc = [None] * doms
                    for e in range(ce):
                        at = pl.ds(pl.multiple_of(e * out_n + i * 32, 32), 32)
                        v = vals[n, at, part].astype(F32)
                        for k in range(doms):
                            term = rows[k][e] * v
                            acc[k] = term if e == 0 else acc[k] + term
                    for k in range(doms):
                        at = pl.ds(pl.multiple_of(k * out_n + i * 32, 32), 32)
                        mixed[n, at, part] = acc[k].astype(BF16)
                    return carry

                lax.fori_loop(0, out_n // 32, mix, 0, unroll=4)
            if keep:
                outs[4].flush(n)
            if send is not None:
                tower = outs[-1]
                for k in range(doms):
                    tower.buf[n, k * th : (k + 1) * th, :] = mm(
                        wt[k], mixed[n, k * out_n : (k + 1) * out_n, :]
                    ).astype(send)
                tower.flush(n)

    kept = [
        plain((ns, ce * hid_n, own), BF16),
        plain((ns, ce * hid_n, own), BF16),
        plain((ns, ce * out_n, own), BF16),
        plain((ns, ke, own), F32),
        plain((ns, doms * out_n, own), BF16),
    ]
    outs = list(kept) if keep else []
    if send is not None:
        outs.append(plain((ns, doms * th, own), send))
    scratch = [
        pltpu.VMEM((ce * hid_n + ke, dim), BF16),
        pltpu.VMEM((ce, out_n, hid_n), BF16),
        pltpu.VMEM((doms, th, out_n), BF16),
        pltpu.VMEM((ce * hid_n + ke, own), F32),
    ]
    if not keep:
        scratch += [pltpu.VMEM(kept[i].shape, kept[i].dtype) for i in (0, 2, 3, 4)]
    ins = [Far(inputs, (ns * own, dim), row_blocks(slots, own))]
    ins += [Far(a) for a in (w1[0], w1[1], w2[0], w2[1], wgate_t, wtower)]
    return staged(body, ins, outs, scratch, name, 40)


def combine(own_part, received, marks, devices):
    _, rows, own = own_part.shape
    doms = rows // LANE

    def body(ins, outs, cols):
        part = ins[0].get()
        got = [s.get() for s in ins[2:]]
        tower, low, message = (o.buf for o in outs)
        cols[...] = jnp.zeros_like(cols)
        for k in range(doms):
            at = slice(k * LANE, (k + 1) * LANE)
            total = part[0, at, :]
            for ref in got:
                total = total + ref[0, at, :].astype(F32)
            tower[at, :] = total
            low[at, :] = total.astype(BF16)
            mean = jnp.sum(total, axis=1, keepdims=True) * (1.0 / own)
            dev = total - mean
            cols[:, k : k + 1] = mean
            cols[:, doms + k : doms + k + 1] = jnp.sum(dev * dev, axis=1, keepdims=True)
        outs[0].flush()
        pair = jnp.concatenate([ins[1].get()[...].astype(F32), jnp.zeros((14, own), F32)], axis=0)
        low[rows:, :] = pair.astype(BF16)
        outs[1].flush()
        tile = cols[...].T[:8, :]
        for d in range(devices):
            message[d * 8 : (d + 1) * 8, :] = tile
        outs[2].flush()

    return staged(
        body,
        [Far(own_part), Far(marks)] + [Near(v) for v in received],
        [plain((rows, own), F32), plain((rows + 16, own), BF16), Near(plain((devices * 8, LANE), F32))],
        [pltpu.VMEM((LANE, LANE), F32)],
        "combine",
        16,
    )


def pick(dom, values):
    got = values[-1]
    for k in range(len(values) - 2, -1, -1):
        got = jnp.where(dom == k, values[k], got)
    return got


def chosen_tower(tower, dom, wide, lanes, doms):
    values = [tower[k * LANE : (k + 1) * LANE, lanes].astype(F32) for k in range(doms)]
    mean, gain, shift, head = (pick(dom, [wide[j * doms + k] for k in range(doms)]) for j in range(4))
    centred = pick(dom, values) - mean
    return values, centred, centred * gain + shift, gain, head


def spread_columns(wide, rows_ref, n):
    cols = rows_ref[...].T
    for j in range(n):
        wide[j] = jnp.broadcast_to(cols[:, j : j + 1], (LANE, LANE))


def normalise(stats, tower, marks, scale, shift, head, devices, count):
    rows, own = tower.shape
    doms = rows // LANE

    def body(ins, outs, prm, wide, q):
        st, tws, mks, sc, sh, hd = ins
        params, message = (o.buf for o in outs)
        prm[...] = jnp.zeros_like(prm)
        got = st.get()[...].reshape(devices, 8, LANE)
        total = jnp.sum(got, axis=0)
        mean = total * (1.0 / devices)
        dev = got - mean[None]
        spread = jnp.sum(dev * dev, axis=0) * float(own)
        var = (total[doms : 2 * doms] + spread[:doms]) * (1.0 / count)
        inv = lax.rsqrt(var + EPS)
        prm[0:doms, :] = mean[:doms]
        prm[doms : 2 * doms, :] = inv * sc.get()[...]
        prm[2 * doms : 3 * doms, :] = sh.get()[...]
        prm[3 * doms : 4 * doms, :] = hd.get()[...]
        prm[4 * doms : 5 * doms, :] = inv
        params[...] = prm[:16, :]
        outs[0].flush()
        spread_columns(wide, prm, 4 * doms)
        tw, mk = tws.get(), mks.get()
        loss = jnp.zeros((1, LANE), F32)
        for u in range(own // LANE):
            part = slice(u * LANE, (u + 1) * LANE)
            dom = mk[0:1, part]
            target = mk[1:2, part].astype(F32)
            _, centred, affine, _, head_w = chosen_tower(tw, dom, wide, part, doms)
            s = sigmoid(affine)
            act = affine * s
            chosen = jnp.sum(act * head_w, axis=0, keepdims=True)
            soft = jnp.maximum(chosen, 0.0) + jnp.log(1.0 + jnp.exp(-jnp.abs(chosen)))
            loss = loss + (soft - target * chosen)
            score_grad = (sigmoid(chosen) - target) * (1.0 / count)
            grad = score_grad * head_w * (s + act * (1.0 - s))
            q[0:LANE, part] = grad
            q[LANE : 2 * LANE, part] = grad * centred
            q[2 * LANE :, part] = score_grad * act
        kinds = lax.broadcasted_iota(jnp.int32, (8, own), 0)
        one_hot = (kinds == mk[0:1, :]).astype(F32)
        sums = mm_t(one_hot, q[...], lax.Precision.HIGHEST)[:doms]
        tile = [sums[:, :LANE], sums[:, LANE : 2 * LANE] * inv, sums[:, 2 * LANE :]]
        rest = jnp.zeros((16 - 3 * doms - 1, LANE), F32)
        all_rows = jnp.concatenate(tile + [loss, rest], axis=0)
        for d in range(devices):
            message[d * 16 : (d + 1) * 16, :] = all_rows
        outs[1].flush()

    return staged(
        body,
        [Near(stats), Far(tower), Far(marks), Far(scale), Far(shift), Far(head)],
        [plain((16, LANE), F32), Near(plain((devices * 16, LANE), F32))],
        [
            pltpu.VMEM((LANE, LANE), F32),
            pltpu.VMEM((4 * doms, LANE, LANE), F32),
            pltpu.VMEM((3 * LANE, own), F32),
        ],
        "normalise",
        16,
    )


def layout(epd, hid_n, out_n, dim, doms, rows_n):
    experts = epd * hid_n * (out_n + dim) // LANE
    towers = -(-(doms * out_n + (dim // LANE) * 32) // (2 * 16 * rows_n)) * 16
    return experts // rows_n, towers


def pieces(epd, hid_n, out_n, dim):
    flat = 0
    for i in range(epd):
        for q in range(out_n // LANE):
            yield 0, i, q, flat
            flat += hid_n
    for i in range(epd):
        for q in range(dim // LANE):
            yield 1, i, q, flat
            flat += hid_n


def backward(sums, params, tower, low_towers, marks, acts, inputs, w2, wgate_t, wtower, devices, rows_n, count):
    ns = 1 + len(low_towers)
    t_rows, own = tower.shape
    total_n = ns * own
    dim = inputs.shape[1]
    epd, hid_n, out_n = w2[0].shape
    ce = 2 * epd
    ke = wgate_t.shape[0]
    doms, _, th = wtower.shape
    exps = ke // doms
    m_exp, m_tow = layout(epd, hid_n, out_n, dim, doms, rows_n)
    step = math.gcd(m_exp, hid_n)

    def body(ins, outs, wide, prm, tg, mg, eg, gg, srow, tgf, facc):
        sm, pr, tw0, mk0 = ins[:4]
        low = ins[4 : 3 + ns]
        vals, gate, mixed, hid, slope, xs, w2o, w2s, wts = ins[3 + ns :]
        small, loss_out, sib, mine, pgs, lgs = outs
        pg, lg = pgs.buf, lgs.buf
        c = lax.rem(lax.axis_index(WIDTH), 2)
        prm[...] = jnp.zeros_like(prm)
        total = jnp.sum(sm.get()[...].reshape(devices, 16, LANE), axis=0)
        small.buf[...] = total
        loss_out.buf[...] = jnp.sum(total[3 * doms : 3 * doms + 1, :], axis=1, keepdims=True) * (1.0 / count)
        small.flush()
        loss_out.flush()
        given = pr.get()[...]
        gain, inv = given[doms : 2 * doms], given[4 * doms : 5 * doms]
        prm[0:16, :] = given
        prm[4 * doms : 5 * doms, :] = gain * total[:doms] * (1.0 / count)
        prm[5 * doms : 6 * doms, :] = gain * inv * total[doms : 2 * doms] * (1.0 / count)
        spread_columns(wide, prm, 6 * doms)
        for u in range(total_n // LANE):
            n = u * LANE // own
            part = slice(u * LANE, (u + 1) * LANE)
            here = slice(u * LANE - n * own, (u + 1) * LANE - n * own)
            if n == 0:
                tw = tw0.get()
                dom = mk0.get()[0:1, here]
                target = mk0.get()[1:2, here].astype(F32)
            else:
                tw = low[n - 1].get()
                pair = tw[t_rows : t_rows + 16, here].astype(F32)
                dom = pair[0:1].astype(jnp.int32)
                target = pair[1:2]
            values, _, affine, gain_s, head_w = chosen_tower(tw, dom, wide, here, doms)
            s = sigmoid(affine)
            a = affine * s
            chosen = jnp.sum(a * head_w, axis=0, keepdims=True)
            score_grad = (sigmoid(chosen) - target) * (1.0 / count)
            grad = gain_s * (score_grad * head_w * (s + a * (1.0 - s)))
            for k in range(doms):
                v = jnp.where(dom == k, grad, 0.0) - wide[4 * doms + k]
                v = v - (values[k] - wide[k]) * wide[5 * doms + k]
                down = v.astype(BF16)
                tg[k * th : (k + 1) * th, part] = down
                srow[k : k + 1, part] = jnp.sum(down.astype(F32) * values[k], axis=0, keepdims=True)
        wt = wts.get()
        for k in range(doms):
            mg[k * out_n : (k + 1) * out_n, :] = mm(wt[k], tg[k * th : (k + 1) * th, :])
        vals, gate = vals.get(), gate.get()
        gg[...] = jnp.zeros_like(gg)
        for u in range(total_n // LANE):
            part = slice(u * LANE, (u + 1) * LANE)
            rows = [[gate[k * exps + e : k * exps + e + 1, part] for e in range(ce)] for k in range(doms)]

            def spread(i, acc):
                up = [mg[pl.ds(pl.multiple_of(k * out_n + i * 16, 16), 16), part] for k in range(doms)]
                acc = list(acc)
                for e in range(ce):
                    at = pl.ds(pl.multiple_of(e * out_n + i * 16, 16), 16)
                    v = vals[at, part].astype(F32)
                    back = None
                    for k in range(doms):
                        term = rows[k][e] * up[k]
                        back = term if k == 0 else back + term
                        prod = up[k] * v
                        acc[k * ce + e] = acc[k * ce + e] + (prod[:8] + prod[8:])
                    eg[at, part] = back.astype(BF16)
                return tuple(acc)

            zero = jnp.zeros((8, LANE), F32)
            acc = lax.fori_loop(0, out_n // 16, spread, (zero,) * (doms * ce), unroll=4)
            for k in range(doms):
                for e in range(ce):
                    dot = jnp.sum(acc[k * ce + e], axis=0, keepdims=True)
                    gg[k * exps + e : k * exps + e + 1, part] = rows[k][e] * (dot - srow[k : k + 1, part])
        lg[...] = mm(reorder(ke, epd), gg[...].astype(BF16)).astype(BF16)
        lgs.flush()
        slope, hid = slope.get(), hid.get()

        def put(kind, slot, values):
            target = mine if slot < epd else sib
            for k, i, q, flat in pieces(epd, hid_n, out_n, dim):
                if k == kind and i == slot % epd:
                    for off in range(0, hid_n, step):
                        j, o = divmod(flat + off, m_exp)
                        target.buf[j, o : o + step, :] = values[off : off + step, q * LANE : (q + 1) * LANE].astype(BF16)

        for g, src in enumerate((w2o, w2s)):
            ref = src.get()
            for i in range(epd):
                e = g * epd + i
                at = slice(e * hid_n, (e + 1) * hid_n)
                at_o = slice(e * out_n, (e + 1) * out_n)
                for u in range(ns):
                    part = slice(u * own, (u + 1) * own)
                    pg[at, part] = (mm(ref[i], eg[at_o, part]) * slope[at, part].astype(F32)).astype(BF16)
        pgs.flush()
        x = xs.get()
        facc[...] = mm(pg[...], x[...])
        for e in range(ce):
            put(1, e, facc[e * hid_n : (e + 1) * hid_n, :])
        for e in range(ce):
            at = slice(e * hid_n, (e + 1) * hid_n)
            at_o = slice(e * out_n, (e + 1) * out_n)
            put(0, e, mm_t(hid[at, :], eg[at_o, :]))
        mixed = mixed.get()
        tgf[doms * out_n :, :] = jnp.zeros((tgf.shape[0] - doms * out_n, LANE), F32)
        for k in range(doms):
            tgf[k * out_n : (k + 1) * out_n, :] = mm_t(
                mixed[k * out_n : (k + 1) * out_n, :], tg[k * th : (k + 1) * th, :]
            )
        part_g = mm(lg[...], x[...])
        for q in range(dim // LANE):
            tgf[doms * out_n + q * 32 : doms * out_n + q * 32 + ke, :] = part_g[:, q * LANE : (q + 1) * LANE]
        for target, core in ((sib, 1 - c), (mine, c)):
            for j in range(rows_n):
                start = pl.multiple_of((core * rows_n + j) * m_tow, 8)
                target.buf[j, m_exp:, :] = tgf[pl.ds(start, m_tow), :].astype(BF16)
            target.flush()

    outs = [
        plain((16, LANE), F32),
        plain((1, 1), F32),
        plain((rows_n, m_exp + m_tow, LANE), BF16),
        plain((rows_n, m_exp + m_tow, LANE), BF16),
        plain((ce * hid_n, total_n), BF16),
        plain((ke, total_n), BF16),
    ]
    scratch = [
        pltpu.VMEM((6 * doms, LANE, LANE), F32),
        pltpu.VMEM((LANE, LANE), F32),
        pltpu.VMEM((doms * th, total_n), BF16),
        pltpu.VMEM((doms * out_n, total_n), F32),
        pltpu.VMEM((ce * out_n, total_n), BF16),
        pltpu.VMEM((ke, total_n), F32),
        pltpu.VMEM((8, total_n), F32),
        pltpu.VMEM((2 * rows_n * m_tow, LANE), F32),
        pltpu.VMEM((ce * hid_n, dim), F32),
    ]

    def side_by_side(which):
        def pairs(refs, buf):
            return [(r.at[n], buf.at[:, i * own : (i + 1) * own]) for i, (r, (_, n)) in enumerate(zip(refs, acts))]

        arrays = [a[which] for a, _ in acts]
        return Far(arrays, (arrays[0].shape[1], total_n), pairs)

    ins = [Near(sums), Far(params), Far(tower), Far(marks)]
    ins += [Far(v) for v in low_towers]
    ins += [side_by_side(which) for which in (2, 3, 4, 0, 1)]
    ins.append(Far(inputs, (total_n, dim), row_blocks(list(range(ns)), own)))
    ins += [Far(a) for a in (w2[0], w2[1], wtower)]
    return staged(body, ins, outs, scratch, "backward", 58)


def backward_inputs(pg, lg, w1, wgate_t, own):
    total_n = pg.shape[1]
    ns = total_n // own
    epd, dim, hid_n = w1[0].shape
    ce = 2 * epd
    ke = wgate_t.shape[0]

    def body(ins, outs, w1c):
        pgs, lgs, w1o, w1s, wgs = ins
        for g, src in enumerate((w1o, w1s)):
            ref = src.get()
            for i in range(epd):
                e = g * epd + i
                w1c[:, e * hid_n : (e + 1) * hid_n] = ref[i]
        wg = jnp.concatenate([wgs.get()[...], jnp.zeros((LANE - ke, dim), BF16)], axis=0)
        w1c[:, ce * hid_n :] = wg.T
        pg_buf = pgs.get()
        lgs.get()
        pg_buf[ce * hid_n + ke :, :] = jnp.zeros((LANE - ke, total_n), BF16)
        pg_buf[ce * hid_n : ce * hid_n + ke, :] = lgs.buf[...]
        for n in range(ns - 1, -1, -1):
            gi = mm(w1c[...], pg_buf[:, n * own : (n + 1) * own])
            if n:
                outs[1].buf[n - 1] = gi.astype(BF16)
                outs[1].flush(n - 1)
            else:
                outs[0].buf[...] = gi
                outs[0].flush()

    return staged(
        body,
        [
            Far(pg, (ce * hid_n + LANE, total_n), lambda refs, buf: [(refs[0], buf.at[: ce * hid_n, :])]),
            Far(lg),
            Far(w1[0]),
            Far(w1[1]),
            Far(wgate_t),
        ],
        [plain((dim, own), F32), plain((max(ns - 1, 1), dim, own), BF16)],
        [pltpu.VMEM((dim, ce * hid_n + LANE), BF16)],
        "backward_inputs",
        32,
    )


def finish_inputs(own_part, received):
    dim, own = own_part.shape

    def body(ins, outs):
        got = [s.get() for s in ins[1:]]
        part = ins[0].get()
        out = outs[0].buf
        for u in range(own // LANE):
            lanes = slice(u * LANE, (u + 1) * LANE)
            total = part[:, lanes]
            for ref in got:
                total = total + ref[:, lanes].astype(F32)
            out[lanes, :] = total.T
            outs[0].flush(pl.ds(u * LANE, LANE))

    return staged(
        body, [Far(own_part)] + [Far(v) for v in received], [plain((own, dim), F32)], [], "finish_inputs", 16
    )[0]


def finish_weights(shares, other, epd, hid_n, out_n, dim, doms, exps, rows_n):
    m_exp, m_tow = layout(epd, hid_n, out_n, dim, doms, rows_n)
    step = math.gcd(m_exp, hid_n)
    ke = doms * exps

    def body(ins, outs, buf, tgf):
        got = ins[0].get()
        out_f, out_s, out_t, out_g = (o.buf for o in outs)
        c = lax.rem(lax.axis_index(WIDTH), 2)
        for kind, i, q, flat in pieces(epd, hid_n, out_n, dim):
            for off in range(0, hid_n, step):
                j, o = divmod(flat + off, m_exp)
                piece = got[j, o : o + step, :].astype(F32)
                if kind == 0:
                    out_s[i, off : off + step, q * LANE : (q + 1) * LANE] = piece
                else:
                    buf[off : off + step, :] = piece
            if kind == 1:
                out_f[i, q * LANE : (q + 1) * LANE, :] = buf[...].T
            if q == (out_n, dim)[kind] // LANE - 1:
                outs[1 - kind].flush(i)
        sib = ins[1].get()
        for j in range(rows_n):
            for core, value in ((c, got[j, m_exp:, :]), (1 - c, sib[j])):
                start = pl.multiple_of((core * rows_n + j) * m_tow, 8)
                tgf[pl.ds(start, m_tow), :] = value.astype(F32)
        for k in range(doms):
            out_t[k] = tgf[k * out_n : (k + 1) * out_n, :]
        outs[2].flush()
        for q in range(dim // LANE):
            at = doms * out_n + q * 32
            out_g[:, q * LANE : (q + 1) * LANE] = tgf[at : at + ke, :]
        outs[3].flush()

    return staged(
        body,
        [Far(shares), Far(other)],
        [
            plain((epd, dim, hid_n), F32),
            plain((epd, hid_n, out_n), F32),
            plain((doms, out_n, LANE), F32),
            plain((ke, dim), F32),
        ],
        [pltpu.VMEM((hid_n, LANE), F32), pltpu.VMEM((2 * rows_n * m_tow, LANE), F32)],
        "finish_weights",
        24,
    )


def swap(value, axis, mask):
    size = lax.axis_size(axis)
    return lax.ppermute(value, axis, [(i, i ^ mask) for i in range(size)])


def local(inputs, w_first, w_second, w_gate, w_tower, norm_scale, norm_shift, w_head, domains, labels):
    n_width, n_rows = lax.axis_size(WIDTH), lax.axis_size(ROWS)
    devices = n_width * n_rows
    own = inputs.shape[0] // n_width
    count = float(own * devices)
    dim = inputs.shape[1]
    epd, _, hid_n = w_first.shape
    out_n = w_second.shape[2]
    doms, _, exps = w_gate.shape
    ke = doms * exps
    n_x = n_width // 2
    others = list(range(1, n_x))
    w1 = (w_first, swap(w_first, WIDTH, 1))
    w2 = (w_second, swap(w_second, WIDTH, 1))
    wgate_t = jnp.transpose(w_gate, (0, 2, 1)).reshape(ke, dim)
    marks = jnp.stack([domains, labels])

    far = forward(others, inputs, w1, w2, wgate_t, w_tower, own, False, BF16, "forward_send")[0]
    sent = [swap(far[s - 1 : s], WIDTH, 2 * s) for s in others]
    mine = forward([0], inputs, w1, w2, wgate_t, w_tower, own, True, F32, "forward_own")
    foreign = forward(others, inputs, w1, w2, wgate_t, w_tower, own, True, None, "forward_foreign")
    tower, low, message = combine(mine[5], sent, marks, devices)
    stats = lax.all_to_all(message, BOTH, 0, 0, tiled=True)
    stats, low = lax.optimization_barrier((stats, low))
    lows = [swap(low, WIDTH, 2 * s) for s in others]
    params, message = normalise(stats, tower, marks, norm_scale, norm_shift, w_head, devices, count)
    sums = lax.all_to_all(message, BOTH, 0, 0, tiled=True)

    acts = [(mine[:5], 0)] + [(foreign[:5], s - 1) for s in others]
    small, loss, sib, own_part, pg, lg = backward(
        sums, params, tower, lows, marks, acts, inputs, w2, wgate_t, w_tower, devices, n_rows, count
    )
    m_exp, m_tow = layout(epd, hid_n, out_n, dim, doms, n_rows)
    payload = (own_part.astype(F32) + swap(sib, WIDTH, 1).astype(F32)).astype(BF16)
    gi_own, gi_out = backward_inputs(pg, lg, w1, wgate_t, own)
    received = [swap(gi_out[s - 1], WIDTH, 2 * s) for s in others]
    grad_inputs = finish_inputs(gi_own, received)
    shares = lax.all_to_all(payload, ROWS, 0, 0)
    towers = jnp.sum(shares[:, m_exp:].astype(F32), axis=0)
    part = towers
    for s in others:
        towers = towers + swap(part, WIDTH, 2 * s)
    experts = jnp.sum(shares[:, :m_exp].astype(F32), axis=0)
    share = jnp.concatenate([experts, towers], axis=0).astype(BF16)
    shares = lax.all_to_all(jnp.broadcast_to(share[None], (n_rows,) + share.shape), ROWS, 0, 0)
    other = swap(shares[:, m_exp:], WIDTH, 1)
    grad_first, grad_second, grad_tower, grad_gate = finish_weights(
        shares, other, epd, hid_n, out_n, dim, doms, exps, n_rows
    )
    return (
        loss[0, 0],
        grad_inputs,
        grad_first,
        grad_second,
        grad_gate.reshape(doms, exps, dim).transpose(0, 2, 1),
        grad_tower,
        small[doms : 2 * doms],
        small[:doms],
        small[2 * doms : 3 * doms],
    )


def solution(mesh):
    placed = (
        P(ROWS, None),
        P(WIDTH, None, None),
        P(WIDTH, None, None),
        P(),
        P(),
        P(),
        P(),
        P(),
        P(BOTH),
        P(BOTH),
    )
    return jax.shard_map(
        local,
        mesh=mesh,
        in_specs=placed,
        out_specs=(
            P(),
            P(BOTH, None),
            P(WIDTH, None, None),
            P(WIDTH, None, None),
            P(),
            P(),
            P(),
            P(),
            P(),
        ),
        check_vma=False,
    )
```

```python
import math

import jax
import jax.numpy as jnp
from jax import lax
from jax.experimental import pallas as pl
from jax.experimental.pallas import tpu as pltpu
from jax.sharding import PartitionSpec as P

F32 = jnp.float32
BF16 = jnp.bfloat16
EPS = 1e-05
LANE = 128
MIB = 1 << 20
ROWS = "rows"
WIDTH = "width"
BOTH = (ROWS, WIDTH)


def mm(a, b):
    return jnp.dot(a, b, preferred_element_type=F32)


def mm_t(a, b, precision=None):
    return lax.dot_general(a, b, (((1,), (1,)), ((), ())), preferred_element_type=F32, precision=precision)


def sigmoid(v):
    return 0.5 * jnp.tanh(0.5 * v) + 0.5


class Source:
    def __init__(self, buf, copies):
        self.buf = buf
        self.waiting = copies
        for copy in copies:
            copy.start()

    def get(self):
        for copy in self.waiting:
            copy.wait()
        self.waiting = []
        return self.buf


class Target:
    def __init__(self, ref, buf, sems):
        self.ref, self.buf, self.sems = ref, buf, sems
        self.waiting = []

    def flush(self, *at):
        if self.ref is None:
            return
        src = self.buf.at[at] if at else self.buf
        dst = self.ref.at[at] if at else self.ref
        copy = pltpu.make_async_copy(src, dst, next(self.sems))
        copy.start()
        self.waiting.append(copy)


class Near:
    def __init__(self, what):
        self.what = what


class Far:
    def __init__(self, arrays, shape=None, pairs=None, moved=False):
        self.moved = moved
        self.arrays = arrays if isinstance(arrays, (list, tuple)) else [arrays]
        self.shape = shape or self.arrays[0].shape
        self.dtype = self.arrays[0].dtype
        self.pairs = pairs or (lambda refs, buf: [(refs[0], buf)])


def staged(body, ins, outs, scratch, name, limit, n_sems=64):
    far_in = [i for i, s in enumerate(ins) if isinstance(s, Far)]
    far_out = [i for i, s in enumerate(outs) if not isinstance(s, Near)]
    args, specs, spans = [], [], []
    hbm = pl.BlockSpec(memory_space=pltpu.HBM)
    vmem = pl.BlockSpec(memory_space=pltpu.VMEM)
    anywhere = pl.BlockSpec(memory_space=pl.ANY)
    for s in ins:
        if isinstance(s, Far):
            spans.append((len(args), len(args) + len(s.arrays)))
            if s.moved:
                args += s.arrays
                specs += [anywhere] * len(s.arrays)
                continue
            args += [pltpu.with_memory_space_constraint(a, pltpu.HBM) for a in s.arrays]
            specs += [hbm] * len(s.arrays)
        else:
            spans.append((len(args), len(args) + 1))
            args.append(s.what)
            specs.append(vmem)
    n_in, n_out = len(args), len(outs)

    def kernel(*refs):
        refs_in, refs_out = refs[:n_in], refs[n_in : n_in + n_out]
        bufs = refs[n_in + n_out :]
        in_bufs = dict(zip(far_in, bufs))
        out_bufs = dict(zip(far_out, bufs[len(far_in) :]))
        rest = bufs[len(far_in) + len(far_out) : -1]
        sems = iter([bufs[-1].at[i] for i in range(n_sems)])
        sources = []
        for i, (start, stop) in enumerate(spans):
            if i in in_bufs:
                pairs = ins[i].pairs(refs_in[start:stop], in_bufs[i])
                sources.append(Source(in_bufs[i], [pltpu.make_async_copy(a, b, next(sems)) for a, b in pairs]))
            else:
                sources.append(Source(refs_in[start], []))
        targets = []
        for i, ref in enumerate(refs_out):
            targets.append(Target(ref, out_bufs[i], sems) if i in out_bufs else Target(None, ref, sems))
        body(sources, targets, *rest)
        for s in sources:
            s.get()
        for t in targets:
            for copy in t.waiting:
                copy.wait()

    return pl.pallas_call(
        kernel,
        out_shape=[o.what if isinstance(o, Near) else pltpu.HBM(o.shape, o.dtype) for o in outs],
        in_specs=specs,
        out_specs=[hbm if i in far_out else vmem for i in range(n_out)],
        scratch_shapes=[pltpu.VMEM(ins[i].shape, ins[i].dtype) for i in far_in]
        + [pltpu.VMEM(outs[i].shape, outs[i].dtype) for i in far_out]
        + list(scratch)
        + [pltpu.SemaphoreType.DMA((n_sems,))],
        compiler_params=pltpu.CompilerParams(vmem_limit_bytes=limit * MIB),
        name=name,
    )(*args)


def plain(shape, dtype):
    return jax.ShapeDtypeStruct(shape, dtype)


def row_blocks(slots, own):
    def pairs(refs, buf):
        w = lax.axis_index(WIDTH)
        got = []
        for n, s in enumerate(slots):
            start = pl.multiple_of(lax.bitwise_xor(w, 2 * s) * own, own)
            got.append((refs[0].at[pl.ds(start, own), :], buf.at[n * own : (n + 1) * own, :]))
        return got

    return pairs


def reorder(ke, epd):
    first = lax.axis_index(WIDTH) * epd
    down = lax.broadcasted_iota(jnp.int32, (ke, ke), 0)
    across = lax.broadcasted_iota(jnp.int32, (ke, ke), 1)
    return jnp.where(lax.bitwise_xor(down, first) == across, 1.0, 0.0).astype(BF16)


def forward(slots, inputs, w1, w2, wgate_t, wtower, own, keep, send, name):
    ns = len(slots)
    dim = inputs.shape[1]
    epd, _, hid_n = w1[0].shape
    out_n = w2[0].shape[2]
    ce = 2 * epd
    ke = wgate_t.shape[0]
    doms, _, th = wtower.shape
    exps = ke // doms

    def body(ins, outs, w1t, w2t, wt, pre, *bufs):
        xs, w1o, w1s, w2o, w2s, wgs, wts = ins
        if keep:
            hid, slope, vals, gate, mixed = (o.buf for o in outs[:5])
        else:
            hid, vals, gate, mixed = bufs
        x = xs.get()
        for g, src in enumerate((w1o, w1s)):
            ref = src.get()
            for i in range(epd):
                e = g * epd + i
                w1t[e * hid_n : (e + 1) * hid_n, :] = ref[i].T
        w1t[ce * hid_n : ce * hid_n + ke, :] = mm(reorder(ke, epd), wgs.get()[...]).astype(BF16)
        for n in range(ns):
            pre[...] = mm_t(w1t[...], x[n * own : (n + 1) * own, :])
            if n == 0:
                for g, src in enumerate((w2o, w2s)):
                    ref = src.get()
                    for i in range(epd):
                        w2t[g * epd + i] = ref[i].T
                ref = wts.get()
                for k in range(doms):
                    wt[k] = ref[k].T
            logits = pre[ce * hid_n : ce * hid_n + ke, :].reshape(doms, exps, own)
            top = jnp.exp(logits - jnp.max(logits, axis=1, keepdims=True))
            soft = top / jnp.sum(top, axis=1, keepdims=True)
            gate[n] = soft.reshape(ke, own)

            def act(i, carry):
                at = pl.ds(pl.multiple_of(i * 16, 16), 16)
                v = pre[at, :]
                s = sigmoid(v)
                h = v * s
                hid[n, at, :] = h.astype(BF16)
                if keep:
                    slope[n, at, :] = (s + h * (1.0 - s)).astype(BF16)
                return carry

            lax.fori_loop(0, ce * hid_n // 16, act, 0, unroll=4)
            for e in range(ce):
                vals[n, e * out_n : (e + 1) * out_n, :] = mm(
                    w2t[e], hid[n, e * hid_n : (e + 1) * hid_n, :]
                ).astype(BF16)
            if keep:
                for o in outs[:4]:
                    o.flush(n)
            for u in range(own // LANE):
                part = slice(u * LANE, (u + 1) * LANE)
                rows = [[gate[n, k * exps + e : k * exps + e + 1, part] for e in range(ce)] for k in range(doms)]

                def mix(i, carry):
                    acc = [None] * doms
                    for e in range(ce):
                        at = pl.ds(pl.multiple_of(e * out_n + i * 32, 32), 32)
                        v = vals[n, at, part].astype(F32)
                        for k in range(doms):
                            term = rows[k][e] * v
                            acc[k] = term if e == 0 else acc[k] + term
                    for k in range(doms):
                        at = pl.ds(pl.multiple_of(k * out_n + i * 32, 32), 32)
                        mixed[n, at, part] = acc[k].astype(BF16)
                    return carry

                lax.fori_loop(0, out_n // 32, mix, 0, unroll=4)
            if keep:
                outs[4].flush(n)
            if send is not None:
                tower = outs[-1]
                for k in range(doms):
                    tower.buf[n, k * th : (k + 1) * th, :] = mm(
                        wt[k], mixed[n, k * out_n : (k + 1) * out_n, :]
                    ).astype(send)
                tower.flush(n)

    kept = [
        plain((ns, ce * hid_n, own), BF16),
        plain((ns, ce * hid_n, own), BF16),
        plain((ns, ce * out_n, own), BF16),
        plain((ns, ke, own), F32),
        plain((ns, doms * out_n, own), BF16),
    ]
    outs = list(kept) if keep else []
    if send is not None:
        outs.append(plain((ns, doms * th, own), send))
    scratch = [
        pltpu.VMEM((ce * hid_n + ke, dim), BF16),
        pltpu.VMEM((ce, out_n, hid_n), BF16),
        pltpu.VMEM((doms, th, out_n), BF16),
        pltpu.VMEM((ce * hid_n + ke, own), F32),
    ]
    if not keep:
        scratch += [pltpu.VMEM(kept[i].shape, kept[i].dtype) for i in (0, 2, 3, 4)]
    ins = [Far(inputs, (ns * own, dim), row_blocks(slots, own))]
    ins += [Far(w1[0]), Far(w1[1], moved=True), Far(w2[0]), Far(w2[1], moved=True), Far(wgate_t), Far(wtower)]
    return staged(body, ins, outs, scratch, name, 40)


def combine(own_part, received, marks, devices):
    _, rows, own = own_part.shape
    doms = rows // LANE

    def body(ins, outs, cols):
        part = ins[0].get()
        got = [s.get() for s in ins[2:]]
        tower, low, message = (o.buf for o in outs)
        cols[...] = jnp.zeros_like(cols)
        for k in range(doms):
            at = slice(k * LANE, (k + 1) * LANE)
            total = part[0, at, :]
            for ref in got:
                total = total + ref[0, at, :].astype(F32)
            tower[at, :] = total
            low[at, :] = total.astype(BF16)
            mean = jnp.sum(total, axis=1, keepdims=True) * (1.0 / own)
            dev = total - mean
            cols[:, k : k + 1] = mean
            cols[:, doms + k : doms + k + 1] = jnp.sum(dev * dev, axis=1, keepdims=True)
        outs[0].flush()
        pair = jnp.concatenate([ins[1].get()[...].astype(F32), jnp.zeros((14, own), F32)], axis=0)
        low[rows:, :] = pair.astype(BF16)
        outs[1].flush()
        tile = cols[...].T[:8, :]
        for d in range(devices):
            message[d * 8 : (d + 1) * 8, :] = tile
        outs[2].flush()

    return staged(
        body,
        [Far(own_part), Far(marks)] + [Far(v, moved=True) for v in received],
        [plain((rows, own), F32), plain((rows + 16, own), BF16), Near(plain((devices * 8, LANE), F32))],
        [pltpu.VMEM((LANE, LANE), F32)],
        "combine",
        16,
    )


def pick(dom, values):
    got = values[-1]
    for k in range(len(values) - 2, -1, -1):
        got = jnp.where(dom == k, values[k], got)
    return got


def chosen_tower(tower, dom, wide, lanes, doms):
    values = [tower[k * LANE : (k + 1) * LANE, lanes].astype(F32) for k in range(doms)]
    mean, gain, shift, head = (pick(dom, [wide[j * doms + k] for k in range(doms)]) for j in range(4))
    centred = pick(dom, values) - mean
    return values, centred, centred * gain + shift, gain, head


def spread_columns(wide, rows_ref, n):
    cols = rows_ref[...].T
    for j in range(n):
        wide[j] = jnp.broadcast_to(cols[:, j : j + 1], (LANE, LANE))


def normalise(stats, tower, marks, scale, shift, head, devices, count):
    rows, own = tower.shape
    doms = rows // LANE

    def body(ins, outs, prm, wide, q):
        st, tws, mks, sc, sh, hd = ins
        params, message = (o.buf for o in outs)
        prm[...] = jnp.zeros_like(prm)
        got = st.get()[...].reshape(devices, 8, LANE)
        total = jnp.sum(got, axis=0)
        mean = total * (1.0 / devices)
        dev = got - mean[None]
        spread = jnp.sum(dev * dev, axis=0) * float(own)
        var = (total[doms : 2 * doms] + spread[:doms]) * (1.0 / count)
        inv = lax.rsqrt(var + EPS)
        prm[0:doms, :] = mean[:doms]
        prm[doms : 2 * doms, :] = inv * sc.get()[...]
        prm[2 * doms : 3 * doms, :] = sh.get()[...]
        prm[3 * doms : 4 * doms, :] = hd.get()[...]
        prm[4 * doms : 5 * doms, :] = inv
        params[...] = prm[:16, :]
        outs[0].flush()
        spread_columns(wide, prm, 4 * doms)
        tw, mk = tws.get(), mks.get()
        loss = jnp.zeros((1, LANE), F32)
        for u in range(own // LANE):
            part = slice(u * LANE, (u + 1) * LANE)
            dom = mk[0:1, part]
            target = mk[1:2, part].astype(F32)
            _, centred, affine, _, head_w = chosen_tower(tw, dom, wide, part, doms)
            s = sigmoid(affine)
            act = affine * s
            chosen = jnp.sum(act * head_w, axis=0, keepdims=True)
            soft = jnp.maximum(chosen, 0.0) + jnp.log(1.0 + jnp.exp(-jnp.abs(chosen)))
            loss = loss + (soft - target * chosen)
            score_grad = (sigmoid(chosen) - target) * (1.0 / count)
            grad = score_grad * head_w * (s + act * (1.0 - s))
            q[0:LANE, part] = grad
            q[LANE : 2 * LANE, part] = grad * centred
            q[2 * LANE :, part] = score_grad * act
        kinds = lax.broadcasted_iota(jnp.int32, (8, own), 0)
        one_hot = (kinds == mk[0:1, :]).astype(F32)
        sums = mm_t(one_hot, q[...], lax.Precision.HIGHEST)[:doms]
        tile = [sums[:, :LANE], sums[:, LANE : 2 * LANE] * inv, sums[:, 2 * LANE :]]
        rest = jnp.zeros((16 - 3 * doms - 1, LANE), F32)
        all_rows = jnp.concatenate(tile + [loss, rest], axis=0)
        for d in range(devices):
            message[d * 16 : (d + 1) * 16, :] = all_rows
        outs[1].flush()

    return staged(
        body,
        [Far(stats, moved=True), Far(tower), Far(marks), Far(scale), Far(shift), Far(head)],
        [plain((16, LANE), F32), Near(plain((devices * 16, LANE), F32))],
        [
            pltpu.VMEM((LANE, LANE), F32),
            pltpu.VMEM((4 * doms, LANE, LANE), F32),
            pltpu.VMEM((3 * LANE, own), F32),
        ],
        "normalise",
        16,
    )


def layout(epd, hid_n, out_n, dim, doms, rows_n):
    second = epd * hid_n * out_n // LANE
    first = epd * hid_n * dim // LANE
    towers = -(-(doms * out_n + (dim // LANE) * 32) // (2 * 16 * rows_n)) * 16
    return second // rows_n, first // rows_n, towers


def pieces(kind, epd, hid_n, out_n, dim):
    flat = 0
    for i in range(epd):
        for q in range((out_n, dim)[kind] // LANE):
            yield i, q, flat
            flat += hid_n


def spots(kind, row, rows_n):
    got = []
    for j in range(rows_n):
        p = lax.bitwise_xor(row, j)
        got.append(p if kind == 0 else (p & 1) * (rows_n // 2) + lax.shift_right_logical(p, 1))
    return got


def backward(sums, params, tower, low_towers, marks, acts, inputs, w2, wgate_t, wtower, devices, rows_n, count):
    ns = 1 + len(low_towers)
    t_rows, own = tower.shape
    total_n = ns * own
    dim = inputs.shape[1]
    epd, hid_n, out_n = w2[0].shape
    ce = 2 * epd
    ke = wgate_t.shape[0]
    doms, _, th = wtower.shape
    exps = ke // doms
    m_sec, m_first, m_tow = layout(epd, hid_n, out_n, dim, doms, rows_n)

    def body(ins, outs, wide, prm, tg, mg, eg, gg, srow, tgf, facc):
        sm, pr, tw0, mk0 = ins[:4]
        low = ins[4 : 3 + ns]
        vals, gate, mixed, hid, slope, xs, w2o, w2s, wts = ins[3 + ns :]
        small, loss_out, sec_sib, first_sib, sec_mine, first_mine, tow_sib, tow_mine, pgs, lgs = outs
        pg, lg = pgs.buf, lgs.buf
        c = lax.rem(lax.axis_index(WIDTH), 2)
        r = lax.axis_index(ROWS)
        at_row = [spots(kind, r, rows_n) for kind in range(2)]
        prm[...] = jnp.zeros_like(prm)
        total = jnp.sum(sm.get()[...].reshape(devices, 16, LANE), axis=0)
        small.buf[...] = total
        loss_out.buf[...] = jnp.sum(total[3 * doms : 3 * doms + 1, :], axis=1, keepdims=True) * (1.0 / count)
        small.flush()
        loss_out.flush()
        given = pr.get()[...]
        gain, inv = given[doms : 2 * doms], given[4 * doms : 5 * doms]
        prm[0:16, :] = given
        prm[4 * doms : 5 * doms, :] = gain * total[:doms] * (1.0 / count)
        prm[5 * doms : 6 * doms, :] = gain * inv * total[doms : 2 * doms] * (1.0 / count)
        spread_columns(wide, prm, 6 * doms)
        for u in range(total_n // LANE):
            n = u * LANE // own
            part = slice(u * LANE, (u + 1) * LANE)
            here = slice(u * LANE - n * own, (u + 1) * LANE - n * own)
            if n == 0:
                tw = tw0.get()
                dom = mk0.get()[0:1, here]
                target = mk0.get()[1:2, here].astype(F32)
            else:
                tw = low[n - 1].get()
                pair = tw[t_rows : t_rows + 16, here].astype(F32)
                dom = pair[0:1].astype(jnp.int32)
                target = pair[1:2]
            values, _, affine, gain_s, head_w = chosen_tower(tw, dom, wide, here, doms)
            s = sigmoid(affine)
            a = affine * s
            chosen = jnp.sum(a * head_w, axis=0, keepdims=True)
            score_grad = (sigmoid(chosen) - target) * (1.0 / count)
            grad = gain_s * (score_grad * head_w * (s + a * (1.0 - s)))
            for k in range(doms):
                v = jnp.where(dom == k, grad, 0.0) - wide[4 * doms + k]
                v = v - (values[k] - wide[k]) * wide[5 * doms + k]
                down = v.astype(BF16)
                tg[k * th : (k + 1) * th, part] = down
                srow[k : k + 1, part] = jnp.sum(down.astype(F32) * values[k], axis=0, keepdims=True)
        wt = wts.get()
        for k in range(doms):
            mg[k * out_n : (k + 1) * out_n, :] = mm(wt[k], tg[k * th : (k + 1) * th, :])
        vals, gate = vals.get(), gate.get()
        gg[...] = jnp.zeros_like(gg)
        for u in range(total_n // LANE):
            part = slice(u * LANE, (u + 1) * LANE)
            rows = [[gate[k * exps + e : k * exps + e + 1, part] for e in range(ce)] for k in range(doms)]

            def spread(i, acc):
                up = [mg[pl.ds(pl.multiple_of(k * out_n + i * 16, 16), 16), part] for k in range(doms)]
                acc = list(acc)
                for e in range(ce):
                    at = pl.ds(pl.multiple_of(e * out_n + i * 16, 16), 16)
                    v = vals[at, part].astype(F32)
                    back = None
                    for k in range(doms):
                        term = rows[k][e] * up[k]
                        back = term if k == 0 else back + term
                        prod = up[k] * v
                        acc[k * ce + e] = acc[k * ce + e] + (prod[:8] + prod[8:])
                    eg[at, part] = back.astype(BF16)
                return tuple(acc)

            zero = jnp.zeros((8, LANE), F32)
            acc = lax.fori_loop(0, out_n // 16, spread, (zero,) * (doms * ce), unroll=4)
            for k in range(doms):
                for e in range(ce):
                    dot = jnp.sum(acc[k * ce + e], axis=0, keepdims=True)
                    gg[k * exps + e : k * exps + e + 1, part] = rows[k][e] * (dot - srow[k : k + 1, part])
        lg[...] = mm(reorder(ke, epd), gg[...].astype(BF16)).astype(BF16)
        lgs.flush()
        slope, hid = slope.get(), hid.get()

        def put(kind, slot, values):
            target = ((sec_sib, first_sib), (sec_mine, first_mine))[slot < epd][kind]
            size = (m_sec, m_first)[kind]
            step = math.gcd(size, hid_n)
            for i, q, flat in pieces(kind, epd, hid_n, out_n, dim):
                if i == slot % epd:
                    for off in range(0, hid_n, step):
                        j, o = divmod(flat + off, size)
                        part = values[off : off + step, q * LANE : (q + 1) * LANE]
                        target.buf[at_row[kind][j], o : o + step, :] = part.astype(BF16)

        for g, src in enumerate((w2o, w2s)):
            ref = src.get()
            for i in range(epd):
                e = g * epd + i
                at = slice(e * hid_n, (e + 1) * hid_n)
                at_o = slice(e * out_n, (e + 1) * out_n)
                for u in range(ns):
                    part = slice(u * own, (u + 1) * own)
                    pg[at, part] = (mm(ref[i], eg[at_o, part]) * slope[at, part].astype(F32)).astype(BF16)
        pgs.flush()
        x = xs.get()
        facc[...] = mm(pg[...], x[...])
        for e in range(ce):
            put(1, e, facc[e * hid_n : (e + 1) * hid_n, :])
        for e in range(ce):
            at = slice(e * hid_n, (e + 1) * hid_n)
            at_o = slice(e * out_n, (e + 1) * out_n)
            put(0, e, mm_t(hid[at, :], eg[at_o, :]))
        for target in (sec_sib, first_sib, sec_mine, first_mine):
            target.flush()
        mixed = mixed.get()
        tgf[doms * out_n :, :] = jnp.zeros((tgf.shape[0] - doms * out_n, LANE), F32)
        for k in range(doms):
            tgf[k * out_n : (k + 1) * out_n, :] = mm_t(
                mixed[k * out_n : (k + 1) * out_n, :], tg[k * th : (k + 1) * th, :]
            )
        part_g = mm(lg[...], x[...])
        for q in range(dim // LANE):
            tgf[doms * out_n + q * 32 : doms * out_n + q * 32 + ke, :] = part_g[:, q * LANE : (q + 1) * LANE]
        for target, core in ((tow_sib, 1 - c), (tow_mine, c)):
            for j in range(rows_n):
                start = pl.multiple_of((core * rows_n + j) * m_tow, 8)
                target.buf[at_row[1][j], :, :] = tgf[pl.ds(start, m_tow), :].astype(BF16)
            target.flush()

    outs = [
        plain((16, LANE), F32),
        plain((1, 1), F32),
        plain((rows_n, m_sec, LANE), BF16),
        plain((rows_n, m_first, LANE), BF16),
        plain((rows_n, m_sec, LANE), BF16),
        plain((rows_n, m_first, LANE), BF16),
        plain((rows_n, m_tow, LANE), BF16),
        plain((rows_n, m_tow, LANE), BF16),
        plain((ce * hid_n, total_n), BF16),
        plain((ke, total_n), BF16),
    ]
    scratch = [
        pltpu.VMEM((6 * doms, LANE, LANE), F32),
        pltpu.VMEM((LANE, LANE), F32),
        pltpu.VMEM((doms * th, total_n), BF16),
        pltpu.VMEM((doms * out_n, total_n), F32),
        pltpu.VMEM((ce * out_n, total_n), BF16),
        pltpu.VMEM((ke, total_n), F32),
        pltpu.VMEM((8, total_n), F32),
        pltpu.VMEM((2 * rows_n * m_tow, LANE), F32),
        pltpu.VMEM((ce * hid_n, dim), F32),
    ]

    def side_by_side(which):
        def pairs(refs, buf):
            return [(r.at[n], buf.at[:, i * own : (i + 1) * own]) for i, (r, (_, n)) in enumerate(zip(refs, acts))]

        arrays = [a[which] for a, _ in acts]
        return Far(arrays, (arrays[0].shape[1], total_n), pairs)

    ins = [Far(sums, moved=True), Far(params), Far(tower), Far(marks)]
    ins += [Far(v, moved=True) for v in low_towers]
    ins += [side_by_side(which) for which in (2, 3, 4, 0, 1)]
    ins.append(Far(inputs, (total_n, dim), row_blocks(list(range(ns)), own)))
    ins += [Far(w2[0]), Far(w2[1], moved=True), Far(wtower)]
    return staged(body, ins, outs, scratch, "backward", 58)


def backward_inputs(pg, lg, w1, wgate_t, own):
    total_n = pg.shape[1]
    ns = total_n // own
    epd, dim, hid_n = w1[0].shape
    ce = 2 * epd
    ke = wgate_t.shape[0]

    def body(ins, outs, w1c):
        pgs, lgs, w1o, w1s, wgs = ins
        for g, src in enumerate((w1o, w1s)):
            ref = src.get()
            for i in range(epd):
                e = g * epd + i
                w1c[:, e * hid_n : (e + 1) * hid_n] = ref[i]
        wg = jnp.concatenate([wgs.get()[...], jnp.zeros((LANE - ke, dim), BF16)], axis=0)
        w1c[:, ce * hid_n :] = wg.T
        pg_buf = pgs.get()
        lgs.get()
        pg_buf[ce * hid_n + ke :, :] = jnp.zeros((LANE - ke, total_n), BF16)
        pg_buf[ce * hid_n : ce * hid_n + ke, :] = lgs.buf[...]
        for n in range(ns - 1, -1, -1):
            gi = mm(w1c[...], pg_buf[:, n * own : (n + 1) * own])
            if n:
                outs[1].buf[n - 1] = gi.astype(BF16)
                outs[1].flush(n - 1)
            else:
                outs[0].buf[...] = gi
                outs[0].flush()

    return staged(
        body,
        [
            Far(pg, (ce * hid_n + LANE, total_n), lambda refs, buf: [(refs[0], buf.at[: ce * hid_n, :])]),
            Far(lg),
            Far(w1[0]),
            Far(w1[1], moved=True),
            Far(wgate_t),
        ],
        [plain((dim, own), F32), plain((max(ns - 1, 1), dim, own), BF16)],
        [pltpu.VMEM((dim, ce * hid_n + LANE), BF16)],
        "backward_inputs",
        32,
    )


def finish_inputs(own_part, received):
    dim, own = own_part.shape

    def body(ins, outs):
        got = [s.get() for s in ins[1:]]
        part = ins[0].get()
        out = outs[0].buf
        for u in range(own // LANE):
            lanes = slice(u * LANE, (u + 1) * LANE)
            total = part[:, lanes]
            for ref in got:
                total = total + ref[:, lanes].astype(F32)
            out[lanes, :] = total.T
            outs[0].flush(pl.ds(u * LANE, LANE))

    return staged(
        body, [Far(own_part)] + [Far(v, moved=True) for v in received], [plain((own, dim), F32)], [], "finish_inputs", 16
    )[0]


def finish_weights(second, first, other, epd, hid_n, out_n, dim, doms, exps, rows_n):
    m_sec, m_first, m_tow = layout(epd, hid_n, out_n, dim, doms, rows_n)
    ke = doms * exps

    def body(ins, outs, buf, tgf):
        out_f, out_s, out_t, out_g = (o.buf for o in outs)
        c = lax.rem(lax.axis_index(WIDTH), 2)
        r = lax.axis_index(ROWS)
        at_row = [spots(kind, r, rows_n) for kind in range(2)]
        for kind, size in ((0, m_sec), (1, m_first)):
            got = ins[kind].get()
            step = math.gcd(size, hid_n)
            for i, q, flat in pieces(kind, epd, hid_n, out_n, dim):
                for off in range(0, hid_n, step):
                    j, o = divmod(flat + off, size)
                    piece = got[at_row[kind][j], o : o + step, :].astype(F32)
                    if kind == 0:
                        out_s[i, off : off + step, q * LANE : (q + 1) * LANE] = piece
                    else:
                        buf[off : off + step, :] = piece
                if kind == 1:
                    out_f[i, q * LANE : (q + 1) * LANE, :] = buf[...].T
                if q == (out_n, dim)[kind] // LANE - 1:
                    outs[1 - kind].flush(i)
        near, sib = ins[1].get(), ins[2].get()
        for j in range(rows_n):
            at = at_row[1][j]
            for core, value in ((c, near[at, m_first:, :]), (1 - c, sib[at])):
                start = pl.multiple_of((core * rows_n + j) * m_tow, 8)
                tgf[pl.ds(start, m_tow), :] = value.astype(F32)
        for k in range(doms):
            out_t[k] = tgf[k * out_n : (k + 1) * out_n, :]
        outs[2].flush()
        for q in range(dim // LANE):
            at = doms * out_n + q * 32
            out_g[:, q * LANE : (q + 1) * LANE] = tgf[at : at + ke, :]
        outs[3].flush()

    def stacked(refs, buf):
        size = rows_n // len(refs)
        return [(ref, buf.at[i * size : (i + 1) * size]) for i, ref in enumerate(refs)]

    return staged(
        body,
        [
            Far(second, (rows_n, m_sec, LANE), stacked, True),
            Far(first, (rows_n, m_first + m_tow, LANE), stacked, True),
            Far(other, moved=True),
        ],
        [
            plain((epd, dim, hid_n), F32),
            plain((epd, hid_n, out_n), F32),
            plain((doms, out_n, LANE), F32),
            plain((ke, dim), F32),
        ],
        [pltpu.VMEM((hid_n, LANE), F32), pltpu.VMEM((2 * rows_n * m_tow, LANE), F32)],
        "finish_weights",
        24,
    )


def swap(value, axis, mask):
    size = lax.axis_size(axis)
    return lax.ppermute(value, axis, [(i, i ^ mask) for i in range(size)])


def total(*values):
    got = values[0].astype(F32)
    for value in values[1:]:
        got = got + value.astype(F32)
    return got


def send(value, axis, mask):
    return swap(value.astype(BF16), axis, mask)


together = lax.optimization_barrier


def reduce_rows(second, first, towers, beside):
    n_rows, n_width = lax.axis_size(ROWS), lax.axis_size(WIDTH)
    half = n_rows // 2
    far = [2 * q for q in range(1, half)]
    low = total(*(v[half:] for v in first)).astype(BF16)
    high = [total(*(v[m : m + 2] for v in second)).astype(BF16) for m in far]
    across = total(*towers).astype(BF16)
    low, high, across = together((low, high, across))
    first_got = swap(low, ROWS, 1)
    second_got = [swap(v, ROWS, m) for v, m in zip(high, far)]
    towers = total(*towers, *(swap(across, WIDTH, mask) for mask in range(2, n_width, 2)))
    tower_low, operand = together((towers[half:].astype(BF16), beside[1]))
    tower_got = swap(tower_low, ROWS, 1)
    inputs_part = tuple(beside[0](operand))
    first_got, second_got, tower_got, inputs_part = together((first_got, second_got, tower_got, inputs_part))

    def piece(q):
        return jnp.concatenate(
            [total(*(v[q] for v in first), first_got[q]), total(towers[q], tower_got[q])], axis=0
        )

    pair = total(*(v[:2] for v in second), *second_got)
    high = [piece(q).astype(BF16) for q in range(1, half)]
    high, low = together((high, pair[1].astype(BF16)))
    moved = [swap(v, ROWS, m) for v, m in zip(high, far)]
    moved, low = together((moved, swap(low, ROWS, 1)))
    return total(pair[0], low).astype(BF16), total(piece(0), *moved).astype(BF16), inputs_part


def gather_rows(second, first, beside):
    half = lax.axis_size(ROWS) // 2
    far = [2 * q for q in range(1, half)]
    second, first = together((second, first))
    low, high = together((swap(second, ROWS, 1), [swap(first, ROWS, m) for m in far]))
    pair, evens = together((jnp.stack([second, low]), jnp.stack([first] + high)))
    low, high = swap(evens, ROWS, 1), [swap(pair, ROWS, m) for m in far]
    low, high, beside = together((low, high, beside))
    return [pair] + high, [evens, low], beside


def local(inputs, w_first, w_second, w_gate, w_tower, norm_scale, norm_shift, w_head, domains, labels):
    n_width, n_rows = lax.axis_size(WIDTH), lax.axis_size(ROWS)
    devices = n_width * n_rows
    own = inputs.shape[0] // n_width
    count = float(own * devices)
    dim = inputs.shape[1]
    epd, _, hid_n = w_first.shape
    out_n = w_second.shape[2]
    doms, _, exps = w_gate.shape
    ke = doms * exps
    n_x = n_width // 2
    others = list(range(1, n_x))
    w1 = (w_first, swap(w_first, WIDTH, 1))
    w2 = (w_second, swap(w_second, WIDTH, 1))
    wgate_t = jnp.transpose(w_gate, (0, 2, 1)).reshape(ke, dim)
    marks = jnp.stack([domains, labels])

    far = forward(others, inputs, w1, w2, wgate_t, w_tower, own, False, BF16, "forward_send")[0]
    sent = [swap(far[s - 1 : s], WIDTH, 2 * s) for s in others]
    mine = forward([0], inputs, w1, w2, wgate_t, w_tower, own, True, F32, "forward_own")
    foreign = forward(others, inputs, w1, w2, wgate_t, w_tower, own, True, None, "forward_foreign")
    tower, low, message = combine(mine[5], sent, marks, devices)
    stats = lax.all_to_all(message, BOTH, 0, 0, tiled=True)
    lows = [swap(low, WIDTH, 2 * s) for s in others]
    stats, lows = lax.optimization_barrier((stats, lows))
    params, message = normalise(stats, tower, marks, norm_scale, norm_shift, w_head, devices, count)
    sums = lax.all_to_all(message, BOTH, 0, 0, tiled=True)

    acts = [(mine[:5], 0)] + [(foreign[:5], s - 1) for s in others]
    small, loss, sec_sib, first_sib, sec_own, first_own, tow_sib, tow_own, pg, lg = backward(
        sums, params, tower, lows, marks, acts, inputs, w2, wgate_t, w_tower, devices, n_rows, count
    )
    second, first, (gi_own, gi_out) = reduce_rows(
        (sec_own, swap(sec_sib, WIDTH, 1)),
        (first_own, swap(first_sib, WIDTH, 1)),
        (tow_own, swap(tow_sib, WIDTH, 1)),
        (lambda grad: backward_inputs(grad, lg, w1, wgate_t, own), pg),
    )
    grad_inputs = finish_inputs(gi_own, [swap(gi_out[s - 1], WIDTH, 2 * s) for s in others])
    second, first, grad_inputs = gather_rows(second, first, grad_inputs)
    m_first = layout(epd, hid_n, out_n, dim, doms, n_rows)[1]
    other = swap(jnp.concatenate([v[:, m_first:] for v in first]), WIDTH, 1)
    grad_first, grad_second, grad_tower, grad_gate = finish_weights(
        second, first, other, epd, hid_n, out_n, dim, doms, exps, n_rows
    )
    return (
        loss[0, 0],
        grad_inputs,
        grad_first,
        grad_second,
        grad_gate.reshape(doms, exps, dim).transpose(0, 2, 1),
        grad_tower,
        small[doms : 2 * doms],
        small[:doms],
        small[2 * doms : 3 * doms],
    )


def solution(mesh):
    placed = (
        P(ROWS, None),
        P(WIDTH, None, None),
        P(WIDTH, None, None),
        P(),
        P(),
        P(),
        P(),
        P(),
        P(BOTH),
        P(BOTH),
    )
    return jax.shard_map(
        local,
        mesh=mesh,
        in_specs=placed,
        out_specs=(
            P(),
            P(BOTH, None),
            P(WIDTH, None, None),
            P(WIDTH, None, None),
            P(),
            P(),
            P(),
            P(),
            P(),
        ),
        check_vma=False,
    )
```

```python
import math

import jax
import jax.numpy as jnp
from jax import lax
from jax.experimental import pallas as pl
from jax.experimental.pallas import tpu as pltpu
from jax.sharding import PartitionSpec as P

F32 = jnp.float32
BF16 = jnp.bfloat16
EPS = 1e-05
LANE = 128
MIB = 1 << 20
ROWS = "rows"
WIDTH = "width"
BOTH = (ROWS, WIDTH)


def mm(a, b):
    return jnp.dot(a, b, preferred_element_type=F32)


def mm_t(a, b, precision=None):
    return lax.dot_general(a, b, (((1,), (1,)), ((), ())), preferred_element_type=F32, precision=precision)


def sigmoid(v):
    return 0.5 * jnp.tanh(0.5 * v) + 0.5


class Source:
    def __init__(self, buf, copies):
        self.buf = buf
        self.waiting = copies
        for copy in copies:
            copy.start()

    def get(self):
        for copy in self.waiting:
            copy.wait()
        self.waiting = []
        return self.buf


class Target:
    def __init__(self, ref, buf, sems):
        self.ref, self.buf, self.sems = ref, buf, sems
        self.waiting = []

    def flush(self, *at):
        if self.ref is None:
            return
        src = self.buf.at[at] if at else self.buf
        dst = self.ref.at[at] if at else self.ref
        copy = pltpu.make_async_copy(src, dst, next(self.sems))
        copy.start()
        self.waiting.append(copy)


class Near:
    def __init__(self, what):
        self.what = what


class Far:
    def __init__(self, arrays, shape=None, pairs=None, moved=False):
        self.moved = moved
        self.arrays = arrays if isinstance(arrays, (list, tuple)) else [arrays]
        self.shape = shape or self.arrays[0].shape
        self.dtype = self.arrays[0].dtype
        self.pairs = pairs or (lambda refs, buf: [(refs[0], buf)])


def staged(body, ins, outs, scratch, name, limit, n_sems=64):
    far_in = [i for i, s in enumerate(ins) if isinstance(s, Far)]
    far_out = [i for i, s in enumerate(outs) if not isinstance(s, Near)]
    args, specs, spans = [], [], []
    hbm = pl.BlockSpec(memory_space=pltpu.HBM)
    vmem = pl.BlockSpec(memory_space=pltpu.VMEM)
    anywhere = pl.BlockSpec(memory_space=pl.ANY)
    for s in ins:
        if isinstance(s, Far):
            spans.append((len(args), len(args) + len(s.arrays)))
            if s.moved:
                args += s.arrays
                specs += [anywhere] * len(s.arrays)
                continue
            args += [pltpu.with_memory_space_constraint(a, pltpu.HBM) for a in s.arrays]
            specs += [hbm] * len(s.arrays)
        else:
            spans.append((len(args), len(args) + 1))
            args.append(s.what)
            specs.append(vmem)
    n_in, n_out = len(args), len(outs)

    def kernel(*refs):
        refs_in, refs_out = refs[:n_in], refs[n_in : n_in + n_out]
        bufs = refs[n_in + n_out :]
        in_bufs = dict(zip(far_in, bufs))
        out_bufs = dict(zip(far_out, bufs[len(far_in) :]))
        rest = bufs[len(far_in) + len(far_out) : -1]
        sems = iter([bufs[-1].at[i] for i in range(n_sems)])
        sources = []
        for i, (start, stop) in enumerate(spans):
            if i in in_bufs:
                pairs = ins[i].pairs(refs_in[start:stop], in_bufs[i])
                sources.append(Source(in_bufs[i], [pltpu.make_async_copy(a, b, next(sems)) for a, b in pairs]))
            else:
                sources.append(Source(refs_in[start], []))
        targets = []
        for i, ref in enumerate(refs_out):
            targets.append(Target(ref, out_bufs[i], sems) if i in out_bufs else Target(None, ref, sems))
        body(sources, targets, *rest)
        for s in sources:
            s.get()
        for t in targets:
            for copy in t.waiting:
                copy.wait()

    return pl.pallas_call(
        kernel,
        out_shape=[o.what if isinstance(o, Near) else pltpu.HBM(o.shape, o.dtype) for o in outs],
        in_specs=specs,
        out_specs=[hbm if i in far_out else vmem for i in range(n_out)],
        scratch_shapes=[pltpu.VMEM(ins[i].shape, ins[i].dtype) for i in far_in]
        + [pltpu.VMEM(outs[i].shape, outs[i].dtype) for i in far_out]
        + list(scratch)
        + [pltpu.SemaphoreType.DMA((n_sems,))],
        compiler_params=pltpu.CompilerParams(vmem_limit_bytes=limit * MIB),
        name=name,
    )(*args)


def plain(shape, dtype):
    return jax.ShapeDtypeStruct(shape, dtype)


def row_blocks(slots, own):
    def pairs(refs, buf):
        w = lax.axis_index(WIDTH)
        got = []
        for n, s in enumerate(slots):
            start = pl.multiple_of(lax.bitwise_xor(w, 2 * s) * own, own)
            got.append((refs[0].at[pl.ds(start, own), :], buf.at[n * own : (n + 1) * own, :]))
        return got

    return pairs


def reorder(ke, epd):
    first = lax.axis_index(WIDTH) * epd
    down = lax.broadcasted_iota(jnp.int32, (ke, ke), 0)
    across = lax.broadcasted_iota(jnp.int32, (ke, ke), 1)
    return jnp.where(lax.bitwise_xor(down, first) == across, 1.0, 0.0).astype(BF16)


def forward(slots, inputs, w1, w2, wgate_t, wtower, own, keep, send, name):
    ns = len(slots)
    dim = inputs.shape[1]
    epd, _, hid_n = w1[0].shape
    out_n = w2[0].shape[2]
    ce = 2 * epd
    ke = wgate_t.shape[0]
    doms, _, th = wtower.shape
    exps = ke // doms

    def body(ins, outs, w1t, w2t, wt, pre, *bufs):
        xs, w1o, w1s, wgs, w2o, w2s, wts = ins
        if keep:
            hid, slope, vals, gate, mixed = (o.buf for o in outs[:5])
        else:
            hid, vals, gate, mixed = bufs
        x = xs.get()
        for g, src in enumerate((w1o, w1s)):
            ref = src.get()
            for i in range(epd):
                e = g * epd + i
                w1t[e * hid_n : (e + 1) * hid_n, :] = ref[i].T
        w1t[ce * hid_n : ce * hid_n + ke, :] = mm(reorder(ke, epd), wgs.get()[...]).astype(BF16)
        for n in range(ns):
            pre[...] = mm_t(w1t[...], x[n * own : (n + 1) * own, :])
            if n == 0:
                for g, src in enumerate((w2o, w2s)):
                    ref = src.get()
                    for i in range(epd):
                        w2t[g * epd + i] = ref[i].T
                ref = wts.get()
                for k in range(doms):
                    wt[k] = ref[k].T
            logits = pre[ce * hid_n : ce * hid_n + ke, :].reshape(doms, exps, own)
            top = jnp.exp(logits - jnp.max(logits, axis=1, keepdims=True))
            soft = top / jnp.sum(top, axis=1, keepdims=True)
            gate[n] = soft.reshape(ke, own)

            def act(i, carry):
                at = pl.ds(pl.multiple_of(i * 16, 16), 16)
                v = pre[at, :]
                s = sigmoid(v)
                h = v * s
                hid[n, at, :] = h.astype(BF16)
                if keep:
                    slope[n, at, :] = (s + h * (1.0 - s)).astype(BF16)
                return carry

            lax.fori_loop(0, ce * hid_n // 16, act, 0, unroll=4)
            for e in range(ce):
                vals[n, e * out_n : (e + 1) * out_n, :] = mm(
                    w2t[e], hid[n, e * hid_n : (e + 1) * hid_n, :]
                ).astype(BF16)
            if keep:
                for o in outs[:4]:
                    o.flush(n)
            for u in range(own // LANE):
                part = slice(u * LANE, (u + 1) * LANE)
                rows = [[gate[n, k * exps + e : k * exps + e + 1, part] for e in range(ce)] for k in range(doms)]

                def mix(i, carry):
                    acc = [None] * doms
                    for e in range(ce):
                        at = pl.ds(pl.multiple_of(e * out_n + i * 32, 32), 32)
                        v = vals[n, at, part].astype(F32)
                        for k in range(doms):
                            term = rows[k][e] * v
                            acc[k] = term if e == 0 else acc[k] + term
                    for k in range(doms):
                        at = pl.ds(pl.multiple_of(k * out_n + i * 32, 32), 32)
                        mixed[n, at, part] = acc[k].astype(BF16)
                    return carry

                lax.fori_loop(0, out_n // 32, mix, 0, unroll=4)
            if keep:
                outs[4].flush(n)
            if n == 0 or not keep:
                tower = outs[-1]
                for k in range(doms):
                    tower.buf[n, k * th : (k + 1) * th, :] = mm(
                        wt[k], mixed[n, k * out_n : (k + 1) * out_n, :]
                    ).astype(send)
                tower.flush(n)

    kept = [
        plain((ns, ce * hid_n, own), BF16),
        plain((ns, ce * hid_n, own), BF16),
        plain((ns, ce * out_n, own), BF16),
        plain((ns, ke, own), F32),
        plain((ns, doms * out_n, own), BF16),
    ]
    outs = list(kept) if keep else []
    outs.append(Near(plain((1 if keep else ns, doms * th, own), send)))
    scratch = [
        pltpu.VMEM((ce * hid_n + ke, dim), BF16),
        pltpu.VMEM((ce, out_n, hid_n), BF16),
        pltpu.VMEM((doms, th, out_n), BF16),
        pltpu.VMEM((ce * hid_n + ke, own), F32),
    ]
    if not keep:
        scratch += [pltpu.VMEM(kept[i].shape, kept[i].dtype) for i in (0, 2, 3, 4)]
    ins = [Far(inputs, (ns * own, dim), row_blocks(slots, own))]
    ins += [Far(w1[0]), Far(w1[1], moved=True), Far(wgate_t), Far(w2[0]), Far(w2[1], moved=True), Far(wtower)]
    return staged(body, ins, outs, scratch, name, 40)


def combine(own_part, received, marks, devices):
    _, rows, own = own_part.shape
    doms = rows // LANE

    def body(ins, outs, cols):
        part = ins[0].get()
        got = [s.get() for s in ins[2:]]
        tower, low, message = (o.buf for o in outs)
        cols[...] = jnp.zeros_like(cols)
        for k in range(doms):
            at = slice(k * LANE, (k + 1) * LANE)
            total = part[0, at, :]
            for ref in got:
                total = total + ref[0, at, :].astype(F32)
            tower[at, :] = total
            low[at, :] = total.astype(BF16)
            mean = jnp.sum(total, axis=1, keepdims=True) * (1.0 / own)
            dev = total - mean
            cols[:, k : k + 1] = mean
            cols[:, doms + k : doms + k + 1] = jnp.sum(dev * dev, axis=1, keepdims=True)
        outs[0].flush()
        pair = jnp.concatenate([ins[1].get()[...].astype(F32), jnp.zeros((14, own), F32)], axis=0)
        low[rows:, :] = pair.astype(BF16)
        outs[1].flush()
        tile = cols[...].T[:8, :]
        for d in range(devices):
            message[d * 8 : (d + 1) * 8, :] = tile
        outs[2].flush()

    return staged(
        body,
        [Near(own_part), Far(marks)] + [Near(v) for v in received],
        [plain((rows, own), F32), Near(plain((rows + 16, own), BF16)), Near(plain((devices * 8, LANE), F32))],
        [pltpu.VMEM((LANE, LANE), F32)],
        "combine",
        16,
    )


def pick(dom, values):
    got = values[-1]
    for k in range(len(values) - 2, -1, -1):
        got = jnp.where(dom == k, values[k], got)
    return got


def chosen_tower(tower, dom, wide, lanes, doms):
    values = [tower[k * LANE : (k + 1) * LANE, lanes].astype(F32) for k in range(doms)]
    mean, gain, shift, head = (pick(dom, [wide[j * doms + k] for k in range(doms)]) for j in range(4))
    centred = pick(dom, values) - mean
    return values, centred, centred * gain + shift, gain, head


def spread_columns(wide, rows_ref, n):
    cols = rows_ref[...].T
    for j in range(n):
        wide[j] = jnp.broadcast_to(cols[:, j : j + 1], (LANE, LANE))


def normalise(stats, tower, marks, scale, shift, head, devices, count):
    rows, own = tower.shape
    doms = rows // LANE

    def body(ins, outs, prm, wide, q):
        st, tws, mks, sc, sh, hd = ins
        params, message = (o.buf for o in outs)
        prm[...] = jnp.zeros_like(prm)
        got = st.get()[...].reshape(devices, 8, LANE)
        total = jnp.sum(got, axis=0)
        mean = total * (1.0 / devices)
        dev = got - mean[None]
        spread = jnp.sum(dev * dev, axis=0) * float(own)
        var = (total[doms : 2 * doms] + spread[:doms]) * (1.0 / count)
        inv = lax.rsqrt(var + EPS)
        prm[0:doms, :] = mean[:doms]
        prm[doms : 2 * doms, :] = inv * sc.get()[...]
        prm[2 * doms : 3 * doms, :] = sh.get()[...]
        prm[3 * doms : 4 * doms, :] = hd.get()[...]
        prm[4 * doms : 5 * doms, :] = inv
        params[:16, :] = prm[:16, :]
        spread_columns(wide, prm, 4 * doms)
        tw, mk = tws.get(), mks.get()
        loss = jnp.zeros((1, LANE), F32)
        for u in range(own // LANE):
            part = slice(u * LANE, (u + 1) * LANE)
            dom = mk[0:1, part]
            target = mk[1:2, part].astype(F32)
            _, centred, affine, _, head_w = chosen_tower(tw, dom, wide, part, doms)
            s = sigmoid(affine)
            act = affine * s
            chosen = jnp.sum(act * head_w, axis=0, keepdims=True)
            soft = jnp.maximum(chosen, 0.0) + jnp.log(1.0 + jnp.exp(-jnp.abs(chosen)))
            loss = loss + (soft - target * chosen)
            score_grad = (sigmoid(chosen) - target) * (1.0 / count)
            grad = score_grad * head_w * (s + act * (1.0 - s))
            q[0:LANE, part] = grad
            q[LANE : 2 * LANE, part] = grad * centred
            q[2 * LANE :, part] = score_grad * act
        kinds = lax.broadcasted_iota(jnp.int32, (8, own), 0)
        one_hot = (kinds == mk[0:1, :]).astype(F32)
        sums = mm_t(one_hot, q[...], lax.Precision.HIGHEST)[:doms]
        tile = [sums[:, :LANE], sums[:, LANE : 2 * LANE] * inv]
        all_rows = jnp.concatenate(tile + [loss, jnp.zeros((1, LANE), F32)], axis=0)
        for d in range(devices):
            message[d * 8 : (d + 1) * 8, :] = all_rows
        params[16:, :] = jnp.concatenate([sums[:, 2 * LANE :], jnp.zeros((8 - doms, LANE), F32)], axis=0)
        outs[0].flush()

    return staged(
        body,
        [Far(stats, moved=True), Far(tower), Far(marks), Far(scale), Far(shift), Far(head)],
        [plain((24, LANE), F32), Near(plain((devices * 8, LANE), F32))],
        [
            pltpu.VMEM((LANE, LANE), F32),
            pltpu.VMEM((4 * doms, LANE, LANE), F32),
            pltpu.VMEM((3 * LANE, own), F32),
        ],
        "normalise",
        16,
    )


def layout(epd, hid_n, out_n, dim, doms, rows_n):
    second = epd * hid_n * out_n // LANE
    first = epd * hid_n * dim // LANE
    towers = -(-(doms * out_n + (dim // LANE) * 32) // (2 * 16 * rows_n)) * 16
    return second // rows_n, first // rows_n, towers


def pieces(kind, epd, hid_n, out_n, dim):
    flat = 0
    for i in range(epd):
        for q in range((out_n, dim)[kind] // LANE):
            yield i, q, flat
            flat += hid_n


def spots(kind, row, rows_n):
    got = []
    for j in range(rows_n):
        p = lax.bitwise_xor(row, j)
        got.append(p if kind == 0 else (p & 1) * (rows_n // 2) + lax.shift_right_logical(p, 1))
    return got


def backward(sums, params, tower, low_towers, marks, acts, inputs, w2, wgate_t, wtower, devices, rows_n, count):
    ns = 1 + len(low_towers)
    t_rows, own = tower.shape
    total_n = ns * own
    dim = inputs.shape[1]
    epd, hid_n, out_n = w2[0].shape
    ce = 2 * epd
    ke = wgate_t.shape[0]
    doms, _, th = wtower.shape
    exps = ke // doms
    m_sec, m_first, m_tow = layout(epd, hid_n, out_n, dim, doms, rows_n)

    def body(ins, outs, wide, prm, tg, mg, eg, gg, srow, tgf, facc):
        sm, pr, tw0, mk0 = ins[:4]
        low = ins[4 : 3 + ns]
        wts, gate, vals, w2o, w2s, slope, xs, hid, mixed = ins[3 + ns :]
        small, loss_out, sec_sib, first_sib, sec_mine, first_mine, tow_sib, tow_mine, pgs, lgs = outs
        pg, lg = pgs.buf, lgs.buf
        c = lax.rem(lax.axis_index(WIDTH), 2)
        r = lax.axis_index(ROWS)
        at_row = [spots(kind, r, rows_n) for kind in range(2)]
        prm[...] = jnp.zeros_like(prm)
        total = jnp.sum(sm.get()[...].reshape(devices, 8, LANE), axis=0)
        small.buf[...] = total
        loss_out.buf[...] = jnp.sum(total[2 * doms : 2 * doms + 1, :], axis=1, keepdims=True) * (1.0 / count)
        small.flush()
        loss_out.flush()
        given = pr.get()[...]
        gain, inv = given[doms : 2 * doms], given[4 * doms : 5 * doms]
        prm[0:16, :] = given[:16]
        prm[4 * doms : 5 * doms, :] = gain * total[:doms] * (1.0 / count)
        prm[5 * doms : 6 * doms, :] = gain * inv * total[doms : 2 * doms] * (1.0 / count)
        spread_columns(wide, prm, 6 * doms)
        for u in range(total_n // LANE):
            n = u * LANE // own
            part = slice(u * LANE, (u + 1) * LANE)
            here = slice(u * LANE - n * own, (u + 1) * LANE - n * own)
            if n == 0:
                tw = tw0.get()
                dom = mk0.get()[0:1, here]
                target = mk0.get()[1:2, here].astype(F32)
            else:
                tw = low[n - 1].get()
                pair = tw[t_rows : t_rows + 16, here].astype(F32)
                dom = pair[0:1].astype(jnp.int32)
                target = pair[1:2]
            values, _, affine, gain_s, head_w = chosen_tower(tw, dom, wide, here, doms)
            s = sigmoid(affine)
            a = affine * s
            chosen = jnp.sum(a * head_w, axis=0, keepdims=True)
            score_grad = (sigmoid(chosen) - target) * (1.0 / count)
            grad = gain_s * (score_grad * head_w * (s + a * (1.0 - s)))
            for k in range(doms):
                v = jnp.where(dom == k, grad, 0.0) - wide[4 * doms + k]
                v = v - (values[k] - wide[k]) * wide[5 * doms + k]
                down = v.astype(BF16)
                tg[k * th : (k + 1) * th, part] = down
                srow[k : k + 1, part] = jnp.sum(down.astype(F32) * values[k], axis=0, keepdims=True)
        wt = wts.get()
        for k in range(doms):
            mg[k * out_n : (k + 1) * out_n, :] = mm(wt[k], tg[k * th : (k + 1) * th, :])
        vals, gate = vals.get(), gate.get()
        gg[...] = jnp.zeros_like(gg)
        for u in range(total_n // LANE):
            part = slice(u * LANE, (u + 1) * LANE)
            rows = [[gate[k * exps + e : k * exps + e + 1, part] for e in range(ce)] for k in range(doms)]

            def spread(i, acc):
                up = [mg[pl.ds(pl.multiple_of(k * out_n + i * 16, 16), 16), part] for k in range(doms)]
                acc = list(acc)
                for e in range(ce):
                    at = pl.ds(pl.multiple_of(e * out_n + i * 16, 16), 16)
                    v = vals[at, part].astype(F32)
                    back = None
                    for k in range(doms):
                        term = rows[k][e] * up[k]
                        back = term if k == 0 else back + term
                        prod = up[k] * v
                        acc[k * ce + e] = acc[k * ce + e] + (prod[:8] + prod[8:])
                    eg[at, part] = back.astype(BF16)
                return tuple(acc)

            zero = jnp.zeros((8, LANE), F32)
            acc = lax.fori_loop(0, out_n // 16, spread, (zero,) * (doms * ce), unroll=4)
            for k in range(doms):
                for e in range(ce):
                    dot = jnp.sum(acc[k * ce + e], axis=0, keepdims=True)
                    gg[k * exps + e : k * exps + e + 1, part] = rows[k][e] * (dot - srow[k : k + 1, part])
        lg[...] = mm(reorder(ke, epd), gg[...].astype(BF16)).astype(BF16)
        lgs.flush()
        slope, hid = slope.get(), hid.get()

        def put(kind, slot, values):
            target = ((sec_sib, first_sib), (sec_mine, first_mine))[slot < epd][kind]
            size = (m_sec, m_first)[kind]
            step = math.gcd(size, hid_n)
            for i, q, flat in pieces(kind, epd, hid_n, out_n, dim):
                if i == slot % epd:
                    for off in range(0, hid_n, step):
                        j, o = divmod(flat + off, size)
                        part = values[off : off + step, q * LANE : (q + 1) * LANE]
                        target.buf[at_row[kind][j], o : o + step, :] = part.astype(BF16)

        for g, src in enumerate((w2o, w2s)):
            ref = src.get()
            for i in range(epd):
                e = g * epd + i
                at = slice(e * hid_n, (e + 1) * hid_n)
                at_o = slice(e * out_n, (e + 1) * out_n)
                for u in range(ns):
                    part = slice(u * own, (u + 1) * own)
                    pg[at, part] = (mm(ref[i], eg[at_o, part]) * slope[at, part].astype(F32)).astype(BF16)
        pgs.flush()
        x = xs.get()
        facc[...] = mm(pg[...], x[...])
        for e in range(ce):
            put(1, e, facc[e * hid_n : (e + 1) * hid_n, :])
        for e in range(ce):
            at = slice(e * hid_n, (e + 1) * hid_n)
            at_o = slice(e * out_n, (e + 1) * out_n)
            put(0, e, mm_t(hid[at, :], eg[at_o, :]))
        for target in (sec_sib, first_sib, sec_mine, first_mine):
            target.flush()
        mixed = mixed.get()
        tgf[doms * out_n :, :] = jnp.zeros((tgf.shape[0] - doms * out_n, LANE), F32)
        for k in range(doms):
            tgf[k * out_n : (k + 1) * out_n, :] = mm_t(
                mixed[k * out_n : (k + 1) * out_n, :], tg[k * th : (k + 1) * th, :]
            )
        part_g = mm(lg[...], x[...])
        for q in range(dim // LANE):
            tgf[doms * out_n + q * 32 : doms * out_n + q * 32 + ke, :] = part_g[:, q * LANE : (q + 1) * LANE]
        tgf[doms * out_n + ke : doms * out_n + 32, :] = given[16 : 48 - ke]
        for target, core in ((tow_sib, 1 - c), (tow_mine, c)):
            for j in range(rows_n):
                start = pl.multiple_of((core * rows_n + j) * m_tow, 8)
                target.buf[at_row[1][j], :, :] = tgf[pl.ds(start, m_tow), :].astype(BF16)
            target.flush()

    outs = [
        plain((8, LANE), F32),
        plain((1, 1), F32),
        Near(plain((rows_n, m_sec, LANE), BF16)),
        Near(plain((rows_n, m_first, LANE), BF16)),
        Near(plain((rows_n, m_sec, LANE), BF16)),
        Near(plain((rows_n, m_first, LANE), BF16)),
        Near(plain((rows_n, m_tow, LANE), BF16)),
        Near(plain((rows_n, m_tow, LANE), BF16)),
        Near(plain((ce * hid_n, total_n), BF16)),
        Near(plain((ke, total_n), BF16)),
    ]
    scratch = [
        pltpu.VMEM((6 * doms, LANE, LANE), F32),
        pltpu.VMEM((LANE, LANE), F32),
        pltpu.VMEM((doms * th, total_n), BF16),
        pltpu.VMEM((doms * out_n, total_n), F32),
        pltpu.VMEM((ce * out_n, total_n), BF16),
        pltpu.VMEM((ke, total_n), F32),
        pltpu.VMEM((8, total_n), F32),
        pltpu.VMEM((2 * rows_n * m_tow, LANE), F32),
        pltpu.VMEM((ce * hid_n, dim), F32),
    ]

    def side_by_side(which):
        def pairs(refs, buf):
            return [(r.at[n], buf.at[:, i * own : (i + 1) * own]) for i, (r, (_, n)) in enumerate(zip(refs, acts))]

        arrays = [a[which] for a, _ in acts]
        return Far(arrays, (arrays[0].shape[1], total_n), pairs)

    ins = [Far(sums, moved=True), Far(params), Far(tower), Far(marks)]
    ins += [Far(v, moved=True) for v in low_towers]
    ins += [Far(wtower), side_by_side(3), side_by_side(2), Far(w2[0]), Far(w2[1], moved=True), side_by_side(1)]
    ins += [Far(inputs, (total_n, dim), row_blocks(list(range(ns)), own)), side_by_side(0), side_by_side(4)]
    return staged(body, ins, outs, scratch, "backward", 44)


def backward_inputs(pg, lg, w1, wgate_t, own):
    total_n = pg.shape[1]
    ns = total_n // own
    epd, dim, hid_n = w1[0].shape
    ce = 2 * epd
    ke = wgate_t.shape[0]

    def body(ins, outs, w1c):
        w1o, w1s, wgs, pgs, lgs = ins
        wg = jnp.concatenate([wgs.get()[...], jnp.zeros((LANE - ke, dim), BF16)], axis=0).T[:, :ke]
        for g, src in enumerate((w1o, w1s)):
            ref = src.get()
            for i in range(epd):
                e = g * epd + i
                w1c[:, e * hid_n : (e + 1) * hid_n] = ref[i]
        pg, lg = pgs.get(), lgs.get()
        for n in range(ns - 1, -1, -1):
            part = slice(n * own, (n + 1) * own)
            gi = mm(w1c[...], pg[:, part]) + mm(wg, lg[:, part])
            if n:
                outs[1].buf[n - 1] = gi.astype(BF16)
                outs[1].flush(n - 1)
            else:
                outs[0].buf[...] = gi
                outs[0].flush()

    return staged(
        body,
        [Far(w1[0]), Far(w1[1], moved=True), Far(wgate_t), Near(pg), Near(lg)],
        [Near(plain((dim, own), F32)), Near(plain((max(ns - 1, 1), dim, own), BF16))],
        [pltpu.VMEM((dim, ce * hid_n), BF16)],
        "backward_inputs",
        16,
    )


def finish_inputs(own_part, received):
    dim, own = own_part.shape

    def body(ins, outs):
        got = [s.get() for s in ins[1:]]
        part = ins[0].get()
        out = outs[0].buf
        for u in range(own // LANE):
            lanes = slice(u * LANE, (u + 1) * LANE)
            total = part[:, lanes]
            for ref in got:
                total = total + ref[:, lanes].astype(F32)
            out[lanes, :] = total.T
            outs[0].flush(pl.ds(u * LANE, LANE))

    return staged(
        body, [Near(own_part)] + [Near(v) for v in received], [plain((own, dim), F32)], [], "finish_inputs", 12
    )[0]


def finish_weights(second, first, other, epd, hid_n, out_n, dim, doms, exps, rows_n):
    m_sec, m_first, m_tow = layout(epd, hid_n, out_n, dim, doms, rows_n)
    ke = doms * exps

    def body(ins, outs, buf, tgf):
        out_f, out_s, out_t, out_g, out_h = (o.buf for o in outs)
        c = lax.rem(lax.axis_index(WIDTH), 2)
        r = lax.axis_index(ROWS)
        at_row = [spots(kind, r, rows_n) for kind in range(2)]
        for kind, size in ((0, m_sec), (1, m_first)):
            got = ins[kind].get()
            step = math.gcd(size, hid_n)
            for i, q, flat in pieces(kind, epd, hid_n, out_n, dim):
                for off in range(0, hid_n, step):
                    j, o = divmod(flat + off, size)
                    piece = got[at_row[kind][j], o : o + step, :].astype(F32)
                    if kind == 0:
                        out_s[i, off : off + step, q * LANE : (q + 1) * LANE] = piece
                    else:
                        buf[off : off + step, :] = piece
                if kind == 1:
                    out_f[i, q * LANE : (q + 1) * LANE, :] = buf[...].T
                if q == (out_n, dim)[kind] // LANE - 1:
                    outs[1 - kind].flush(i)
        near, sib = ins[1].get(), ins[2].get()
        for j in range(rows_n):
            at = at_row[1][j]
            for core, value in ((c, near[at, m_first:, :]), (1 - c, sib[at])):
                start = pl.multiple_of((core * rows_n + j) * m_tow, 8)
                tgf[pl.ds(start, m_tow), :] = value.astype(F32)
        for k in range(doms):
            out_t[k] = tgf[k * out_n : (k + 1) * out_n, :]
        outs[2].flush()
        for q in range(dim // LANE):
            at = doms * out_n + q * 32
            out_g[:, q * LANE : (q + 1) * LANE] = tgf[at : at + ke, :]
        outs[3].flush()
        out_h[...] = tgf[doms * out_n + ke : doms * out_n + ke + doms, :]
        outs[4].flush()

    return staged(
        body,
        [Near(second), Near(first), Near(other)],
        [
            plain((epd, dim, hid_n), F32),
            plain((epd, hid_n, out_n), F32),
            plain((doms, out_n, LANE), F32),
            plain((ke, dim), F32),
            plain((doms, LANE), F32),
        ],
        [pltpu.VMEM((hid_n, LANE), F32), pltpu.VMEM((2 * rows_n * m_tow, LANE), F32)],
        "finish_weights",
        16,
    )


def swap(value, axis, mask):
    size = lax.axis_size(axis)
    return lax.ppermute(value, axis, [(i, i ^ mask) for i in range(size)])


def total(*values):
    got = values[0].astype(F32)
    for value in values[1:]:
        got = got + value.astype(F32)
    return got


def send(value, axis, mask):
    return swap(value.astype(BF16), axis, mask)


together = lax.optimization_barrier


def reduce_rows(second, first, towers, beside):
    n_rows, n_width = lax.axis_size(ROWS), lax.axis_size(WIDTH)
    half = n_rows // 2
    far = [2 * q for q in range(1, half)]
    low = total(*(v[half:] for v in first)).astype(BF16)
    high = [total(*(v[m : m + 2] for v in second)).astype(BF16) for m in far]
    across = total(*towers).astype(BF16)
    first_got = swap(low, ROWS, 1)
    second_got = [swap(v, ROWS, m) for v, m in zip(high, far)]
    towers = total(*towers, *(swap(across, WIDTH, mask) for mask in range(2, n_width, 2)))
    tower_got = swap(towers[half:].astype(BF16), ROWS, 1)
    first_got, second_got, tower_got, operand = together((first_got, second_got, tower_got, beside[1]))

    def piece(q):
        return jnp.concatenate(
            [total(*(v[q] for v in first), first_got[q]), total(towers[q], tower_got[q])], axis=0
        )

    pair = total(*(v[:2] for v in second), *second_got)
    high = [piece(q).astype(BF16) for q in range(1, half)]
    high, low = together((high, pair[1].astype(BF16)))
    moved = [swap(v, ROWS, m) for v, m in zip(high, far)]
    inputs_part = tuple(beside[0](operand))
    moved, low, inputs_part = together((moved, swap(low, ROWS, 1), inputs_part))
    return total(pair[0], low).astype(BF16), total(piece(0), *moved).astype(BF16), inputs_part


def gather_rows(second, first, m_first, beside):
    half = lax.axis_size(ROWS) // 2
    far = [2 * q for q in range(1, half)]
    second, first = together((second, first))
    low, high = together((swap(second, ROWS, 1), [swap(first, ROWS, m) for m in far]))
    pair, evens = together((jnp.stack([second, low]), jnp.stack([first] + high)))
    low, high = swap(evens, ROWS, 1), [swap(pair, ROWS, m) for m in far]
    low, high, beside = together((low, high, beside))
    second, first = jnp.concatenate([pair] + high), jnp.concatenate([evens, low])
    return second, first, swap(first[:, m_first:], WIDTH, 1), beside


def local(inputs, w_first, w_second, w_gate, w_tower, norm_scale, norm_shift, w_head, domains, labels):
    n_width, n_rows = lax.axis_size(WIDTH), lax.axis_size(ROWS)
    devices = n_width * n_rows
    own = inputs.shape[0] // n_width
    count = float(own * devices)
    dim = inputs.shape[1]
    epd, _, hid_n = w_first.shape
    out_n = w_second.shape[2]
    doms, _, exps = w_gate.shape
    ke = doms * exps
    n_x = n_width // 2
    others = list(range(1, n_x))
    w1 = (w_first, swap(w_first, WIDTH, 1))
    w2 = (w_second, swap(w_second, WIDTH, 1))
    wgate_t = jnp.transpose(w_gate, (0, 2, 1)).reshape(ke, dim)
    marks = jnp.stack([domains, labels])

    far = forward(others, inputs, w1, w2, wgate_t, w_tower, own, False, BF16, "forward_send")[0]
    sent = [swap(far[s - 1 : s], WIDTH, 2 * s) for s in others]
    kept = forward([0] + others, inputs, w1, w2, wgate_t, w_tower, own, True, F32, "forward_keep")
    tower, low, message = combine(kept[5], sent, marks, devices)
    stats = lax.all_to_all(message, BOTH, 0, 0, tiled=True)
    lows = [swap(low, WIDTH, 2 * s) for s in others]
    stats, lows = lax.optimization_barrier((stats, lows))
    params, message = normalise(stats, tower, marks, norm_scale, norm_shift, w_head, devices, count)
    sums = lax.all_to_all(message, BOTH, 0, 0, tiled=True)

    acts = [(kept[:5], s) for s in range(n_x)]
    small, loss, sec_sib, first_sib, sec_own, first_own, tow_sib, tow_own, pg, lg = backward(
        sums, params, tower, lows, marks, acts, inputs, w2, wgate_t, w_tower, devices, n_rows, count
    )
    first_sib = swap(first_sib, WIDTH, 1)
    first_sib, sec_sib, tow_sib = together((first_sib, sec_sib, tow_sib))
    second, first, (gi_own, gi_out) = reduce_rows(
        (sec_own, swap(sec_sib, WIDTH, 1)),
        (first_own, first_sib),
        (tow_own, swap(tow_sib, WIDTH, 1)),
        (lambda grad: backward_inputs(grad, lg, w1, wgate_t, own), pg),
    )
    grad_inputs = finish_inputs(gi_own, [swap(gi_out[s - 1], WIDTH, 2 * s) for s in others])
    m_first = layout(epd, hid_n, out_n, dim, doms, n_rows)[1]
    second, first, other, grad_inputs = gather_rows(second, first, m_first, grad_inputs)
    grad_first, grad_second, grad_tower, grad_gate, grad_head = finish_weights(
        second, first, other, epd, hid_n, out_n, dim, doms, exps, n_rows
    )
    return (
        loss[0, 0],
        grad_inputs,
        grad_first,
        grad_second,
        grad_gate.reshape(doms, exps, dim).transpose(0, 2, 1),
        grad_tower,
        small[doms : 2 * doms],
        small[:doms],
        grad_head,
    )


def solution(mesh):
    placed = (
        P(ROWS, None),
        P(WIDTH, None, None),
        P(WIDTH, None, None),
        P(),
        P(),
        P(),
        P(),
        P(),
        P(BOTH),
        P(BOTH),
    )
    return jax.shard_map(
        local,
        mesh=mesh,
        in_specs=placed,
        out_specs=(
            P(),
            P(BOTH, None),
            P(WIDTH, None, None),
            P(WIDTH, None, None),
            P(),
            P(),
            P(),
            P(),
            P(),
        ),
        check_vma=False,
    )
```

```python
import math

import jax
import jax.numpy as jnp
from jax import lax
from jax.experimental import pallas as pl
from jax.experimental.pallas import tpu as pltpu
from jax.sharding import PartitionSpec as P

F32 = jnp.float32
BF16 = jnp.bfloat16
EPS = 1e-05
LANE = 128
MIB = 1 << 20
ROWS = "rows"
WIDTH = "width"
BOTH = (ROWS, WIDTH)


def mm(a, b):
    return jnp.dot(a, b, preferred_element_type=F32)


def mm_t(a, b):
    return lax.dot_general(a, b, (((1,), (1,)), ((), ())), preferred_element_type=F32)


def sigmoid(v):
    return 0.5 * jnp.tanh(0.5 * v) + 0.5


class Source:
    def __init__(self, buf, copies):
        self.buf = buf
        self.waiting = copies
        for copy in copies:
            copy.start()

    def get(self):
        for copy in self.waiting:
            copy.wait()
        self.waiting = []
        return self.buf


class Target:
    def __init__(self, ref, buf, sems):
        self.ref, self.buf, self.sems = ref, buf, sems
        self.waiting = []

    def flush(self, *at):
        if self.ref is None:
            return
        src = self.buf.at[at] if at else self.buf
        dst = self.ref.at[at] if at else self.ref
        copy = pltpu.make_async_copy(src, dst, next(self.sems))
        copy.start()
        self.waiting.append(copy)


class Near:
    def __init__(self, what):
        self.what = what


class Far:
    def __init__(self, arrays, shape=None, pairs=None, moved=False):
        self.moved = moved
        self.arrays = arrays if isinstance(arrays, (list, tuple)) else [arrays]
        self.shape = shape or self.arrays[0].shape
        self.dtype = self.arrays[0].dtype
        self.pairs = pairs or (lambda refs, buf: [(refs[0], buf)])


def staged(body, ins, outs, scratch, name, limit, n_sems=64):
    far_in = [i for i, s in enumerate(ins) if isinstance(s, Far)]
    far_out = [i for i, s in enumerate(outs) if not isinstance(s, Near)]
    args, specs, spans = [], [], []
    hbm = pl.BlockSpec(memory_space=pltpu.HBM)
    vmem = pl.BlockSpec(memory_space=pltpu.VMEM)
    anywhere = pl.BlockSpec(memory_space=pl.ANY)
    for s in ins:
        if isinstance(s, Far):
            spans.append((len(args), len(args) + len(s.arrays)))
            if s.moved:
                args += s.arrays
                specs += [anywhere] * len(s.arrays)
                continue
            args += [pltpu.with_memory_space_constraint(a, pltpu.HBM) for a in s.arrays]
            specs += [hbm] * len(s.arrays)
        else:
            spans.append((len(args), len(args) + 1))
            args.append(s.what)
            specs.append(vmem)
    n_in, n_out = len(args), len(outs)

    def kernel(*refs):
        refs_in, refs_out = refs[:n_in], refs[n_in : n_in + n_out]
        bufs = refs[n_in + n_out :]
        in_bufs = dict(zip(far_in, bufs))
        out_bufs = dict(zip(far_out, bufs[len(far_in) :]))
        rest = bufs[len(far_in) + len(far_out) : -1]
        sems = iter([bufs[-1].at[i] for i in range(n_sems)])
        sources = []
        for i, (start, stop) in enumerate(spans):
            if i in in_bufs:
                pairs = ins[i].pairs(refs_in[start:stop], in_bufs[i])
                sources.append(Source(in_bufs[i], [pltpu.make_async_copy(a, b, next(sems)) for a, b in pairs]))
            else:
                sources.append(Source(refs_in[start], []))
        targets = []
        for i, ref in enumerate(refs_out):
            targets.append(Target(ref, out_bufs[i], sems) if i in out_bufs else Target(None, ref, sems))
        body(sources, targets, *rest)
        for s in sources:
            s.get()
        for t in targets:
            for copy in t.waiting:
                copy.wait()

    return pl.pallas_call(
        kernel,
        out_shape=[o.what if isinstance(o, Near) else pltpu.HBM(o.shape, o.dtype) for o in outs],
        in_specs=specs,
        out_specs=[hbm if i in far_out else vmem for i in range(n_out)],
        scratch_shapes=[pltpu.VMEM(ins[i].shape, ins[i].dtype) for i in far_in]
        + [pltpu.VMEM(outs[i].shape, outs[i].dtype) for i in far_out]
        + list(scratch)
        + [pltpu.SemaphoreType.DMA((n_sems,))],
        compiler_params=pltpu.CompilerParams(vmem_limit_bytes=limit * MIB),
        name=name,
    )(*args)


def plain(shape, dtype):
    return jax.ShapeDtypeStruct(shape, dtype)


def row_blocks(slots, own):
    def pairs(refs, buf):
        w = lax.axis_index(WIDTH)
        got = []
        for n, s in enumerate(slots):
            start = pl.multiple_of(lax.bitwise_xor(w, 2 * s) * own, own)
            got.append((refs[0].at[pl.ds(start, own), :], buf.at[n * own : (n + 1) * own, :]))
        return got

    return pairs


def reorder(ke, epd):
    first = lax.axis_index(WIDTH) * epd
    down = lax.broadcasted_iota(jnp.int32, (ke, ke), 0)
    across = lax.broadcasted_iota(jnp.int32, (ke, ke), 1)
    return jnp.where(lax.bitwise_xor(down, first) == across, 1.0, 0.0).astype(BF16)


def prepare(slots, inputs, w1, w2, wgate_t, wtower, own):
    dim = inputs.shape[1]
    epd, _, hid_n = w1.shape
    out_n = w2.shape[2]
    ke = wgate_t.shape[0]
    doms, _, th = wtower.shape

    def body(ins, outs):
        xs, w1s, wgs, w2s, wts = ins
        x_out, w1t, w2t, wt = (o.buf for o in outs)
        w1_buf = w1s.get()
        for i in range(epd):
            w1t[i * hid_n : (i + 1) * hid_n, :] = w1_buf[i].T
        w1t[epd * hid_n :, :] = mm(reorder(ke, epd), wgs.get()[...]).astype(BF16)
        w2_buf = w2s.get()
        for i in range(epd):
            w2t[i] = w2_buf[i].T
        wt_buf = wts.get()
        for k in range(doms):
            wt[k] = wt_buf[k].T
        x_out[...] = xs.get()[...]

    return staged(
        body,
        [Far(inputs, (len(slots) * own, dim), row_blocks(slots, own))] + [Far(a) for a in (w1, wgate_t, w2, wtower)],
        [
            Near(plain((len(slots) * own, dim), BF16)),
            Near(plain((epd * hid_n + ke, dim), BF16)),
            Near(plain((epd, out_n, hid_n), BF16)),
            Near(plain((doms, th, out_n), BF16)),
        ],
        [],
        "prepare",
        12,
    )


def forward(blocks, w1, w2, wt, own, doms, keep, tower_out, name):
    epd, dim, hid_n = w1[1].shape
    out_n = w2[1].shape[2]
    ce = 2 * epd
    half = epd * hid_n
    ke = w1[0].shape[0] - half
    th = wt.shape[1]
    exps = ke // doms
    sizes = [(b.what if isinstance(b, Near) else b).shape[0] // own for b in blocks]
    ns = sum(sizes)

    def body(ins, outs, w1t, w2t, pre, *bufs):
        xs = ins[: len(blocks)]
        w1o, w1s, w2o, w2s, wts = ins[len(blocks) :]
        if keep:
            hid, slope, vals, gate, mixed = (o.buf for o in outs[:5])
        else:
            hid, vals, gate, mixed = bufs
        wt = wts.get()
        for i in range(epd):
            w1t[i * hid_n : (i + 1) * hid_n, :] = w1s.get()[i].T
            w2t[i] = w2s.get()[i].T
        parts = [(src, n) for src, size in zip(xs, sizes) for n in range(size)]
        for n, (src, place) in enumerate(parts):
            x = src.get()[place * own : (place + 1) * own, :]
            got = mm_t(w1o.get()[...], x)
            pre[:half, :] = got[:half]
            pre[ce * hid_n :, :] = got[half:]
            pre[half : ce * hid_n, :] = mm_t(w1t[...], x)
            logits = pre[ce * hid_n : ce * hid_n + ke, :].reshape(doms, exps, own)
            top = jnp.exp(logits - jnp.max(logits, axis=1, keepdims=True))
            soft = top / jnp.sum(top, axis=1, keepdims=True)
            gate[n] = soft.reshape(ke, own)

            def act(i, carry):
                at = pl.ds(pl.multiple_of(i * 16, 16), 16)
                v = pre[at, :]
                s = sigmoid(v)
                h = v * s
                hid[n, at, :] = h.astype(BF16)
                if keep:
                    slope[n, at, :] = (s + h * (1.0 - s)).astype(BF16)
                return carry

            lax.fori_loop(0, ce * hid_n // 16, act, 0, unroll=4 if keep else ce * hid_n // 16)
            for e in range(ce):
                w = w2o.get()[e] if e < epd else w2t[e - epd]
                vals[n, e * out_n : (e + 1) * out_n, :] = mm(w, hid[n, e * hid_n : (e + 1) * hid_n, :]).astype(BF16)
            if keep:
                for o in outs[:4]:
                    o.flush(n)
            for u in range(own // LANE):
                part = slice(u * LANE, (u + 1) * LANE)
                rows = [[gate[n, k * exps + e : k * exps + e + 1, part] for e in range(ce)] for k in range(doms)]

                def mix(i, carry):
                    acc = [None] * doms
                    for e in range(ce):
                        at = pl.ds(pl.multiple_of(e * out_n + i * 32, 32), 32)
                        v = vals[n, at, part].astype(F32)
                        for k in range(doms):
                            term = rows[k][e] * v
                            acc[k] = term if e == 0 else acc[k] + term
                    for k in range(doms):
                        at = pl.ds(pl.multiple_of(k * out_n + i * 32, 32), 32)
                        mixed[n, at, part] = acc[k].astype(BF16)
                    return carry

                lax.fori_loop(0, out_n // 32, mix, 0, unroll=4 if keep else out_n // 32)
            if keep:
                outs[4].flush(n)
            if n == 0 or not keep:
                tower = outs[-1]
                for k in range(doms):
                    tower.buf[n, k * th : (k + 1) * th, :] = mm(
                        wt[k], mixed[n, k * out_n : (k + 1) * out_n, :]
                    ).astype(tower_out)
                tower.flush(n)

    kept = [
        plain((ns, ce * hid_n, own), BF16),
        plain((ns, ce * hid_n, own), BF16),
        plain((ns, ce * out_n, own), BF16),
        plain((ns, ke, own), F32),
        plain((ns, doms * out_n, own), BF16),
    ]
    outs = list(kept) if keep else []
    outs.append(Near(plain((1 if keep else ns, doms * th, own), tower_out)))
    scratch = [
        pltpu.VMEM((half, dim), BF16),
        pltpu.VMEM((epd, out_n, hid_n), BF16),
        pltpu.VMEM((ce * hid_n + ke, own), F32),
    ]
    if not keep:
        scratch += [pltpu.VMEM(kept[i].shape, kept[i].dtype) for i in (0, 2, 3, 4)]
    ins = blocks + [Near(a) for a in (w1[0], w1[1], w2[0], w2[1], wt)]
    return staged(body, ins, outs, scratch, name, 40)


def combine(own_part, received, marks, devices):
    _, rows, own = own_part.shape
    doms = rows // LANE

    def body(ins, outs, cols):
        part = ins[0].get()
        got = [s.get() for s in ins[2:]]
        tower, low, message = (o.buf for o in outs)
        cols[...] = jnp.zeros_like(cols)
        for k in range(doms):
            at = slice(k * LANE, (k + 1) * LANE)
            total = part[0, at, :]
            for ref in got:
                total = total + ref[0, at, :].astype(F32)
            tower[at, :] = total
            low[at, :] = total.astype(BF16)
            mean = jnp.sum(total, axis=1, keepdims=True) * (1.0 / own)
            dev = total - mean
            cols[:, k : k + 1] = mean
            cols[:, doms + k : doms + k + 1] = jnp.sum(dev * dev, axis=1, keepdims=True)
        outs[0].flush()
        pair = jnp.concatenate([ins[1].get()[...].astype(F32), jnp.zeros((14, own), F32)], axis=0)
        low[rows:, :] = pair.astype(BF16)
        outs[1].flush()
        tile = cols[...].T[:8, :]
        for d in range(devices):
            message[d * 8 : (d + 1) * 8, :] = tile
        outs[2].flush()

    return staged(
        body,
        [Near(own_part), Far(marks)] + [Near(v) for v in received],
        [Near(plain((rows, own), F32)), Near(plain((rows + 16, own), BF16)), Near(plain((devices * 8, LANE), F32))],
        [pltpu.VMEM((LANE, LANE), F32)],
        "combine",
        16,
    )


def pick(dom, values):
    got = values[-1]
    for k in range(len(values) - 2, -1, -1):
        got = jnp.where(dom == k, values[k], got)
    return got


def chosen_tower(tower, dom, wide, lanes, doms):
    values = [tower[k * LANE : (k + 1) * LANE, lanes].astype(F32) for k in range(doms)]
    mean, gain, shift, head = (pick(dom, [wide[j * doms + k] for k in range(doms)]) for j in range(4))
    centred = pick(dom, values) - mean
    return values, centred, centred * gain + shift, gain, head


def spread_columns(wide, rows_ref, n):
    cols = rows_ref[...].T
    for j in range(n):
        wide[j] = jnp.broadcast_to(cols[:, j : j + 1], (LANE, LANE))


def normalise(stats, tower, marks, scale, shift, head, devices, count):
    rows, own = tower.shape
    doms = rows // LANE

    def body(ins, outs, prm, wide, q):
        st, tws, mks, sc, sh, hd = ins
        params, message = (o.buf for o in outs)
        prm[...] = jnp.zeros_like(prm)
        got = st.get()[...].reshape(devices, 8, LANE)
        total = jnp.sum(got, axis=0)
        mean = total * (1.0 / devices)
        dev = got - mean[None]
        spread = jnp.sum(dev * dev, axis=0) * float(own)
        var = (total[doms : 2 * doms] + spread[:doms]) * (1.0 / count)
        inv = lax.rsqrt(var + EPS)
        prm[0:doms, :] = mean[:doms]
        prm[doms : 2 * doms, :] = inv * sc.get()[...]
        prm[2 * doms : 3 * doms, :] = sh.get()[...]
        prm[3 * doms : 4 * doms, :] = hd.get()[...]
        prm[4 * doms : 5 * doms, :] = inv
        params[:16, :] = prm[:16, :]
        spread_columns(wide, prm, 4 * doms)
        tw, mk = tws.get(), mks.get()
        loss = jnp.zeros((1, LANE), F32)
        for u in range(own // LANE):
            part = slice(u * LANE, (u + 1) * LANE)
            dom = mk[0:1, part]
            target = mk[1:2, part].astype(F32)
            _, centred, affine, _, head_w = chosen_tower(tw, dom, wide, part, doms)
            s = sigmoid(affine)
            act = affine * s
            chosen = jnp.sum(act * head_w, axis=0, keepdims=True)
            soft = jnp.maximum(chosen, 0.0) + jnp.log(1.0 + jnp.exp(-jnp.abs(chosen)))
            loss = loss + (soft - target * chosen)
            score_grad = (sigmoid(chosen) - target) * (1.0 / count)
            grad = score_grad * head_w * (s + act * (1.0 - s))
            q[0:LANE, part] = grad
            q[LANE : 2 * LANE, part] = grad * centred
            q[2 * LANE :, part] = score_grad * act
        kinds = lax.broadcasted_iota(jnp.int32, (8, own), 0)
        one_hot = (kinds == mk[0:1, :]).astype(F32).astype(BF16)
        high = q[...].astype(BF16)
        sums = (mm_t(one_hot, high) + mm_t(one_hot, (q[...] - high.astype(F32)).astype(BF16)))[:doms]
        tile = [sums[:, :LANE], sums[:, LANE : 2 * LANE] * inv]
        all_rows = tile + [loss, jnp.zeros((1, LANE), F32)]
        twice = jnp.concatenate(all_rows + all_rows, axis=0).astype(BF16)
        for d in range(devices // 2):
            message[d * 16 : (d + 1) * 16, :] = twice
        params[16:, :] = jnp.concatenate([sums[:, 2 * LANE :], jnp.zeros((8 - doms, LANE), F32)], axis=0)
        outs[0].flush()

    return staged(
        body,
        [Near(stats), Near(tower), Far(marks), Far(scale), Far(shift), Far(head)],
        [Near(plain((24, LANE), F32)), Near(plain((devices * 8, LANE), BF16))],
        [
            pltpu.VMEM((LANE, LANE), F32),
            pltpu.VMEM((4 * doms, LANE, LANE), F32),
            pltpu.VMEM((3 * LANE, own), F32),
        ],
        "normalise",
        16,
    )


def layout(epd, hid_n, out_n, dim, doms, rows_n):
    second = epd * hid_n * out_n // LANE
    first = epd * hid_n * dim // LANE
    towers = -(-(doms * out_n + (dim // LANE) * 32) // (2 * 16 * rows_n)) * 16
    return second // rows_n, first // rows_n, towers


def pieces(kind, epd, hid_n, out_n, dim):
    flat = 0
    for i in range(epd):
        for q in range((out_n, dim)[kind] // LANE):
            yield i, q, flat
            flat += hid_n


def spots(kind, row, rows_n):
    got = []
    for j in range(rows_n):
        p = lax.bitwise_xor(row, j)
        got.append(p if kind == 0 else (p & 1) * (rows_n // 2) + lax.shift_right_logical(p, 1))
    return got


def backward(sums, params, tower, low_towers, marks, acts, inputs, w2, wgate_t, wtower, devices, rows_n, count):
    ns = 1 + len(low_towers)
    t_rows, own = tower.shape
    total_n = ns * own
    dim = inputs.shape[1]
    epd, hid_n, out_n = w2[0].shape
    ce = 2 * epd
    ke = wgate_t.shape[0]
    doms, _, th = wtower.shape
    exps = ke // doms
    m_sec, m_first, m_tow = layout(epd, hid_n, out_n, dim, doms, rows_n)

    def body(ins, outs, wide, prm, tg, mg, eg, gg, srow, tgf, facc):
        sm, pr, tw0, mk0 = ins[:4]
        low = ins[4 : 3 + ns]
        wts, gate, vals, w2o, w2s, slope, xs, hid, mixed = ins[3 + ns :]
        small, loss_out, sec_sib, first_sib, sec_mine, first_mine, tow_sib, tow_mine, pgs, lgs = outs
        pg, lg = pgs.buf, lgs.buf
        c = lax.rem(lax.axis_index(WIDTH), 2)
        r = lax.axis_index(ROWS)
        at_row = [spots(kind, r, rows_n) for kind in range(2)]
        prm[...] = jnp.zeros_like(prm)
        total = jnp.sum(sm.get()[...].astype(F32).reshape(devices, 8, LANE), axis=0)
        small.buf[...] = total
        loss_out.buf[...] = jnp.sum(total[2 * doms : 2 * doms + 1, :], axis=1, keepdims=True) * (1.0 / count)
        small.flush()
        loss_out.flush()
        given = pr.get()[...]
        gain, inv = given[doms : 2 * doms], given[4 * doms : 5 * doms]
        prm[0:16, :] = given[:16]
        prm[4 * doms : 5 * doms, :] = gain * total[:doms] * (1.0 / count)
        prm[5 * doms : 6 * doms, :] = gain * inv * total[doms : 2 * doms] * (1.0 / count)
        spread_columns(wide, prm, 6 * doms)
        for u in range(total_n // LANE):
            n = u * LANE // own
            part = slice(u * LANE, (u + 1) * LANE)
            here = slice(u * LANE - n * own, (u + 1) * LANE - n * own)
            if n == 0:
                tw = tw0.get()
                dom = mk0.get()[0:1, here]
                target = mk0.get()[1:2, here].astype(F32)
            else:
                tw = low[n - 1].get()
                pair = tw[t_rows : t_rows + 16, here].astype(F32)
                dom = pair[0:1].astype(jnp.int32)
                target = pair[1:2]
            values, _, affine, gain_s, head_w = chosen_tower(tw, dom, wide, here, doms)
            s = sigmoid(affine)
            a = affine * s
            chosen = jnp.sum(a * head_w, axis=0, keepdims=True)
            score_grad = (sigmoid(chosen) - target) * (1.0 / count)
            grad = gain_s * (score_grad * head_w * (s + a * (1.0 - s)))
            for k in range(doms):
                v = jnp.where(dom == k, grad, 0.0) - wide[4 * doms + k]
                v = v - (values[k] - wide[k]) * wide[5 * doms + k]
                down = v.astype(BF16)
                tg[k * th : (k + 1) * th, part] = down
                srow[k : k + 1, part] = jnp.sum(down.astype(F32) * values[k], axis=0, keepdims=True)
        wt = wts.get()
        for k in range(doms):
            mg[k * out_n : (k + 1) * out_n, :] = mm(wt[k], tg[k * th : (k + 1) * th, :])
        vals, gate = vals.get(), gate.get()
        gg[...] = jnp.zeros_like(gg)

        def tower_part(k):
            tgf[k * out_n : (k + 1) * out_n, :] = mm_t(
                mixed.get()[k * out_n : (k + 1) * out_n, :], tg[k * th : (k + 1) * th, :]
            )

        def hidden_part(n, e):
            at = slice(e * hid_n, (e + 1) * hid_n)
            part = slice(n * own, (n + 1) * own)
            w = (w2o, w2s)[e // epd].get()[e % epd]
            grad = mm(w, eg[e * out_n : (e + 1) * out_n, part])
            pg[at, part] = (grad * slope.get()[at, part].astype(F32)).astype(BF16)

        ready = []
        for u in range(total_n // LANE):
            part = slice(u * LANE, (u + 1) * LANE)
            rows = [[gate[k * exps + e : k * exps + e + 1, part] for e in range(ce)] for k in range(doms)]

            def spread(i, acc):
                up = [mg[pl.ds(pl.multiple_of(k * out_n + i * 16, 16), 16), part] for k in range(doms)]
                acc = list(acc)
                for e in range(ce):
                    at = pl.ds(pl.multiple_of(e * out_n + i * 16, 16), 16)
                    v = vals[at, part].astype(F32)
                    back = None
                    for k in range(doms):
                        term = rows[k][e] * up[k]
                        back = term if k == 0 else back + term
                        prod = up[k] * v
                        acc[k * ce + e] = acc[k * ce + e] + (prod[:8] + prod[8:])
                    eg[at, part] = back.astype(BF16)
                return tuple(acc)

            zero = jnp.zeros((8, LANE), F32)
            acc = lax.fori_loop(0, out_n // 16, spread, (zero,) * (doms * ce), unroll=out_n // 16)
            for k in range(doms):
                for e in range(ce):
                    gg[k * exps + e : k * exps + e + 1, part] = jnp.sum(acc[k * ce + e], axis=0, keepdims=True)
            if (u + 1) * LANE % own == 0:
                ready += [(hidden_part, (u * LANE // own, e)) for e in range(ce)]
            if ready:
                task, args = ready.pop(0)
                task(*args)
        for task, args in ready:
            task(*args)
        pgs.flush()
        here = lax.broadcasted_iota(jnp.int32, (exps, total_n), 0) < ce
        for k in range(doms):
            at = slice(k * exps, (k + 1) * exps)
            gg[at, :] = jnp.where(here, gate[at, :] * (gg[at, :] - srow[k : k + 1, :]), 0.0)
        lg[...] = mm(reorder(ke, epd), gg[...].astype(BF16)).astype(BF16)
        lgs.flush()
        hid = hid.get()

        def put(kind, slot, values):
            target = ((sec_sib, first_sib), (sec_mine, first_mine))[slot < epd][kind]
            size = (m_sec, m_first)[kind]
            step = math.gcd(size, hid_n)
            for i, q, flat in pieces(kind, epd, hid_n, out_n, dim):
                if i == slot % epd:
                    for off in range(0, hid_n, step):
                        j, o = divmod(flat + off, size)
                        part = values[off : off + step, q * LANE : (q + 1) * LANE]
                        target.buf[at_row[kind][j], o : o + step, :] = part.astype(BF16)

        x = xs.get()
        facc[...] = mm(pg[...], x[...])
        for e in range(ce):
            put(1, e, facc[e * hid_n : (e + 1) * hid_n, :])
        for e in range(ce):
            at = slice(e * hid_n, (e + 1) * hid_n)
            at_o = slice(e * out_n, (e + 1) * out_n)
            put(0, e, mm_t(hid[at, :], eg[at_o, :]))
        for target in (sec_sib, first_sib, sec_mine, first_mine):
            target.flush()
        for k in range(doms):
            tower_part(k)
        tgf[doms * out_n :, :] = jnp.zeros((tgf.shape[0] - doms * out_n, LANE), F32)
        part_g = mm(lg[...], x[...])
        for q in range(dim // LANE):
            tgf[doms * out_n + q * 32 : doms * out_n + q * 32 + ke, :] = part_g[:, q * LANE : (q + 1) * LANE]
        tgf[doms * out_n + ke : doms * out_n + 32, :] = given[16 : 48 - ke]
        for target, core in ((tow_sib, 1 - c), (tow_mine, c)):
            for j in range(rows_n):
                start = pl.multiple_of((core * rows_n + j) * m_tow, 8)
                target.buf[at_row[1][j], :, :] = tgf[pl.ds(start, m_tow), :].astype(BF16)
            target.flush()

    outs = [
        plain((8, LANE), F32),
        plain((1, 1), F32),
        Near(plain((rows_n, m_sec, LANE), BF16)),
        Near(plain((rows_n, m_first, LANE), BF16)),
        Near(plain((rows_n, m_sec, LANE), BF16)),
        Near(plain((rows_n, m_first, LANE), BF16)),
        Near(plain((rows_n, m_tow, LANE), BF16)),
        Near(plain((rows_n, m_tow, LANE), BF16)),
        Near(plain((ce * hid_n, total_n), BF16)),
        Near(plain((ke, total_n), BF16)),
    ]
    scratch = [
        pltpu.VMEM((6 * doms, LANE, LANE), F32),
        pltpu.VMEM((LANE, LANE), F32),
        pltpu.VMEM((doms * th, total_n), BF16),
        pltpu.VMEM((doms * out_n, total_n), F32),
        pltpu.VMEM((ce * out_n, total_n), BF16),
        pltpu.VMEM((ke, total_n), F32),
        pltpu.VMEM((8, total_n), F32),
        pltpu.VMEM((2 * rows_n * m_tow, LANE), F32),
        pltpu.VMEM((ce * hid_n, dim), F32),
    ]

    def side_by_side(which):
        def pairs(refs, buf):
            return [(r.at[n], buf.at[:, i * own : (i + 1) * own]) for i, (r, (_, n)) in enumerate(zip(refs, acts))]

        arrays = [a[which] for a, _ in acts]
        return Far(arrays, (arrays[0].shape[1], total_n), pairs)

    ins = [Near(sums), Near(params), Near(tower), Far(marks)]
    ins += [Far(v, moved=True) for v in low_towers]
    ins += [Far(wtower), side_by_side(3), side_by_side(2), Far(w2[0]), Far(w2[1], moved=True), side_by_side(1)]
    ins += [Far(inputs, (total_n, dim), row_blocks(list(range(ns)), own)), side_by_side(0), side_by_side(4)]
    return staged(body, ins, outs, scratch, "backward", 44)


def backward_inputs(pg, lg, w1, wgate_t, own):
    total_n = pg.shape[1]
    ns = total_n // own
    epd, dim, hid_n = w1[0].shape
    ce = 2 * epd
    ke = wgate_t.shape[0]

    def body(ins, outs, w1c):
        w1o, w1s, wgs, pgs, lgs = ins
        wg = jnp.concatenate([wgs.get()[...], jnp.zeros((LANE - ke, dim), BF16)], axis=0).T[:, :ke]
        for g, src in enumerate((w1o, w1s)):
            ref = src.get()
            for i in range(epd):
                e = g * epd + i
                w1c[:, e * hid_n : (e + 1) * hid_n] = ref[i]
        pg, lg = pgs.get(), lgs.get()
        for n in range(ns - 1, -1, -1):
            part = slice(n * own, (n + 1) * own)
            gi = mm(w1c[...], pg[:, part]) + mm(wg, lg[:, part])
            if n:
                outs[1].buf[n - 1] = gi.astype(BF16)
                outs[1].flush(n - 1)
            else:
                outs[0].buf[...] = gi
                outs[0].flush()

    return staged(
        body,
        [Far(w1[0]), Far(w1[1], moved=True), Far(wgate_t), Near(pg), Near(lg)],
        [Near(plain((dim, own), F32)), Near(plain((max(ns - 1, 1), dim, own), BF16))],
        [pltpu.VMEM((dim, ce * hid_n), BF16)],
        "backward_inputs",
        16,
    )


def finish(inputs_own, inputs_got, second, first, other, epd, hid_n, out_n, dim, doms, exps, rows_n):
    own = inputs_own.shape[1]
    m_sec, m_first, m_tow = layout(epd, hid_n, out_n, dim, doms, rows_n)
    ke = doms * exps

    def body(ins, outs, buf, tgf):
        out_f, out_s, out_t, out_g, out_h, out_i = (o.buf for o in outs)
        for u in range(own // LANE):
            lanes = slice(u * LANE, (u + 1) * LANE)
            part = ins[3].buf[:, lanes]
            for src in ins[4:]:
                part = part + src.buf[:, lanes].astype(F32)
            out_i[lanes, :] = part.T
            outs[5].flush(pl.ds(u * LANE, LANE))
        c = lax.rem(lax.axis_index(WIDTH), 2)
        r = lax.axis_index(ROWS)
        at_row = [spots(kind, r, rows_n) for kind in range(2)]
        for kind, size in ((0, m_sec), (1, m_first)):
            got = ins[kind].get()
            step = math.gcd(size, hid_n)
            for i, q, flat in pieces(kind, epd, hid_n, out_n, dim):
                for off in range(0, hid_n, step):
                    j, o = divmod(flat + off, size)
                    piece = got[at_row[kind][j], o : o + step, :].astype(F32)
                    if kind == 0:
                        out_s[i, off : off + step, q * LANE : (q + 1) * LANE] = piece
                    else:
                        buf[off : off + step, :] = piece
                if kind == 1:
                    out_f[i, q * LANE : (q + 1) * LANE, :] = buf[...].T
                if q == (out_n, dim)[kind] // LANE - 1:
                    outs[1 - kind].flush(i)
        near, sib = ins[1].get(), ins[2].get()
        for j in range(rows_n):
            at = at_row[1][j]
            for core, value in ((c, near[at, m_first:, :]), (1 - c, sib[at])):
                start = pl.multiple_of((core * rows_n + j) * m_tow, 8)
                tgf[pl.ds(start, m_tow), :] = value.astype(F32)
        for k in range(doms):
            out_t[k] = tgf[k * out_n : (k + 1) * out_n, :]
        outs[2].flush()
        for q in range(dim // LANE):
            at = doms * out_n + q * 32
            out_g[:, q * LANE : (q + 1) * LANE] = tgf[at : at + ke, :]
        outs[3].flush()
        out_h[...] = tgf[doms * out_n + ke : doms * out_n + ke + doms, :]
        outs[4].flush()

    return staged(
        body,
        [Near(second), Near(first), Near(other), Near(inputs_own)] + [Near(v) for v in inputs_got],
        [
            plain((epd, dim, hid_n), F32),
            plain((epd, hid_n, out_n), F32),
            plain((doms, out_n, LANE), F32),
            plain((ke, dim), F32),
            plain((doms, LANE), F32),
            plain((own, dim), F32),
        ],
        [pltpu.VMEM((hid_n, LANE), F32), pltpu.VMEM((2 * rows_n * m_tow, LANE), F32)],
        "finish",
        16,
    )


def swap(value, axis, mask):
    size = lax.axis_size(axis)
    return lax.ppermute(value, axis, [(i, i ^ mask) for i in range(size)])


def total(*values):
    got = values[0].astype(F32)
    for value in values[1:]:
        got = got + value.astype(F32)
    return got


def send(value, axis, mask):
    return swap(value.astype(BF16), axis, mask)


together = lax.optimization_barrier


def reduce_rows(second, first, towers, beside):
    n_rows, n_width = lax.axis_size(ROWS), lax.axis_size(WIDTH)
    half = n_rows // 2
    far = [2 * q for q in range(1, half)]
    low = total(*(v[half:] for v in first)).astype(BF16)
    high = [total(*(v[m : m + 2] for v in second)).astype(BF16) for m in far]
    across = total(*towers).astype(BF16)
    first_got = swap(low, ROWS, 1)
    second_got = [swap(v, ROWS, m) for v, m in zip(high, far)]
    towers = total(*towers, *(swap(across, WIDTH, mask) for mask in range(2, n_width, 2)))
    tower_low, operand = together((towers[half:].astype(BF16), beside[1]))
    tower_got = swap(tower_low, ROWS, 1)
    inputs_part = tuple(beside[0](operand))
    first_got, second_got, tower_got, inputs_part = together((first_got, second_got, tower_got, inputs_part))

    def piece(q):
        return jnp.concatenate(
            [total(*(v[q] for v in first), first_got[q]), total(towers[q], tower_got[q])], axis=0
        )

    pair = total(*(v[:2] for v in second), *second_got)
    high = [piece(q).astype(BF16) for q in range(1, half)]
    high, low = together((high, pair.astype(BF16)))
    moved = [swap(v, ROWS, m) for v, m in zip(high, far)]
    moved, low = together((moved, swap(low, ROWS, 1)))
    pair = total(pair, low[::-1])
    return pair.astype(BF16), total(piece(0), *moved).astype(BF16), inputs_part


def gather_rows(pair, first, m_first, beside):
    half = lax.axis_size(ROWS) // 2
    far = [2 * q for q in range(1, half)]
    pair, first = together((pair, first))
    high, beside = together(([swap(first, ROWS, m) for m in far], beside))
    pair, evens = together((pair, jnp.stack([first] + high)))
    low, high = swap(evens, ROWS, 1), [swap(pair, ROWS, m) for m in far]
    low, high, beside = together((low, high, beside))
    second, first = jnp.concatenate([pair] + high), jnp.concatenate([evens, low])
    return second, first, swap(first[:, m_first:], WIDTH, 1), beside


def local(inputs, w_first, w_second, w_gate, w_tower, norm_scale, norm_shift, w_head, domains, labels):
    n_width, n_rows = lax.axis_size(WIDTH), lax.axis_size(ROWS)
    devices = n_width * n_rows
    own = inputs.shape[0] // n_width
    count = float(own * devices)
    dim = inputs.shape[1]
    epd, _, hid_n = w_first.shape
    out_n = w_second.shape[2]
    doms, _, exps = w_gate.shape
    ke = doms * exps
    n_x = n_width // 2
    others = list(range(1, n_x))
    w1 = (w_first, swap(w_first, WIDTH, 1))
    w2 = (w_second, swap(w_second, WIDTH, 1))
    wgate_t = jnp.transpose(w_gate, (0, 2, 1)).reshape(ke, dim)
    marks = jnp.stack([domains, labels])

    x_far, w1_own, w2_own, wt = prepare(others, inputs, w_first, w_second, wgate_t, w_tower, own)
    w1t, w2t = (w1_own, w1[1]), (w2_own, w2[1])
    far = forward([Near(x_far)], w1t, w2t, wt, own, doms, False, BF16, "forward_send")[0]
    sent = [swap(far[s - 1 : s], WIDTH, 2 * s) for s in others]
    blocks = [Far(inputs, (own, dim), row_blocks([0], own)), Near(x_far)]
    kept = forward(blocks, w1t, w2t, wt, own, doms, True, F32, "forward_keep")
    tower, low, message = combine(kept[5], sent, marks, devices)
    stats = lax.all_to_all(message, BOTH, 0, 0, tiled=True)
    stats, low = together((stats, low))
    lows = [swap(low, WIDTH, 2 * s) for s in others]
    params, message = normalise(stats, tower, marks, norm_scale, norm_shift, w_head, devices, count)
    sums = lax.all_to_all(message, BOTH, 0, 0, tiled=True)

    acts = [(kept[:5], s) for s in range(n_x)]
    small, loss, sec_sib, first_sib, sec_own, first_own, tow_sib, tow_own, pg, lg = backward(
        sums, params, tower, lows, marks, acts, inputs, w2, wgate_t, w_tower, devices, n_rows, count
    )
    first_sib = swap(first_sib, WIDTH, 1)
    first_sib, sec_sib, tow_sib = together((first_sib, sec_sib, tow_sib))
    second, first, (gi_own, gi_out) = reduce_rows(
        (sec_own, swap(sec_sib, WIDTH, 1)),
        (first_own, first_sib),
        (tow_own, swap(tow_sib, WIDTH, 1)),
        (lambda grad: backward_inputs(grad, lg, w1, wgate_t, own), pg),
    )
    inputs_got = [swap(gi_out[s - 1], WIDTH, 2 * s) for s in others]
    m_first = layout(epd, hid_n, out_n, dim, doms, n_rows)[1]
    second, first, other, inputs_got = gather_rows(second, first, m_first, inputs_got)
    grad_first, grad_second, grad_tower, grad_gate, grad_head, grad_inputs = finish(
        gi_own, inputs_got, second, first, other, epd, hid_n, out_n, dim, doms, exps, n_rows
    )
    return (
        loss[0, 0],
        grad_inputs,
        grad_first,
        grad_second,
        grad_gate.reshape(doms, exps, dim).transpose(0, 2, 1),
        grad_tower,
        small[doms : 2 * doms],
        small[:doms],
        grad_head,
    )


def solution(mesh):
    placed = (
        P(ROWS, None),
        P(WIDTH, None, None),
        P(WIDTH, None, None),
        P(),
        P(),
        P(),
        P(),
        P(),
        P(BOTH),
        P(BOTH),
    )
    return jax.shard_map(
        local,
        mesh=mesh,
        in_specs=placed,
        out_specs=(
            P(),
            P(BOTH, None),
            P(WIDTH, None, None),
            P(WIDTH, None, None),
            P(),
            P(),
            P(),
            P(),
            P(),
        ),
        check_vma=False,
    )
```

```python
import math

import jax
import jax.numpy as jnp
from jax import lax
from jax.experimental import pallas as pl
from jax.experimental.pallas import tpu as pltpu
from jax.sharding import PartitionSpec as P

F32 = jnp.float32
BF16 = jnp.bfloat16
EPS = 1e-05
LANE = 128
MIB = 1 << 20
ROWS = "rows"
WIDTH = "width"
BOTH = (ROWS, WIDTH)


def mm(a, b):
    return jnp.dot(a, b, preferred_element_type=F32)


def mm_t(a, b):
    return lax.dot_general(a, b, (((1,), (1,)), ((), ())), preferred_element_type=F32)


def sigmoid(v):
    return 0.5 * jnp.tanh(0.5 * v) + 0.5


class Source:
    def __init__(self, buf, copies):
        self.buf = buf
        self.waiting = copies
        for copy in copies:
            copy.start()

    def get(self):
        for copy in self.waiting:
            copy.wait()
        self.waiting = []
        return self.buf


class Target:
    def __init__(self, ref, buf, sems):
        self.ref, self.buf, self.sems = ref, buf, sems
        self.waiting = []

    def flush(self, *at):
        if self.ref is None:
            return
        src = self.buf.at[at] if at else self.buf
        dst = self.ref.at[at] if at else self.ref
        copy = pltpu.make_async_copy(src, dst, next(self.sems))
        copy.start()
        self.waiting.append(copy)


class Near:
    def __init__(self, what):
        self.what = what


class Far:
    def __init__(self, arrays, shape=None, pairs=None, moved=False, into=None):
        self.moved = moved
        self.into = into
        self.arrays = arrays if isinstance(arrays, (list, tuple)) else [arrays]
        self.shape = shape or self.arrays[0].shape
        self.dtype = self.arrays[0].dtype
        self.pairs = pairs or (lambda refs, buf: [(refs[0], buf)])


def staged(body, ins, outs, scratch, name, limit, n_sems=64):
    far_in = [i for i, s in enumerate(ins) if isinstance(s, Far) and s.into is None]
    far_out = [i for i, s in enumerate(outs) if not isinstance(s, Near)]
    args, specs, spans = [], [], []
    hbm = pl.BlockSpec(memory_space=pltpu.HBM)
    vmem = pl.BlockSpec(memory_space=pltpu.VMEM)
    anywhere = pl.BlockSpec(memory_space=pl.ANY)
    for s in ins:
        if isinstance(s, Far):
            spans.append((len(args), len(args) + len(s.arrays)))
            if s.moved:
                args += s.arrays
                specs += [anywhere] * len(s.arrays)
                continue
            args += [pltpu.with_memory_space_constraint(a, pltpu.HBM) for a in s.arrays]
            specs += [hbm] * len(s.arrays)
        else:
            spans.append((len(args), len(args) + 1))
            args.append(s.what)
            specs.append(vmem)
    n_in, n_out = len(args), len(outs)

    def kernel(*refs):
        refs_in, refs_out = refs[:n_in], refs[n_in : n_in + n_out]
        bufs = refs[n_in + n_out :]
        in_bufs = dict(zip(far_in, bufs))
        in_bufs.update({i: refs_out[s.into] for i, s in enumerate(ins) if isinstance(s, Far) and s.into is not None})
        out_bufs = dict(zip(far_out, bufs[len(far_in) :]))
        rest = bufs[len(far_in) + len(far_out) : -1]
        sems = iter([bufs[-1].at[i] for i in range(n_sems)])
        sources = []
        for i, (start, stop) in enumerate(spans):
            if i in in_bufs:
                pairs = ins[i].pairs(refs_in[start:stop], in_bufs[i])
                sources.append(Source(in_bufs[i], [pltpu.make_async_copy(a, b, next(sems)) for a, b in pairs]))
            else:
                sources.append(Source(refs_in[start], []))
        targets = []
        for i, ref in enumerate(refs_out):
            targets.append(Target(ref, out_bufs[i], sems) if i in out_bufs else Target(None, ref, sems))
        body(sources, targets, *rest)
        for s in sources:
            s.get()
        for t in targets:
            for copy in t.waiting:
                copy.wait()

    return pl.pallas_call(
        kernel,
        out_shape=[o.what if isinstance(o, Near) else pltpu.HBM(o.shape, o.dtype) for o in outs],
        in_specs=specs,
        out_specs=[hbm if i in far_out else vmem for i in range(n_out)],
        scratch_shapes=[pltpu.VMEM(ins[i].shape, ins[i].dtype) for i in far_in]
        + [pltpu.VMEM(outs[i].shape, outs[i].dtype) for i in far_out]
        + list(scratch)
        + [pltpu.SemaphoreType.DMA((n_sems,))],
        compiler_params=pltpu.CompilerParams(vmem_limit_bytes=limit * MIB),
        name=name,
    )(*args)


def plain(shape, dtype):
    return jax.ShapeDtypeStruct(shape, dtype)


def row_blocks(slots, own):
    def pairs(refs, buf):
        w = lax.axis_index(WIDTH)
        got = []
        for n, s in enumerate(slots):
            start = pl.multiple_of(lax.bitwise_xor(w, 2 * s) * own, own)
            got.append((refs[0].at[pl.ds(start, own), :], buf.at[n * own : (n + 1) * own, :]))
        return got

    return pairs


def reorder(ke, epd):
    first = lax.axis_index(WIDTH) * epd
    down = lax.broadcasted_iota(jnp.int32, (ke, ke), 0)
    across = lax.broadcasted_iota(jnp.int32, (ke, ke), 1)
    return jnp.where(lax.bitwise_xor(down, first) == across, 1.0, 0.0).astype(BF16)


def prepare(slots, inputs, w1, w2, wgate_t, wtower, own):
    dim = inputs.shape[1]
    epd, _, hid_n = w1.shape
    out_n = w2.shape[2]
    ke = wgate_t.shape[0]
    doms, _, th = wtower.shape

    def body(ins, outs):
        w1s, wgs, w2s, wts, _ = ins
        _, w1t, w2t, wt = (o.buf for o in outs)
        w1_buf = w1s.get()
        for i in range(epd):
            w1t[i * hid_n : (i + 1) * hid_n, :] = w1_buf[i].T
        w1t[epd * hid_n :, :] = mm(reorder(ke, epd), wgs.get()[...]).astype(BF16)
        w2_buf = w2s.get()
        for i in range(epd):
            w2t[i] = w2_buf[i].T
        wt_buf = wts.get()
        for k in range(doms):
            wt[k] = wt_buf[k].T
    return staged(
        body,
        [Far(a) for a in (w1, wgate_t, w2, wtower)]
        + [Far(inputs, (len(slots) * own, dim), row_blocks(slots, own), into=0)],
        [
            Near(plain((len(slots) * own, dim), BF16)),
            Near(plain((epd * hid_n + ke, dim), BF16)),
            Near(plain((epd, out_n, hid_n), BF16)),
            Near(plain((doms, th, out_n), BF16)),
        ],
        [],
        "prepare",
        12,
    )


def forward(blocks, w1, w2, wt, own, doms, keep, tower_out, name):
    epd, dim, hid_n = w1[1].shape
    out_n = w2[1].shape[2]
    ce = 2 * epd
    half = epd * hid_n
    ke = w1[0].shape[0] - half
    th = wt.shape[1]
    exps = ke // doms
    sizes = [(b.what if isinstance(b, Near) else b).shape[0] // own for b in blocks]
    ns = sum(sizes)

    def body(ins, outs, w1t, w2t, pre, *bufs):
        xs = ins[: len(blocks)]
        w1o, w1s, w2o, w2s, wts = ins[len(blocks) :]
        if keep:
            hid, slope, vals, gate, mixed = (o.buf for o in outs[:5])
        else:
            hid, vals, gate, mixed = bufs
        wt = wts.get()
        for i in range(epd):
            w1t[i * hid_n : (i + 1) * hid_n, :] = w1s.get()[i].T
            w2t[i] = w2s.get()[i].T
        parts = [(src, n) for src, size in zip(xs, sizes) for n in range(size)]
        for n, (src, place) in enumerate(parts):
            x = src.get()[place * own : (place + 1) * own, :]
            got = mm_t(w1o.get()[...], x)
            pre[:half, :] = got[:half]
            pre[ce * hid_n :, :] = got[half:]
            pre[half : ce * hid_n, :] = mm_t(w1t[...], x)
            logits = pre[ce * hid_n : ce * hid_n + ke, :].reshape(doms, exps, own)
            top = jnp.exp(logits - jnp.max(logits, axis=1, keepdims=True))
            soft = top / jnp.sum(top, axis=1, keepdims=True)
            gate[n] = soft.reshape(ke, own)

            def act(i, carry):
                at = pl.ds(pl.multiple_of(i * 16, 16), 16)
                v = pre[at, :]
                s = sigmoid(v)
                h = v * s
                hid[n, at, :] = h.astype(BF16)
                if keep:
                    slope[n, at, :] = (s + h * (1.0 - s)).astype(BF16)
                return carry

            lax.fori_loop(0, ce * hid_n // 16, act, 0, unroll=4 if keep else ce * hid_n // 16)
            for e in range(ce):
                w = w2o.get()[e] if e < epd else w2t[e - epd]
                vals[n, e * out_n : (e + 1) * out_n, :] = mm(w, hid[n, e * hid_n : (e + 1) * hid_n, :]).astype(BF16)
            if keep:
                for o in outs[:4]:
                    o.flush(n)
            for u in range(own // LANE):
                part = slice(u * LANE, (u + 1) * LANE)
                rows = [[gate[n, k * exps + e : k * exps + e + 1, part] for e in range(ce)] for k in range(doms)]

                def mix(i, carry):
                    acc = [None] * doms
                    for e in range(ce):
                        at = pl.ds(pl.multiple_of(e * out_n + i * 32, 32), 32)
                        v = vals[n, at, part].astype(F32)
                        for k in range(doms):
                            term = rows[k][e] * v
                            acc[k] = term if e == 0 else acc[k] + term
                    for k in range(doms):
                        at = pl.ds(pl.multiple_of(k * out_n + i * 32, 32), 32)
                        mixed[n, at, part] = acc[k].astype(BF16)
                    return carry

                lax.fori_loop(0, out_n // 32, mix, 0, unroll=4 if keep else out_n // 32)
            if keep:
                outs[4].flush(n)
            if n == 0 or not keep:
                tower = outs[-1]
                for k in range(doms):
                    tower.buf[n, k * th : (k + 1) * th, :] = mm(
                        wt[k], mixed[n, k * out_n : (k + 1) * out_n, :]
                    ).astype(tower_out)
                tower.flush(n)

    kept = [
        plain((ns, ce * hid_n, own), BF16),
        plain((ns, ce * hid_n, own), BF16),
        plain((ns, ce * out_n, own), BF16),
        plain((ns, ke, own), F32),
        plain((ns, doms * out_n, own), BF16),
    ]
    outs = list(kept) if keep else []
    outs.append(Near(plain((1 if keep else ns, doms * th, own), tower_out)))
    scratch = [
        pltpu.VMEM((half, dim), BF16),
        pltpu.VMEM((epd, out_n, hid_n), BF16),
        pltpu.VMEM((ce * hid_n + ke, own), F32),
    ]
    if not keep:
        scratch += [pltpu.VMEM(kept[i].shape, kept[i].dtype) for i in (0, 2, 3, 4)]
    ins = blocks + [Near(a) for a in (w1[0], w1[1], w2[0], w2[1], wt)]
    return staged(body, ins, outs, scratch, name, 40)


def combine(own_part, received, marks, devices):
    _, rows, own = own_part.shape
    doms = rows // LANE

    def body(ins, outs, cols):
        part = ins[0].get()
        got = [s.get() for s in ins[2:]]
        tower, low, message = (o.buf for o in outs)
        cols[...] = jnp.zeros_like(cols)
        for k in range(doms):
            at = slice(k * LANE, (k + 1) * LANE)
            total = part[0, at, :]
            for ref in got:
                total = total + ref[0, at, :].astype(F32)
            tower[at, :] = total
            low[at, :] = total.astype(BF16)
            mean = jnp.sum(total, axis=1, keepdims=True) * (1.0 / own)
            dev = total - mean
            cols[:, k : k + 1] = mean
            cols[:, doms + k : doms + k + 1] = jnp.sum(dev * dev, axis=1, keepdims=True)
        outs[0].flush()
        pair = jnp.concatenate([ins[1].get()[...].astype(F32), jnp.zeros((14, own), F32)], axis=0)
        low[rows:, :] = pair.astype(BF16)
        outs[1].flush()
        tile = cols[...].T[:8, :]
        for d in range(devices):
            message[d * 8 : (d + 1) * 8, :] = tile
        outs[2].flush()

    return staged(
        body,
        [Near(own_part), Far(marks)] + [Near(v) for v in received],
        [Near(plain((rows, own), F32)), Near(plain((rows + 16, own), BF16)), Near(plain((devices * 8, LANE), F32))],
        [pltpu.VMEM((LANE, LANE), F32)],
        "combine",
        16,
    )


def pick(dom, values):
    got = values[-1]
    for k in range(len(values) - 2, -1, -1):
        got = jnp.where(dom == k, values[k], got)
    return got


def chosen_tower(tower, dom, wide, lanes, doms):
    values = [tower[k * LANE : (k + 1) * LANE, lanes].astype(F32) for k in range(doms)]
    mean, gain, shift, head = (pick(dom, [wide[j * doms + k] for k in range(doms)]) for j in range(4))
    centred = pick(dom, values) - mean
    return values, centred, centred * gain + shift, gain, head


def spread_columns(wide, rows_ref, n):
    cols = rows_ref[...].T
    for j in range(n):
        wide[j] = jnp.broadcast_to(cols[:, j : j + 1], (LANE, LANE))


def normalise(stats, tower, marks, scale, shift, head, devices, count):
    rows, own = tower.shape
    doms = rows // LANE

    def body(ins, outs, prm, wide, q):
        st, tws, mks, sc, sh, hd = ins
        params, message = (o.buf for o in outs)
        prm[...] = jnp.zeros_like(prm)
        got = st.get()[...].reshape(devices, 8, LANE)
        total = jnp.sum(got, axis=0)
        mean = total * (1.0 / devices)
        dev = got - mean[None]
        spread = jnp.sum(dev * dev, axis=0) * float(own)
        var = (total[doms : 2 * doms] + spread[:doms]) * (1.0 / count)
        inv = lax.rsqrt(var + EPS)
        prm[0:doms, :] = mean[:doms]
        prm[doms : 2 * doms, :] = inv * sc.get()[...]
        prm[2 * doms : 3 * doms, :] = sh.get()[...]
        prm[3 * doms : 4 * doms, :] = hd.get()[...]
        prm[4 * doms : 5 * doms, :] = inv
        params[:16, :] = prm[:16, :]
        spread_columns(wide, prm, 4 * doms)
        tw, mk = tws.get(), mks.get()
        loss = jnp.zeros((1, LANE), F32)
        for u in range(own // LANE):
            part = slice(u * LANE, (u + 1) * LANE)
            dom = mk[0:1, part]
            target = mk[1:2, part].astype(F32)
            _, centred, affine, _, head_w = chosen_tower(tw, dom, wide, part, doms)
            s = sigmoid(affine)
            act = affine * s
            chosen = jnp.sum(act * head_w, axis=0, keepdims=True)
            soft = jnp.maximum(chosen, 0.0) + jnp.log(1.0 + jnp.exp(-jnp.abs(chosen)))
            loss = loss + (soft - target * chosen)
            score_grad = (sigmoid(chosen) - target) * (1.0 / count)
            grad = score_grad * head_w * (s + act * (1.0 - s))
            q[0:LANE, part] = grad
            q[LANE : 2 * LANE, part] = grad * centred
            q[2 * LANE :, part] = score_grad * act
        kinds = lax.broadcasted_iota(jnp.int32, (8, own), 0)
        one_hot = (kinds == mk[0:1, :]).astype(F32).astype(BF16)
        high = q[...].astype(BF16)
        sums = (mm_t(one_hot, high) + mm_t(one_hot, (q[...] - high.astype(F32)).astype(BF16)))[:doms]
        tile = [sums[:, :LANE], sums[:, LANE : 2 * LANE] * inv]
        all_rows = tile + [loss, jnp.zeros((1, LANE), F32)]
        twice = jnp.concatenate(all_rows + all_rows, axis=0).astype(BF16)
        for d in range(devices // 2):
            message[d * 16 : (d + 1) * 16, :] = twice
        params[16:, :] = jnp.concatenate([sums[:, 2 * LANE :], jnp.zeros((8 - doms, LANE), F32)], axis=0)
        outs[0].flush()

    return staged(
        body,
        [Near(stats), Near(tower), Far(marks), Far(scale), Far(shift), Far(head)],
        [Near(plain((24, LANE), F32)), Near(plain((devices * 8, LANE), BF16))],
        [
            pltpu.VMEM((LANE, LANE), F32),
            pltpu.VMEM((4 * doms, LANE, LANE), F32),
            pltpu.VMEM((3 * LANE, own), F32),
        ],
        "normalise",
        16,
    )


def layout(epd, hid_n, out_n, dim, doms, rows_n):
    second = epd * hid_n * out_n // LANE
    first = epd * hid_n * dim // LANE
    towers = -(-(doms * out_n + (dim // LANE) * 32) // (2 * 16 * rows_n)) * 16
    return second // rows_n, first // rows_n, towers


def pieces(kind, epd, hid_n, out_n, dim):
    flat = 0
    for i in range(epd):
        for q in range((out_n, dim)[kind] // LANE):
            yield i, q, flat
            flat += hid_n


def spots(kind, row, rows_n):
    got = []
    for j in range(rows_n):
        p = lax.bitwise_xor(row, j)
        got.append(p if kind == 0 else (p & 1) * (rows_n // 2) + lax.shift_right_logical(p, 1))
    return got


def backward(sums, params, tower, low_towers, marks, acts, inputs, w2, wgate_t, wtower, devices, rows_n, count):
    ns = 1 + len(low_towers)
    t_rows, own = tower.shape
    total_n = ns * own
    dim = inputs.shape[1]
    epd, hid_n, out_n = w2[0].shape
    ce = 2 * epd
    ke = wgate_t.shape[0]
    doms, _, th = wtower.shape
    exps = ke // doms
    m_sec, m_first, m_tow = layout(epd, hid_n, out_n, dim, doms, rows_n)

    def body(ins, outs, wide, prm, tg, mg, eg, gg, srow, tgf, facc):
        sm, pr, tw0, mk0 = ins[:4]
        low = ins[4 : 3 + ns]
        wts, gate, vals, w2o, w2s, slope, xs, hid, mixed = ins[3 + ns :]
        shift_out, scale_out, loss_out, sec_sib, first_sib, sec_mine, first_mine, tow_sib, tow_mine, pgs, lgs = outs
        pg, lg = pgs.buf, lgs.buf
        c = lax.rem(lax.axis_index(WIDTH), 2)
        r = lax.axis_index(ROWS)
        at_row = [spots(kind, r, rows_n) for kind in range(2)]
        prm[...] = jnp.zeros_like(prm)
        total = jnp.sum(sm.get()[...].astype(F32).reshape(devices, 8, LANE), axis=0)
        shift_out.buf[...] = total[:doms]
        scale_out.buf[...] = total[doms : 2 * doms]
        loss_out.buf[...] = jnp.sum(total[2 * doms : 2 * doms + 1, :], axis=1, keepdims=True) * (1.0 / count)
        for target in (shift_out, scale_out, loss_out):
            target.flush()
        given = pr.get()[...]
        gain, inv = given[doms : 2 * doms], given[4 * doms : 5 * doms]
        prm[0:16, :] = given[:16]
        prm[4 * doms : 5 * doms, :] = gain * total[:doms] * (1.0 / count)
        prm[5 * doms : 6 * doms, :] = gain * inv * total[doms : 2 * doms] * (1.0 / count)
        spread_columns(wide, prm, 6 * doms)
        for u in range(total_n // LANE):
            n = u * LANE // own
            part = slice(u * LANE, (u + 1) * LANE)
            here = slice(u * LANE - n * own, (u + 1) * LANE - n * own)
            if n == 0:
                tw = tw0.get()
                dom = mk0.get()[0:1, here]
                target = mk0.get()[1:2, here].astype(F32)
            else:
                tw = low[n - 1].get()
                pair = tw[t_rows : t_rows + 16, here].astype(F32)
                dom = pair[0:1].astype(jnp.int32)
                target = pair[1:2]
            values, _, affine, gain_s, head_w = chosen_tower(tw, dom, wide, here, doms)
            s = sigmoid(affine)
            a = affine * s
            chosen = jnp.sum(a * head_w, axis=0, keepdims=True)
            score_grad = (sigmoid(chosen) - target) * (1.0 / count)
            grad = gain_s * (score_grad * head_w * (s + a * (1.0 - s)))
            for k in range(doms):
                v = jnp.where(dom == k, grad, 0.0) - wide[4 * doms + k]
                v = v - (values[k] - wide[k]) * wide[5 * doms + k]
                down = v.astype(BF16)
                tg[k * th : (k + 1) * th, part] = down
                srow[k : k + 1, part] = jnp.sum(down.astype(F32) * values[k], axis=0, keepdims=True)
        wt = wts.get()
        for k in range(doms):
            mg[k * out_n : (k + 1) * out_n, :] = mm(wt[k], tg[k * th : (k + 1) * th, :])
        vals, gate = vals.get(), gate.get()
        gg[...] = jnp.zeros_like(gg)

        def tower_part(k):
            tgf[k * out_n : (k + 1) * out_n, :] = mm_t(
                mixed.get()[k * out_n : (k + 1) * out_n, :], tg[k * th : (k + 1) * th, :]
            )

        def hidden_part(n, e):
            at = slice(e * hid_n, (e + 1) * hid_n)
            part = slice(n * own, (n + 1) * own)
            w = (w2o, w2s)[e // epd].get()[e % epd]
            grad = mm(w, eg[e * out_n : (e + 1) * out_n, part])
            pg[at, part] = (grad * slope.get()[at, part].astype(F32)).astype(BF16)

        ready = []
        for u in range(total_n // LANE):
            part = slice(u * LANE, (u + 1) * LANE)
            rows = [[gate[k * exps + e : k * exps + e + 1, part] for e in range(ce)] for k in range(doms)]

            def spread(i, acc):
                up = [mg[pl.ds(pl.multiple_of(k * out_n + i * 16, 16), 16), part] for k in range(doms)]
                acc = list(acc)
                for e in range(ce):
                    at = pl.ds(pl.multiple_of(e * out_n + i * 16, 16), 16)
                    v = vals[at, part].astype(F32)
                    back = None
                    for k in range(doms):
                        term = rows[k][e] * up[k]
                        back = term if k == 0 else back + term
                        prod = up[k] * v
                        acc[k * ce + e] = acc[k * ce + e] + (prod[:8] + prod[8:])
                    eg[at, part] = back.astype(BF16)
                return tuple(acc)

            zero = jnp.zeros((8, LANE), F32)
            acc = lax.fori_loop(0, out_n // 16, spread, (zero,) * (doms * ce), unroll=out_n // 16)
            for k in range(doms):
                for e in range(ce):
                    gg[k * exps + e : k * exps + e + 1, part] = jnp.sum(acc[k * ce + e], axis=0, keepdims=True)
            if (u + 1) * LANE % own == 0:
                ready += [(hidden_part, (u * LANE // own, e)) for e in range(ce)]
            if ready:
                task, args = ready.pop(0)
                task(*args)
        for task, args in ready:
            task(*args)
        pgs.flush()
        here = lax.broadcasted_iota(jnp.int32, (exps, total_n), 0) < ce
        for k in range(doms):
            at = slice(k * exps, (k + 1) * exps)
            gg[at, :] = jnp.where(here, gate[at, :] * (gg[at, :] - srow[k : k + 1, :]), 0.0)
        lg[...] = mm(reorder(ke, epd), gg[...].astype(BF16)).astype(BF16)
        lgs.flush()
        hid = hid.get()

        def put(kind, slot, values):
            target = ((sec_sib, first_sib), (sec_mine, first_mine))[slot < epd][kind]
            size = (m_sec, m_first)[kind]
            step = math.gcd(size, hid_n)
            for i, q, flat in pieces(kind, epd, hid_n, out_n, dim):
                if i == slot % epd:
                    for off in range(0, hid_n, step):
                        j, o = divmod(flat + off, size)
                        part = values[off : off + step, q * LANE : (q + 1) * LANE]
                        target.buf[at_row[kind][j], o : o + step, :] = part.astype(BF16)

        x = xs.get()
        facc[...] = mm(pg[...], x[...])
        for e in range(ce):
            put(1, e, facc[e * hid_n : (e + 1) * hid_n, :])
        for e in range(ce):
            at = slice(e * hid_n, (e + 1) * hid_n)
            at_o = slice(e * out_n, (e + 1) * out_n)
            put(0, e, mm_t(hid[at, :], eg[at_o, :]))
        for target in (sec_sib, first_sib, sec_mine, first_mine):
            target.flush()
        for k in range(doms):
            tower_part(k)
        tgf[doms * out_n :, :] = jnp.zeros((tgf.shape[0] - doms * out_n, LANE), F32)
        part_g = mm(lg[...], x[...])
        for q in range(dim // LANE):
            tgf[doms * out_n + q * 32 : doms * out_n + q * 32 + ke, :] = part_g[:, q * LANE : (q + 1) * LANE]
        tgf[doms * out_n + ke : doms * out_n + 32, :] = given[16 : 48 - ke]
        for target, core in ((tow_sib, 1 - c), (tow_mine, c)):
            for j in range(rows_n):
                start = pl.multiple_of((core * rows_n + j) * m_tow, 8)
                target.buf[at_row[1][j], :, :] = tgf[pl.ds(start, m_tow), :].astype(BF16)
            target.flush()

    outs = [
        plain((doms, LANE), F32),
        plain((doms, LANE), F32),
        plain((1, 1), F32),
        Near(plain((rows_n, m_sec, LANE), BF16)),
        Near(plain((rows_n, m_first, LANE), BF16)),
        Near(plain((rows_n, m_sec, LANE), BF16)),
        Near(plain((rows_n, m_first, LANE), BF16)),
        Near(plain((rows_n, m_tow, LANE), BF16)),
        Near(plain((rows_n, m_tow, LANE), BF16)),
        Near(plain((ce * hid_n, total_n), BF16)),
        Near(plain((ke, total_n), BF16)),
    ]
    scratch = [
        pltpu.VMEM((6 * doms, LANE, LANE), F32),
        pltpu.VMEM((LANE, LANE), F32),
        pltpu.VMEM((doms * th, total_n), BF16),
        pltpu.VMEM((doms * out_n, total_n), F32),
        pltpu.VMEM((ce * out_n, total_n), BF16),
        pltpu.VMEM((ke, total_n), F32),
        pltpu.VMEM((8, total_n), F32),
        pltpu.VMEM((2 * rows_n * m_tow, LANE), F32),
        pltpu.VMEM((ce * hid_n, dim), F32),
    ]

    def side_by_side(which):
        def pairs(refs, buf):
            return [(r.at[n], buf.at[:, i * own : (i + 1) * own]) for i, (r, (_, n)) in enumerate(zip(refs, acts))]

        arrays = [a[which] for a, _ in acts]
        return Far(arrays, (arrays[0].shape[1], total_n), pairs)

    ins = [Near(sums), Near(params), Near(tower), Far(marks)]
    ins += [Far(v, moved=True) for v in low_towers]
    ins += [Far(wtower), side_by_side(3), side_by_side(2), Far(w2[0]), Far(w2[1], moved=True), side_by_side(1)]
    ins += [Far(inputs, (total_n, dim), row_blocks(list(range(ns)), own)), side_by_side(0), side_by_side(4)]
    return staged(body, ins, outs, scratch, "backward", 44)


def backward_inputs(pg, lg, w1, wgate_t, own):
    total_n = pg.shape[1]
    ns = total_n // own
    epd, dim, hid_n = w1[0].shape
    ce = 2 * epd
    ke = wgate_t.shape[0]

    def body(ins, outs, w1c):
        w1o, w1s, wgs, pgs, lgs = ins
        wg = jnp.concatenate([wgs.get()[...], jnp.zeros((LANE - ke, dim), BF16)], axis=0).T[:, :ke]
        for g, src in enumerate((w1o, w1s)):
            ref = src.get()
            for i in range(epd):
                e = g * epd + i
                w1c[:, e * hid_n : (e + 1) * hid_n] = ref[i]
        pg, lg = pgs.get(), lgs.get()
        for n in range(ns - 1, -1, -1):
            part = slice(n * own, (n + 1) * own)
            gi = mm(w1c[...], pg[:, part]) + mm(wg, lg[:, part])
            if n:
                outs[1].buf[n - 1] = gi.astype(BF16)
                outs[1].flush(n - 1)
            else:
                outs[0].buf[...] = gi
                outs[0].flush()

    return staged(
        body,
        [Far(w1[0]), Far(w1[1], moved=True), Far(wgate_t), Near(pg), Near(lg)],
        [Near(plain((dim, own), F32)), Near(plain((max(ns - 1, 1), dim, own), BF16))],
        [pltpu.VMEM((dim, ce * hid_n), BF16)],
        "backward_inputs",
        16,
    )


def finish_inputs(own_part, received):
    dim, own = own_part.shape

    def body(ins, outs):
        for u in range(own // LANE):
            lanes = slice(u * LANE, (u + 1) * LANE)
            part = total(*(src.buf[:, lanes] for src in ins))
            outs[0].buf[lanes, :] = part.T
            outs[0].flush(pl.ds(u * LANE, LANE))

    return staged(
        body, [Near(own_part)] + [Near(v) for v in received], [plain((own, dim), F32)], [], "finish_inputs", 12
    )[0]


def finish_weights(second, first, other, epd, hid_n, out_n, dim, doms, exps, rows_n):
    m_sec, m_first, m_tow = layout(epd, hid_n, out_n, dim, doms, rows_n)
    ke = doms * exps

    def body(ins, outs, buf, tgf):
        out_f, out_s, out_t, out_g, out_h = (o.buf for o in outs)
        c = lax.rem(lax.axis_index(WIDTH), 2)
        r = lax.axis_index(ROWS)
        at_row = [spots(kind, r, rows_n) for kind in range(2)]
        for kind, size in ((0, m_sec), (1, m_first)):
            got = ins[kind].get()
            step = math.gcd(size, hid_n)
            for i, q, flat in pieces(kind, epd, hid_n, out_n, dim):
                for off in range(0, hid_n, step):
                    j, o = divmod(flat + off, size)
                    piece = got[at_row[kind][j], o : o + step, :].astype(F32)
                    if kind == 0:
                        out_s[i, off : off + step, q * LANE : (q + 1) * LANE] = piece
                    else:
                        buf[off : off + step, :] = piece
                if kind == 1:
                    out_f[i, q * LANE : (q + 1) * LANE, :] = buf[...].T
                if q == (out_n, dim)[kind] // LANE - 1:
                    outs[1 - kind].flush(i)
        near, sib = ins[1].get(), ins[2].get()
        for j in range(rows_n):
            at = at_row[1][j]
            for core, value in ((c, near[at, m_first:, :]), (1 - c, sib[at])):
                start = pl.multiple_of((core * rows_n + j) * m_tow, 8)
                tgf[pl.ds(start, m_tow), :] = value.astype(F32)
        for k in range(doms):
            out_t[k] = tgf[k * out_n : (k + 1) * out_n, :]
        outs[2].flush()
        for q in range(dim // LANE):
            at = doms * out_n + q * 32
            out_g[:, q * LANE : (q + 1) * LANE] = tgf[at : at + ke, :]
        outs[3].flush()
        out_h[...] = tgf[doms * out_n + ke : doms * out_n + ke + doms, :]
        outs[4].flush()

    return staged(
        body,
        [Near(second), Near(first), Near(other)],
        [
            plain((epd, dim, hid_n), F32),
            plain((epd, hid_n, out_n), F32),
            plain((doms, out_n, LANE), F32),
            plain((ke, dim), F32),
            plain((doms, LANE), F32),
        ],
        [pltpu.VMEM((hid_n, LANE), F32), pltpu.VMEM((2 * rows_n * m_tow, LANE), F32)],
        "finish_weights",
        16,
    )


def swap(value, axis, mask):
    size = lax.axis_size(axis)
    return lax.ppermute(value, axis, [(i, i ^ mask) for i in range(size)])


def total(*values):
    got = values[0].astype(F32)
    for value in values[1:]:
        got = got + value.astype(F32)
    return got


def send(value, axis, mask):
    return swap(value.astype(BF16), axis, mask)


together = lax.optimization_barrier


def reduce_rows(second, first, towers, beside):
    n_rows, n_width = lax.axis_size(ROWS), lax.axis_size(WIDTH)
    half = n_rows // 2
    far = [2 * q for q in range(1, half)]
    low = total(*(v[half:] for v in first)).astype(BF16)
    high = [total(*(v[m : m + 2] for v in second)).astype(BF16) for m in far]
    across = total(*towers).astype(BF16)
    first_got = swap(low, ROWS, 1)
    second_got = [swap(v, ROWS, m) for v, m in zip(high, far)]
    towers = total(*towers, *(swap(across, WIDTH, mask) for mask in range(2, n_width, 2)))
    tower_low, operand = together((towers[half:].astype(BF16), beside[1]))
    tower_got = swap(tower_low, ROWS, 1)
    inputs_part = tuple(beside[0](operand))
    first_got, second_got, tower_got, inputs_part = together((first_got, second_got, tower_got, inputs_part))

    def piece(q):
        return jnp.concatenate(
            [total(*(v[q] for v in first), first_got[q]), total(towers[q], tower_got[q])], axis=0
        )

    pair = total(*(v[:2] for v in second), *second_got)
    high = [piece(q).astype(BF16) for q in range(1, half)]
    high, low = together((high, pair.astype(BF16)))
    moved = [swap(v, ROWS, m) for v, m in zip(high, far)]
    moved, low = together((moved, swap(low, ROWS, 1)))
    pair = total(pair, low[::-1])
    return pair.astype(BF16), total(piece(0), *moved).astype(BF16), inputs_part


def gather_rows(pair, first, m_first, beside):
    half = lax.axis_size(ROWS) // 2
    far = [2 * q for q in range(1, half)]
    pair, first = together((pair, first))
    high, beside = together(([swap(first, ROWS, m) for m in far], beside))
    pair, evens = together((pair, jnp.stack([first] + high)))
    low, high = swap(evens, ROWS, 1), [swap(pair, ROWS, m) for m in far]
    low, high, beside = together((low, high, finish_inputs(*beside)))
    second, first = jnp.concatenate([pair] + high), jnp.concatenate([evens, low])
    return second, first, swap(first[:, m_first:], WIDTH, 1), beside


def local(inputs, w_first, w_second, w_gate, w_tower, norm_scale, norm_shift, w_head, domains, labels):
    n_width, n_rows = lax.axis_size(WIDTH), lax.axis_size(ROWS)
    devices = n_width * n_rows
    own = inputs.shape[0] // n_width
    count = float(own * devices)
    dim = inputs.shape[1]
    epd, _, hid_n = w_first.shape
    out_n = w_second.shape[2]
    doms, _, exps = w_gate.shape
    ke = doms * exps
    n_x = n_width // 2
    others = list(range(1, n_x))
    w1 = (w_first, swap(w_first, WIDTH, 1))
    w2 = (w_second, swap(w_second, WIDTH, 1))
    wgate_t = jnp.transpose(w_gate, (0, 2, 1)).reshape(ke, dim)
    marks = jnp.stack([domains, labels])

    x_far, w1_own, w2_own, wt = prepare(others, inputs, w_first, w_second, wgate_t, w_tower, own)
    w1t, w2t = (w1_own, w1[1]), (w2_own, w2[1])
    far = forward([Near(x_far)], w1t, w2t, wt, own, doms, False, BF16, "forward_send")[0]
    sent = [swap(far[s - 1 : s], WIDTH, 2 * s) for s in others]
    blocks = [Far(inputs, (own, dim), row_blocks([0], own)), Near(x_far)]
    kept = forward(blocks, w1t, w2t, wt, own, doms, True, F32, "forward_keep")
    tower, low, message = combine(kept[5], sent, marks, devices)
    stats = lax.all_to_all(message, BOTH, 0, 0, tiled=True)
    stats, low = together((stats, low))
    lows = [swap(low, WIDTH, 2 * s) for s in others]
    params, message = normalise(stats, tower, marks, norm_scale, norm_shift, w_head, devices, count)
    sums = lax.all_to_all(message, BOTH, 0, 0, tiled=True)

    acts = [(kept[:5], s) for s in range(n_x)]
    grad_shift, grad_scale, loss, sec_sib, first_sib, sec_own, first_own, tow_sib, tow_own, pg, lg = backward(
        sums, params, tower, lows, marks, acts, inputs, w2, wgate_t, w_tower, devices, n_rows, count
    )
    first_sib = swap(first_sib, WIDTH, 1)
    first_sib, sec_sib, tow_sib = together((first_sib, sec_sib, tow_sib))
    second, first, (gi_own, gi_out) = reduce_rows(
        (sec_own, swap(sec_sib, WIDTH, 1)),
        (first_own, first_sib),
        (tow_own, swap(tow_sib, WIDTH, 1)),
        (lambda grad: backward_inputs(grad, lg, w1, wgate_t, own), pg),
    )
    inputs_got = [swap(gi_out[s - 1], WIDTH, 2 * s) for s in others]
    m_first = layout(epd, hid_n, out_n, dim, doms, n_rows)[1]
    second, first, other, grad_inputs = gather_rows(second, first, m_first, (gi_own, inputs_got))
    grad_first, grad_second, grad_tower, grad_gate, grad_head = finish_weights(
        second, first, other, epd, hid_n, out_n, dim, doms, exps, n_rows
    )
    return (
        loss[0, 0],
        grad_inputs,
        grad_first,
        grad_second,
        grad_gate.reshape(doms, exps, dim).transpose(0, 2, 1),
        grad_tower,
        grad_scale,
        grad_shift,
        grad_head,
    )


def solution(mesh):
    placed = (
        P(ROWS, None),
        P(WIDTH, None, None),
        P(WIDTH, None, None),
        P(),
        P(),
        P(),
        P(),
        P(),
        P(BOTH),
        P(BOTH),
    )
    return jax.shard_map(
        local,
        mesh=mesh,
        in_specs=placed,
        out_specs=(
            P(),
            P(BOTH, None),
            P(WIDTH, None, None),
            P(WIDTH, None, None),
            P(),
            P(),
            P(),
            P(),
            P(),
        ),
        check_vma=False,
    )
```

```python
import math

import jax
import jax.numpy as jnp
from jax import lax
from jax.experimental import pallas as pl
from jax.experimental.pallas import tpu as pltpu
from jax.sharding import PartitionSpec as P

F32 = jnp.float32
BF16 = jnp.bfloat16
EPS = 1e-05
LANE = 128
MIB = 1 << 20
ROWS = "rows"
WIDTH = "width"
BOTH = (ROWS, WIDTH)


def mm(a, b):
    return jnp.dot(a, b, preferred_element_type=F32)


def mm_t(a, b):
    return lax.dot_general(a, b, (((1,), (1,)), ((), ())), preferred_element_type=F32)


def sigmoid(v):
    return 0.5 * jnp.tanh(0.5 * v) + 0.5


class Source:
    def __init__(self, buf, copies):
        self.buf = buf
        self.waiting = copies
        for copy in copies:
            copy.start()

    def get(self):
        for copy in self.waiting:
            copy.wait()
        self.waiting = []
        return self.buf


class Target:
    def __init__(self, ref, buf, sems):
        self.ref, self.buf, self.sems = ref, buf, sems
        self.waiting = []

    def flush(self, *at):
        if self.ref is None:
            return
        src = self.buf.at[at] if at else self.buf
        dst = self.ref.at[at] if at else self.ref
        copy = pltpu.make_async_copy(src, dst, next(self.sems))
        copy.start()
        self.waiting.append(copy)


class Near:
    def __init__(self, what):
        self.what = what


class Far:
    def __init__(self, arrays, shape=None, pairs=None, moved=False, into=None):
        self.into = into
        self.arrays = arrays if isinstance(arrays, (list, tuple)) else [arrays]
        self.moved = moved if isinstance(moved, list) else [moved] * len(self.arrays)
        self.shape = shape or self.arrays[0].shape
        self.dtype = self.arrays[0].dtype
        self.pairs = pairs or (lambda refs, buf: [(refs[0], buf)])


def staged(body, ins, outs, scratch, name, limit, n_sems=64):
    far_in = [i for i, s in enumerate(ins) if isinstance(s, Far) and s.into is None]
    far_out = [i for i, s in enumerate(outs) if not isinstance(s, Near)]
    args, specs, spans = [], [], []
    hbm = pl.BlockSpec(memory_space=pltpu.HBM)
    vmem = pl.BlockSpec(memory_space=pltpu.VMEM)
    anywhere = pl.BlockSpec(memory_space=pl.ANY)
    for s in ins:
        if isinstance(s, Far):
            spans.append((len(args), len(args) + len(s.arrays)))
            for a, moved in zip(s.arrays, s.moved):
                args.append(a if moved else pltpu.with_memory_space_constraint(a, pltpu.HBM))
                specs.append(anywhere if moved else hbm)
        else:
            spans.append((len(args), len(args) + 1))
            args.append(s.what)
            specs.append(vmem)
    n_in, n_out = len(args), len(outs)

    def kernel(*refs):
        refs_in, refs_out = refs[:n_in], refs[n_in : n_in + n_out]
        bufs = refs[n_in + n_out :]
        in_bufs = dict(zip(far_in, bufs))
        in_bufs.update({i: refs_out[s.into] for i, s in enumerate(ins) if isinstance(s, Far) and s.into is not None})
        out_bufs = dict(zip(far_out, bufs[len(far_in) :]))
        rest = bufs[len(far_in) + len(far_out) : -1]
        sems = iter([bufs[-1].at[i] for i in range(n_sems)])
        sources = []
        for i, (start, stop) in enumerate(spans):
            if i in in_bufs:
                pairs = ins[i].pairs(refs_in[start:stop], in_bufs[i])
                sources.append(Source(in_bufs[i], [pltpu.make_async_copy(a, b, next(sems)) for a, b in pairs]))
            else:
                sources.append(Source(refs_in[start], []))
        targets = []
        for i, ref in enumerate(refs_out):
            targets.append(Target(ref, out_bufs[i], sems) if i in out_bufs else Target(None, ref, sems))
        body(sources, targets, *rest)
        for s in sources:
            s.get()
        for t in targets:
            for copy in t.waiting:
                copy.wait()

    return pl.pallas_call(
        kernel,
        out_shape=[o.what if isinstance(o, Near) else pltpu.HBM(o.shape, o.dtype) for o in outs],
        in_specs=specs,
        out_specs=[hbm if i in far_out else vmem for i in range(n_out)],
        scratch_shapes=[pltpu.VMEM(ins[i].shape, ins[i].dtype) for i in far_in]
        + [pltpu.VMEM(outs[i].shape, outs[i].dtype) for i in far_out]
        + list(scratch)
        + [pltpu.SemaphoreType.DMA((n_sems,))],
        compiler_params=pltpu.CompilerParams(vmem_limit_bytes=limit * MIB),
        name=name,
    )(*args)


def plain(shape, dtype):
    return jax.ShapeDtypeStruct(shape, dtype)


def row_blocks(slots, own):
    def pairs(refs, buf):
        w = lax.axis_index(WIDTH)
        got = []
        for n, s in enumerate(slots):
            start = pl.multiple_of(lax.bitwise_xor(w, 2 * s) * own, own)
            got.append((refs[0].at[pl.ds(start, own), :], buf.at[n * own : (n + 1) * own, :]))
        return got

    return pairs


def reorder(ke, epd):
    first = lax.axis_index(WIDTH) * epd
    down = lax.broadcasted_iota(jnp.int32, (ke, ke), 0)
    across = lax.broadcasted_iota(jnp.int32, (ke, ke), 1)
    return jnp.where(lax.bitwise_xor(down, first) == across, 1.0, 0.0).astype(BF16)


def prepare(slots, inputs, w1, w2, wgate_t, wtower, own):
    dim = inputs.shape[1]
    epd, _, hid_n = w1.shape
    out_n = w2.shape[2]
    ke = wgate_t.shape[0]
    doms, _, th = wtower.shape

    def body(ins, outs):
        w1s, wgs, w2s, wts, _ = ins
        _, w1t, w2t, wt = (o.buf for o in outs)
        w1_buf = w1s.get()
        for i in range(epd):
            w1t[i * hid_n : (i + 1) * hid_n, :] = w1_buf[i].T
        w1t[epd * hid_n :, :] = mm(reorder(ke, epd), wgs.get()[...]).astype(BF16)
        w2_buf = w2s.get()
        for i in range(epd):
            w2t[i] = w2_buf[i].T
        wt_buf = wts.get()
        for k in range(doms):
            wt[k] = wt_buf[k].T
    return staged(
        body,
        [Far(a) for a in (w1, wgate_t, w2, wtower)]
        + [Far(inputs, (len(slots) * own, dim), row_blocks(slots, own), into=0)],
        [
            Near(plain((len(slots) * own, dim), BF16)),
            Near(plain((epd * hid_n + ke, dim), BF16)),
            Near(plain((epd, out_n, hid_n), BF16)),
            Near(plain((doms, th, out_n), BF16)),
        ],
        [],
        "prepare",
        12,
    )


def forward(blocks, w1, w2, wt, own, doms, keep, tower_out, name):
    epd, dim, hid_n = w1[1].shape
    out_n = w2[1].shape[2]
    ce = 2 * epd
    half = epd * hid_n
    ke = w1[0].shape[0] - half
    th = wt.shape[1]
    exps = ke // doms
    sizes = [(b.what if isinstance(b, Near) else b).shape[0] // own for b in blocks]
    ns = sum(sizes)

    def body(ins, outs, w1t, w2t, pre, *bufs):
        xs = ins[: len(blocks)]
        w1o, w1s, w2o, w2s, wts = ins[len(blocks) :]
        if keep:
            hid, slope, vals, gate, mixed = (o.buf for o in outs[:5])
        else:
            hid, vals, gate, mixed = bufs
        wt = wts.get()
        for i in range(epd):
            w1t[i * hid_n : (i + 1) * hid_n, :] = w1s.get()[i].T
            w2t[i] = w2s.get()[i].T
        parts = [(src, n) for src, size in zip(xs, sizes) for n in range(size)]
        for n, (src, place) in enumerate(parts):
            x = src.get()[place * own : (place + 1) * own, :]
            got = mm_t(w1o.get()[...], x)
            pre[:half, :] = got[:half]
            pre[ce * hid_n :, :] = got[half:]
            pre[half : ce * hid_n, :] = mm_t(w1t[...], x)
            logits = pre[ce * hid_n : ce * hid_n + ke, :].reshape(doms, exps, own)
            top = jnp.exp(logits - jnp.max(logits, axis=1, keepdims=True))
            soft = top / jnp.sum(top, axis=1, keepdims=True)
            gate[n] = soft.reshape(ke, own)

            def act(i, carry):
                at = pl.ds(pl.multiple_of(i * 16, 16), 16)
                v = pre[at, :]
                s = sigmoid(v)
                h = v * s
                hid[n, at, :] = h.astype(BF16)
                if keep:
                    slope[n, at, :] = (s + h * (1.0 - s)).astype(BF16)
                return carry

            lax.fori_loop(0, ce * hid_n // 16, act, 0, unroll=4 if keep else ce * hid_n // 16)
            for e in range(ce):
                w = w2o.get()[e] if e < epd else w2t[e - epd]
                vals[n, e * out_n : (e + 1) * out_n, :] = mm(w, hid[n, e * hid_n : (e + 1) * hid_n, :]).astype(BF16)
            if keep:
                for o in outs[:4]:
                    o.flush(n)
            for u in range(own // LANE):
                part = slice(u * LANE, (u + 1) * LANE)
                rows = [[gate[n, k * exps + e : k * exps + e + 1, part] for e in range(ce)] for k in range(doms)]

                def mix(i, carry):
                    acc = [None] * doms
                    for e in range(ce):
                        at = pl.ds(pl.multiple_of(e * out_n + i * 32, 32), 32)
                        v = vals[n, at, part].astype(F32)
                        for k in range(doms):
                            term = rows[k][e] * v
                            acc[k] = term if e == 0 else acc[k] + term
                    for k in range(doms):
                        at = pl.ds(pl.multiple_of(k * out_n + i * 32, 32), 32)
                        mixed[n, at, part] = acc[k].astype(BF16)
                    return carry

                lax.fori_loop(0, out_n // 32, mix, 0, unroll=4 if keep else out_n // 32)
            if keep:
                outs[4].flush(n)
            if n == 0 or not keep:
                tower = outs[-1]
                for k in range(doms):
                    tower.buf[n, k * th : (k + 1) * th, :] = mm(
                        wt[k], mixed[n, k * out_n : (k + 1) * out_n, :]
                    ).astype(tower_out)
                tower.flush(n)

    kept = [
        plain((ns, ce * hid_n, own), BF16),
        plain((ns, ce * hid_n, own), BF16),
        plain((ns, ce * out_n, own), BF16),
        plain((ns, ke, own), F32),
        plain((ns, doms * out_n, own), BF16),
    ]
    outs = list(kept) if keep else []
    outs.append(Near(plain((1 if keep else ns, doms * th, own), tower_out)))
    scratch = [
        pltpu.VMEM((half, dim), BF16),
        pltpu.VMEM((epd, out_n, hid_n), BF16),
        pltpu.VMEM((ce * hid_n + ke, own), F32),
    ]
    if not keep:
        scratch += [pltpu.VMEM(kept[i].shape, kept[i].dtype) for i in (0, 2, 3, 4)]
    ins = blocks + [Near(a) for a in (w1[0], w1[1], w2[0], w2[1], wt)]
    return staged(body, ins, outs, scratch, name, 40)


def combine(own_part, received, marks, devices):
    _, rows, own = own_part.shape
    doms = rows // LANE

    def body(ins, outs, cols):
        part = ins[0].get()
        got = [s.get() for s in ins[2:]]
        tower, low, message = (o.buf for o in outs)
        cols[...] = jnp.zeros_like(cols)
        for k in range(doms):
            at = slice(k * LANE, (k + 1) * LANE)
            total = part[0, at, :]
            for ref in got:
                total = total + ref[0, at, :].astype(F32)
            tower[at, :] = total
            low[at, :] = total.astype(BF16)
            mean = jnp.sum(total, axis=1, keepdims=True) * (1.0 / own)
            dev = total - mean
            cols[:, k : k + 1] = mean
            cols[:, doms + k : doms + k + 1] = jnp.sum(dev * dev, axis=1, keepdims=True)
        outs[0].flush()
        pair = jnp.concatenate([ins[1].get()[...].astype(F32), jnp.zeros((14, own), F32)], axis=0)
        low[rows:, :] = pair.astype(BF16)
        outs[1].flush()
        tile = cols[...].T[:8, :]
        for d in range(devices):
            message[d * 8 : (d + 1) * 8, :] = tile
        outs[2].flush()

    return staged(
        body,
        [Near(own_part), Near(marks)] + [Near(v) for v in received],
        [Near(plain((rows, own), F32)), Near(plain((rows + 16, own), BF16)), Near(plain((devices * 8, LANE), F32))],
        [pltpu.VMEM((LANE, LANE), F32)],
        "combine",
        16,
    )


def pick(dom, values):
    got = values[-1]
    for k in range(len(values) - 2, -1, -1):
        got = jnp.where(dom == k, values[k], got)
    return got


def chosen_tower(tower, dom, wide, lanes, doms):
    values = [tower[k * LANE : (k + 1) * LANE, lanes].astype(F32) for k in range(doms)]
    mean, gain, shift, head = (pick(dom, [wide[j * doms + k] for k in range(doms)]) for j in range(4))
    centred = pick(dom, values) - mean
    return values, centred, centred * gain + shift, gain, head


def spread_columns(wide, rows_ref, n):
    cols = rows_ref[...].T
    for j in range(n):
        wide[j] = jnp.broadcast_to(cols[:, j : j + 1], (LANE, LANE))


def normalise(stats, tower, marks, scale, shift, head, devices, count):
    rows, own = tower.shape
    doms = rows // LANE

    def body(ins, outs, prm, wide, q):
        st, tws, mks, sc, sh, hd = ins
        params, message = (o.buf for o in outs)
        prm[...] = jnp.zeros_like(prm)
        got = st.get()[...].reshape(devices, 8, LANE)
        total = jnp.sum(got, axis=0)
        mean = total * (1.0 / devices)
        dev = got - mean[None]
        spread = jnp.sum(dev * dev, axis=0) * float(own)
        var = (total[doms : 2 * doms] + spread[:doms]) * (1.0 / count)
        inv = lax.rsqrt(var + EPS)
        prm[0:doms, :] = mean[:doms]
        prm[doms : 2 * doms, :] = inv * sc.get()[...]
        prm[2 * doms : 3 * doms, :] = sh.get()[...]
        prm[3 * doms : 4 * doms, :] = hd.get()[...]
        prm[4 * doms : 5 * doms, :] = inv
        params[:16, :] = prm[:16, :]
        spread_columns(wide, prm, 4 * doms)
        tw, mk = tws.get(), mks.get()
        loss = jnp.zeros((1, LANE), F32)
        for u in range(own // LANE):
            part = slice(u * LANE, (u + 1) * LANE)
            dom = mk[0:1, part]
            target = mk[1:2, part].astype(F32)
            _, centred, affine, _, head_w = chosen_tower(tw, dom, wide, part, doms)
            s = sigmoid(affine)
            act = affine * s
            chosen = jnp.sum(act * head_w, axis=0, keepdims=True)
            soft = jnp.maximum(chosen, 0.0) + jnp.log(1.0 + jnp.exp(-jnp.abs(chosen)))
            loss = loss + (soft - target * chosen)
            score_grad = (sigmoid(chosen) - target) * (1.0 / count)
            grad = score_grad * head_w * (s + act * (1.0 - s))
            q[0:LANE, part] = grad
            q[LANE : 2 * LANE, part] = grad * centred
            q[2 * LANE :, part] = score_grad * act
        kinds = lax.broadcasted_iota(jnp.int32, (8, own), 0)
        one_hot = (kinds == mk[0:1, :]).astype(F32).astype(BF16)
        high = q[...].astype(BF16)
        sums = (mm_t(one_hot, high) + mm_t(one_hot, (q[...] - high.astype(F32)).astype(BF16)))[:doms]
        tile = [sums[:, :LANE], sums[:, LANE : 2 * LANE] * inv]
        all_rows = tile + [loss, jnp.zeros((1, LANE), F32)]
        twice = jnp.concatenate(all_rows + all_rows, axis=0).astype(BF16)
        for d in range(devices // 2):
            message[d * 16 : (d + 1) * 16, :] = twice
        params[16:, :] = jnp.concatenate([sums[:, 2 * LANE :], jnp.zeros((8 - doms, LANE), F32)], axis=0)
        outs[0].flush()

    return staged(
        body,
        [Near(v) for v in (stats, tower, marks, scale, shift, head)],
        [Near(plain((24, LANE), F32)), Near(plain((devices * 8, LANE), BF16))],
        [
            pltpu.VMEM((LANE, LANE), F32),
            pltpu.VMEM((4 * doms, LANE, LANE), F32),
            pltpu.VMEM((3 * LANE, own), F32),
        ],
        "normalise",
        16,
    )


def layout(epd, hid_n, out_n, dim, doms, rows_n):
    second = epd * hid_n * out_n // LANE
    first = epd * hid_n * dim // LANE
    towers = -(-(doms * out_n + (dim // LANE) * 32) // (2 * 16 * rows_n)) * 16
    return second // rows_n, first // rows_n, towers


def pieces(kind, epd, hid_n, out_n, dim):
    flat = 0
    for i in range(epd):
        for q in range((out_n, dim)[kind] // LANE):
            yield i, q, flat
            flat += hid_n


def spots(kind, row, rows_n):
    got = []
    for j in range(rows_n):
        p = lax.bitwise_xor(row, j)
        got.append(p if kind == 0 else (p & 1) * (rows_n // 2) + lax.shift_right_logical(p, 1))
    return got


def backward(
    sums, params, tower, low_towers, marks, acts, inputs, w1, w2, wgate_t, wtower, devices, rows_n, count
):
    ns = 1 + len(low_towers)
    t_rows, own = tower.shape
    total_n = ns * own
    dim = inputs.shape[1]
    epd, hid_n, out_n = w2[0].shape
    ce = 2 * epd
    ke = wgate_t.shape[0]
    doms, _, th = wtower.shape
    exps = ke // doms
    m_sec, m_first, m_tow = layout(epd, hid_n, out_n, dim, doms, rows_n)

    def body(ins, outs, wide, prm, tg, mg, eg, gg, srow, tgf, facc):
        sm, pr, tw0, mk0 = ins[:4]
        low = ins[4 : 3 + ns]
        wts, gate, vals, w2o, w2s, slope, xs, hid, mixed, _ = ins[3 + ns :]
        shift_out, scale_out, loss_out, sec_sib, first_sib, sec_mine, first_mine, tow_sib, tow_mine, pgs, lgs, _ = outs
        pg, lg = pgs.buf, lgs.buf
        c = lax.rem(lax.axis_index(WIDTH), 2)
        r = lax.axis_index(ROWS)
        at_row = [spots(kind, r, rows_n) for kind in range(2)]
        prm[...] = jnp.zeros_like(prm)
        total = jnp.sum(sm.get()[...].astype(F32).reshape(devices, 8, LANE), axis=0)
        shift_out.buf[...] = total[:doms]
        scale_out.buf[...] = total[doms : 2 * doms]
        loss_out.buf[...] = jnp.sum(total[2 * doms : 2 * doms + 1, :], axis=1, keepdims=True) * (1.0 / count)
        for target in (shift_out, scale_out, loss_out):
            target.flush()
        given = pr.get()[...]
        gain, inv = given[doms : 2 * doms], given[4 * doms : 5 * doms]
        prm[0:16, :] = given[:16]
        prm[4 * doms : 5 * doms, :] = gain * total[:doms] * (1.0 / count)
        prm[5 * doms : 6 * doms, :] = gain * inv * total[doms : 2 * doms] * (1.0 / count)
        spread_columns(wide, prm, 6 * doms)
        for u in range(total_n // LANE):
            n = u * LANE // own
            part = slice(u * LANE, (u + 1) * LANE)
            here = slice(u * LANE - n * own, (u + 1) * LANE - n * own)
            if n == 0:
                tw = tw0.get()
                dom = mk0.get()[0:1, here]
                target = mk0.get()[1:2, here].astype(F32)
            else:
                tw = low[n - 1].get()
                pair = tw[t_rows : t_rows + 16, here].astype(F32)
                dom = pair[0:1].astype(jnp.int32)
                target = pair[1:2]
            values, _, affine, gain_s, head_w = chosen_tower(tw, dom, wide, here, doms)
            s = sigmoid(affine)
            a = affine * s
            chosen = jnp.sum(a * head_w, axis=0, keepdims=True)
            score_grad = (sigmoid(chosen) - target) * (1.0 / count)
            grad = gain_s * (score_grad * head_w * (s + a * (1.0 - s)))
            for k in range(doms):
                v = jnp.where(dom == k, grad, 0.0) - wide[4 * doms + k]
                v = v - (values[k] - wide[k]) * wide[5 * doms + k]
                down = v.astype(BF16)
                tg[k * th : (k + 1) * th, part] = down
                srow[k : k + 1, part] = jnp.sum(down.astype(F32) * values[k], axis=0, keepdims=True)
        wt = wts.get()
        for k in range(doms):
            mg[k * out_n : (k + 1) * out_n, :] = mm(wt[k], tg[k * th : (k + 1) * th, :])
        vals, gate = vals.get(), gate.get()
        gg[...] = jnp.zeros_like(gg)

        def tower_part(k):
            tgf[k * out_n : (k + 1) * out_n, :] = mm_t(
                mixed.get()[k * out_n : (k + 1) * out_n, :], tg[k * th : (k + 1) * th, :]
            )

        def hidden_part(n, e):
            at = slice(e * hid_n, (e + 1) * hid_n)
            part = slice(n * own, (n + 1) * own)
            w = (w2o, w2s)[e // epd].get()[e % epd]
            grad = mm(w, eg[e * out_n : (e + 1) * out_n, part])
            pg[at, part] = (grad * slope.get()[at, part].astype(F32)).astype(BF16)

        ready = []
        for u in range(total_n // LANE):
            part = slice(u * LANE, (u + 1) * LANE)
            rows = [[gate[k * exps + e : k * exps + e + 1, part] for e in range(ce)] for k in range(doms)]

            def spread(i, acc):
                up = [mg[pl.ds(pl.multiple_of(k * out_n + i * 16, 16), 16), part] for k in range(doms)]
                acc = list(acc)
                for e in range(ce):
                    at = pl.ds(pl.multiple_of(e * out_n + i * 16, 16), 16)
                    v = vals[at, part].astype(F32)
                    back = None
                    for k in range(doms):
                        term = rows[k][e] * up[k]
                        back = term if k == 0 else back + term
                        prod = up[k] * v
                        acc[k * ce + e] = acc[k * ce + e] + (prod[:8] + prod[8:])
                    eg[at, part] = back.astype(BF16)
                return tuple(acc)

            zero = jnp.zeros((8, LANE), F32)
            acc = lax.fori_loop(0, out_n // 16, spread, (zero,) * (doms * ce), unroll=out_n // 16)
            for k in range(doms):
                for e in range(ce):
                    gg[k * exps + e : k * exps + e + 1, part] = jnp.sum(acc[k * ce + e], axis=0, keepdims=True)
            if (u + 1) * LANE % own == 0:
                ready += [(hidden_part, (u * LANE // own, e)) for e in range(ce)]
            if ready:
                task, args = ready.pop(0)
                task(*args)
        for task, args in ready:
            task(*args)
        pgs.flush()
        here = lax.broadcasted_iota(jnp.int32, (exps, total_n), 0) < ce
        for k in range(doms):
            at = slice(k * exps, (k + 1) * exps)
            gg[at, :] = jnp.where(here, gate[at, :] * (gg[at, :] - srow[k : k + 1, :]), 0.0)
        lg[...] = mm(reorder(ke, epd), gg[...].astype(BF16)).astype(BF16)
        lgs.flush()
        hid = hid.get()

        def put(kind, slot, values):
            target = ((sec_sib, first_sib), (sec_mine, first_mine))[slot < epd][kind]
            size = (m_sec, m_first)[kind]
            step = math.gcd(size, hid_n)
            for i, q, flat in pieces(kind, epd, hid_n, out_n, dim):
                if i == slot % epd:
                    for off in range(0, hid_n, step):
                        j, o = divmod(flat + off, size)
                        part = values[off : off + step, q * LANE : (q + 1) * LANE]
                        target.buf[at_row[kind][j], o : o + step, :] = part.astype(BF16)

        x = xs.get()
        facc[...] = mm(pg[...], x[...])
        for e in range(ce):
            put(1, e, facc[e * hid_n : (e + 1) * hid_n, :])
        for e in range(ce):
            at = slice(e * hid_n, (e + 1) * hid_n)
            at_o = slice(e * out_n, (e + 1) * out_n)
            put(0, e, mm_t(hid[at, :], eg[at_o, :]))
        for target in (sec_sib, first_sib, sec_mine, first_mine):
            target.flush()
        for k in range(doms):
            tower_part(k)
        tgf[doms * out_n :, :] = jnp.zeros((tgf.shape[0] - doms * out_n, LANE), F32)
        part_g = mm(lg[...], x[...])
        for q in range(dim // LANE):
            tgf[doms * out_n + q * 32 : doms * out_n + q * 32 + ke, :] = part_g[:, q * LANE : (q + 1) * LANE]
        tgf[doms * out_n + ke : doms * out_n + 32, :] = given[16 : 48 - ke]
        for target, core in ((tow_sib, 1 - c), (tow_mine, c)):
            for j in range(rows_n):
                start = pl.multiple_of((core * rows_n + j) * m_tow, 8)
                target.buf[at_row[1][j], :, :] = tgf[pl.ds(start, m_tow), :].astype(BF16)
            target.flush()

    outs = [
        plain((doms, LANE), F32),
        plain((doms, LANE), F32),
        plain((1, 1), F32),
        Near(plain((rows_n, m_sec, LANE), BF16)),
        Near(plain((rows_n, m_first, LANE), BF16)),
        Near(plain((rows_n, m_sec, LANE), BF16)),
        Near(plain((rows_n, m_first, LANE), BF16)),
        Near(plain((rows_n, m_tow, LANE), BF16)),
        Near(plain((rows_n, m_tow, LANE), BF16)),
        Near(plain((ce * hid_n, total_n), BF16)),
        Near(plain((ke, total_n), BF16)),
        Near(plain((dim, ce * hid_n), BF16)),
    ]
    scratch = [
        pltpu.VMEM((6 * doms, LANE, LANE), F32),
        pltpu.VMEM((LANE, LANE), F32),
        pltpu.VMEM((doms * th, total_n), BF16),
        pltpu.VMEM((doms * out_n, total_n), F32),
        pltpu.VMEM((ce * out_n, total_n), BF16),
        pltpu.VMEM((ke, total_n), F32),
        pltpu.VMEM((8, total_n), F32),
        pltpu.VMEM((2 * rows_n * m_tow, LANE), F32),
        pltpu.VMEM((ce * hid_n, dim), F32),
    ]

    def side_by_side(which):
        def pairs(refs, buf):
            return [(r.at[n], buf.at[:, i * own : (i + 1) * own]) for i, (r, (_, n)) in enumerate(zip(refs, acts))]

        arrays = [a[which] for a, _ in acts]
        return Far(arrays, (arrays[0].shape[1], total_n), pairs)

    ins = [Near(sums), Near(params), Near(tower), Near(marks)]
    ins += [Near(v) for v in low_towers]
    ins += [Far(wtower), side_by_side(3), side_by_side(2), Far(w2[0]), Far(w2[1], moved=True), side_by_side(1)]
    ins += [Far(inputs, (total_n, dim), row_blocks(list(range(ns)), own)), side_by_side(0), side_by_side(4)]

    def joined(refs, buf):
        slots = [(refs[e // epd].at[e % epd], e) for e in range(ce)]
        return [(ref, buf.at[:, e * hid_n : (e + 1) * hid_n]) for ref, e in slots]

    ins.append(Far(w1, pairs=joined, moved=[False, True], into=len(outs) - 1))
    return staged(body, ins, outs, scratch, "backward", 44)


def backward_inputs(pg, lg, w1, wgate_t, own):
    total_n = pg.shape[1]
    ns = total_n // own
    dim = w1.shape[0]
    ke = wgate_t.shape[0]

    def body(ins, outs):
        w1c, wgs, pgs, lgs = ins
        wg = jnp.concatenate([wgs.get()[...], jnp.zeros((LANE - ke, dim), BF16)], axis=0).T[:, :ke]
        pg, lg, w1c = pgs.get(), lgs.get(), w1c.get()
        for n in range(ns - 1, -1, -1):
            part = slice(n * own, (n + 1) * own)
            gi = mm(w1c[...], pg[:, part]) + mm(wg, lg[:, part])
            if n:
                outs[1].buf[n - 1] = gi.astype(BF16)
                outs[1].flush(n - 1)
            else:
                outs[0].buf[...] = gi
                outs[0].flush()

    return staged(
        body,
        [Near(w1), Near(wgate_t), Near(pg), Near(lg)],
        [Near(plain((dim, own), F32)), Near(plain((max(ns - 1, 1), dim, own), BF16))],
        [],
        "backward_inputs",
        16,
    )


def finish_inputs(own_part, received):
    dim, own = own_part.shape

    def body(ins, outs):
        for u in range(own // LANE):
            lanes = slice(u * LANE, (u + 1) * LANE)
            part = total(*(src.buf[:, lanes] for src in ins))
            outs[0].buf[lanes, :] = part.T
            outs[0].flush(pl.ds(u * LANE, LANE))

    return staged(
        body, [Near(own_part)] + [Near(v) for v in received], [plain((own, dim), F32)], [], "finish_inputs", 12
    )[0]


def finish_weights(second, first, other, epd, hid_n, out_n, dim, doms, exps, rows_n):
    m_sec, m_first, m_tow = layout(epd, hid_n, out_n, dim, doms, rows_n)
    ke = doms * exps

    def body(ins, outs, buf, tgf):
        out_f, out_s, out_t, out_g, out_h = (o.buf for o in outs)
        c = lax.rem(lax.axis_index(WIDTH), 2)
        r = lax.axis_index(ROWS)
        at_row = [spots(kind, r, rows_n) for kind in range(2)]
        for kind, size in ((0, m_sec), (1, m_first)):
            got = ins[kind].get()
            step = math.gcd(size, hid_n)
            for i, q, flat in pieces(kind, epd, hid_n, out_n, dim):
                for off in range(0, hid_n, step):
                    j, o = divmod(flat + off, size)
                    piece = got[at_row[kind][j], o : o + step, :].astype(F32)
                    if kind == 0:
                        out_s[i, off : off + step, q * LANE : (q + 1) * LANE] = piece
                    else:
                        buf[off : off + step, :] = piece
                if kind == 1:
                    out_f[i, q * LANE : (q + 1) * LANE, :] = buf[...].T
                if q == (out_n, dim)[kind] // LANE - 1:
                    outs[1 - kind].flush(i)
        near, sib = ins[1].get(), ins[2].get()
        for j in range(rows_n):
            at = at_row[1][j]
            for core, value in ((c, near[at, m_first:, :]), (1 - c, sib[at])):
                start = pl.multiple_of((core * rows_n + j) * m_tow, 8)
                tgf[pl.ds(start, m_tow), :] = value.astype(F32)
        for k in range(doms):
            out_t[k] = tgf[k * out_n : (k + 1) * out_n, :]
        outs[2].flush()
        for q in range(dim // LANE):
            at = doms * out_n + q * 32
            out_g[:, q * LANE : (q + 1) * LANE] = tgf[at : at + ke, :]
        outs[3].flush()
        out_h[...] = tgf[doms * out_n + ke : doms * out_n + ke + doms, :]
        outs[4].flush()

    return staged(
        body,
        [Near(second), Near(first), Near(other)],
        [
            plain((epd, dim, hid_n), F32),
            plain((epd, hid_n, out_n), F32),
            plain((doms, out_n, LANE), F32),
            plain((ke, dim), F32),
            plain((doms, LANE), F32),
        ],
        [pltpu.VMEM((hid_n, LANE), F32), pltpu.VMEM((2 * rows_n * m_tow, LANE), F32)],
        "finish_weights",
        16,
    )


def swap(value, axis, mask):
    size = lax.axis_size(axis)
    return lax.ppermute(value, axis, [(i, i ^ mask) for i in range(size)])


def total(*values):
    got = values[0].astype(F32)
    for value in values[1:]:
        got = got + value.astype(F32)
    return got


def send(value, axis, mask):
    return swap(value.astype(BF16), axis, mask)


together = lax.optimization_barrier


def reduce_rows(second, first, towers, beside):
    n_rows, n_width = lax.axis_size(ROWS), lax.axis_size(WIDTH)
    half = n_rows // 2
    far = [2 * q for q in range(1, half)]
    low = total(*(v[half:] for v in first)).astype(BF16)
    high = [total(*(v[m : m + 2] for v in second)).astype(BF16) for m in far]
    across = total(*towers).astype(BF16)
    first_got = swap(low, ROWS, 1)
    second_got = [swap(v, ROWS, m) for v, m in zip(high, far)]
    towers = total(*towers, *(swap(across, WIDTH, mask) for mask in range(2, n_width, 2)))
    tower_low, operand = together((towers[half:].astype(BF16), beside[1]))
    tower_got = swap(tower_low, ROWS, 1)
    inputs_part = tuple(beside[0](operand))
    first_got, second_got, tower_got, inputs_part = together((first_got, second_got, tower_got, inputs_part))

    def piece(q):
        return jnp.concatenate(
            [total(*(v[q] for v in first), first_got[q]), total(towers[q], tower_got[q])], axis=0
        )

    pair = total(*(v[:2] for v in second), *second_got)
    high = [piece(q).astype(BF16) for q in range(1, half)]
    high, low = together((high, pair.astype(BF16)))
    moved = [swap(v, ROWS, m) for v, m in zip(high, far)]
    moved, low = together((moved, swap(low, ROWS, 1)))
    pair = total(pair, low[::-1])
    return pair.astype(BF16), total(piece(0), *moved).astype(BF16), inputs_part


def gather_rows(pair, first, m_first, beside):
    half = lax.axis_size(ROWS) // 2
    far = [2 * q for q in range(1, half)]
    pair, first = together((pair, first))
    high, beside = together(([swap(first, ROWS, m) for m in far], beside))
    pair, evens = together((pair, jnp.stack([first] + high)))
    low, high = swap(evens, ROWS, 1), [swap(pair, ROWS, m) for m in far]
    low, high, beside = together((low, high, finish_inputs(*beside)))
    second, first = jnp.concatenate([pair] + high), jnp.concatenate([evens, low])
    return second, first, swap(first[:, m_first:], WIDTH, 1), beside


def local(inputs, w_first, w_second, w_gate, w_tower, norm_scale, norm_shift, w_head, domains, labels):
    n_width, n_rows = lax.axis_size(WIDTH), lax.axis_size(ROWS)
    devices = n_width * n_rows
    own = inputs.shape[0] // n_width
    count = float(own * devices)
    dim = inputs.shape[1]
    epd, _, hid_n = w_first.shape
    out_n = w_second.shape[2]
    doms, _, exps = w_gate.shape
    ke = doms * exps
    n_x = n_width // 2
    others = list(range(1, n_x))
    w1 = (w_first, swap(w_first, WIDTH, 1))
    w2 = (w_second, swap(w_second, WIDTH, 1))
    wgate_t = jnp.transpose(w_gate, (0, 2, 1)).reshape(ke, dim)
    marks = jnp.stack([domains, labels])

    x_far, w1_own, w2_own, wt = prepare(others, inputs, w_first, w_second, wgate_t, w_tower, own)
    w1t, w2t = (w1_own, w1[1]), (w2_own, w2[1])
    far = forward([Near(x_far)], w1t, w2t, wt, own, doms, False, BF16, "forward_send")[0]
    sent = [swap(far[s - 1 : s], WIDTH, 2 * s) for s in others]
    blocks = [Far(inputs, (own, dim), row_blocks([0], own)), Near(x_far)]
    kept = forward(blocks, w1t, w2t, wt, own, doms, True, F32, "forward_keep")
    tower, low, message = combine(kept[5], sent, marks, devices)
    stats = lax.all_to_all(message, BOTH, 0, 0, tiled=True)
    stats, low = together((stats, low))
    lows = [swap(low, WIDTH, 2 * s) for s in others]
    params, message = normalise(stats, tower, marks, norm_scale, norm_shift, w_head, devices, count)
    sums = lax.all_to_all(message, BOTH, 0, 0, tiled=True)

    acts = [(kept[:5], s) for s in range(n_x)]
    grad_shift, grad_scale, loss, sec_sib, first_sib, sec_own, first_own, tow_sib, tow_own, pg, lg, w1_joined = backward(
        sums, params, tower, lows, marks, acts, inputs, w1, w2, wgate_t, w_tower, devices, n_rows, count
    )
    first_sib = swap(first_sib, WIDTH, 1)
    first_sib, sec_sib, tow_sib = together((first_sib, sec_sib, tow_sib))
    second, first, (gi_own, gi_out) = reduce_rows(
        (sec_own, swap(sec_sib, WIDTH, 1)),
        (first_own, first_sib),
        (tow_own, swap(tow_sib, WIDTH, 1)),
        (lambda grad: backward_inputs(grad, lg, w1_joined, wgate_t, own), pg),
    )
    inputs_got = [swap(gi_out[s - 1], WIDTH, 2 * s) for s in others]
    m_first = layout(epd, hid_n, out_n, dim, doms, n_rows)[1]
    second, first, other, grad_inputs = gather_rows(second, first, m_first, (gi_own, inputs_got))
    grad_first, grad_second, grad_tower, grad_gate, grad_head = finish_weights(
        second, first, other, epd, hid_n, out_n, dim, doms, exps, n_rows
    )
    return (
        loss[0, 0],
        grad_inputs,
        grad_first,
        grad_second,
        grad_gate.reshape(doms, exps, dim).transpose(0, 2, 1),
        grad_tower,
        grad_scale,
        grad_shift,
        grad_head,
    )


def solution(mesh):
    placed = (
        P(ROWS, None),
        P(WIDTH, None, None),
        P(WIDTH, None, None),
        P(),
        P(),
        P(),
        P(),
        P(),
        P(BOTH),
        P(BOTH),
    )
    return jax.shard_map(
        local,
        mesh=mesh,
        in_specs=placed,
        out_specs=(
            P(),
            P(BOTH, None),
            P(WIDTH, None, None),
            P(WIDTH, None, None),
            P(),
            P(),
            P(),
            P(),
            P(),
        ),
        check_vma=False,
    )
```

```python
import math

import jax
import jax.numpy as jnp
from jax import lax
from jax.experimental import pallas as pl
from jax.experimental.pallas import tpu as pltpu
from jax.sharding import PartitionSpec as P

F32 = jnp.float32
BF16 = jnp.bfloat16
EPS = 1e-05
LANE = 128
MIB = 1 << 20
ROWS = "rows"
WIDTH = "width"
BOTH = (ROWS, WIDTH)


def mm(a, b):
    return jnp.dot(a, b, preferred_element_type=F32)


def mm_t(a, b):
    return lax.dot_general(a, b, (((1,), (1,)), ((), ())), preferred_element_type=F32)


def sigmoid(v):
    return 0.5 * jnp.tanh(0.5 * v) + 0.5


PLAIN = 8


def base(values):
    first = values[:, :PLAIN].astype(BF16).astype(F32)
    return jnp.sum(first, axis=1, keepdims=True) * (1.0 / PLAIN)


def encode(values):
    lane = lax.broadcasted_iota(jnp.int32, values.shape, 1)
    return jnp.where(lane < PLAIN, values, values - base(values)).astype(BF16)


def decode(values, added, start=0):
    lane = lax.broadcasted_iota(jnp.int32, values.shape, 1)
    values = values.astype(F32)
    return jnp.where(lane < PLAIN - start, values, values + added)


class Source:
    def __init__(self, buf, copies):
        self.buf = buf
        self.waiting = copies
        for copy in copies:
            copy.start()

    def get(self):
        for copy in self.waiting:
            copy.wait()
        self.waiting = []
        return self.buf


class Target:
    def __init__(self, ref, buf, sems):
        self.ref, self.buf, self.sems = ref, buf, sems
        self.waiting = []

    def flush(self, *at):
        if self.ref is None:
            return
        src = self.buf.at[at] if at else self.buf
        dst = self.ref.at[at] if at else self.ref
        copy = pltpu.make_async_copy(src, dst, next(self.sems))
        copy.start()
        self.waiting.append(copy)


class Near:
    def __init__(self, what):
        self.what = what


class Far:
    def __init__(self, arrays, shape=None, pairs=None, moved=False, into=None):
        self.into = into
        self.arrays = arrays if isinstance(arrays, (list, tuple)) else [arrays]
        self.moved = moved if isinstance(moved, list) else [moved] * len(self.arrays)
        self.shape = shape or self.arrays[0].shape
        self.dtype = self.arrays[0].dtype
        self.pairs = pairs or (lambda refs, buf: [(refs[0], buf)])


def staged(body, ins, outs, scratch, name, limit, n_sems=64):
    far_in = [i for i, s in enumerate(ins) if isinstance(s, Far) and s.into is None]
    far_out = [i for i, s in enumerate(outs) if not isinstance(s, Near)]
    args, specs, spans = [], [], []
    hbm = pl.BlockSpec(memory_space=pltpu.HBM)
    vmem = pl.BlockSpec(memory_space=pltpu.VMEM)
    anywhere = pl.BlockSpec(memory_space=pl.ANY)
    for s in ins:
        if isinstance(s, Far):
            spans.append((len(args), len(args) + len(s.arrays)))
            for a, moved in zip(s.arrays, s.moved):
                args.append(a if moved else pltpu.with_memory_space_constraint(a, pltpu.HBM))
                specs.append(anywhere if moved else hbm)
        else:
            spans.append((len(args), len(args) + 1))
            args.append(s.what)
            specs.append(vmem)
    n_in, n_out = len(args), len(outs)

    def kernel(*refs):
        refs_in, refs_out = refs[:n_in], refs[n_in : n_in + n_out]
        bufs = refs[n_in + n_out :]
        in_bufs = dict(zip(far_in, bufs))
        in_bufs.update({i: refs_out[s.into] for i, s in enumerate(ins) if isinstance(s, Far) and s.into is not None})
        out_bufs = dict(zip(far_out, bufs[len(far_in) :]))
        rest = bufs[len(far_in) + len(far_out) : -1]
        sems = iter([bufs[-1].at[i] for i in range(n_sems)])
        sources = []
        for i, (start, stop) in enumerate(spans):
            if i in in_bufs:
                pairs = ins[i].pairs(refs_in[start:stop], in_bufs[i])
                sources.append(Source(in_bufs[i], [pltpu.make_async_copy(a, b, next(sems)) for a, b in pairs]))
            else:
                sources.append(Source(refs_in[start], []))
        targets = []
        for i, ref in enumerate(refs_out):
            targets.append(Target(ref, out_bufs[i], sems) if i in out_bufs else Target(None, ref, sems))
        body(sources, targets, *rest)
        for s in sources:
            s.get()
        for t in targets:
            for copy in t.waiting:
                copy.wait()

    return pl.pallas_call(
        kernel,
        out_shape=[o.what if isinstance(o, Near) else pltpu.HBM(o.shape, o.dtype) for o in outs],
        in_specs=specs,
        out_specs=[hbm if i in far_out else vmem for i in range(n_out)],
        scratch_shapes=[pltpu.VMEM(ins[i].shape, ins[i].dtype) for i in far_in]
        + [pltpu.VMEM(outs[i].shape, outs[i].dtype) for i in far_out]
        + list(scratch)
        + [pltpu.SemaphoreType.DMA((n_sems,))],
        compiler_params=pltpu.CompilerParams(vmem_limit_bytes=limit * MIB),
        name=name,
    )(*args)


def plain(shape, dtype):
    return jax.ShapeDtypeStruct(shape, dtype)


def row_blocks(slots, own):
    def pairs(refs, buf):
        w = lax.axis_index(WIDTH)
        got = []
        for n, s in enumerate(slots):
            start = pl.multiple_of(lax.bitwise_xor(w, 2 * s) * own, own)
            got.append((refs[0].at[pl.ds(start, own), :], buf.at[n * own : (n + 1) * own, :]))
        return got

    return pairs


def reorder(ke, epd):
    first = lax.axis_index(WIDTH) * epd
    down = lax.broadcasted_iota(jnp.int32, (ke, ke), 0)
    across = lax.broadcasted_iota(jnp.int32, (ke, ke), 1)
    return jnp.where(lax.bitwise_xor(down, first) == across, 1.0, 0.0).astype(BF16)


def prepare(slots, inputs, w1, w2, wgate_t, wtower, own):
    dim = inputs.shape[1]
    epd, _, hid_n = w1.shape
    out_n = w2.shape[2]
    ke = wgate_t.shape[0]
    doms, _, th = wtower.shape

    def body(ins, outs):
        w1s, wgs, w2s, wts, _ = ins
        _, w1t, w2t, wt = (o.buf for o in outs)
        w1_buf = w1s.get()
        for i in range(epd):
            w1t[i * hid_n : (i + 1) * hid_n, :] = w1_buf[i].T
        w1t[epd * hid_n :, :] = mm(reorder(ke, epd), wgs.get()[...]).astype(BF16)
        w2_buf = w2s.get()
        for i in range(epd):
            w2t[i] = w2_buf[i].T
        wt_buf = wts.get()
        for k in range(doms):
            wt[k] = wt_buf[k].T
    return staged(
        body,
        [Far(a) for a in (w1, wgate_t, w2, wtower)]
        + [Far(inputs, (len(slots) * own, dim), row_blocks(slots, own), into=0)],
        [
            Near(plain((len(slots) * own, dim), BF16)),
            Near(plain((epd * hid_n + ke, dim), BF16)),
            Near(plain((epd, out_n, hid_n), BF16)),
            Near(plain((doms, th, out_n), BF16)),
        ],
        [],
        "prepare",
        12,
    )


def forward(blocks, w1, w2, wt, own, doms, keep, tower_out, name):
    epd, dim, hid_n = w1[1].shape
    out_n = w2[1].shape[2]
    ce = 2 * epd
    half = epd * hid_n
    ke = w1[0].shape[0] - half
    th = wt.shape[1]
    exps = ke // doms
    sizes = [(b.what if isinstance(b, Near) else b).shape[0] // own for b in blocks]
    ns = sum(sizes)

    def body(ins, outs, w1t, w2t, pre, *bufs):
        xs = ins[: len(blocks)]
        w1o, w1s, w2o, w2s, wts = ins[len(blocks) :]
        if keep:
            hid, slope, vals, gate, mixed = (o.buf for o in outs[:5])
        else:
            hid, vals, gate, mixed = bufs
        wt = wts.get()
        for i in range(epd):
            w1t[i * hid_n : (i + 1) * hid_n, :] = w1s.get()[i].T
            w2t[i] = w2s.get()[i].T
        parts = [(src, n) for src, size in zip(xs, sizes) for n in range(size)]
        for n, (src, place) in enumerate(parts):
            x = src.get()[place * own : (place + 1) * own, :]
            got = mm_t(w1o.get()[...], x)
            pre[:half, :] = got[:half]
            pre[ce * hid_n :, :] = got[half:]
            pre[half : ce * hid_n, :] = mm_t(w1t[...], x)
            logits = pre[ce * hid_n : ce * hid_n + ke, :].reshape(doms, exps, own)
            top = jnp.exp(logits - jnp.max(logits, axis=1, keepdims=True))
            soft = top / jnp.sum(top, axis=1, keepdims=True)
            gate[n] = soft.reshape(ke, own)

            def act(i, carry):
                at = pl.ds(pl.multiple_of(i * 16, 16), 16)
                v = pre[at, :]
                s = sigmoid(v)
                h = v * s
                hid[n, at, :] = h.astype(BF16)
                if keep:
                    slope[n, at, :] = (s + h * (1.0 - s)).astype(BF16)
                return carry

            lax.fori_loop(0, ce * hid_n // 16, act, 0, unroll=4 if keep else ce * hid_n // 16)
            for e in range(ce):
                w = w2o.get()[e] if e < epd else w2t[e - epd]
                vals[n, e * out_n : (e + 1) * out_n, :] = mm(w, hid[n, e * hid_n : (e + 1) * hid_n, :]).astype(BF16)
            if keep:
                for o in outs[:4]:
                    o.flush(n)
            for u in range(own // LANE):
                part = slice(u * LANE, (u + 1) * LANE)
                rows = [[gate[n, k * exps + e : k * exps + e + 1, part] for e in range(ce)] for k in range(doms)]

                def mix(i, carry):
                    acc = [None] * doms
                    for e in range(ce):
                        at = pl.ds(pl.multiple_of(e * out_n + i * 32, 32), 32)
                        v = vals[n, at, part].astype(F32)
                        for k in range(doms):
                            term = rows[k][e] * v
                            acc[k] = term if e == 0 else acc[k] + term
                    for k in range(doms):
                        at = pl.ds(pl.multiple_of(k * out_n + i * 32, 32), 32)
                        mixed[n, at, part] = acc[k].astype(BF16)
                    return carry

                lax.fori_loop(0, out_n // 32, mix, 0, unroll=4 if keep else out_n // 32)
            if keep:
                outs[4].flush(n)
            if n == 0 or not keep:
                tower = outs[-1]
                for k in range(doms):
                    sums = mm(wt[k], mixed[n, k * out_n : (k + 1) * out_n, :])
                    tower.buf[n, k * th : (k + 1) * th, :] = sums if keep else encode(sums)
                tower.flush(n)

    kept = [
        plain((ns, ce * hid_n, own), BF16),
        plain((ns, ce * hid_n, own), BF16),
        plain((ns, ce * out_n, own), BF16),
        plain((ns, ke, own), F32),
        plain((ns, doms * out_n, own), BF16),
    ]
    outs = list(kept) if keep else []
    outs.append(Near(plain((1 if keep else ns, doms * th, own), tower_out)))
    scratch = [
        pltpu.VMEM((half, dim), BF16),
        pltpu.VMEM((epd, out_n, hid_n), BF16),
        pltpu.VMEM((ce * hid_n + ke, own), F32),
    ]
    if not keep:
        scratch += [pltpu.VMEM(kept[i].shape, kept[i].dtype) for i in (0, 2, 3, 4)]
    ins = blocks + [Near(a) for a in (w1[0], w1[1], w2[0], w2[1], wt)]
    return staged(body, ins, outs, scratch, name, 40)


def combine(own_part, received, marks, devices):
    _, rows, own = own_part.shape
    doms = rows // LANE

    def body(ins, outs, cols):
        part = ins[0].get()
        got = [s.get() for s in ins[2:]]
        tower, low, message = (o.buf for o in outs)
        cols[...] = jnp.zeros_like(cols)
        for k in range(doms):
            at = slice(k * LANE, (k + 1) * LANE)
            total = part[0, at, :]
            for ref in got:
                total = total + decode(ref[0, at, :], base(ref[0, at, :LANE]))
            tower[at, :] = total
            low[at, :] = encode(total)
            mean = jnp.sum(total, axis=1, keepdims=True) * (1.0 / own)
            dev = total - mean
            cols[:, k : k + 1] = mean
            cols[:, doms + k : doms + k + 1] = jnp.sum(dev * dev, axis=1, keepdims=True)
        outs[0].flush()
        pair = jnp.concatenate([ins[1].get()[...].astype(F32), jnp.zeros((14, own), F32)], axis=0)
        low[rows:, :] = pair.astype(BF16)
        outs[1].flush()
        tile = cols[...].T[:8, :]
        for d in range(devices):
            message[d * 8 : (d + 1) * 8, :] = tile
        outs[2].flush()

    return staged(
        body,
        [Near(own_part), Near(marks)] + [Near(v) for v in received],
        [Near(plain((rows, own), F32)), Near(plain((rows + 16, own), BF16)), Near(plain((devices * 8, LANE), F32))],
        [pltpu.VMEM((LANE, LANE), F32)],
        "combine",
        16,
    )


def pick(dom, values):
    got = values[-1]
    for k in range(len(values) - 2, -1, -1):
        got = jnp.where(dom == k, values[k], got)
    return got


def chosen_tower(values, dom, wide, doms):
    mean, gain, shift, head = (pick(dom, [wide[j * doms + k] for k in range(doms)]) for j in range(4))
    centred = pick(dom, values) - mean
    return centred, centred * gain + shift, gain, head


def spread_columns(wide, rows_ref, n):
    cols = rows_ref[...].T
    for j in range(n):
        wide[j] = jnp.broadcast_to(cols[:, j : j + 1], (LANE, LANE))


def normalise(stats, tower, marks, scale, shift, head, devices, count):
    rows, own = tower.shape
    doms = rows // LANE

    def body(ins, outs, prm, wide, q):
        st, tws, mks, sc, sh, hd = ins
        params, message = (o.buf for o in outs)
        prm[...] = jnp.zeros_like(prm)
        got = st.get()[...].reshape(devices, 8, LANE)
        total = jnp.sum(got, axis=0)
        mean = total * (1.0 / devices)
        dev = got - mean[None]
        spread = jnp.sum(dev * dev, axis=0) * float(own)
        var = (total[doms : 2 * doms] + spread[:doms]) * (1.0 / count)
        inv = lax.rsqrt(var + EPS)
        prm[0:doms, :] = mean[:doms]
        prm[doms : 2 * doms, :] = inv * sc.get()[...]
        prm[2 * doms : 3 * doms, :] = sh.get()[...]
        prm[3 * doms : 4 * doms, :] = hd.get()[...]
        prm[4 * doms : 5 * doms, :] = inv
        params[:16, :] = prm[:16, :]
        spread_columns(wide, prm, 4 * doms)
        tw, mk = tws.get(), mks.get()
        loss = jnp.zeros((1, LANE), F32)
        for u in range(own // LANE):
            part = slice(u * LANE, (u + 1) * LANE)
            dom = mk[0:1, part]
            target = mk[1:2, part].astype(F32)
            values = [tw[k * LANE : (k + 1) * LANE, part] for k in range(doms)]
            centred, affine, _, head_w = chosen_tower(values, dom, wide, doms)
            s = sigmoid(affine)
            act = affine * s
            chosen = jnp.sum(act * head_w, axis=0, keepdims=True)
            soft = jnp.maximum(chosen, 0.0) + jnp.log(1.0 + jnp.exp(-jnp.abs(chosen)))
            loss = loss + (soft - target * chosen)
            score_grad = (sigmoid(chosen) - target) * (1.0 / count)
            grad = score_grad * head_w * (s + act * (1.0 - s))
            q[0:LANE, part] = grad
            q[LANE : 2 * LANE, part] = grad * centred
            q[2 * LANE :, part] = score_grad * act
        kinds = lax.broadcasted_iota(jnp.int32, (8, own), 0)
        one_hot = (kinds == mk[0:1, :]).astype(F32).astype(BF16)
        high = q[...].astype(BF16)
        sums = (mm_t(one_hot, high) + mm_t(one_hot, (q[...] - high.astype(F32)).astype(BF16)))[:doms]
        tile = [sums[:, :LANE], sums[:, LANE : 2 * LANE] * inv]
        all_rows = tile + [loss, jnp.zeros((1, LANE), F32)]
        all_rows = jnp.concatenate(all_rows, axis=0)
        for d in range(devices):
            message[d * 8 : (d + 1) * 8, :] = all_rows
        params[16:, :] = jnp.concatenate([sums[:, 2 * LANE :], jnp.zeros((8 - doms, LANE), F32)], axis=0)
        outs[0].flush()

    return staged(
        body,
        [Near(v) for v in (stats, tower, marks, scale, shift, head)],
        [Near(plain((24, LANE), F32)), Near(plain((devices * 8, LANE), F32))],
        [
            pltpu.VMEM((LANE, LANE), F32),
            pltpu.VMEM((4 * doms, LANE, LANE), F32),
            pltpu.VMEM((3 * LANE, own), F32),
        ],
        "normalise",
        16,
    )


def layout(epd, hid_n, out_n, dim, doms, rows_n):
    second = epd * hid_n * out_n // LANE
    first = epd * hid_n * dim // LANE
    towers = -(-(doms * out_n + (dim // LANE) * 32) // (2 * 16 * rows_n)) * 16
    return second // rows_n, first // rows_n, towers


def pieces(kind, epd, hid_n, out_n, dim):
    flat = 0
    for i in range(epd):
        for q in range((out_n, dim)[kind] // LANE):
            yield i, q, flat
            flat += hid_n


def spots(kind, row, rows_n):
    got = []
    for j in range(rows_n):
        p = lax.bitwise_xor(row, j)
        got.append(p if kind == 0 else (p & 1) * (rows_n // 2) + lax.shift_right_logical(p, 1))
    return got


def backward(
    sums, params, tower, low_towers, marks, acts, inputs, w1, w2, wgate_t, wtower, devices, rows_n, count
):
    ns = 1 + len(low_towers)
    t_rows, own = tower.shape
    total_n = ns * own
    dim = inputs.shape[1]
    epd, hid_n, out_n = w2[0].shape
    ce = 2 * epd
    ke = wgate_t.shape[0]
    doms, _, th = wtower.shape
    exps = ke // doms
    m_sec, m_first, m_tow = layout(epd, hid_n, out_n, dim, doms, rows_n)

    def body(ins, outs, wide, prm, tg, mg, eg, gg, srow, tgf, facc):
        sm, pr, tw0, mk0 = ins[:4]
        low = ins[4 : 3 + ns]
        wts, gate, vals, w2o, w2s, slope, xs, hid, mixed, _ = ins[3 + ns :]
        shift_out, scale_out, loss_out, sec_sib, first_sib, sec_mine, first_mine, tow_sib, tow_mine, pgs, lgs, _ = outs
        pg, lg = pgs.buf, lgs.buf
        c = lax.rem(lax.axis_index(WIDTH), 2)
        r = lax.axis_index(ROWS)
        at_row = [spots(kind, r, rows_n) for kind in range(2)]
        prm[...] = jnp.zeros_like(prm)
        total = jnp.sum(sm.get()[...].reshape(devices, 8, LANE), axis=0)
        shift_out.buf[...] = total[:doms]
        scale_out.buf[...] = total[doms : 2 * doms]
        loss_out.buf[...] = jnp.sum(total[2 * doms : 2 * doms + 1, :], axis=1, keepdims=True) * (1.0 / count)
        for target in (shift_out, scale_out, loss_out):
            target.flush()
        given = pr.get()[...]
        gain, inv = given[doms : 2 * doms], given[4 * doms : 5 * doms]
        prm[0:16, :] = given[:16]
        prm[4 * doms : 5 * doms, :] = gain * total[:doms] * (1.0 / count)
        prm[5 * doms : 6 * doms, :] = gain * inv * total[doms : 2 * doms] * (1.0 / count)
        spread_columns(wide, prm, 6 * doms)
        for u in range(total_n // LANE):
            n = u * LANE // own
            part = slice(u * LANE, (u + 1) * LANE)
            here = slice(u * LANE - n * own, (u + 1) * LANE - n * own)
            if n == 0:
                tw = tw0.get()
                dom = mk0.get()[0:1, here]
                target = mk0.get()[1:2, here].astype(F32)
            else:
                tw = low[n - 1].get()
                pair = tw[t_rows : t_rows + 16, here].astype(F32)
                dom = pair[0:1].astype(jnp.int32)
                target = pair[1:2]
            values = [tw[k * LANE : (k + 1) * LANE, here] for k in range(doms)]
            if n:
                if here.start == 0:
                    added = [jnp.broadcast_to(base(v), (LANE, LANE)) for v in values]
                values = [decode(v, a, here.start) for v, a in zip(values, added)]
            _, affine, gain_s, head_w = chosen_tower(values, dom, wide, doms)
            s = sigmoid(affine)
            act = affine * s
            chosen = jnp.sum(act * head_w, axis=0, keepdims=True)
            score_grad = (sigmoid(chosen) - target) * (1.0 / count)
            grad = gain_s * (score_grad * head_w * (s + act * (1.0 - s)))
            for k in range(doms):
                v = jnp.where(dom == k, grad, 0.0) - wide[4 * doms + k]
                v = v - (values[k] - wide[k]) * wide[5 * doms + k]
                down = v.astype(BF16)
                tg[k * th : (k + 1) * th, part] = down
                srow[k : k + 1, part] = jnp.sum(down.astype(F32) * values[k], axis=0, keepdims=True)
        wt = wts.get()
        for k in range(doms):
            mg[k * out_n : (k + 1) * out_n, :] = mm(wt[k], tg[k * th : (k + 1) * th, :])
        vals, gate = vals.get(), gate.get()
        gg[...] = jnp.zeros_like(gg)

        def tower_part(k):
            tgf[k * out_n : (k + 1) * out_n, :] = mm_t(
                mixed.get()[k * out_n : (k + 1) * out_n, :], tg[k * th : (k + 1) * th, :]
            )

        def hidden_part(n, e):
            at = slice(e * hid_n, (e + 1) * hid_n)
            part = slice(n * own, (n + 1) * own)
            w = (w2o, w2s)[e // epd].get()[e % epd]
            grad = mm(w, eg[e * out_n : (e + 1) * out_n, part])
            pg[at, part] = (grad * slope.get()[at, part].astype(F32)).astype(BF16)

        ready = []
        for u in range(total_n // LANE):
            part = slice(u * LANE, (u + 1) * LANE)
            rows = [[gate[k * exps + e : k * exps + e + 1, part] for e in range(ce)] for k in range(doms)]

            def spread(i, acc):
                up = [mg[pl.ds(pl.multiple_of(k * out_n + i * 16, 16), 16), part] for k in range(doms)]
                acc = list(acc)
                for e in range(ce):
                    at = pl.ds(pl.multiple_of(e * out_n + i * 16, 16), 16)
                    v = vals[at, part].astype(F32)
                    back = None
                    for k in range(doms):
                        term = rows[k][e] * up[k]
                        back = term if k == 0 else back + term
                        prod = up[k] * v
                        acc[k * ce + e] = acc[k * ce + e] + (prod[:8] + prod[8:])
                    eg[at, part] = back.astype(BF16)
                return tuple(acc)

            zero = jnp.zeros((8, LANE), F32)
            acc = lax.fori_loop(0, out_n // 16, spread, (zero,) * (doms * ce), unroll=out_n // 16)
            for k in range(doms):
                for e in range(ce):
                    gg[k * exps + e : k * exps + e + 1, part] = jnp.sum(acc[k * ce + e], axis=0, keepdims=True)
            if (u + 1) * LANE % own == 0:
                ready += [(hidden_part, (u * LANE // own, e)) for e in range(ce)]
            if ready:
                task, args = ready.pop(0)
                task(*args)
        for task, args in ready:
            task(*args)
        pgs.flush()
        here = lax.broadcasted_iota(jnp.int32, (exps, total_n), 0) < ce
        for k in range(doms):
            at = slice(k * exps, (k + 1) * exps)
            gg[at, :] = jnp.where(here, gate[at, :] * (gg[at, :] - srow[k : k + 1, :]), 0.0)
        lg[...] = mm(reorder(ke, epd), gg[...].astype(BF16)).astype(BF16)
        lgs.flush()
        hid = hid.get()

        def put(kind, slot, values):
            target = ((sec_sib, first_sib), (sec_mine, first_mine))[slot < epd][kind]
            size = (m_sec, m_first)[kind]
            step = math.gcd(size, hid_n)
            for i, q, flat in pieces(kind, epd, hid_n, out_n, dim):
                if i == slot % epd:
                    for off in range(0, hid_n, step):
                        j, o = divmod(flat + off, size)
                        part = values[off : off + step, q * LANE : (q + 1) * LANE]
                        target.buf[at_row[kind][j], o : o + step, :] = part.astype(target.buf.dtype)

        x = xs.get()
        facc[...] = mm(pg[...], x[...])
        for e in range(ce):
            put(1, e, facc[e * hid_n : (e + 1) * hid_n, :])
        for e in range(ce):
            at = slice(e * hid_n, (e + 1) * hid_n)
            at_o = slice(e * out_n, (e + 1) * out_n)
            put(0, e, mm_t(hid[at, :], eg[at_o, :]))
        for target in (sec_sib, first_sib, sec_mine, first_mine):
            target.flush()
        for k in range(doms):
            tower_part(k)
        tgf[doms * out_n :, :] = jnp.zeros((tgf.shape[0] - doms * out_n, LANE), F32)
        part_g = mm(lg[...], x[...])
        for q in range(dim // LANE):
            tgf[doms * out_n + q * 32 : doms * out_n + q * 32 + ke, :] = part_g[:, q * LANE : (q + 1) * LANE]
        tgf[doms * out_n + ke : doms * out_n + 32, :] = given[16 : 48 - ke]
        for target, core in ((tow_sib, 1 - c), (tow_mine, c)):
            for j in range(rows_n):
                start = pl.multiple_of((core * rows_n + j) * m_tow, 8)
                target.buf[at_row[1][j], :, :] = tgf[pl.ds(start, m_tow), :].astype(target.buf.dtype)
            target.flush()

    outs = [
        plain((doms, LANE), F32),
        plain((doms, LANE), F32),
        plain((1, 1), F32),
        Near(plain((rows_n, m_sec, LANE), BF16)),
        Near(plain((rows_n, m_first, LANE), BF16)),
        Near(plain((rows_n, m_sec, LANE), F32)),
        Near(plain((rows_n, m_first, LANE), F32)),
        Near(plain((rows_n, m_tow, LANE), BF16)),
        Near(plain((rows_n, m_tow, LANE), F32)),
        Near(plain((ce * hid_n, total_n), BF16)),
        Near(plain((ke, total_n), BF16)),
        Near(plain((dim, ce * hid_n), BF16)),
    ]
    scratch = [
        pltpu.VMEM((6 * doms, LANE, LANE), F32),
        pltpu.VMEM((LANE, LANE), F32),
        pltpu.VMEM((doms * th, total_n), BF16),
        pltpu.VMEM((doms * out_n, total_n), F32),
        pltpu.VMEM((ce * out_n, total_n), BF16),
        pltpu.VMEM((ke, total_n), F32),
        pltpu.VMEM((8, total_n), F32),
        pltpu.VMEM((2 * rows_n * m_tow, LANE), F32),
        pltpu.VMEM((ce * hid_n, dim), F32),
    ]

    def side_by_side(which):
        def pairs(refs, buf):
            return [(r.at[n], buf.at[:, i * own : (i + 1) * own]) for i, (r, (_, n)) in enumerate(zip(refs, acts))]

        arrays = [a[which] for a, _ in acts]
        return Far(arrays, (arrays[0].shape[1], total_n), pairs)

    ins = [Near(sums), Near(params), Near(tower), Near(marks)]
    ins += [Near(v) for v in low_towers]
    ins += [Far(wtower), side_by_side(3), side_by_side(2), Far(w2[0]), Far(w2[1], moved=True), side_by_side(1)]
    ins += [Far(inputs, (total_n, dim), row_blocks(list(range(ns)), own)), side_by_side(0), side_by_side(4)]

    def joined(refs, buf):
        slots = [(refs[e // epd].at[e % epd], e) for e in range(ce)]
        return [(ref, buf.at[:, e * hid_n : (e + 1) * hid_n]) for ref, e in slots]

    ins.append(Far(w1, pairs=joined, moved=[False, True], into=len(outs) - 1))
    return staged(body, ins, outs, scratch, "backward", 44)


def backward_inputs(pg, lg, w1, wgate_t, own):
    total_n = pg.shape[1]
    ns = total_n // own
    dim = w1.shape[0]
    ke = wgate_t.shape[0]

    def body(ins, outs):
        w1c, wgs, pgs, lgs = ins
        wg = jnp.concatenate([wgs.get()[...], jnp.zeros((LANE - ke, dim), BF16)], axis=0).T[:, :ke]
        pg, lg, w1c = pgs.get(), lgs.get(), w1c.get()
        for n in range(ns - 1, -1, -1):
            part = slice(n * own, (n + 1) * own)
            gi = mm(w1c[...], pg[:, part]) + mm(wg, lg[:, part])
            if n:
                outs[1].buf[n - 1] = gi.astype(BF16)
                outs[1].flush(n - 1)
            else:
                outs[0].buf[...] = gi
                outs[0].flush()

    return staged(
        body,
        [Near(w1), Near(wgate_t), Near(pg), Near(lg)],
        [Near(plain((dim, own), F32)), Near(plain((max(ns - 1, 1), dim, own), BF16))],
        [],
        "backward_inputs",
        16,
    )


def finish_inputs(own_part, received):
    dim, own = own_part.shape

    def body(ins, outs):
        for u in range(own // LANE):
            lanes = slice(u * LANE, (u + 1) * LANE)
            part = total(*(src.buf[:, lanes] for src in ins))
            outs[0].buf[lanes, :] = part.T
            outs[0].flush(pl.ds(u * LANE, LANE))

    return staged(
        body, [Near(own_part)] + [Near(v) for v in received], [plain((own, dim), F32)], [], "finish_inputs", 12
    )[0]


def finish_weights(second, first, other, epd, hid_n, out_n, dim, doms, exps, rows_n):
    m_sec, m_first, m_tow = layout(epd, hid_n, out_n, dim, doms, rows_n)
    ke = doms * exps

    def body(ins, outs, buf, tgf):
        out_f, out_s, out_t, out_g, out_h = (o.buf for o in outs)
        c = lax.rem(lax.axis_index(WIDTH), 2)
        r = lax.axis_index(ROWS)
        at_row = [spots(kind, r, rows_n) for kind in range(2)]
        for kind, size in ((0, m_sec), (1, m_first)):
            got = ins[kind].get()
            step = math.gcd(size, hid_n)
            for i, q, flat in pieces(kind, epd, hid_n, out_n, dim):
                for off in range(0, hid_n, step):
                    j, o = divmod(flat + off, size)
                    piece = got[at_row[kind][j], o : o + step, :].astype(F32)
                    if kind == 0:
                        out_s[i, off : off + step, q * LANE : (q + 1) * LANE] = piece
                    else:
                        buf[off : off + step, :] = piece
                if kind == 1:
                    out_f[i, q * LANE : (q + 1) * LANE, :] = buf[...].T
                if q == (out_n, dim)[kind] // LANE - 1:
                    outs[1 - kind].flush(i)
        near, sib = ins[1].get(), ins[2].get()
        for j in range(rows_n):
            at = at_row[1][j]
            for core, value in ((c, near[at, m_first:, :]), (1 - c, sib[at])):
                start = pl.multiple_of((core * rows_n + j) * m_tow, 8)
                tgf[pl.ds(start, m_tow), :] = value.astype(F32)
        for k in range(doms):
            out_t[k] = tgf[k * out_n : (k + 1) * out_n, :]
        outs[2].flush()
        for q in range(dim // LANE):
            at = doms * out_n + q * 32
            out_g[:, q * LANE : (q + 1) * LANE] = tgf[at : at + ke, :]
        outs[3].flush()
        out_h[...] = tgf[doms * out_n + ke : doms * out_n + ke + doms, :]
        outs[4].flush()

    return staged(
        body,
        [Near(second), Near(first), Near(other)],
        [
            plain((epd, dim, hid_n), F32),
            plain((epd, hid_n, out_n), F32),
            plain((doms, out_n, LANE), F32),
            plain((ke, dim), F32),
            plain((doms, LANE), F32),
        ],
        [pltpu.VMEM((hid_n, LANE), F32), pltpu.VMEM((2 * rows_n * m_tow, LANE), F32)],
        "finish_weights",
        16,
    )


def swap(value, axis, mask):
    size = lax.axis_size(axis)
    return lax.ppermute(value, axis, [(i, i ^ mask) for i in range(size)])


def total(*values):
    got = values[0].astype(F32)
    for value in values[1:]:
        got = got + value.astype(F32)
    return got


def send(value, axis, mask):
    return swap(value.astype(BF16), axis, mask)


together = lax.optimization_barrier


def reduce_rows(second, first, towers, beside):
    n_rows, n_width = lax.axis_size(ROWS), lax.axis_size(WIDTH)
    half = n_rows // 2
    far = [2 * q for q in range(1, half)]
    low = total(*(v[half:] for v in first)).astype(BF16)
    high = [total(*(v[m : m + 2] for v in second)).astype(BF16) for m in far]
    across = total(*towers).astype(BF16)
    first_got = swap(low, ROWS, 1)
    second_got = [swap(v, ROWS, m) for v, m in zip(high, far)]
    towers = total(*towers, *(swap(across, WIDTH, mask) for mask in range(2, n_width, 2)))
    tower_low, operand = together((towers[half:].astype(BF16), beside[1]))
    tower_got = swap(tower_low, ROWS, 1)
    inputs_part = tuple(beside[0](operand))
    first_got, second_got, tower_got, inputs_part = together((first_got, second_got, tower_got, inputs_part))

    def piece(q):
        return jnp.concatenate(
            [total(*(v[q] for v in first), first_got[q]), total(towers[q], tower_got[q])], axis=0
        )

    pair = total(*(v[:2] for v in second), *second_got)
    high = [piece(q).astype(BF16) for q in range(1, half)]
    high, low = together((high, pair.astype(BF16)))
    moved = [swap(v, ROWS, m) for v, m in zip(high, far)]
    moved, low = together((moved, swap(low, ROWS, 1)))
    pair = total(pair, low[::-1])
    return pair.astype(BF16), total(piece(0), *moved).astype(BF16), inputs_part


def gather_rows(pair, first, m_first, beside):
    half = lax.axis_size(ROWS) // 2
    far = [2 * q for q in range(1, half)]
    pair, first = together((pair, first))
    high, beside = together(([swap(first, ROWS, m) for m in far], beside))
    pair, evens = together((pair, jnp.stack([first] + high)))
    low, high = swap(evens, ROWS, 1), [swap(pair, ROWS, m) for m in far]
    low, high, beside = together((low, high, finish_inputs(*beside)))
    second, first = jnp.concatenate([pair] + high), jnp.concatenate([evens, low])
    return second, first, swap(first[:, m_first:], WIDTH, 1), beside


def local(inputs, w_first, w_second, w_gate, w_tower, norm_scale, norm_shift, w_head, domains, labels):
    n_width, n_rows = lax.axis_size(WIDTH), lax.axis_size(ROWS)
    devices = n_width * n_rows
    own = inputs.shape[0] // n_width
    count = float(own * devices)
    dim = inputs.shape[1]
    epd, _, hid_n = w_first.shape
    out_n = w_second.shape[2]
    doms, _, exps = w_gate.shape
    ke = doms * exps
    n_x = n_width // 2
    others = list(range(1, n_x))
    w1 = (w_first, swap(w_first, WIDTH, 1))
    w2 = (w_second, swap(w_second, WIDTH, 1))
    wgate_t = jnp.transpose(w_gate, (0, 2, 1)).reshape(ke, dim)
    marks = jnp.stack([domains, labels])

    x_far, w1_own, w2_own, wt = prepare(others, inputs, w_first, w_second, wgate_t, w_tower, own)
    w1t, w2t = (w1_own, w1[1]), (w2_own, w2[1])
    far = forward([Near(x_far)], w1t, w2t, wt, own, doms, False, BF16, "forward_send")[0]
    sent = [swap(far[s - 1 : s], WIDTH, 2 * s) for s in others]
    blocks = [Far(inputs, (own, dim), row_blocks([0], own)), Near(x_far)]
    kept = forward(blocks, w1t, w2t, wt, own, doms, True, F32, "forward_keep")
    tower, low, message = combine(kept[5], sent, marks, devices)
    stats = lax.all_to_all(message, BOTH, 0, 0, tiled=True)
    stats, low = together((stats, low))
    lows = [swap(low, WIDTH, 2 * s) for s in others]
    params, message = normalise(stats, tower, marks, norm_scale, norm_shift, w_head, devices, count)
    sums = lax.all_to_all(message, BOTH, 0, 0, tiled=True)

    acts = [(kept[:5], s) for s in range(n_x)]
    grad_shift, grad_scale, loss, sec_sib, first_sib, sec_own, first_own, tow_sib, tow_own, pg, lg, w1_joined = backward(
        sums, params, tower, lows, marks, acts, inputs, w1, w2, wgate_t, w_tower, devices, n_rows, count
    )
    first_sib = swap(first_sib, WIDTH, 1)
    first_sib, sec_sib, tow_sib = together((first_sib, sec_sib, tow_sib))
    second, first, (gi_own, gi_out) = reduce_rows(
        (sec_own, swap(sec_sib, WIDTH, 1)),
        (first_own, first_sib),
        (tow_own, swap(tow_sib, WIDTH, 1)),
        (lambda grad: backward_inputs(grad, lg, w1_joined, wgate_t, own), pg),
    )
    inputs_got = [swap(gi_out[s - 1], WIDTH, 2 * s) for s in others]
    m_first = layout(epd, hid_n, out_n, dim, doms, n_rows)[1]
    second, first, other, grad_inputs = gather_rows(second, first, m_first, (gi_own, inputs_got))
    grad_first, grad_second, grad_tower, grad_gate, grad_head = finish_weights(
        second, first, other, epd, hid_n, out_n, dim, doms, exps, n_rows
    )
    return (
        loss[0, 0],
        grad_inputs,
        grad_first,
        grad_second,
        grad_gate.reshape(doms, exps, dim).transpose(0, 2, 1),
        grad_tower,
        grad_scale,
        grad_shift,
        grad_head,
    )


def solution(mesh):
    placed = (
        P(ROWS, None),
        P(WIDTH, None, None),
        P(WIDTH, None, None),
        P(),
        P(),
        P(),
        P(),
        P(),
        P(BOTH),
        P(BOTH),
    )
    return jax.shard_map(
        local,
        mesh=mesh,
        in_specs=placed,
        out_specs=(
            P(),
            P(BOTH, None),
            P(WIDTH, None, None),
            P(WIDTH, None, None),
            P(),
            P(),
            P(),
            P(),
            P(),
        ),
        check_vma=False,
    )
```

```python
import math

import jax
import jax.numpy as jnp
from jax import lax
from jax.experimental import pallas as pl
from jax.experimental.pallas import tpu as pltpu
from jax.sharding import PartitionSpec as P

F32 = jnp.float32
BF16 = jnp.bfloat16
EPS = 1e-05
LANE = 128
MIB = 1 << 20
ROWS = "rows"
WIDTH = "width"
BOTH = (ROWS, WIDTH)


def mm(a, b):
    return jnp.dot(a, b, preferred_element_type=F32)


def mm_t(a, b):
    return lax.dot_general(a, b, (((1,), (1,)), ((), ())), preferred_element_type=F32)


def sigmoid(v):
    return 0.5 * jnp.tanh(0.5 * v) + 0.5


PLAIN = 8


def base(values):
    first = values[:, :PLAIN].astype(BF16).astype(F32)
    return jnp.sum(first, axis=1, keepdims=True) * (1.0 / PLAIN)


def encode(values):
    lane = lax.broadcasted_iota(jnp.int32, values.shape, 1)
    return jnp.where(lane < PLAIN, values, values - base(values)).astype(BF16)


def decode(values, added, start=0):
    lane = lax.broadcasted_iota(jnp.int32, values.shape, 1)
    values = values.astype(F32)
    return jnp.where(lane < PLAIN - start, values, values + added)


class Source:
    def __init__(self, buf, copies):
        self.buf = buf
        self.waiting = copies
        for copy in copies:
            copy.start()

    def get(self):
        for copy in self.waiting:
            copy.wait()
        self.waiting = []
        return self.buf


class Target:
    def __init__(self, ref, buf, sems):
        self.ref, self.buf, self.sems = ref, buf, sems
        self.waiting = []

    def flush(self, *at):
        if self.ref is None:
            return
        src = self.buf.at[at] if at else self.buf
        dst = self.ref.at[at] if at else self.ref
        copy = pltpu.make_async_copy(src, dst, next(self.sems))
        copy.start()
        self.waiting.append(copy)


class Near:
    def __init__(self, what):
        self.what = what


class Far:
    def __init__(self, arrays, shape=None, pairs=None, moved=False, into=None):
        self.into = into
        self.arrays = arrays if isinstance(arrays, (list, tuple)) else [arrays]
        self.moved = moved if isinstance(moved, list) else [moved] * len(self.arrays)
        self.shape = shape or self.arrays[0].shape
        self.dtype = self.arrays[0].dtype
        self.pairs = pairs or (lambda refs, buf: [(refs[0], buf)])


def staged(body, ins, outs, scratch, name, limit, n_sems=64):
    far_in = [i for i, s in enumerate(ins) if isinstance(s, Far) and s.into is None]
    far_out = [i for i, s in enumerate(outs) if not isinstance(s, Near)]
    args, specs, spans = [], [], []
    hbm = pl.BlockSpec(memory_space=pltpu.HBM)
    vmem = pl.BlockSpec(memory_space=pltpu.VMEM)
    anywhere = pl.BlockSpec(memory_space=pl.ANY)
    for s in ins:
        if isinstance(s, Far):
            spans.append((len(args), len(args) + len(s.arrays)))
            for a, moved in zip(s.arrays, s.moved):
                args.append(a if moved else pltpu.with_memory_space_constraint(a, pltpu.HBM))
                specs.append(anywhere if moved else hbm)
        else:
            spans.append((len(args), len(args) + 1))
            args.append(s.what)
            specs.append(vmem)
    n_in, n_out = len(args), len(outs)

    def kernel(*refs):
        refs_in, refs_out = refs[:n_in], refs[n_in : n_in + n_out]
        bufs = refs[n_in + n_out :]
        in_bufs = dict(zip(far_in, bufs))
        in_bufs.update({i: refs_out[s.into] for i, s in enumerate(ins) if isinstance(s, Far) and s.into is not None})
        out_bufs = dict(zip(far_out, bufs[len(far_in) :]))
        rest = bufs[len(far_in) + len(far_out) : -1]
        sems = iter([bufs[-1].at[i] for i in range(n_sems)])
        sources = []
        for i, (start, stop) in enumerate(spans):
            if i in in_bufs:
                pairs = ins[i].pairs(refs_in[start:stop], in_bufs[i])
                sources.append(Source(in_bufs[i], [pltpu.make_async_copy(a, b, next(sems)) for a, b in pairs]))
            else:
                sources.append(Source(refs_in[start], []))
        targets = []
        for i, ref in enumerate(refs_out):
            targets.append(Target(ref, out_bufs[i], sems) if i in out_bufs else Target(None, ref, sems))
        body(sources, targets, *rest)
        for s in sources:
            s.get()
        for t in targets:
            for copy in t.waiting:
                copy.wait()

    return pl.pallas_call(
        kernel,
        out_shape=[o.what if isinstance(o, Near) else pltpu.HBM(o.shape, o.dtype) for o in outs],
        in_specs=specs,
        out_specs=[hbm if i in far_out else vmem for i in range(n_out)],
        scratch_shapes=[pltpu.VMEM(ins[i].shape, ins[i].dtype) for i in far_in]
        + [pltpu.VMEM(outs[i].shape, outs[i].dtype) for i in far_out]
        + list(scratch)
        + [pltpu.SemaphoreType.DMA((n_sems,))],
        compiler_params=pltpu.CompilerParams(vmem_limit_bytes=limit * MIB),
        name=name,
    )(*args)


def plain(shape, dtype):
    return jax.ShapeDtypeStruct(shape, dtype)


def row_blocks(slots, own):
    def pairs(refs, buf):
        w = lax.axis_index(WIDTH)
        got = []
        for n, s in enumerate(slots):
            start = pl.multiple_of(lax.bitwise_xor(w, 2 * s) * own, own)
            got.append((refs[0].at[pl.ds(start, own), :], buf.at[n * own : (n + 1) * own, :]))
        return got

    return pairs


def reorder(ke, epd):
    first = lax.axis_index(WIDTH) * epd
    down = lax.broadcasted_iota(jnp.int32, (ke, ke), 0)
    across = lax.broadcasted_iota(jnp.int32, (ke, ke), 1)
    return jnp.where(lax.bitwise_xor(down, first) == across, 1.0, 0.0).astype(BF16)


def prepare(slots, inputs, w1, w2, wgate_t, wtower, own):
    dim = inputs.shape[1]
    epd, _, hid_n = w1.shape
    out_n = w2.shape[2]
    ke = wgate_t.shape[0]
    doms, _, th = wtower.shape

    def body(ins, outs):
        w1s, wgs, w2s, wts, _ = ins
        _, w1t, w2t, wt = (o.buf for o in outs)
        w1_buf = w1s.get()
        for i in range(epd):
            w1t[i * hid_n : (i + 1) * hid_n, :] = w1_buf[i].T
        w1t[epd * hid_n :, :] = mm(reorder(ke, epd), wgs.get()[...]).astype(BF16)
        w2_buf = w2s.get()
        for i in range(epd):
            w2t[i] = w2_buf[i].T
        wt_buf = wts.get()
        for k in range(doms):
            wt[k] = wt_buf[k].T
    return staged(
        body,
        [Far(a) for a in (w1, wgate_t, w2, wtower)]
        + [Far(inputs, (len(slots) * own, dim), row_blocks(slots, own), into=0)],
        [
            Near(plain((len(slots) * own, dim), BF16)),
            Near(plain((epd * hid_n + ke, dim), BF16)),
            Near(plain((epd, out_n, hid_n), BF16)),
            Near(plain((doms, th, out_n), BF16)),
        ],
        [],
        "prepare",
        12,
    )


def forward(blocks, w1, w2, wt, own, doms, keep, tower_out, name):
    epd, dim, hid_n = w1[1].shape
    out_n = w2[1].shape[2]
    ce = 2 * epd
    half = epd * hid_n
    ke = w1[0].shape[0] - half
    th = wt.shape[1]
    exps = ke // doms
    sizes = [(b.what if isinstance(b, Near) else b).shape[0] // own for b in blocks]
    ns = sum(sizes)

    def body(ins, outs, w1t, w2t, pre, *bufs):
        xs = ins[: len(blocks)]
        w1o, w1s, w2o, w2s, wts = ins[len(blocks) :]
        if keep:
            hid, slope, vals, gate, mixed = (o.buf for o in outs[:5])
        else:
            hid, vals, gate = bufs
        wt = wts.get()
        for i in range(epd):
            w1t[i * hid_n : (i + 1) * hid_n, :] = w1s.get()[i].T
            w2t[i] = w2s.get()[i].T
        parts = [(src, n) for src, size in zip(xs, sizes) for n in range(size)]
        for n, (src, place) in enumerate(parts):
            x = src.get()[place * own : (place + 1) * own, :]
            got = mm_t(w1o.get()[...], x)
            pre[:half, :] = got[:half]
            pre[ce * hid_n :, :] = got[half:]
            pre[half : ce * hid_n, :] = mm_t(w1t[...], x)
            logits = pre[ce * hid_n : ce * hid_n + ke, :].reshape(doms, exps, own)
            top = jnp.exp(logits - jnp.max(logits, axis=1, keepdims=True))
            soft = top / jnp.sum(top, axis=1, keepdims=True)
            gate[n] = soft.reshape(ke, own)

            def act(i, carry):
                at = pl.ds(pl.multiple_of(i * 16, 16), 16)
                v = pre[at, :]
                s = sigmoid(v)
                h = v * s
                hid[n, at, :] = h.astype(BF16)
                if keep:
                    slope[n, at, :] = (s + h * (1.0 - s)).astype(BF16)
                return carry

            lax.fori_loop(0, ce * hid_n // 16, act, 0, unroll=4 if keep else ce * hid_n // 16)
            for e in range(ce):
                w = w2o.get()[e] if e < epd else w2t[e - epd]
                vals[n, e * out_n : (e + 1) * out_n, :] = mm(w, hid[n, e * hid_n : (e + 1) * hid_n, :]).astype(BF16)
            if not keep:
                tower = outs[-1]
                for k in range(doms):
                    sums = None
                    for e in range(ce):
                        term = mm(wt[k], vals[n, e * out_n : (e + 1) * out_n, :])
                        term = gate[n, k * exps + e : k * exps + e + 1, :] * term
                        sums = term if e == 0 else sums + term
                    tower.buf[n, k * th : (k + 1) * th, :] = encode(sums)
                tower.flush(n)
                continue
            for o in outs[:4]:
                o.flush(n)
            for u in range(own // LANE):
                part = slice(u * LANE, (u + 1) * LANE)
                rows = [[gate[n, k * exps + e : k * exps + e + 1, part] for e in range(ce)] for k in range(doms)]

                def mix(i, carry):
                    acc = [None] * doms
                    for e in range(ce):
                        at = pl.ds(pl.multiple_of(e * out_n + i * 32, 32), 32)
                        v = vals[n, at, part].astype(F32)
                        for k in range(doms):
                            term = rows[k][e] * v
                            acc[k] = term if e == 0 else acc[k] + term
                    for k in range(doms):
                        at = pl.ds(pl.multiple_of(k * out_n + i * 32, 32), 32)
                        mixed[n, at, part] = acc[k].astype(BF16)
                    return carry

                lax.fori_loop(0, out_n // 32, mix, 0, unroll=4)
            outs[4].flush(n)
            if n == 0:
                tower = outs[-1]
                for k in range(doms):
                    tower.buf[n, k * th : (k + 1) * th, :] = mm(wt[k], mixed[n, k * out_n : (k + 1) * out_n, :])
                tower.flush(n)

    kept = [
        plain((ns, ce * hid_n, own), BF16),
        plain((ns, ce * hid_n, own), BF16),
        plain((ns, ce * out_n, own), BF16),
        plain((ns, ke, own), F32),
        plain((ns, doms * out_n, own), BF16),
    ]
    outs = list(kept) if keep else []
    outs.append(Near(plain((1 if keep else ns, doms * th, own), tower_out)))
    scratch = [
        pltpu.VMEM((half, dim), BF16),
        pltpu.VMEM((epd, out_n, hid_n), BF16),
        pltpu.VMEM((ce * hid_n + ke, own), F32),
    ]
    if not keep:
        scratch += [pltpu.VMEM(kept[i].shape, kept[i].dtype) for i in (0, 2, 3)]
    ins = blocks + [Near(a) for a in (w1[0], w1[1], w2[0], w2[1], wt)]
    return staged(body, ins, outs, scratch, name, 40)


def combine(own_part, received, marks, devices):
    _, rows, own = own_part.shape
    doms = rows // LANE

    def body(ins, outs, cols):
        part = ins[0].get()
        got = [s.get() for s in ins[2:]]
        tower, low, message = (o.buf for o in outs)
        cols[...] = jnp.zeros_like(cols)
        for k in range(doms):
            at = slice(k * LANE, (k + 1) * LANE)
            total = part[0, at, :]
            for ref in got:
                total = total + decode(ref[0, at, :], base(ref[0, at, :LANE]))
            tower[at, :] = total
            low[at, :] = encode(total)
            mean = jnp.sum(total, axis=1, keepdims=True) * (1.0 / own)
            dev = total - mean
            cols[:, k : k + 1] = mean
            cols[:, doms + k : doms + k + 1] = jnp.sum(dev * dev, axis=1, keepdims=True)
        outs[0].flush()
        pair = jnp.concatenate([ins[1].get()[...].astype(F32), jnp.zeros((14, own), F32)], axis=0)
        low[rows:, :] = pair.astype(BF16)
        outs[1].flush()
        tile = cols[...].T[:8, :]
        for d in range(devices):
            message[d * 8 : (d + 1) * 8, :] = tile
        outs[2].flush()

    return staged(
        body,
        [Near(own_part), Near(marks)] + [Near(v) for v in received],
        [Near(plain((rows, own), F32)), Near(plain((rows + 16, own), BF16)), Near(plain((devices * 8, LANE), F32))],
        [pltpu.VMEM((LANE, LANE), F32)],
        "combine",
        16,
    )


def pick(dom, values):
    got = values[-1]
    for k in range(len(values) - 2, -1, -1):
        got = jnp.where(dom == k, values[k], got)
    return got


def chosen_tower(values, dom, wide, doms):
    mean, gain, shift, head = (pick(dom, [wide[j * doms + k] for k in range(doms)]) for j in range(4))
    centred = pick(dom, values) - mean
    return centred, centred * gain + shift, gain, head


def spread_columns(wide, rows_ref, n):
    cols = rows_ref[...].T
    for j in range(n):
        wide[j] = jnp.broadcast_to(cols[:, j : j + 1], (LANE, LANE))


def normalise(stats, tower, marks, scale, shift, head, devices, count):
    rows, own = tower.shape
    doms = rows // LANE

    def body(ins, outs, prm, wide, q):
        st, tws, mks, sc, sh, hd = ins
        params, message = (o.buf for o in outs)
        prm[...] = jnp.zeros_like(prm)
        got = st.get()[...].reshape(devices, 8, LANE)
        total = jnp.sum(got, axis=0)
        mean = total * (1.0 / devices)
        dev = got - mean[None]
        spread = jnp.sum(dev * dev, axis=0) * float(own)
        var = (total[doms : 2 * doms] + spread[:doms]) * (1.0 / count)
        inv = lax.rsqrt(var + EPS)
        prm[0:doms, :] = mean[:doms]
        prm[doms : 2 * doms, :] = inv * sc.get()[...]
        prm[2 * doms : 3 * doms, :] = sh.get()[...]
        prm[3 * doms : 4 * doms, :] = hd.get()[...]
        prm[4 * doms : 5 * doms, :] = inv
        params[:16, :] = prm[:16, :]
        spread_columns(wide, prm, 4 * doms)
        tw, mk = tws.get(), mks.get()
        loss = jnp.zeros((1, LANE), F32)
        for u in range(own // LANE):
            part = slice(u * LANE, (u + 1) * LANE)
            dom = mk[0:1, part]
            target = mk[1:2, part].astype(F32)
            values = [tw[k * LANE : (k + 1) * LANE, part] for k in range(doms)]
            centred, affine, _, head_w = chosen_tower(values, dom, wide, doms)
            s = sigmoid(affine)
            act = affine * s
            chosen = jnp.sum(act * head_w, axis=0, keepdims=True)
            soft = jnp.maximum(chosen, 0.0) + jnp.log(1.0 + jnp.exp(-jnp.abs(chosen)))
            loss = loss + (soft - target * chosen)
            score_grad = (sigmoid(chosen) - target) * (1.0 / count)
            grad = score_grad * head_w * (s + act * (1.0 - s))
            q[0:LANE, part] = grad
            q[LANE : 2 * LANE, part] = grad * centred
            q[2 * LANE :, part] = score_grad * act
        kinds = lax.broadcasted_iota(jnp.int32, (8, own), 0)
        one_hot = (kinds == mk[0:1, :]).astype(F32).astype(BF16)
        high = q[...].astype(BF16)
        sums = (mm_t(one_hot, high) + mm_t(one_hot, (q[...] - high.astype(F32)).astype(BF16)))[:doms]
        tile = [sums[:, :LANE], sums[:, LANE : 2 * LANE] * inv]
        all_rows = tile + [loss, jnp.zeros((1, LANE), F32)]
        all_rows = jnp.concatenate(all_rows, axis=0)
        for d in range(devices):
            message[d * 8 : (d + 1) * 8, :] = all_rows
        params[16:, :] = jnp.concatenate([sums[:, 2 * LANE :], jnp.zeros((8 - doms, LANE), F32)], axis=0)
        outs[0].flush()

    return staged(
        body,
        [Near(v) for v in (stats, tower, marks, scale, shift, head)],
        [Near(plain((24, LANE), F32)), Near(plain((devices * 8, LANE), F32))],
        [
            pltpu.VMEM((LANE, LANE), F32),
            pltpu.VMEM((4 * doms, LANE, LANE), F32),
            pltpu.VMEM((3 * LANE, own), F32),
        ],
        "normalise",
        16,
    )


def layout(epd, hid_n, out_n, dim, doms, rows_n):
    second = epd * hid_n * out_n // LANE
    first = epd * hid_n * dim // LANE
    towers = -(-(doms * out_n + (dim // LANE) * 32) // (2 * 16 * rows_n)) * 16
    return second // rows_n, first // rows_n, towers


def pieces(kind, epd, hid_n, out_n, dim):
    flat = 0
    for i in range(epd):
        for q in range((out_n, dim)[kind] // LANE):
            yield i, q, flat
            flat += hid_n


def spots(kind, row, rows_n):
    got = []
    for j in range(rows_n):
        p = lax.bitwise_xor(row, j)
        got.append(p if kind == 0 else (p & 1) * (rows_n // 2) + lax.shift_right_logical(p, 1))
    return got


def backward(
    sums, params, tower, low_towers, marks, acts, inputs, w1, w2, wgate_t, wtower, devices, rows_n, count
):
    ns = 1 + len(low_towers)
    t_rows, own = tower.shape
    total_n = ns * own
    dim = inputs.shape[1]
    epd, hid_n, out_n = w2[0].shape
    ce = 2 * epd
    ke = wgate_t.shape[0]
    doms, _, th = wtower.shape
    exps = ke // doms
    m_sec, m_first, m_tow = layout(epd, hid_n, out_n, dim, doms, rows_n)

    def body(ins, outs, wide, prm, tg, mg, eg, gg, srow, tgf, facc):
        sm, pr, tw0, mk0 = ins[:4]
        low = ins[4 : 3 + ns]
        wts, gate, vals, w2o, w2s, slope, xs, hid, mixed, _ = ins[3 + ns :]
        shift_out, scale_out, loss_out, sec_sib, first_sib, sec_mine, first_mine, tow_sib, tow_mine, pgs, lgs, _ = outs
        pg, lg = pgs.buf, lgs.buf
        c = lax.rem(lax.axis_index(WIDTH), 2)
        r = lax.axis_index(ROWS)
        at_row = [spots(kind, r, rows_n) for kind in range(2)]
        prm[...] = jnp.zeros_like(prm)
        total = jnp.sum(sm.get()[...].reshape(devices, 8, LANE), axis=0)
        shift_out.buf[...] = total[:doms]
        scale_out.buf[...] = total[doms : 2 * doms]
        loss_out.buf[...] = jnp.sum(total[2 * doms : 2 * doms + 1, :], axis=1, keepdims=True) * (1.0 / count)
        for target in (shift_out, scale_out, loss_out):
            target.flush()
        given = pr.get()[...]
        gain, inv = given[doms : 2 * doms], given[4 * doms : 5 * doms]
        prm[0:16, :] = given[:16]
        prm[4 * doms : 5 * doms, :] = gain * total[:doms] * (1.0 / count)
        prm[5 * doms : 6 * doms, :] = gain * inv * total[doms : 2 * doms] * (1.0 / count)
        spread_columns(wide, prm, 6 * doms)
        for u in range(total_n // LANE):
            n = u * LANE // own
            part = slice(u * LANE, (u + 1) * LANE)
            here = slice(u * LANE - n * own, (u + 1) * LANE - n * own)
            if n == 0:
                tw = tw0.get()
                dom = mk0.get()[0:1, here]
                target = mk0.get()[1:2, here].astype(F32)
            else:
                tw = low[n - 1].get()
                pair = tw[t_rows : t_rows + 16, here].astype(F32)
                dom = pair[0:1].astype(jnp.int32)
                target = pair[1:2]
            values = [tw[k * LANE : (k + 1) * LANE, here] for k in range(doms)]
            if n:
                if here.start == 0:
                    added = [jnp.broadcast_to(base(v), (LANE, LANE)) for v in values]
                values = [decode(v, a, here.start) for v, a in zip(values, added)]
            _, affine, gain_s, head_w = chosen_tower(values, dom, wide, doms)
            s = sigmoid(affine)
            act = affine * s
            chosen = jnp.sum(act * head_w, axis=0, keepdims=True)
            score_grad = (sigmoid(chosen) - target) * (1.0 / count)
            grad = gain_s * (score_grad * head_w * (s + act * (1.0 - s)))
            for k in range(doms):
                v = jnp.where(dom == k, grad, 0.0) - wide[4 * doms + k]
                v = v - (values[k] - wide[k]) * wide[5 * doms + k]
                down = v.astype(BF16)
                tg[k * th : (k + 1) * th, part] = down
                srow[k : k + 1, part] = jnp.sum(down.astype(F32) * values[k], axis=0, keepdims=True)
        wt = wts.get()
        for k in range(doms):
            mg[k * out_n : (k + 1) * out_n, :] = mm(wt[k], tg[k * th : (k + 1) * th, :])
        vals, gate = vals.get(), gate.get()
        gg[...] = jnp.zeros_like(gg)

        def tower_part(k):
            tgf[k * out_n : (k + 1) * out_n, :] = mm_t(
                mixed.get()[k * out_n : (k + 1) * out_n, :], tg[k * th : (k + 1) * th, :]
            )

        def hidden_part(n, e):
            at = slice(e * hid_n, (e + 1) * hid_n)
            part = slice(n * own, (n + 1) * own)
            w = (w2o, w2s)[e // epd].get()[e % epd]
            grad = mm(w, eg[e * out_n : (e + 1) * out_n, part])
            pg[at, part] = (grad * slope.get()[at, part].astype(F32)).astype(BF16)

        ready = []
        for u in range(total_n // LANE):
            part = slice(u * LANE, (u + 1) * LANE)
            rows = [[gate[k * exps + e : k * exps + e + 1, part] for e in range(ce)] for k in range(doms)]

            def spread(i, acc):
                up = [mg[pl.ds(pl.multiple_of(k * out_n + i * 16, 16), 16), part] for k in range(doms)]
                acc = list(acc)
                for e in range(ce):
                    at = pl.ds(pl.multiple_of(e * out_n + i * 16, 16), 16)
                    v = vals[at, part].astype(F32)
                    back = None
                    for k in range(doms):
                        term = rows[k][e] * up[k]
                        back = term if k == 0 else back + term
                        prod = up[k] * v
                        acc[k * ce + e] = acc[k * ce + e] + (prod[:8] + prod[8:])
                    eg[at, part] = back.astype(BF16)
                return tuple(acc)

            zero = jnp.zeros((8, LANE), F32)
            acc = lax.fori_loop(0, out_n // 16, spread, (zero,) * (doms * ce), unroll=out_n // 16)
            for k in range(doms):
                for e in range(ce):
                    gg[k * exps + e : k * exps + e + 1, part] = jnp.sum(acc[k * ce + e], axis=0, keepdims=True)
            if (u + 1) * LANE % own == 0:
                ready += [(hidden_part, (u * LANE // own, e)) for e in range(ce)]
            if ready:
                task, args = ready.pop(0)
                task(*args)
        for task, args in ready:
            task(*args)
        pgs.flush()
        here = lax.broadcasted_iota(jnp.int32, (exps, total_n), 0) < ce
        for k in range(doms):
            at = slice(k * exps, (k + 1) * exps)
            gg[at, :] = jnp.where(here, gate[at, :] * (gg[at, :] - srow[k : k + 1, :]), 0.0)
        lg[...] = mm(reorder(ke, epd), gg[...].astype(BF16)).astype(BF16)
        lgs.flush()
        hid = hid.get()

        def put(kind, slot, values):
            target = ((sec_sib, first_sib), (sec_mine, first_mine))[slot < epd][kind]
            size = (m_sec, m_first)[kind]
            step = math.gcd(size, hid_n)
            for i, q, flat in pieces(kind, epd, hid_n, out_n, dim):
                if i == slot % epd:
                    for off in range(0, hid_n, step):
                        j, o = divmod(flat + off, size)
                        part = values[off : off + step, q * LANE : (q + 1) * LANE]
                        target.buf[at_row[kind][j], o : o + step, :] = part.astype(target.buf.dtype)

        x = xs.get()
        facc[...] = mm(pg[...], x[...])
        for e in range(ce):
            put(1, e, facc[e * hid_n : (e + 1) * hid_n, :])
        for e in range(ce):
            at = slice(e * hid_n, (e + 1) * hid_n)
            at_o = slice(e * out_n, (e + 1) * out_n)
            put(0, e, mm_t(hid[at, :], eg[at_o, :]))
        for target in (sec_sib, first_sib, sec_mine, first_mine):
            target.flush()
        for k in range(doms):
            tower_part(k)
        tgf[doms * out_n :, :] = jnp.zeros((tgf.shape[0] - doms * out_n, LANE), F32)
        part_g = mm(lg[...], x[...])
        for q in range(dim // LANE):
            tgf[doms * out_n + q * 32 : doms * out_n + q * 32 + ke, :] = part_g[:, q * LANE : (q + 1) * LANE]
        tgf[doms * out_n + ke : doms * out_n + 32, :] = given[16 : 48 - ke]
        for target, core in ((tow_sib, 1 - c), (tow_mine, c)):
            for j in range(rows_n):
                start = pl.multiple_of((core * rows_n + j) * m_tow, 8)
                target.buf[at_row[1][j], :, :] = tgf[pl.ds(start, m_tow), :].astype(target.buf.dtype)
            target.flush()

    outs = [
        plain((doms, LANE), F32),
        plain((doms, LANE), F32),
        plain((1, 1), F32),
        Near(plain((rows_n, m_sec, LANE), BF16)),
        Near(plain((rows_n, m_first, LANE), BF16)),
        Near(plain((rows_n, m_sec, LANE), F32)),
        Near(plain((rows_n, m_first, LANE), F32)),
        Near(plain((rows_n, m_tow, LANE), BF16)),
        Near(plain((rows_n, m_tow, LANE), F32)),
        Near(plain((ce * hid_n, total_n), BF16)),
        Near(plain((ke, total_n), BF16)),
        Near(plain((dim, ce * hid_n), BF16)),
    ]
    scratch = [
        pltpu.VMEM((6 * doms, LANE, LANE), F32),
        pltpu.VMEM((LANE, LANE), F32),
        pltpu.VMEM((doms * th, total_n), BF16),
        pltpu.VMEM((doms * out_n, total_n), F32),
        pltpu.VMEM((ce * out_n, total_n), BF16),
        pltpu.VMEM((ke, total_n), F32),
        pltpu.VMEM((8, total_n), F32),
        pltpu.VMEM((2 * rows_n * m_tow, LANE), F32),
        pltpu.VMEM((ce * hid_n, dim), F32),
    ]

    def side_by_side(which):
        def pairs(refs, buf):
            return [(r.at[n], buf.at[:, i * own : (i + 1) * own]) for i, (r, (_, n)) in enumerate(zip(refs, acts))]

        arrays = [a[which] for a, _ in acts]
        return Far(arrays, (arrays[0].shape[1], total_n), pairs)

    ins = [Near(sums), Near(params), Near(tower), Near(marks)]
    ins += [Near(v) for v in low_towers]
    ins += [Far(wtower), side_by_side(3), side_by_side(2), Far(w2[0]), Far(w2[1], moved=True), side_by_side(1)]
    ins += [Far(inputs, (total_n, dim), row_blocks(list(range(ns)), own)), side_by_side(0), side_by_side(4)]

    def joined(refs, buf):
        slots = [(refs[e // epd].at[e % epd], e) for e in range(ce)]
        return [(ref, buf.at[:, e * hid_n : (e + 1) * hid_n]) for ref, e in slots]

    ins.append(Far(w1, pairs=joined, moved=[False, True], into=len(outs) - 1))
    return staged(body, ins, outs, scratch, "backward", 44)


def backward_inputs(pg, lg, w1, wgate_t, own):
    total_n = pg.shape[1]
    ns = total_n // own
    dim = w1.shape[0]
    ke = wgate_t.shape[0]

    def body(ins, outs):
        w1c, wgs, pgs, lgs = ins
        wg = jnp.concatenate([wgs.get()[...], jnp.zeros((LANE - ke, dim), BF16)], axis=0).T[:, :ke]
        pg, lg, w1c = pgs.get(), lgs.get(), w1c.get()
        for n in range(ns - 1, -1, -1):
            part = slice(n * own, (n + 1) * own)
            gi = mm(w1c[...], pg[:, part]) + mm(wg, lg[:, part])
            if n:
                outs[1].buf[n - 1] = gi.astype(BF16)
                outs[1].flush(n - 1)
            else:
                outs[0].buf[...] = gi
                outs[0].flush()

    return staged(
        body,
        [Near(w1), Near(wgate_t), Near(pg), Near(lg)],
        [Near(plain((dim, own), F32)), Near(plain((max(ns - 1, 1), dim, own), BF16))],
        [],
        "backward_inputs",
        16,
    )


def finish_inputs(own_part, received):
    dim, own = own_part.shape

    def body(ins, outs):
        for u in range(own // LANE):
            lanes = slice(u * LANE, (u + 1) * LANE)
            part = total(*(src.buf[:, lanes] for src in ins))
            outs[0].buf[lanes, :] = part.T
            outs[0].flush(pl.ds(u * LANE, LANE))

    return staged(
        body, [Near(own_part)] + [Near(v) for v in received], [plain((own, dim), F32)], [], "finish_inputs", 12
    )[0]


def finish_weights(second, first, other, epd, hid_n, out_n, dim, doms, exps, rows_n):
    m_sec, m_first, m_tow = layout(epd, hid_n, out_n, dim, doms, rows_n)
    ke = doms * exps

    def body(ins, outs, buf, tgf):
        out_f, out_s, out_t, out_g, out_h = (o.buf for o in outs)
        c = lax.rem(lax.axis_index(WIDTH), 2)
        r = lax.axis_index(ROWS)
        at_row = [spots(kind, r, rows_n) for kind in range(2)]
        for kind, size in ((0, m_sec), (1, m_first)):
            got = ins[kind].get()
            step = math.gcd(size, hid_n)
            for i, q, flat in pieces(kind, epd, hid_n, out_n, dim):
                for off in range(0, hid_n, step):
                    j, o = divmod(flat + off, size)
                    piece = got[at_row[kind][j], o : o + step, :].astype(F32)
                    if kind == 0:
                        out_s[i, off : off + step, q * LANE : (q + 1) * LANE] = piece
                    else:
                        buf[off : off + step, :] = piece
                if kind == 1:
                    out_f[i, q * LANE : (q + 1) * LANE, :] = buf[...].T
                if q == (out_n, dim)[kind] // LANE - 1:
                    outs[1 - kind].flush(i)
        near, sib = ins[1].get(), ins[2].get()
        for j in range(rows_n):
            at = at_row[1][j]
            for core, value in ((c, near[at, m_first:, :]), (1 - c, sib[at])):
                start = pl.multiple_of((core * rows_n + j) * m_tow, 8)
                tgf[pl.ds(start, m_tow), :] = value.astype(F32)
        for k in range(doms):
            out_t[k] = tgf[k * out_n : (k + 1) * out_n, :]
        outs[2].flush()
        for q in range(dim // LANE):
            at = doms * out_n + q * 32
            out_g[:, q * LANE : (q + 1) * LANE] = tgf[at : at + ke, :]
        outs[3].flush()
        out_h[...] = tgf[doms * out_n + ke : doms * out_n + ke + doms, :]
        outs[4].flush()

    return staged(
        body,
        [Near(second), Near(first), Near(other)],
        [
            plain((epd, dim, hid_n), F32),
            plain((epd, hid_n, out_n), F32),
            plain((doms, out_n, LANE), F32),
            plain((ke, dim), F32),
            plain((doms, LANE), F32),
        ],
        [pltpu.VMEM((hid_n, LANE), F32), pltpu.VMEM((2 * rows_n * m_tow, LANE), F32)],
        "finish_weights",
        16,
    )


def swap(value, axis, mask):
    size = lax.axis_size(axis)
    return lax.ppermute(value, axis, [(i, i ^ mask) for i in range(size)])


def total(*values):
    got = values[0].astype(F32)
    for value in values[1:]:
        got = got + value.astype(F32)
    return got


def send(value, axis, mask):
    return swap(value.astype(BF16), axis, mask)


together = lax.optimization_barrier


def reduce_rows(second, first, towers, beside):
    n_rows, n_width = lax.axis_size(ROWS), lax.axis_size(WIDTH)
    half = n_rows // 2
    far = [2 * q for q in range(1, half)]
    low = total(*(v[half:] for v in first)).astype(BF16)
    high = [total(*(v[m : m + 2] for v in second)).astype(BF16) for m in far]
    across = total(*towers).astype(BF16)
    first_got = swap(low, ROWS, 1)
    second_got = [swap(v, ROWS, m) for v, m in zip(high, far)]
    towers = total(*towers, *(swap(across, WIDTH, mask) for mask in range(2, n_width, 2)))
    tower_low, operand = together((towers[half:].astype(BF16), beside[1]))
    tower_got = swap(tower_low, ROWS, 1)
    inputs_part = tuple(beside[0](operand))
    first_got, second_got, tower_got, inputs_part = together((first_got, second_got, tower_got, inputs_part))

    def piece(q):
        return jnp.concatenate(
            [total(*(v[q] for v in first), first_got[q]), total(towers[q], tower_got[q])], axis=0
        )

    pair = total(*(v[:2] for v in second), *second_got)
    high = [piece(q).astype(BF16) for q in range(1, half)]
    high, low = together((high, pair.astype(BF16)))
    moved = [swap(v, ROWS, m) for v, m in zip(high, far)]
    moved, low = together((moved, swap(low, ROWS, 1)))
    pair = total(pair, low[::-1])
    return pair.astype(BF16), total(piece(0), *moved).astype(BF16), inputs_part


def gather_rows(pair, first, m_first, beside):
    half = lax.axis_size(ROWS) // 2
    far = [2 * q for q in range(1, half)]
    pair, first = together((pair, first))
    high, beside = together(([swap(first, ROWS, m) for m in far], beside))
    pair, evens = together((pair, jnp.stack([first] + high)))
    low, high = swap(evens, ROWS, 1), [swap(pair, ROWS, m) for m in far]
    low, high, beside = together((low, high, finish_inputs(*beside)))
    second, first = jnp.concatenate([pair] + high), jnp.concatenate([evens, low])
    return second, first, swap(first[:, m_first:], WIDTH, 1), beside


def local(inputs, w_first, w_second, w_gate, w_tower, norm_scale, norm_shift, w_head, domains, labels):
    n_width, n_rows = lax.axis_size(WIDTH), lax.axis_size(ROWS)
    devices = n_width * n_rows
    own = inputs.shape[0] // n_width
    count = float(own * devices)
    dim = inputs.shape[1]
    epd, _, hid_n = w_first.shape
    out_n = w_second.shape[2]
    doms, _, exps = w_gate.shape
    ke = doms * exps
    n_x = n_width // 2
    others = list(range(1, n_x))
    w1 = (w_first, swap(w_first, WIDTH, 1))
    w2 = (w_second, swap(w_second, WIDTH, 1))
    wgate_t = jnp.transpose(w_gate, (0, 2, 1)).reshape(ke, dim)
    marks = jnp.stack([domains, labels])

    x_far, w1_own, w2_own, wt = prepare(others, inputs, w_first, w_second, wgate_t, w_tower, own)
    w1t, w2t = (w1_own, w1[1]), (w2_own, w2[1])
    far = forward([Near(x_far)], w1t, w2t, wt, own, doms, False, BF16, "forward_send")[0]
    sent = [swap(far[s - 1 : s], WIDTH, 2 * s) for s in others]
    blocks = [Far(inputs, (own, dim), row_blocks([0], own)), Near(x_far)]
    kept = forward(blocks, w1t, w2t, wt, own, doms, True, F32, "forward_keep")
    tower, low, message = combine(kept[5], sent, marks, devices)
    stats = lax.all_to_all(message, BOTH, 0, 0, tiled=True)
    stats, low = together((stats, low))
    lows = [swap(low, WIDTH, 2 * s) for s in others]
    params, message = normalise(stats, tower, marks, norm_scale, norm_shift, w_head, devices, count)
    sums = lax.all_to_all(message, BOTH, 0, 0, tiled=True)

    acts = [(kept[:5], s) for s in range(n_x)]
    grad_shift, grad_scale, loss, sec_sib, first_sib, sec_own, first_own, tow_sib, tow_own, pg, lg, w1_joined = backward(
        sums, params, tower, lows, marks, acts, inputs, w1, w2, wgate_t, w_tower, devices, n_rows, count
    )
    first_sib = swap(first_sib, WIDTH, 1)
    first_sib, sec_sib, tow_sib = together((first_sib, sec_sib, tow_sib))
    second, first, (gi_own, gi_out) = reduce_rows(
        (sec_own, swap(sec_sib, WIDTH, 1)),
        (first_own, first_sib),
        (tow_own, swap(tow_sib, WIDTH, 1)),
        (lambda grad: backward_inputs(grad, lg, w1_joined, wgate_t, own), pg),
    )
    inputs_got = [swap(gi_out[s - 1], WIDTH, 2 * s) for s in others]
    m_first = layout(epd, hid_n, out_n, dim, doms, n_rows)[1]
    second, first, other, grad_inputs = gather_rows(second, first, m_first, (gi_own, inputs_got))
    grad_first, grad_second, grad_tower, grad_gate, grad_head = finish_weights(
        second, first, other, epd, hid_n, out_n, dim, doms, exps, n_rows
    )
    return (
        loss[0, 0],
        grad_inputs,
        grad_first,
        grad_second,
        grad_gate.reshape(doms, exps, dim).transpose(0, 2, 1),
        grad_tower,
        grad_scale,
        grad_shift,
        grad_head,
    )


def solution(mesh):
    placed = (
        P(ROWS, None),
        P(WIDTH, None, None),
        P(WIDTH, None, None),
        P(),
        P(),
        P(),
        P(),
        P(),
        P(BOTH),
        P(BOTH),
    )
    return jax.shard_map(
        local,
        mesh=mesh,
        in_specs=placed,
        out_specs=(
            P(),
            P(BOTH, None),
            P(WIDTH, None, None),
            P(WIDTH, None, None),
            P(),
            P(),
            P(),
            P(),
            P(),
        ),
        check_vma=False,
    )
```

```python
import math

import jax
import jax.numpy as jnp
from jax import lax
from jax.experimental import pallas as pl
from jax.experimental.pallas import tpu as pltpu
from jax.sharding import PartitionSpec as P

F32 = jnp.float32
BF16 = jnp.bfloat16
EPS = 1e-05
LANE = 128
MIB = 1 << 20
ROWS = "rows"
WIDTH = "width"
BOTH = (ROWS, WIDTH)


def mm(a, b):
    return jnp.dot(a, b, preferred_element_type=F32)


def mm_t(a, b):
    return lax.dot_general(a, b, (((1,), (1,)), ((), ())), preferred_element_type=F32)


def sigmoid(v):
    return 0.5 * jnp.tanh(0.5 * v) + 0.5


PLAIN = 8


def base(values):
    first = values[:, :PLAIN].astype(BF16).astype(F32)
    return jnp.sum(first, axis=1, keepdims=True) * (1.0 / PLAIN)


def encode(values):
    lane = lax.broadcasted_iota(jnp.int32, values.shape, 1)
    return jnp.where(lane < PLAIN, values, values - base(values)).astype(BF16)


def decode(values, added, start=0):
    lane = lax.broadcasted_iota(jnp.int32, values.shape, 1)
    values = values.astype(F32)
    return jnp.where(lane < PLAIN - start, values, values + added)


class Source:
    def __init__(self, buf, copies):
        self.buf = buf
        self.waiting = copies
        for copy in copies:
            copy.start()

    def get(self):
        for copy in self.waiting:
            copy.wait()
        self.waiting = []
        return self.buf


class Target:
    def __init__(self, ref, buf, sems):
        self.ref, self.buf, self.sems = ref, buf, sems
        self.waiting = []

    def flush(self, *at):
        if self.ref is None:
            return
        src = self.buf.at[at] if at else self.buf
        dst = self.ref.at[at] if at else self.ref
        copy = pltpu.make_async_copy(src, dst, next(self.sems))
        copy.start()
        self.waiting.append(copy)


class Near:
    def __init__(self, what):
        self.what = what


class Far:
    def __init__(self, arrays, shape=None, pairs=None, moved=False, into=None):
        self.into = into
        self.arrays = arrays if isinstance(arrays, (list, tuple)) else [arrays]
        self.moved = moved if isinstance(moved, list) else [moved] * len(self.arrays)
        self.shape = shape or self.arrays[0].shape
        self.dtype = self.arrays[0].dtype
        self.pairs = pairs or (lambda refs, buf: [(refs[0], buf)])


def staged(body, ins, outs, scratch, name, limit, n_sems=64):
    far_in = [i for i, s in enumerate(ins) if isinstance(s, Far) and s.into is None]
    far_out = [i for i, s in enumerate(outs) if not isinstance(s, Near)]
    args, specs, spans = [], [], []
    hbm = pl.BlockSpec(memory_space=pltpu.HBM)
    vmem = pl.BlockSpec(memory_space=pltpu.VMEM)
    anywhere = pl.BlockSpec(memory_space=pl.ANY)
    for s in ins:
        if isinstance(s, Far):
            spans.append((len(args), len(args) + len(s.arrays)))
            for a, moved in zip(s.arrays, s.moved):
                args.append(a if moved else pltpu.with_memory_space_constraint(a, pltpu.HBM))
                specs.append(anywhere if moved else hbm)
        else:
            spans.append((len(args), len(args) + 1))
            args.append(s.what)
            specs.append(vmem)
    n_in, n_out = len(args), len(outs)

    def kernel(*refs):
        refs_in, refs_out = refs[:n_in], refs[n_in : n_in + n_out]
        bufs = refs[n_in + n_out :]
        in_bufs = dict(zip(far_in, bufs))
        in_bufs.update({i: refs_out[s.into] for i, s in enumerate(ins) if isinstance(s, Far) and s.into is not None})
        out_bufs = dict(zip(far_out, bufs[len(far_in) :]))
        rest = bufs[len(far_in) + len(far_out) : -1]
        sems = iter([bufs[-1].at[i] for i in range(n_sems)])
        sources = []
        for i, (start, stop) in enumerate(spans):
            if i in in_bufs:
                pairs = ins[i].pairs(refs_in[start:stop], in_bufs[i])
                sources.append(Source(in_bufs[i], [pltpu.make_async_copy(a, b, next(sems)) for a, b in pairs]))
            else:
                sources.append(Source(refs_in[start], []))
        targets = []
        for i, ref in enumerate(refs_out):
            targets.append(Target(ref, out_bufs[i], sems) if i in out_bufs else Target(None, ref, sems))
        body(sources, targets, *rest)
        for s in sources:
            s.get()
        for t in targets:
            for copy in t.waiting:
                copy.wait()

    return pl.pallas_call(
        kernel,
        out_shape=[o.what if isinstance(o, Near) else pltpu.HBM(o.shape, o.dtype) for o in outs],
        in_specs=specs,
        out_specs=[hbm if i in far_out else vmem for i in range(n_out)],
        scratch_shapes=[pltpu.VMEM(ins[i].shape, ins[i].dtype) for i in far_in]
        + [pltpu.VMEM(outs[i].shape, outs[i].dtype) for i in far_out]
        + list(scratch)
        + [pltpu.SemaphoreType.DMA((n_sems,))],
        compiler_params=pltpu.CompilerParams(vmem_limit_bytes=limit * MIB),
        name=name,
    )(*args)


def plain(shape, dtype):
    return jax.ShapeDtypeStruct(shape, dtype)


def row_blocks(slots, own):
    def pairs(refs, buf):
        w = lax.axis_index(WIDTH)
        got = []
        for n, s in enumerate(slots):
            start = pl.multiple_of(lax.bitwise_xor(w, 2 * s) * own, own)
            got.append((refs[0].at[pl.ds(start, own), :], buf.at[n * own : (n + 1) * own, :]))
        return got

    return pairs


def reorder(ke, epd):
    first = lax.axis_index(WIDTH) * epd
    down = lax.broadcasted_iota(jnp.int32, (ke, ke), 0)
    across = lax.broadcasted_iota(jnp.int32, (ke, ke), 1)
    return jnp.where(lax.bitwise_xor(down, first) == across, 1.0, 0.0).astype(BF16)


def prepare(slots, inputs, w1, w2, wgate_t, wtower, own):
    dim = inputs.shape[1]
    epd, _, hid_n = w1.shape
    out_n = w2.shape[2]
    ke = wgate_t.shape[0]
    doms, _, th = wtower.shape

    def body(ins, outs):
        w1s, wgs, w2s, wts, _ = ins
        _, w1t, w2t, wt = (o.buf for o in outs)
        w1_buf = w1s.get()
        for i in range(epd):
            w1t[i * hid_n : (i + 1) * hid_n, :] = w1_buf[i].T
        w1t[epd * hid_n :, :] = mm(reorder(ke, epd), wgs.get()[...]).astype(BF16)
        w2_buf = w2s.get()
        for i in range(epd):
            w2t[i] = w2_buf[i].T
        wt_buf = wts.get()
        for k in range(doms):
            wt[k] = wt_buf[k].T
    return staged(
        body,
        [Far(a) for a in (w1, wgate_t, w2, wtower)]
        + [Far(inputs, (len(slots) * own, dim), row_blocks(slots, own), into=0)],
        [
            Near(plain((len(slots) * own, dim), BF16)),
            Near(plain((epd * hid_n + ke, dim), BF16)),
            Near(plain((epd, out_n, hid_n), BF16)),
            Near(plain((doms, th, out_n), BF16)),
        ],
        [],
        "prepare",
        12,
    )


def forward(blocks, w1, w2, wt, own, doms, keep, tower_out, name):
    epd, dim, hid_n = w1[1].shape
    out_n = w2[1].shape[2]
    ce = 2 * epd
    half = epd * hid_n
    ke = w1[0].shape[0] - half
    th = wt.shape[1]
    exps = ke // doms
    sizes = [(b.what if isinstance(b, Near) else b).shape[0] // own for b in blocks]
    ns = sum(sizes)

    def body(ins, outs, w1t, w2t, pre, *bufs):
        xs = ins[: len(blocks)]
        w1o, w1s, w2o, w2s, wts = ins[len(blocks) :]
        if keep:
            hid, slope, vals, gate, mixed = (o.buf for o in outs[:5])
        else:
            hid, vals, gate = bufs
        wt = wts.get()
        for i in range(epd):
            w1t[i * hid_n : (i + 1) * hid_n, :] = w1s.get()[i].T
            w2t[i] = w2s.get()[i].T
        parts = [(src, n) for src, size in zip(xs, sizes) for n in range(size)]
        for n, (src, place) in enumerate(parts):
            x = src.get()[place * own : (place + 1) * own, :]
            got = mm_t(w1o.get()[...], x)
            pre[:half, :] = got[:half]
            pre[ce * hid_n :, :] = got[half:]
            pre[half : ce * hid_n, :] = mm_t(w1t[...], x)
            logits = pre[ce * hid_n : ce * hid_n + ke, :].reshape(doms, exps, own)
            top = jnp.exp(logits - jnp.max(logits, axis=1, keepdims=True))
            soft = top / jnp.sum(top, axis=1, keepdims=True)
            gate[n] = soft.reshape(ke, own)

            def act(i, carry):
                at = pl.ds(pl.multiple_of(i * 16, 16), 16)
                v = pre[at, :]
                s = sigmoid(v)
                h = v * s
                hid[n, at, :] = h.astype(BF16)
                if keep:
                    slope[n, at, :] = (s + h * (1.0 - s)).astype(BF16)
                return carry

            lax.fori_loop(0, ce * hid_n // 16, act, 0, unroll=4 if keep else ce * hid_n // 16)
            for e in range(ce):
                w = w2o.get()[e] if e < epd else w2t[e - epd]
                vals[n, e * out_n : (e + 1) * out_n, :] = mm(w, hid[n, e * hid_n : (e + 1) * hid_n, :]).astype(BF16)
            if not keep:
                tower = outs[-1]
                for k in range(doms):
                    sums = None
                    for e in range(ce):
                        term = mm(wt[k], vals[n, e * out_n : (e + 1) * out_n, :])
                        term = gate[n, k * exps + e : k * exps + e + 1, :] * term
                        sums = term if e == 0 else sums + term
                    tower.buf[n, k * th : (k + 1) * th, :] = encode(sums)
                tower.flush(n)
                continue
            for o in outs[:4]:
                o.flush(n)
            for u in range(own // LANE):
                part = slice(u * LANE, (u + 1) * LANE)
                rows = [[gate[n, k * exps + e : k * exps + e + 1, part] for e in range(ce)] for k in range(doms)]

                def mix(i, carry):
                    acc = [None] * doms
                    for e in range(ce):
                        at = pl.ds(pl.multiple_of(e * out_n + i * 32, 32), 32)
                        v = vals[n, at, part].astype(F32)
                        for k in range(doms):
                            term = rows[k][e] * v
                            acc[k] = term if e == 0 else acc[k] + term
                    for k in range(doms):
                        at = pl.ds(pl.multiple_of(k * out_n + i * 32, 32), 32)
                        mixed[n, at, part] = acc[k].astype(BF16)
                    return carry

                lax.fori_loop(0, out_n // 32, mix, 0, unroll=4)
            outs[4].flush(n)
            if n == 0:
                tower = outs[-1]
                for k in range(doms):
                    tower.buf[n, k * th : (k + 1) * th, :] = mm(wt[k], mixed[n, k * out_n : (k + 1) * out_n, :])
                tower.flush(n)

    kept = [
        plain((ns, ce * hid_n, own), BF16),
        plain((ns, ce * hid_n, own), BF16),
        plain((ns, ce * out_n, own), BF16),
        plain((ns, ke, own), F32),
        plain((ns, doms * out_n, own), BF16),
    ]
    outs = list(kept) if keep else []
    outs.append(Near(plain((1 if keep else ns, doms * th, own), tower_out)))
    scratch = [
        pltpu.VMEM((half, dim), BF16),
        pltpu.VMEM((epd, out_n, hid_n), BF16),
        pltpu.VMEM((ce * hid_n + ke, own), F32),
    ]
    if not keep:
        scratch += [pltpu.VMEM(kept[i].shape, kept[i].dtype) for i in (0, 2, 3)]
    ins = blocks + [Near(a) for a in (w1[0], w1[1], w2[0], w2[1], wt)]
    return staged(body, ins, outs, scratch, name, 40)


def combine(own_part, received, marks, devices):
    _, rows, own = own_part.shape
    doms = rows // LANE

    def body(ins, outs, cols):
        part = ins[0].get()
        got = [s.get() for s in ins[2:]]
        tower, low, message = (o.buf for o in outs)
        cols[...] = jnp.zeros_like(cols)
        for k in range(doms):
            at = slice(k * LANE, (k + 1) * LANE)
            total = part[0, at, :]
            for ref in got:
                total = total + decode(ref[0, at, :], base(ref[0, at, :LANE]))
            tower[at, :] = total
            low[at, :] = encode(total)
            mean = jnp.sum(total, axis=1, keepdims=True) * (1.0 / own)
            dev = total - mean
            cols[:, k : k + 1] = mean
            cols[:, doms + k : doms + k + 1] = jnp.sum(dev * dev, axis=1, keepdims=True)
        outs[0].flush()
        pair = jnp.concatenate([ins[1].get()[...].astype(F32), jnp.zeros((14, own), F32)], axis=0)
        low[rows:, :] = pair.astype(BF16)
        outs[1].flush()
        tile = cols[...].T[:8, :]
        for d in range(devices):
            message[d * 8 : (d + 1) * 8, :] = tile
        outs[2].flush()

    return staged(
        body,
        [Near(own_part), Near(marks)] + [Near(v) for v in received],
        [Near(plain((rows, own), F32)), Near(plain((rows + 16, own), BF16)), Near(plain((devices * 8, LANE), F32))],
        [pltpu.VMEM((LANE, LANE), F32)],
        "combine",
        16,
    )


def pick(dom, values):
    got = values[-1]
    for k in range(len(values) - 2, -1, -1):
        got = jnp.where(dom == k, values[k], got)
    return got


def chosen_tower(values, dom, wide, doms):
    mean, gain, shift, head = (pick(dom, [wide[j * doms + k] for k in range(doms)]) for j in range(4))
    centred = pick(dom, values) - mean
    return centred, centred * gain + shift, gain, head


def spread_columns(wide, rows_ref, n):
    cols = rows_ref[...].T
    for j in range(n):
        wide[j] = jnp.broadcast_to(cols[:, j : j + 1], (LANE, LANE))


def normalise(stats, tower, marks, scale, shift, head, devices, count):
    rows, own = tower.shape
    doms = rows // LANE

    def body(ins, outs, prm, wide, q):
        st, tws, mks, sc, sh, hd = ins
        params, message = (o.buf for o in outs)
        prm[...] = jnp.zeros_like(prm)
        got = st.get()[...].reshape(devices, 8, LANE)
        total = jnp.sum(got, axis=0)
        mean = total * (1.0 / devices)
        dev = got - mean[None]
        spread = jnp.sum(dev * dev, axis=0) * float(own)
        var = (total[doms : 2 * doms] + spread[:doms]) * (1.0 / count)
        inv = lax.rsqrt(var + EPS)
        prm[0:doms, :] = mean[:doms]
        prm[doms : 2 * doms, :] = inv * sc.get()[...]
        prm[2 * doms : 3 * doms, :] = sh.get()[...]
        prm[3 * doms : 4 * doms, :] = hd.get()[...]
        prm[4 * doms : 5 * doms, :] = inv
        params[:16, :] = prm[:16, :]
        spread_columns(wide, prm, 4 * doms)
        tw, mk = tws.get(), mks.get()
        loss = jnp.zeros((1, LANE), F32)
        for u in range(own // LANE):
            part = slice(u * LANE, (u + 1) * LANE)
            dom = mk[0:1, part]
            target = mk[1:2, part].astype(F32)
            values = [tw[k * LANE : (k + 1) * LANE, part] for k in range(doms)]
            centred, affine, _, head_w = chosen_tower(values, dom, wide, doms)
            s = sigmoid(affine)
            act = affine * s
            chosen = jnp.sum(act * head_w, axis=0, keepdims=True)
            soft = jnp.maximum(chosen, 0.0) + jnp.log(1.0 + jnp.exp(-jnp.abs(chosen)))
            loss = loss + (soft - target * chosen)
            score_grad = (sigmoid(chosen) - target) * (1.0 / count)
            grad = score_grad * head_w * (s + act * (1.0 - s))
            q[0:LANE, part] = grad
            q[LANE : 2 * LANE, part] = grad * centred
            q[2 * LANE :, part] = score_grad * act
        kinds = lax.broadcasted_iota(jnp.int32, (8, own), 0)
        one_hot = (kinds == mk[0:1, :]).astype(F32).astype(BF16)
        high = q[...].astype(BF16)
        sums = (mm_t(one_hot, high) + mm_t(one_hot, (q[...] - high.astype(F32)).astype(BF16)))[:doms]
        tile = [sums[:, :LANE], sums[:, LANE : 2 * LANE] * inv]
        all_rows = tile + [loss, jnp.zeros((1, LANE), F32)]
        all_rows = jnp.concatenate(all_rows, axis=0)
        for d in range(devices):
            message[d * 8 : (d + 1) * 8, :] = all_rows
        params[16:, :] = jnp.concatenate([sums[:, 2 * LANE :], jnp.zeros((8 - doms, LANE), F32)], axis=0)
        outs[0].flush()

    return staged(
        body,
        [Near(v) for v in (stats, tower, marks, scale, shift, head)],
        [Near(plain((24, LANE), F32)), Near(plain((devices * 8, LANE), F32))],
        [
            pltpu.VMEM((LANE, LANE), F32),
            pltpu.VMEM((4 * doms, LANE, LANE), F32),
            pltpu.VMEM((3 * LANE, own), F32),
        ],
        "normalise",
        16,
    )


def layout(epd, hid_n, out_n, dim, doms, rows_n):
    second = epd * hid_n * out_n // LANE
    first = epd * hid_n * dim // LANE
    towers = -(-(doms * out_n + (dim // LANE) * 32) // (2 * 16 * rows_n)) * 16
    return second // rows_n, first // rows_n, towers


def pieces(kind, epd, hid_n, out_n, dim):
    flat = 0
    for i in range(epd):
        for q in range((out_n, dim)[kind] // LANE):
            yield i, q, flat
            flat += hid_n


def spots(kind, row, rows_n):
    got = []
    for j in range(rows_n):
        p = lax.bitwise_xor(row, j)
        got.append(p if kind == 0 else (p & 1) * (rows_n // 2) + lax.shift_right_logical(p, 1))
    return got


def backward(
    sums, params, tower, low_towers, marks, acts, inputs, w1, w2, wgate_t, wtower, devices, rows_n, count
):
    ns = 1 + len(low_towers)
    t_rows, own = tower.shape
    total_n = ns * own
    dim = inputs.shape[1]
    epd, hid_n, out_n = w2[0].shape
    ce = 2 * epd
    ke = wgate_t.shape[0]
    doms, _, th = wtower.shape
    exps = ke // doms
    m_sec, m_first, m_tow = layout(epd, hid_n, out_n, dim, doms, rows_n)

    def body(ins, outs, wide, prm, tg, mg, eg, gg, srow, tgf, facc):
        sm, pr, tw0, mk0 = ins[:4]
        low = ins[4 : 3 + ns]
        wts, gate, vals, w2o, w2s, slope, xs, hid, mixed, _ = ins[3 + ns :]
        shift_out, scale_out, loss_out, sec_sib, first_sib, sec_mine, first_mine, tow_sib, tow_mine, pgs, lgs, _ = outs
        pg, lg = pgs.buf, lgs.buf
        c = lax.rem(lax.axis_index(WIDTH), 2)
        r = lax.axis_index(ROWS)
        at_row = [spots(kind, r, rows_n) for kind in range(2)]
        prm[...] = jnp.zeros_like(prm)
        total = jnp.sum(sm.get()[...].reshape(devices, 8, LANE), axis=0)
        shift_out.buf[...] = total[:doms]
        scale_out.buf[...] = total[doms : 2 * doms]
        loss_out.buf[...] = jnp.sum(total[2 * doms : 2 * doms + 1, :], axis=1, keepdims=True) * (1.0 / count)
        for target in (shift_out, scale_out, loss_out):
            target.flush()
        given = pr.get()[...]
        gain, inv = given[doms : 2 * doms], given[4 * doms : 5 * doms]
        prm[0:16, :] = given[:16]
        prm[4 * doms : 5 * doms, :] = gain * total[:doms] * (1.0 / count)
        prm[5 * doms : 6 * doms, :] = gain * inv * total[doms : 2 * doms] * (1.0 / count)
        spread_columns(wide, prm, 6 * doms)
        for u in range(total_n // LANE):
            n = u * LANE // own
            part = slice(u * LANE, (u + 1) * LANE)
            here = slice(u * LANE - n * own, (u + 1) * LANE - n * own)
            if n == 0:
                tw = tw0.get()
                dom = mk0.get()[0:1, here]
                target = mk0.get()[1:2, here].astype(F32)
            else:
                tw = low[n - 1].get()
                pair = tw[t_rows : t_rows + 16, here].astype(F32)
                dom = pair[0:1].astype(jnp.int32)
                target = pair[1:2]
            values = [tw[k * LANE : (k + 1) * LANE, here] for k in range(doms)]
            if n:
                if here.start == 0:
                    added = [jnp.broadcast_to(base(v), (LANE, LANE)) for v in values]
                values = [decode(v, a, here.start) for v, a in zip(values, added)]
            _, affine, gain_s, head_w = chosen_tower(values, dom, wide, doms)
            s = sigmoid(affine)
            act = affine * s
            chosen = jnp.sum(act * head_w, axis=0, keepdims=True)
            score_grad = (sigmoid(chosen) - target) * (1.0 / count)
            grad = gain_s * (score_grad * head_w * (s + act * (1.0 - s)))
            for k in range(doms):
                v = jnp.where(dom == k, grad, 0.0) - wide[4 * doms + k]
                v = v - (values[k] - wide[k]) * wide[5 * doms + k]
                down = v.astype(BF16)
                tg[k * th : (k + 1) * th, part] = down
                srow[k : k + 1, part] = jnp.sum(down.astype(F32) * values[k], axis=0, keepdims=True)
        wt = wts.get()
        for k in range(doms):
            mg[k * out_n : (k + 1) * out_n, :] = mm(wt[k], tg[k * th : (k + 1) * th, :])
        vals, gate = vals.get(), gate.get()
        gg[...] = jnp.zeros_like(gg)

        def tower_part(k):
            tgf[k * out_n : (k + 1) * out_n, :] = mm_t(
                mixed.get()[k * out_n : (k + 1) * out_n, :], tg[k * th : (k + 1) * th, :]
            )

        def hidden_part(n, e):
            at = slice(e * hid_n, (e + 1) * hid_n)
            part = slice(n * own, (n + 1) * own)
            w = (w2o, w2s)[e // epd].get()[e % epd]
            grad = mm(w, eg[e * out_n : (e + 1) * out_n, part])
            pg[at, part] = (grad * slope.get()[at, part].astype(F32)).astype(BF16)

        ready = []
        for u in range(total_n // LANE):
            part = slice(u * LANE, (u + 1) * LANE)
            rows = [[gate[k * exps + e : k * exps + e + 1, part] for e in range(ce)] for k in range(doms)]

            def spread(i, acc):
                up = [mg[pl.ds(pl.multiple_of(k * out_n + i * 16, 16), 16), part] for k in range(doms)]
                acc = list(acc)
                for e in range(ce):
                    at = pl.ds(pl.multiple_of(e * out_n + i * 16, 16), 16)
                    v = vals[at, part].astype(F32)
                    back = None
                    for k in range(doms):
                        term = rows[k][e] * up[k]
                        back = term if k == 0 else back + term
                        prod = up[k] * v
                        acc[k * ce + e] = acc[k * ce + e] + (prod[:8] + prod[8:])
                    eg[at, part] = back.astype(BF16)
                return tuple(acc)

            zero = jnp.zeros((8, LANE), F32)
            acc = lax.fori_loop(0, out_n // 16, spread, (zero,) * (doms * ce), unroll=out_n // 16)
            for k in range(doms):
                for e in range(ce):
                    gg[k * exps + e : k * exps + e + 1, part] = jnp.sum(acc[k * ce + e], axis=0, keepdims=True)
            if (u + 1) * LANE % own == 0:
                ready += [(hidden_part, (u * LANE // own, e)) for e in range(ce)]
            if ready:
                task, args = ready.pop(0)
                task(*args)
        for task, args in ready:
            task(*args)
        pgs.flush()
        here = lax.broadcasted_iota(jnp.int32, (exps, total_n), 0) < ce
        for k in range(doms):
            at = slice(k * exps, (k + 1) * exps)
            gg[at, :] = jnp.where(here, gate[at, :] * (gg[at, :] - srow[k : k + 1, :]), 0.0)
        lg[...] = mm(reorder(ke, epd), gg[...].astype(BF16)).astype(BF16)
        lgs.flush()
        hid = hid.get()

        def put(kind, slot, values):
            target = ((sec_sib, first_sib), (sec_mine, first_mine))[slot < epd][kind]
            size = (m_sec, m_first)[kind]
            step = math.gcd(size, hid_n)
            for i, q, flat in pieces(kind, epd, hid_n, out_n, dim):
                if i == slot % epd:
                    for off in range(0, hid_n, step):
                        j, o = divmod(flat + off, size)
                        part = values[off : off + step, q * LANE : (q + 1) * LANE]
                        target.buf[at_row[kind][j], o : o + step, :] = part.astype(target.buf.dtype)

        x = xs.get()
        facc[...] = mm(pg[...], x[...])
        for e in range(ce):
            put(1, e, facc[e * hid_n : (e + 1) * hid_n, :])
        for e in range(ce):
            at = slice(e * hid_n, (e + 1) * hid_n)
            at_o = slice(e * out_n, (e + 1) * out_n)
            put(0, e, mm_t(hid[at, :], eg[at_o, :]))
        for target in (sec_sib, first_sib, sec_mine, first_mine):
            target.flush()
        for k in range(doms):
            tower_part(k)
        tgf[doms * out_n :, :] = jnp.zeros((tgf.shape[0] - doms * out_n, LANE), F32)
        part_g = mm(lg[...], x[...])
        for q in range(dim // LANE):
            tgf[doms * out_n + q * 32 : doms * out_n + q * 32 + ke, :] = part_g[:, q * LANE : (q + 1) * LANE]
        tgf[doms * out_n + ke : doms * out_n + 32, :] = given[16 : 48 - ke]
        for target, core in ((tow_sib, 1 - c), (tow_mine, c)):
            for j in range(rows_n):
                start = pl.multiple_of((core * rows_n + j) * m_tow, 8)
                target.buf[at_row[1][j], :, :] = tgf[pl.ds(start, m_tow), :].astype(target.buf.dtype)
            target.flush()

    outs = [
        plain((doms, LANE), F32),
        plain((doms, LANE), F32),
        plain((1, 1), F32),
        Near(plain((rows_n, m_sec, LANE), BF16)),
        Near(plain((rows_n, m_first, LANE), BF16)),
        Near(plain((rows_n, m_sec, LANE), F32)),
        Near(plain((rows_n, m_first, LANE), F32)),
        Near(plain((rows_n, m_tow, LANE), BF16)),
        Near(plain((rows_n, m_tow, LANE), F32)),
        Near(plain((ce * hid_n, total_n), BF16)),
        Near(plain((ke, total_n), BF16)),
        Near(plain((dim, ce * hid_n), BF16)),
    ]
    scratch = [
        pltpu.VMEM((6 * doms, LANE, LANE), F32),
        pltpu.VMEM((LANE, LANE), F32),
        pltpu.VMEM((doms * th, total_n), BF16),
        pltpu.VMEM((doms * out_n, total_n), F32),
        pltpu.VMEM((ce * out_n, total_n), BF16),
        pltpu.VMEM((ke, total_n), F32),
        pltpu.VMEM((8, total_n), F32),
        pltpu.VMEM((2 * rows_n * m_tow, LANE), F32),
        pltpu.VMEM((ce * hid_n, dim), F32),
    ]

    def side_by_side(which):
        def pairs(refs, buf):
            return [(r.at[n], buf.at[:, i * own : (i + 1) * own]) for i, (r, (_, n)) in enumerate(zip(refs, acts))]

        arrays = [a[which] for a, _ in acts]
        return Far(arrays, (arrays[0].shape[1], total_n), pairs)

    ins = [Near(sums), Near(params), Near(tower), Near(marks)]
    ins += [Near(v) for v in low_towers]
    ins += [Far(wtower), side_by_side(3), side_by_side(2), Far(w2[0]), Far(w2[1], moved=True), side_by_side(1)]
    ins += [Far(inputs, (total_n, dim), row_blocks(list(range(ns)), own)), side_by_side(0), side_by_side(4)]

    def joined(refs, buf):
        slots = [(refs[e // epd].at[e % epd], e) for e in range(ce)]
        return [(ref, buf.at[:, e * hid_n : (e + 1) * hid_n]) for ref, e in slots]

    ins.append(Far(w1, pairs=joined, moved=[False, True], into=len(outs) - 1))
    return staged(body, ins, outs, scratch, "backward", 44)


def backward_inputs(pg, lg, w1, wgate_t, own):
    total_n = pg.shape[1]
    ns = total_n // own
    dim = w1.shape[0]
    ke = wgate_t.shape[0]

    def body(ins, outs):
        w1c, wgs, pgs, lgs = ins
        wg = jnp.concatenate([wgs.get()[...], jnp.zeros((LANE - ke, dim), BF16)], axis=0).T[:, :ke]
        pg, lg, w1c = pgs.get(), lgs.get(), w1c.get()
        for n in range(ns - 1, -1, -1):
            part = slice(n * own, (n + 1) * own)
            gi = mm(w1c[...], pg[:, part]) + mm(wg, lg[:, part])
            if n:
                outs[1].buf[n - 1] = gi.astype(BF16)
                outs[1].flush(n - 1)
            else:
                outs[0].buf[...] = gi
                outs[0].flush()

    return staged(
        body,
        [Near(w1), Near(wgate_t), Near(pg), Near(lg)],
        [Near(plain((dim, own), F32)), Near(plain((max(ns - 1, 1), dim, own), BF16))],
        [],
        "backward_inputs",
        16,
    )


def finish_inputs(own_part, received):
    dim, own = own_part.shape

    def body(ins, outs):
        for u in range(own // LANE):
            lanes = slice(u * LANE, (u + 1) * LANE)
            part = total(*(src.buf[:, lanes] for src in ins))
            outs[0].buf[lanes, :] = part.T
            outs[0].flush(pl.ds(u * LANE, LANE))

    return staged(
        body, [Near(own_part)] + [Near(v) for v in received], [plain((own, dim), F32)], [], "finish_inputs", 12
    )[0]


def finish_weights(second, first, other, epd, hid_n, out_n, dim, doms, exps, rows_n):
    m_sec, m_first, m_tow = layout(epd, hid_n, out_n, dim, doms, rows_n)
    ke = doms * exps

    def body(ins, outs, buf, tgf):
        out_f, out_s, out_t, out_g, out_h = (o.buf for o in outs)
        c = lax.rem(lax.axis_index(WIDTH), 2)
        r = lax.axis_index(ROWS)
        at_row = [spots(kind, r, rows_n) for kind in range(2)]
        for kind, size in ((0, m_sec), (1, m_first)):
            got = ins[kind].get()
            step = math.gcd(size, hid_n)
            for i, q, flat in pieces(kind, epd, hid_n, out_n, dim):
                for off in range(0, hid_n, step):
                    j, o = divmod(flat + off, size)
                    piece = got[at_row[kind][j], o : o + step, :].astype(F32)
                    if kind == 0:
                        out_s[i, off : off + step, q * LANE : (q + 1) * LANE] = piece
                    else:
                        buf[off : off + step, :] = piece
                if kind == 1:
                    out_f[i, q * LANE : (q + 1) * LANE, :] = buf[...].T
                if q == (out_n, dim)[kind] // LANE - 1:
                    outs[1 - kind].flush(i)
        near, sib = ins[1].get(), ins[2].get()
        for j in range(rows_n):
            at = at_row[1][j]
            for core, value in ((c, near[at, m_first:, :]), (1 - c, sib[at])):
                start = pl.multiple_of((core * rows_n + j) * m_tow, 8)
                tgf[pl.ds(start, m_tow), :] = value.astype(F32)
        for k in range(doms):
            out_t[k] = tgf[k * out_n : (k + 1) * out_n, :]
        outs[2].flush()
        for q in range(dim // LANE):
            at = doms * out_n + q * 32
            out_g[:, q * LANE : (q + 1) * LANE] = tgf[at : at + ke, :]
        outs[3].flush()
        out_h[...] = tgf[doms * out_n + ke : doms * out_n + ke + doms, :]
        outs[4].flush()

    return staged(
        body,
        [Near(second), Near(first), Near(other)],
        [
            plain((epd, dim, hid_n), F32),
            plain((epd, hid_n, out_n), F32),
            plain((doms, out_n, LANE), F32),
            plain((ke, dim), F32),
            plain((doms, LANE), F32),
        ],
        [pltpu.VMEM((hid_n, LANE), F32), pltpu.VMEM((2 * rows_n * m_tow, LANE), F32)],
        "finish_weights",
        16,
    )


def swap(value, axis, mask):
    size = lax.axis_size(axis)
    return lax.ppermute(value, axis, [(i, i ^ mask) for i in range(size)])


def total(*values):
    got = values[0].astype(F32)
    for value in values[1:]:
        got = got + value.astype(F32)
    return got


def send(value, axis, mask):
    return swap(value.astype(BF16), axis, mask)


together = lax.optimization_barrier


def reduce_rows(second, first, towers, beside):
    n_rows, n_width = lax.axis_size(ROWS), lax.axis_size(WIDTH)
    half = n_rows // 2
    far = [2 * q for q in range(1, half)]
    low = total(*(v[half:] for v in first)).astype(BF16)
    high = [total(*(v[m : m + 2] for v in second)).astype(BF16) for m in far]
    across = total(*towers).astype(BF16)
    first_got = swap(low, ROWS, 1)
    second_got = [swap(v, ROWS, m) for v, m in zip(high, far)]
    towers = total(*towers, *(swap(across, WIDTH, mask) for mask in range(2, n_width, 2)))
    tower_low, operand = together((towers[half:].astype(BF16), beside[1]))
    tower_got = swap(tower_low, ROWS, 1)
    inputs_part = tuple(beside[0](operand))
    first_got, second_got, tower_got, inputs_part = together((first_got, second_got, tower_got, inputs_part))

    def piece(q):
        return jnp.concatenate(
            [total(*(v[q] for v in first), first_got[q]), total(towers[q], tower_got[q])], axis=0
        )

    pair = total(*(v[:2] for v in second), *second_got)
    high = [piece(q).astype(BF16) for q in range(1, half)]
    high, low = together((high, pair.astype(BF16)))
    moved = [swap(v, ROWS, m) for v, m in zip(high, far)]
    moved, low = together((moved, swap(low, ROWS, 1)))
    pair = total(pair, low[::-1])
    return pair.astype(BF16), total(piece(0), *moved).astype(BF16), inputs_part


def gather_rows(pair, first, m_first, beside):
    half = lax.axis_size(ROWS) // 2
    far = [2 * q for q in range(1, half)]
    pair, first = together((pair, first))
    high, beside = together(([swap(first, ROWS, m) for m in far], beside))
    pair, evens = together((pair, jnp.stack([first] + high)))
    low, high = swap(evens, ROWS, 1), [swap(pair, ROWS, m) for m in far]
    other = swap(evens[:, m_first:], WIDTH, 1)
    other = [other, swap(other, ROWS, 1)]
    low, high, other, beside = together((low, high, other, finish_inputs(*beside)))
    second, first = jnp.concatenate([pair] + high), jnp.concatenate([evens, low])
    return second, first, jnp.concatenate(other), beside


def local(inputs, w_first, w_second, w_gate, w_tower, norm_scale, norm_shift, w_head, domains, labels):
    n_width, n_rows = lax.axis_size(WIDTH), lax.axis_size(ROWS)
    devices = n_width * n_rows
    own = inputs.shape[0] // n_width
    count = float(own * devices)
    dim = inputs.shape[1]
    epd, _, hid_n = w_first.shape
    out_n = w_second.shape[2]
    doms, _, exps = w_gate.shape
    ke = doms * exps
    n_x = n_width // 2
    others = list(range(1, n_x))
    w1 = (w_first, swap(w_first, WIDTH, 1))
    w2 = (w_second, swap(w_second, WIDTH, 1))
    wgate_t = jnp.transpose(w_gate, (0, 2, 1)).reshape(ke, dim)
    marks = jnp.stack([domains, labels])

    x_far, w1_own, w2_own, wt = prepare(others, inputs, w_first, w_second, wgate_t, w_tower, own)
    w1t, w2t = (w1_own, w1[1]), (w2_own, w2[1])
    far = forward([Near(x_far)], w1t, w2t, wt, own, doms, False, BF16, "forward_send")[0]
    sent = [swap(far[s - 1 : s], WIDTH, 2 * s) for s in others]
    blocks = [Far(inputs, (own, dim), row_blocks([0], own)), Near(x_far)]
    kept = forward(blocks, w1t, w2t, wt, own, doms, True, F32, "forward_keep")
    tower, low, message = combine(kept[5], sent, marks, devices)
    stats = lax.all_to_all(message, BOTH, 0, 0, tiled=True)
    stats, low = together((stats, low))
    lows = [swap(low, WIDTH, 2 * s) for s in others]
    params, message = normalise(stats, tower, marks, norm_scale, norm_shift, w_head, devices, count)
    sums = lax.all_to_all(message, BOTH, 0, 0, tiled=True)

    acts = [(kept[:5], s) for s in range(n_x)]
    grad_shift, grad_scale, loss, sec_sib, first_sib, sec_own, first_own, tow_sib, tow_own, pg, lg, w1_joined = backward(
        sums, params, tower, lows, marks, acts, inputs, w1, w2, wgate_t, w_tower, devices, n_rows, count
    )
    first_sib = swap(first_sib, WIDTH, 1)
    first_sib, sec_sib, tow_sib = together((first_sib, sec_sib, tow_sib))
    second, first, (gi_own, gi_out) = reduce_rows(
        (sec_own, swap(sec_sib, WIDTH, 1)),
        (first_own, first_sib),
        (tow_own, swap(tow_sib, WIDTH, 1)),
        (lambda grad: backward_inputs(grad, lg, w1_joined, wgate_t, own), pg),
    )
    inputs_got = [swap(gi_out[s - 1], WIDTH, 2 * s) for s in others]
    m_first = layout(epd, hid_n, out_n, dim, doms, n_rows)[1]
    second, first, other, grad_inputs = gather_rows(second, first, m_first, (gi_own, inputs_got))
    grad_first, grad_second, grad_tower, grad_gate, grad_head = finish_weights(
        second, first, other, epd, hid_n, out_n, dim, doms, exps, n_rows
    )
    return (
        loss[0, 0],
        grad_inputs,
        grad_first,
        grad_second,
        grad_gate.reshape(doms, exps, dim).transpose(0, 2, 1),
        grad_tower,
        grad_scale,
        grad_shift,
        grad_head,
    )


def solution(mesh):
    placed = (
        P(ROWS, None),
        P(WIDTH, None, None),
        P(WIDTH, None, None),
        P(),
        P(),
        P(),
        P(),
        P(),
        P(BOTH),
        P(BOTH),
    )
    return jax.shard_map(
        local,
        mesh=mesh,
        in_specs=placed,
        out_specs=(
            P(),
            P(BOTH, None),
            P(WIDTH, None, None),
            P(WIDTH, None, None),
            P(),
            P(),
            P(),
            P(),
            P(),
        ),
        check_vma=False,
    )
```

```python
import math

import jax
import jax.numpy as jnp
from jax import lax
from jax.experimental import pallas as pl
from jax.experimental.pallas import tpu as pltpu
from jax.sharding import PartitionSpec as P

F32 = jnp.float32
BF16 = jnp.bfloat16
EPS = 1e-05
LANE = 128
MIB = 1 << 20
ROWS = "rows"
WIDTH = "width"
BOTH = (ROWS, WIDTH)


def mm(a, b):
    return jnp.dot(a, b, preferred_element_type=F32)


def mm_t(a, b):
    return lax.dot_general(a, b, (((1,), (1,)), ((), ())), preferred_element_type=F32)


def sigmoid(v):
    return 0.5 * jnp.tanh(0.5 * v) + 0.5


PLAIN = 8


def base(values):
    first = values[:, :PLAIN].astype(BF16).astype(F32)
    return jnp.sum(first, axis=1, keepdims=True) * (1.0 / PLAIN)


def encode(values):
    lane = lax.broadcasted_iota(jnp.int32, values.shape, 1)
    return jnp.where(lane < PLAIN, values, values - base(values)).astype(BF16)


def decode(values, added, start=0):
    lane = lax.broadcasted_iota(jnp.int32, values.shape, 1)
    values = values.astype(F32)
    return jnp.where(lane < PLAIN - start, values, values + added)


class Source:
    def __init__(self, buf, copies):
        self.buf = buf
        self.waiting = copies
        for copy in copies:
            copy.start()

    def get(self):
        for copy in self.waiting:
            copy.wait()
        self.waiting = []
        return self.buf


class Target:
    def __init__(self, ref, buf, sems):
        self.ref, self.buf, self.sems = ref, buf, sems
        self.waiting = []

    def flush(self, *at):
        if self.ref is None:
            return
        src = self.buf.at[at] if at else self.buf
        dst = self.ref.at[at] if at else self.ref
        copy = pltpu.make_async_copy(src, dst, next(self.sems))
        copy.start()
        self.waiting.append(copy)


class Near:
    def __init__(self, what):
        self.what = what


class Far:
    def __init__(self, arrays, shape=None, pairs=None, moved=False, into=None):
        self.into = into
        self.arrays = arrays if isinstance(arrays, (list, tuple)) else [arrays]
        self.moved = moved if isinstance(moved, list) else [moved] * len(self.arrays)
        self.shape = shape or self.arrays[0].shape
        self.dtype = self.arrays[0].dtype
        self.pairs = pairs or (lambda refs, buf: [(refs[0], buf)])


def staged(body, ins, outs, scratch, name, limit, n_sems=64):
    far_in = [i for i, s in enumerate(ins) if isinstance(s, Far) and s.into is None]
    far_out = [i for i, s in enumerate(outs) if not isinstance(s, Near)]
    args, specs, spans = [], [], []
    hbm = pl.BlockSpec(memory_space=pltpu.HBM)
    vmem = pl.BlockSpec(memory_space=pltpu.VMEM)
    anywhere = pl.BlockSpec(memory_space=pl.ANY)
    for s in ins:
        if isinstance(s, Far):
            spans.append((len(args), len(args) + len(s.arrays)))
            for a, moved in zip(s.arrays, s.moved):
                args.append(a if moved else pltpu.with_memory_space_constraint(a, pltpu.HBM))
                specs.append(anywhere if moved else hbm)
        else:
            spans.append((len(args), len(args) + 1))
            args.append(s.what)
            specs.append(vmem)
    n_in, n_out = len(args), len(outs)

    def kernel(*refs):
        refs_in, refs_out = refs[:n_in], refs[n_in : n_in + n_out]
        bufs = refs[n_in + n_out :]
        in_bufs = dict(zip(far_in, bufs))
        in_bufs.update({i: refs_out[s.into] for i, s in enumerate(ins) if isinstance(s, Far) and s.into is not None})
        out_bufs = dict(zip(far_out, bufs[len(far_in) :]))
        rest = bufs[len(far_in) + len(far_out) : -1]
        sems = iter([bufs[-1].at[i] for i in range(n_sems)])
        sources = []
        for i, (start, stop) in enumerate(spans):
            if i in in_bufs:
                pairs = ins[i].pairs(refs_in[start:stop], in_bufs[i])
                sources.append(Source(in_bufs[i], [pltpu.make_async_copy(a, b, next(sems)) for a, b in pairs]))
            else:
                sources.append(Source(refs_in[start], []))
        targets = []
        for i, ref in enumerate(refs_out):
            targets.append(Target(ref, out_bufs[i], sems) if i in out_bufs else Target(None, ref, sems))
        body(sources, targets, *rest)
        for s in sources:
            s.get()
        for t in targets:
            for copy in t.waiting:
                copy.wait()

    return pl.pallas_call(
        kernel,
        out_shape=[o.what if isinstance(o, Near) else pltpu.HBM(o.shape, o.dtype) for o in outs],
        in_specs=specs,
        out_specs=[hbm if i in far_out else vmem for i in range(n_out)],
        scratch_shapes=[pltpu.VMEM(ins[i].shape, ins[i].dtype) for i in far_in]
        + [pltpu.VMEM(outs[i].shape, outs[i].dtype) for i in far_out]
        + list(scratch)
        + [pltpu.SemaphoreType.DMA((n_sems,))],
        compiler_params=pltpu.CompilerParams(vmem_limit_bytes=limit * MIB),
        name=name,
    )(*args)


def plain(shape, dtype):
    return jax.ShapeDtypeStruct(shape, dtype)


def row_blocks(slots, own):
    def pairs(refs, buf):
        w = lax.axis_index(WIDTH)
        got = []
        for n, s in enumerate(slots):
            start = pl.multiple_of(lax.bitwise_xor(w, 2 * s) * own, own)
            got.append((refs[0].at[pl.ds(start, own), :], buf.at[n * own : (n + 1) * own, :]))
        return got

    return pairs


def reorder(ke, epd):
    first = lax.axis_index(WIDTH) * epd
    down = lax.broadcasted_iota(jnp.int32, (ke, ke), 0)
    across = lax.broadcasted_iota(jnp.int32, (ke, ke), 1)
    return jnp.where(lax.bitwise_xor(down, first) == across, 1.0, 0.0).astype(BF16)


def prepare(slots, inputs, w1, w2, wgate_t, wtower, own):
    dim = inputs.shape[1]
    epd, _, hid_n = w1.shape
    out_n = w2.shape[2]
    ke = wgate_t.shape[0]
    doms, _, th = wtower.shape

    def body(ins, outs):
        w1s, wgs, w2s, wts, _ = ins
        _, w1t, w2t, wt = (o.buf for o in outs)
        w1_buf = w1s.get()
        for i in range(epd):
            w1t[i * hid_n : (i + 1) * hid_n, :] = w1_buf[i].T
        w1t[epd * hid_n :, :] = mm(reorder(ke, epd), wgs.get()[...]).astype(BF16)
        w2_buf = w2s.get()
        for i in range(epd):
            w2t[i] = w2_buf[i].T
        wt_buf = wts.get()
        for k in range(doms):
            wt[k] = wt_buf[k].T
    return staged(
        body,
        [Far(a) for a in (w1, wgate_t, w2, wtower)]
        + [Far(inputs, (len(slots) * own, dim), row_blocks(slots, own), into=0)],
        [
            Near(plain((len(slots) * own, dim), BF16)),
            Near(plain((epd * hid_n + ke, dim), BF16)),
            Near(plain((epd, out_n, hid_n), BF16)),
            Near(plain((doms, th, out_n), BF16)),
        ],
        [],
        "prepare",
        12,
    )


def forward(blocks, w1, w2, wt, own, doms, keep, tower_out, name):
    epd, dim, hid_n = w1[1].shape
    out_n = w2[1].shape[2]
    ce = 2 * epd
    half = epd * hid_n
    ke = w1[0].shape[0] - half
    th = wt.shape[1]
    exps = ke // doms
    sizes = [(b.what if isinstance(b, Near) else b).shape[0] // own for b in blocks]
    ns = sum(sizes)

    def body(ins, outs, w1t, w2t, pre, *bufs):
        xs = ins[: len(blocks)]
        w1o, w1s, w2o, w2s, wts = ins[len(blocks) :]
        if keep:
            hid, slope, vals, gate, mixed = (o.buf for o in outs[:5])
        else:
            hid, vals, gate = bufs
        wt = wts.get()
        for i in range(epd):
            w1t[i * hid_n : (i + 1) * hid_n, :] = w1s.get()[i].T
            w2t[i] = w2s.get()[i].T
        parts = [(src, n) for src, size in zip(xs, sizes) for n in range(size)]
        for n, (src, place) in enumerate(parts):
            x = src.get()[place * own : (place + 1) * own, :]
            got = mm_t(w1o.get()[...], x)
            pre[:half, :] = got[:half]
            pre[ce * hid_n :, :] = got[half:]
            pre[half : ce * hid_n, :] = mm_t(w1t[...], x)
            logits = pre[ce * hid_n : ce * hid_n + ke, :].reshape(doms, exps, own)
            top = jnp.exp(logits - jnp.max(logits, axis=1, keepdims=True))
            soft = top / jnp.sum(top, axis=1, keepdims=True)
            gate[n] = soft.reshape(ke, own)

            def act(i, carry):
                at = pl.ds(pl.multiple_of(i * 16, 16), 16)
                v = pre[at, :]
                s = sigmoid(v)
                h = v * s
                hid[n, at, :] = h.astype(BF16)
                if keep:
                    slope[n, at, :] = (s + h * (1.0 - s)).astype(BF16)
                return carry

            lax.fori_loop(0, ce * hid_n // 16, act, 0, unroll=4 if keep else ce * hid_n // 16)
            for e in range(ce):
                w = w2o.get()[e] if e < epd else w2t[e - epd]
                vals[n, e * out_n : (e + 1) * out_n, :] = mm(w, hid[n, e * hid_n : (e + 1) * hid_n, :]).astype(BF16)
            if not keep:
                tower = outs[-1]
                for k in range(doms):
                    sums = None
                    for e in range(ce):
                        term = mm(wt[k], vals[n, e * out_n : (e + 1) * out_n, :])
                        term = gate[n, k * exps + e : k * exps + e + 1, :] * term
                        sums = term if e == 0 else sums + term
                    tower.buf[n, k * th : (k + 1) * th, :] = encode(sums)
                tower.flush(n)
                continue
            for o in outs[:4]:
                o.flush(n)
            for u in range(own // LANE):
                part = slice(u * LANE, (u + 1) * LANE)
                rows = [[gate[n, k * exps + e : k * exps + e + 1, part] for e in range(ce)] for k in range(doms)]

                def mix(i, carry):
                    acc = [None] * doms
                    for e in range(ce):
                        at = pl.ds(pl.multiple_of(e * out_n + i * 32, 32), 32)
                        v = vals[n, at, part].astype(F32)
                        for k in range(doms):
                            term = rows[k][e] * v
                            acc[k] = term if e == 0 else acc[k] + term
                    for k in range(doms):
                        at = pl.ds(pl.multiple_of(k * out_n + i * 32, 32), 32)
                        mixed[n, at, part] = acc[k].astype(BF16)
                    return carry

                lax.fori_loop(0, out_n // 32, mix, 0, unroll=4)
            outs[4].flush(n)
            if n == 0:
                tower = outs[-1]
                for k in range(doms):
                    tower.buf[n, k * th : (k + 1) * th, :] = mm(wt[k], mixed[n, k * out_n : (k + 1) * out_n, :])
                tower.flush(n)

    kept = [
        plain((ns, ce * hid_n, own), BF16),
        plain((ns, ce * hid_n, own), BF16),
        plain((ns, ce * out_n, own), BF16),
        plain((ns, ke, own), F32),
        plain((ns, doms * out_n, own), BF16),
    ]
    outs = list(kept) if keep else []
    outs.append(Near(plain((1 if keep else ns, doms * th, own), tower_out)))
    scratch = [
        pltpu.VMEM((half, dim), BF16),
        pltpu.VMEM((epd, out_n, hid_n), BF16),
        pltpu.VMEM((ce * hid_n + ke, own), F32),
    ]
    if not keep:
        scratch += [pltpu.VMEM(kept[i].shape, kept[i].dtype) for i in (0, 2, 3)]
    ins = blocks + [Near(a) for a in (w1[0], w1[1], w2[0], w2[1], wt)]
    return staged(body, ins, outs, scratch, name, 40)


def combine(own_part, received, marks, devices):
    _, rows, own = own_part.shape
    doms = rows // LANE

    def body(ins, outs, cols):
        part = ins[0].get()
        got = [s.get() for s in ins[2:]]
        tower, low, message = (o.buf for o in outs)
        cols[...] = jnp.zeros_like(cols)
        for k in range(doms):
            at = slice(k * LANE, (k + 1) * LANE)
            total = part[0, at, :]
            for ref in got:
                total = total + decode(ref[0, at, :], base(ref[0, at, :LANE]))
            tower[at, :] = total
            low[at, :] = encode(total)
            mean = jnp.sum(total, axis=1, keepdims=True) * (1.0 / own)
            dev = total - mean
            cols[:, k : k + 1] = mean
            cols[:, doms + k : doms + k + 1] = jnp.sum(dev * dev, axis=1, keepdims=True)
        outs[0].flush()
        pair = jnp.concatenate([ins[1].get()[...].astype(F32), jnp.zeros((14, own), F32)], axis=0)
        low[rows:, :] = pair.astype(BF16)
        outs[1].flush()
        tile = cols[...].T[:8, :]
        for d in range(devices):
            message[d * 8 : (d + 1) * 8, :] = tile
        outs[2].flush()

    return staged(
        body,
        [Near(own_part), Near(marks)] + [Near(v) for v in received],
        [Near(plain((rows, own), F32)), Near(plain((rows + 16, own), BF16)), Near(plain((devices * 8, LANE), F32))],
        [pltpu.VMEM((LANE, LANE), F32)],
        "combine",
        16,
    )


def pick(dom, values):
    got = values[-1]
    for k in range(len(values) - 2, -1, -1):
        got = jnp.where(dom == k, values[k], got)
    return got


def chosen_tower(values, dom, wide, doms):
    mean, gain, shift, head = (pick(dom, [wide[j * doms + k] for k in range(doms)]) for j in range(4))
    centred = pick(dom, values) - mean
    return centred, centred * gain + shift, gain, head


def spread_columns(wide, rows_ref, n):
    cols = rows_ref[...].T
    for j in range(n):
        wide[j] = jnp.broadcast_to(cols[:, j : j + 1], (LANE, LANE))


def normalise(stats, tower, marks, scale, shift, head, devices, count):
    rows, own = tower.shape
    doms = rows // LANE

    def body(ins, outs, prm, wide, q):
        st, tws, mks, sc, sh, hd = ins
        params, message = (o.buf for o in outs)
        prm[...] = jnp.zeros_like(prm)
        got = st.get()[...].reshape(devices, 8, LANE)
        total = jnp.sum(got, axis=0)
        mean = total * (1.0 / devices)
        dev = got - mean[None]
        spread = jnp.sum(dev * dev, axis=0) * float(own)
        var = (total[doms : 2 * doms] + spread[:doms]) * (1.0 / count)
        inv = lax.rsqrt(var + EPS)
        prm[0:doms, :] = mean[:doms]
        prm[doms : 2 * doms, :] = inv * sc.get()[...]
        prm[2 * doms : 3 * doms, :] = sh.get()[...]
        prm[3 * doms : 4 * doms, :] = hd.get()[...]
        prm[4 * doms : 5 * doms, :] = inv
        params[:16, :] = prm[:16, :]
        spread_columns(wide, prm, 4 * doms)
        tw, mk = tws.get(), mks.get()
        loss = jnp.zeros((1, LANE), F32)
        for u in range(own // LANE):
            part = slice(u * LANE, (u + 1) * LANE)
            dom = mk[0:1, part]
            target = mk[1:2, part].astype(F32)
            values = [tw[k * LANE : (k + 1) * LANE, part] for k in range(doms)]
            centred, affine, _, head_w = chosen_tower(values, dom, wide, doms)
            s = sigmoid(affine)
            act = affine * s
            chosen = jnp.sum(act * head_w, axis=0, keepdims=True)
            soft = jnp.maximum(chosen, 0.0) + jnp.log(1.0 + jnp.exp(-jnp.abs(chosen)))
            loss = loss + (soft - target * chosen)
            score_grad = (sigmoid(chosen) - target) * (1.0 / count)
            grad = score_grad * head_w * (s + act * (1.0 - s))
            q[0:LANE, part] = grad
            q[LANE : 2 * LANE, part] = grad * centred
            q[2 * LANE :, part] = score_grad * act
        kinds = lax.broadcasted_iota(jnp.int32, (8, own), 0)
        one_hot = (kinds == mk[0:1, :]).astype(F32).astype(BF16)
        high = q[...].astype(BF16)
        sums = (mm_t(one_hot, high) + mm_t(one_hot, (q[...] - high.astype(F32)).astype(BF16)))[:doms]
        tile = [sums[:, :LANE], sums[:, LANE : 2 * LANE] * inv]
        all_rows = tile + [loss, jnp.zeros((1, LANE), F32)]
        all_rows = jnp.concatenate(all_rows, axis=0)
        for d in range(devices):
            message[d * 8 : (d + 1) * 8, :] = all_rows
        params[16:, :] = jnp.concatenate([sums[:, 2 * LANE :], jnp.zeros((8 - doms, LANE), F32)], axis=0)
        outs[0].flush()

    return staged(
        body,
        [Near(v) for v in (stats, tower, marks, scale, shift, head)],
        [Near(plain((24, LANE), F32)), Near(plain((devices * 8, LANE), F32))],
        [
            pltpu.VMEM((LANE, LANE), F32),
            pltpu.VMEM((4 * doms, LANE, LANE), F32),
            pltpu.VMEM((3 * LANE, own), F32),
        ],
        "normalise",
        16,
    )


def layout(epd, hid_n, out_n, dim, doms, rows_n):
    second = epd * hid_n * out_n // LANE
    first = epd * hid_n * dim // LANE
    towers = -(-(doms * out_n + (dim // LANE) * 32) // (2 * 16 * rows_n)) * 16
    return second // rows_n, first // rows_n, towers


def pieces(kind, epd, hid_n, out_n, dim):
    flat = 0
    for i in range(epd):
        for q in range((out_n, dim)[kind] // LANE):
            yield i, q, flat
            flat += hid_n


def spots(kind, row, rows_n):
    got = []
    for j in range(rows_n):
        p = lax.bitwise_xor(row, j)
        got.append(p if kind == 0 else (p & 1) * (rows_n // 2) + lax.shift_right_logical(p, 1))
    return got


def backward(
    sums, params, tower, low_towers, marks, acts, inputs, w1, w2, wgate_t, wtower, devices, rows_n, count
):
    ns = 1 + len(low_towers)
    t_rows, own = tower.shape
    total_n = ns * own
    dim = inputs.shape[1]
    epd, hid_n, out_n = w2[0].shape
    ce = 2 * epd
    ke = wgate_t.shape[0]
    doms, _, th = wtower.shape
    exps = ke // doms
    m_sec, m_first, m_tow = layout(epd, hid_n, out_n, dim, doms, rows_n)

    def body(ins, outs, wide, prm, tg, mg, eg, gg, srow, tgf, facc):
        sm, pr, tw0, mk0 = ins[:4]
        low = ins[4 : 3 + ns]
        wts, gate, vals, w2o, w2s, slope, xs, hid, mixed, _ = ins[3 + ns :]
        shift_out, scale_out, loss_out, sec_sib, first_sib, sec_mine, first_mine, tow_sib, tow_mine, pgs, lgs, _ = outs
        pg, lg = pgs.buf, lgs.buf
        c = lax.rem(lax.axis_index(WIDTH), 2)
        r = lax.axis_index(ROWS)
        at_row = [spots(kind, r, rows_n) for kind in range(2)]
        prm[...] = jnp.zeros_like(prm)
        total = jnp.sum(sm.get()[...].reshape(devices, 8, LANE), axis=0)
        shift_out.buf[...] = total[:doms]
        scale_out.buf[...] = total[doms : 2 * doms]
        loss_out.buf[...] = jnp.sum(total[2 * doms : 2 * doms + 1, :], axis=1, keepdims=True) * (1.0 / count)
        for target in (shift_out, scale_out, loss_out):
            target.flush()
        given = pr.get()[...]
        gain, inv = given[doms : 2 * doms], given[4 * doms : 5 * doms]
        prm[0:16, :] = given[:16]
        prm[4 * doms : 5 * doms, :] = gain * total[:doms] * (1.0 / count)
        prm[5 * doms : 6 * doms, :] = gain * inv * total[doms : 2 * doms] * (1.0 / count)
        spread_columns(wide, prm, 6 * doms)
        for u in range(total_n // LANE):
            n = u * LANE // own
            part = slice(u * LANE, (u + 1) * LANE)
            here = slice(u * LANE - n * own, (u + 1) * LANE - n * own)
            if n == 0:
                tw = tw0.get()
                dom = mk0.get()[0:1, here]
                target = mk0.get()[1:2, here].astype(F32)
            else:
                tw = low[n - 1].get()
                pair = tw[t_rows : t_rows + 16, here].astype(F32)
                dom = pair[0:1].astype(jnp.int32)
                target = pair[1:2]
            values = [tw[k * LANE : (k + 1) * LANE, here] for k in range(doms)]
            if n:
                if here.start == 0:
                    added = [jnp.broadcast_to(base(v), (LANE, LANE)) for v in values]
                values = [decode(v, a, here.start) for v, a in zip(values, added)]
            _, affine, gain_s, head_w = chosen_tower(values, dom, wide, doms)
            s = sigmoid(affine)
            act = affine * s
            chosen = jnp.sum(act * head_w, axis=0, keepdims=True)
            score_grad = (sigmoid(chosen) - target) * (1.0 / count)
            grad = gain_s * (score_grad * head_w * (s + act * (1.0 - s)))
            for k in range(doms):
                v = jnp.where(dom == k, grad, 0.0) - wide[4 * doms + k]
                v = v - (values[k] - wide[k]) * wide[5 * doms + k]
                down = v.astype(BF16)
                tg[k * th : (k + 1) * th, part] = down
                srow[k : k + 1, part] = jnp.sum(down.astype(F32) * values[k], axis=0, keepdims=True)
        wt = wts.get()
        for k in range(doms):
            mg[k * out_n : (k + 1) * out_n, :] = mm(wt[k], tg[k * th : (k + 1) * th, :])
        vals, gate = vals.get(), gate.get()
        gg[...] = jnp.zeros_like(gg)

        def tower_part(k):
            tgf[k * out_n : (k + 1) * out_n, :] = mm_t(
                mixed.get()[k * out_n : (k + 1) * out_n, :], tg[k * th : (k + 1) * th, :]
            )

        def hidden_part(n, e):
            at = slice(e * hid_n, (e + 1) * hid_n)
            part = slice(n * own, (n + 1) * own)
            w = (w2o, w2s)[e // epd].get()[e % epd]
            grad = mm(w, eg[e * out_n : (e + 1) * out_n, part])
            pg[at, part] = (grad * slope.get()[at, part].astype(F32)).astype(BF16)

        ready = []
        for u in range(total_n // LANE):
            part = slice(u * LANE, (u + 1) * LANE)
            rows = [[gate[k * exps + e : k * exps + e + 1, part] for e in range(ce)] for k in range(doms)]

            def spread(i, acc):
                up = [mg[pl.ds(pl.multiple_of(k * out_n + i * 16, 16), 16), part] for k in range(doms)]
                acc = list(acc)
                for e in range(ce):
                    at = pl.ds(pl.multiple_of(e * out_n + i * 16, 16), 16)
                    v = vals[at, part].astype(F32)
                    back = None
                    for k in range(doms):
                        term = rows[k][e] * up[k]
                        back = term if k == 0 else back + term
                        prod = up[k] * v
                        acc[k * ce + e] = acc[k * ce + e] + (prod[:8] + prod[8:])
                    eg[at, part] = back.astype(BF16)
                return tuple(acc)

            zero = jnp.zeros((8, LANE), F32)
            acc = lax.fori_loop(0, out_n // 16, spread, (zero,) * (doms * ce), unroll=out_n // 16)
            for k in range(doms):
                for e in range(ce):
                    gg[k * exps + e : k * exps + e + 1, part] = jnp.sum(acc[k * ce + e], axis=0, keepdims=True)
            if (u + 1) * LANE % own == 0:
                ready += [(hidden_part, (u * LANE // own, e)) for e in range(ce)]
            if ready:
                task, args = ready.pop(0)
                task(*args)
        for task, args in ready:
            task(*args)
        pgs.flush()
        here = lax.broadcasted_iota(jnp.int32, (exps, total_n), 0) < ce
        for k in range(doms):
            at = slice(k * exps, (k + 1) * exps)
            gg[at, :] = jnp.where(here, gate[at, :] * (gg[at, :] - srow[k : k + 1, :]), 0.0)
        lg[...] = mm(reorder(ke, epd), gg[...].astype(BF16)).astype(BF16)
        lgs.flush()
        hid = hid.get()

        def put(kind, slot, values):
            target = ((sec_sib, first_sib), (sec_mine, first_mine))[slot < epd][kind]
            size = (m_sec, m_first)[kind]
            step = math.gcd(size, hid_n)
            for i, q, flat in pieces(kind, epd, hid_n, out_n, dim):
                if i == slot % epd:
                    for off in range(0, hid_n, step):
                        j, o = divmod(flat + off, size)
                        part = values[off : off + step, q * LANE : (q + 1) * LANE]
                        target.buf[at_row[kind][j], o : o + step, :] = part.astype(target.buf.dtype)

        x = xs.get()
        facc[...] = mm(pg[...], x[...])
        for e in range(ce):
            put(1, e, facc[e * hid_n : (e + 1) * hid_n, :])
        for e in range(ce):
            at = slice(e * hid_n, (e + 1) * hid_n)
            at_o = slice(e * out_n, (e + 1) * out_n)
            put(0, e, mm_t(hid[at, :], eg[at_o, :]))
        for target in (sec_sib, first_sib, sec_mine, first_mine):
            target.flush()
        for k in range(doms):
            tower_part(k)
        tgf[doms * out_n :, :] = jnp.zeros((tgf.shape[0] - doms * out_n, LANE), F32)
        part_g = mm(lg[...], x[...])
        for q in range(dim // LANE):
            tgf[doms * out_n + q * 32 : doms * out_n + q * 32 + ke, :] = part_g[:, q * LANE : (q + 1) * LANE]
        tgf[doms * out_n + ke : doms * out_n + 32, :] = given[16 : 48 - ke]
        for target, core in ((tow_sib, 1 - c), (tow_mine, c)):
            for j in range(rows_n):
                start = pl.multiple_of((core * rows_n + j) * m_tow, 8)
                target.buf[at_row[1][j], :, :] = tgf[pl.ds(start, m_tow), :].astype(target.buf.dtype)
            target.flush()

    outs = [
        plain((doms, LANE), F32),
        plain((doms, LANE), F32),
        plain((1, 1), F32),
        Near(plain((rows_n, m_sec, LANE), BF16)),
        Near(plain((rows_n, m_first, LANE), BF16)),
        Near(plain((rows_n, m_sec, LANE), F32)),
        Near(plain((rows_n, m_first, LANE), F32)),
        Near(plain((rows_n, m_tow, LANE), BF16)),
        Near(plain((rows_n, m_tow, LANE), F32)),
        Near(plain((ce * hid_n, total_n), BF16)),
        Near(plain((ke, total_n), BF16)),
        Near(plain((dim, ce * hid_n), BF16)),
    ]
    scratch = [
        pltpu.VMEM((6 * doms, LANE, LANE), F32),
        pltpu.VMEM((LANE, LANE), F32),
        pltpu.VMEM((doms * th, total_n), BF16),
        pltpu.VMEM((doms * out_n, total_n), F32),
        pltpu.VMEM((ce * out_n, total_n), BF16),
        pltpu.VMEM((ke, total_n), F32),
        pltpu.VMEM((8, total_n), F32),
        pltpu.VMEM((2 * rows_n * m_tow, LANE), F32),
        pltpu.VMEM((ce * hid_n, dim), F32),
    ]

    def side_by_side(which):
        def pairs(refs, buf):
            return [(r.at[n], buf.at[:, i * own : (i + 1) * own]) for i, (r, (_, n)) in enumerate(zip(refs, acts))]

        arrays = [a[which] for a, _ in acts]
        return Far(arrays, (arrays[0].shape[1], total_n), pairs)

    ins = [Near(sums), Near(params), Near(tower), Near(marks)]
    ins += [Near(v) for v in low_towers]
    ins += [Near(wtower), side_by_side(3), side_by_side(2), Near(w2[0]), Far(w2[1], moved=True), side_by_side(1)]
    ins += [Far(inputs, (total_n, dim), row_blocks(list(range(ns)), own)), side_by_side(0), side_by_side(4)]

    def joined(refs, buf):
        slots = [(refs[e // epd].at[e % epd], e) for e in range(ce)]
        return [(ref, buf.at[:, e * hid_n : (e + 1) * hid_n]) for ref, e in slots]

    ins.append(Far(w1, pairs=joined, moved=[False, True], into=len(outs) - 1))
    return staged(body, ins, outs, scratch, "backward", 44)


def backward_inputs(pg, lg, w1, wgate_t, own):
    total_n = pg.shape[1]
    ns = total_n // own
    dim = w1.shape[0]
    ke = wgate_t.shape[0]

    def body(ins, outs):
        w1c, wgs, pgs, lgs = ins
        wg = jnp.concatenate([wgs.get()[...], jnp.zeros((LANE - ke, dim), BF16)], axis=0).T[:, :ke]
        pg, lg, w1c = pgs.get(), lgs.get(), w1c.get()
        for n in range(ns - 1, -1, -1):
            part = slice(n * own, (n + 1) * own)
            gi = mm(w1c[...], pg[:, part]) + mm(wg, lg[:, part])
            if n:
                outs[1].buf[n - 1] = gi.astype(BF16)
                outs[1].flush(n - 1)
            else:
                outs[0].buf[...] = gi
                outs[0].flush()

    return staged(
        body,
        [Near(w1), Near(wgate_t), Near(pg), Near(lg)],
        [Near(plain((dim, own), F32)), Near(plain((max(ns - 1, 1), dim, own), BF16))],
        [],
        "backward_inputs",
        16,
    )


def finish_inputs(own_part, received):
    dim, own = own_part.shape

    def body(ins, outs):
        for u in range(own // LANE):
            lanes = slice(u * LANE, (u + 1) * LANE)
            part = total(*(src.buf[:, lanes] for src in ins))
            outs[0].buf[lanes, :] = part.T
            outs[0].flush(pl.ds(u * LANE, LANE))

    return staged(
        body, [Near(own_part)] + [Near(v) for v in received], [plain((own, dim), F32)], [], "finish_inputs", 12
    )[0]


def finish_weights(second, first, other, epd, hid_n, out_n, dim, doms, exps, rows_n):
    m_sec, m_first, m_tow = layout(epd, hid_n, out_n, dim, doms, rows_n)
    ke = doms * exps

    def body(ins, outs, buf, tgf):
        out_f, out_s, out_t, out_g, out_h = (o.buf for o in outs)
        c = lax.rem(lax.axis_index(WIDTH), 2)
        r = lax.axis_index(ROWS)
        at_row = [spots(kind, r, rows_n) for kind in range(2)]
        for kind, size in ((0, m_sec), (1, m_first)):
            got = ins[kind].get()
            step = math.gcd(size, hid_n)
            for i, q, flat in pieces(kind, epd, hid_n, out_n, dim):
                for off in range(0, hid_n, step):
                    j, o = divmod(flat + off, size)
                    piece = got[at_row[kind][j], o : o + step, :].astype(F32)
                    if kind == 0:
                        out_s[i, off : off + step, q * LANE : (q + 1) * LANE] = piece
                    else:
                        buf[off : off + step, :] = piece
                if kind == 1:
                    out_f[i, q * LANE : (q + 1) * LANE, :] = buf[...].T
                if q == (out_n, dim)[kind] // LANE - 1:
                    outs[1 - kind].flush(i)
        near, sib = ins[1].get(), ins[2].get()
        for j in range(rows_n):
            at = at_row[1][j]
            for core, value in ((c, near[at, m_first:, :]), (1 - c, sib[at])):
                start = pl.multiple_of((core * rows_n + j) * m_tow, 8)
                tgf[pl.ds(start, m_tow), :] = value.astype(F32)
        for k in range(doms):
            out_t[k] = tgf[k * out_n : (k + 1) * out_n, :]
        outs[2].flush()
        for q in range(dim // LANE):
            at = doms * out_n + q * 32
            out_g[:, q * LANE : (q + 1) * LANE] = tgf[at : at + ke, :]
        outs[3].flush()
        out_h[...] = tgf[doms * out_n + ke : doms * out_n + ke + doms, :]
        outs[4].flush()

    return staged(
        body,
        [Near(second), Near(first), Near(other)],
        [
            plain((epd, dim, hid_n), F32),
            plain((epd, hid_n, out_n), F32),
            plain((doms, out_n, LANE), F32),
            plain((ke, dim), F32),
            plain((doms, LANE), F32),
        ],
        [pltpu.VMEM((hid_n, LANE), F32), pltpu.VMEM((2 * rows_n * m_tow, LANE), F32)],
        "finish_weights",
        16,
    )


def swap(value, axis, mask):
    size = lax.axis_size(axis)
    return lax.ppermute(value, axis, [(i, i ^ mask) for i in range(size)])


def total(*values):
    got = values[0].astype(F32)
    for value in values[1:]:
        got = got + value.astype(F32)
    return got


def send(value, axis, mask):
    return swap(value.astype(BF16), axis, mask)


together = lax.optimization_barrier


def reduce_rows(second, first, towers, beside):
    n_rows, n_width = lax.axis_size(ROWS), lax.axis_size(WIDTH)
    half = n_rows // 2
    far = [2 * q for q in range(1, half)]
    low = total(*(v[half:] for v in first)).astype(BF16)
    high = [total(*(v[m : m + 2] for v in second)).astype(BF16) for m in far]
    across = total(*towers).astype(BF16)
    first_got = swap(low, ROWS, 1)
    second_got = [swap(v, ROWS, m) for v, m in zip(high, far)]
    towers = total(*towers, *(swap(across, WIDTH, mask) for mask in range(2, n_width, 2)))
    tower_low, operand = together((towers[half:].astype(BF16), beside[1]))
    tower_got = swap(tower_low, ROWS, 1)
    inputs_part = tuple(beside[0](operand))
    first_got, second_got, tower_got, inputs_part = together((first_got, second_got, tower_got, inputs_part))

    def piece(q):
        return jnp.concatenate(
            [total(*(v[q] for v in first), first_got[q]), total(towers[q], tower_got[q])], axis=0
        )

    pair = total(*(v[:2] for v in second), *second_got)
    high = [piece(q).astype(BF16) for q in range(1, half)]
    high, low = together((high, pair.astype(BF16)))
    moved = [swap(v, ROWS, m) for v, m in zip(high, far)]
    moved, low = together((moved, swap(low, ROWS, 1)))
    pair = total(pair, low[::-1])
    return pair.astype(BF16), total(piece(0), *moved).astype(BF16), inputs_part


def gather_rows(pair, first, m_first, beside):
    half = lax.axis_size(ROWS) // 2
    far = [2 * q for q in range(1, half)]
    pair, first = together((pair, first))
    high, beside = together(([swap(first, ROWS, m) for m in far], beside))
    pair, evens = together((pair, jnp.stack([first] + high)))
    low, high = swap(evens, ROWS, 1), [swap(pair, ROWS, m) for m in far]
    other = swap(evens[:, m_first:], WIDTH, 1)
    other = [other, swap(other, ROWS, 1)]
    low, high, other, beside = together((low, high, other, finish_inputs(*beside)))
    second, first = jnp.concatenate([pair] + high), jnp.concatenate([evens, low])
    return second, first, jnp.concatenate(other), beside


def local(inputs, w_first, w_second, w_gate, w_tower, norm_scale, norm_shift, w_head, domains, labels):
    n_width, n_rows = lax.axis_size(WIDTH), lax.axis_size(ROWS)
    devices = n_width * n_rows
    own = inputs.shape[0] // n_width
    count = float(own * devices)
    dim = inputs.shape[1]
    epd, _, hid_n = w_first.shape
    out_n = w_second.shape[2]
    doms, _, exps = w_gate.shape
    ke = doms * exps
    n_x = n_width // 2
    others = list(range(1, n_x))
    w1 = (w_first, swap(w_first, WIDTH, 1))
    w2 = (w_second, swap(w_second, WIDTH, 1))
    wgate_t = jnp.transpose(w_gate, (0, 2, 1)).reshape(ke, dim)
    marks = jnp.stack([domains, labels])

    x_far, w1_own, w2_own, wt = prepare(others, inputs, w_first, w_second, wgate_t, w_tower, own)
    w1t, w2t = (w1_own, w1[1]), (w2_own, w2[1])
    far = forward([Near(x_far)], w1t, w2t, wt, own, doms, False, BF16, "forward_send")[0]
    sent = [swap(far[s - 1 : s], WIDTH, 2 * s) for s in others]
    blocks = [Far(inputs, (own, dim), row_blocks([0], own)), Near(x_far)]
    kept = forward(blocks, w1t, w2t, wt, own, doms, True, F32, "forward_keep")
    tower, low, message = combine(kept[5], sent, marks, devices)
    stats = lax.all_to_all(message, BOTH, 0, 0, tiled=True)
    stats, low = together((stats, low))
    lows = [swap(low, WIDTH, 2 * s) for s in others]
    params, message = normalise(stats, tower, marks, norm_scale, norm_shift, w_head, devices, count)
    sums = lax.all_to_all(message, BOTH, 0, 0, tiled=True)

    acts = [(kept[:5], s) for s in range(n_x)]
    grad_shift, grad_scale, loss, sec_sib, first_sib, sec_own, first_own, tow_sib, tow_own, pg, lg, w1_joined = backward(
        sums, params, tower, lows, marks, acts, inputs, w1, w2, wgate_t, w_tower, devices, n_rows, count
    )
    first_sib = swap(first_sib, WIDTH, 1)
    first_sib, sec_sib, tow_sib = together((first_sib, sec_sib, tow_sib))
    second, first, (gi_own, gi_out) = reduce_rows(
        (sec_own, swap(sec_sib, WIDTH, 1)),
        (first_own, first_sib),
        (tow_own, swap(tow_sib, WIDTH, 1)),
        (lambda grad: backward_inputs(grad, lg, w1_joined, wgate_t, own), pg),
    )
    inputs_got = [swap(gi_out[s - 1], WIDTH, 2 * s) for s in others]
    m_first = layout(epd, hid_n, out_n, dim, doms, n_rows)[1]
    second, first, other, grad_inputs = gather_rows(second, first, m_first, (gi_own, inputs_got))
    grad_first, grad_second, grad_tower, grad_gate, grad_head = finish_weights(
        second, first, other, epd, hid_n, out_n, dim, doms, exps, n_rows
    )
    return (
        loss[0, 0],
        grad_inputs,
        grad_first,
        grad_second,
        grad_gate.reshape(doms, exps, dim).transpose(0, 2, 1),
        grad_tower,
        grad_scale,
        grad_shift,
        grad_head,
    )


def solution(mesh):
    placed = (
        P(ROWS, None),
        P(WIDTH, None, None),
        P(WIDTH, None, None),
        P(),
        P(),
        P(),
        P(),
        P(),
        P(BOTH),
        P(BOTH),
    )
    return jax.shard_map(
        local,
        mesh=mesh,
        in_specs=placed,
        out_specs=(
            P(),
            P(BOTH, None),
            P(WIDTH, None, None),
            P(WIDTH, None, None),
            P(),
            P(),
            P(),
            P(),
            P(),
        ),
        check_vma=False,
    )
```
